32 devices in a mesh: seq: 8 (over z, y), row: 4 (over x, core).
Axes of the slice: x: 2, y: 2, z: 4, core: 2. Of those that a mesh axis runs over, the one named last changes fastest.
Arguments:
- tokens: bfloat16 [4, 1152, 1024], P('row', 'seq'), may hold values from -6 to 6
- attn_in: bfloat16 [2, 1024, 3072], P(None, ('seq', 'row')), may hold values from -0.1875 to 0.1875
- attn_out: bfloat16 [2, 1024, 1024], P(None, ('seq', 'row')), may hold values from -0.75 to 0.75
- ffn_up: bfloat16 [2, 1024, 4096], P(None, ('seq', 'row')), may hold values from -0.1875 to 0.1875
- ffn_down: bfloat16 [2, 4096, 1024], P(None, ('seq', 'row')), may hold values from -0.09375 to 0.09375
- norm_gains: bfloat16 [2, 2048], P(None, ('seq', 'row')), may hold values from 0.5 to 1.5
- biases: bfloat16 [2, 11264], P(None, ('seq', 'row')), may hold values from -1 to 1
- colbert: bfloat16 [1024, 128], P(('seq', 'row')), may hold values from -0.1875 to 0.1875
- log_scale: float32 [1], replicated, may hold values from 1.1 to 2.1
- cotangent: bfloat16 [4, 1152, 1024], P('row', 'seq'), may hold values from -6 to 6
- seg_lengths: int32 [4, 8], P('row'), may hold values from 1 to 1008, as said below
- seg_kinds: int32 [4, 8], P('row'), may hold values from 0 to 1, as said below
- pairing: int32 [4, 4], P('row'), may hold values from 0 to 3
Outputs:
- hidden_out: bfloat16 [4, 1152, 1024], P('row', 'seq')
- loss: float32 [1], replicated
- tokens_grad: float32 [4, 1152, 1024], P('row', 'seq')
- attn_in_grad: float32 [2, 1024, 3072], P(None, ('seq', 'row'))
- attn_out_grad: float32 [2, 1024, 1024], P(None, ('seq', 'row'))
- ffn_up_grad: float32 [2, 1024, 4096], P(None, ('seq', 'row'))
- ffn_down_grad: float32 [2, 4096, 1024], P(None, ('seq', 'row'))
- norm_gains_grad: float32 [2, 2048], P(None, ('seq', 'row'))
- biases_grad: float32 [2, 11264], P(None, ('seq', 'row'))
- colbert_grad: float32 [1024, 128], P(('seq', 'row'))
- log_scale_grad: float32 [1], replicated
The draws below stay inside these ranges and needn't reach their ends.
Inputs may be any that keep to these rules, and one draw needn't show every extreme that they name: `seg_lengths`: each row's lengths sum to 1152; every query segment has exactly 32 tokens; each row has one document of 1008 tokens that begins among the first 144 positions. `seg_kinds`: each row has exactly 4 query segments and 4 documents.
All inputs are finite; a program needn't handle non-finite values.
Results may differ from the reference program's by a relative error of at most 0.033.
Values may be sent and summed in bfloat16 or wider, within the bound.
No kernel may reach another device: no remote copies, remote signals or barrier semaphores. Data moves between devices by JAX's collectives and lax.ppermute only.
A program may use at most 320 MiB of HBM per device.

```python
import math
import jax
import jax.numpy as jnp
from jax import lax

D = 1024
HEADS = 16
FF = 4096
CB = 128
LAYERS = 2
QLEN = 32
NQ = 4
NSD = 3
TOK_DEV = 144
ROW_LEN = 1152
ROWS = 4
NDOC = 4
BIAS = 11264


def layout_rows(key):
    short_total = TOK_DEV - NQ * QLEN
    short_count = NQ + NSD

    def one_row(row_key):
        cut_key, order_key, split_key = jax.random.split(row_key, 3)
        cut_points = jnp.sort(jax.random.permutation(cut_key, short_total - 1)[:NSD - 1].astype(jnp.int32) + 1)
        edge_list = jnp.concatenate([jnp.zeros((1,), jnp.int32), cut_points, jnp.full((1,), short_total, jnp.int32)])
        doc_lengths = edge_list[1:] - edge_list[:-1]
        short_lengths = jnp.concatenate([jnp.full((NQ,), QLEN, jnp.int32), doc_lengths])
        short_kinds = jnp.concatenate([jnp.ones((NQ,), jnp.int32), jnp.zeros((NSD,), jnp.int32)])
        ordering = jax.random.permutation(order_key, short_count)
        placed_lengths = short_lengths[ordering]
        placed_kinds = short_kinds[ordering]
        split_at = jax.random.randint(split_key, (), 1, short_count).astype(jnp.int32)
        slot_index = jnp.arange(short_count + 1, dtype=jnp.int32)
        source_slot = jnp.clip(jnp.where(slot_index < split_at, slot_index, slot_index - 1), 0, short_count - 1)
        row_lengths = jnp.where(slot_index == split_at, ROW_LEN - TOK_DEV, placed_lengths[source_slot])
        row_kinds = jnp.where(slot_index == split_at, 0, placed_kinds[source_slot])
        return (row_lengths.astype(jnp.int32), row_kinds.astype(jnp.int32))
    return jax.vmap(one_row)(jax.random.split(key, ROWS))


def draw_seg_lengths(key, part):
    row_lengths, row_kinds = layout_rows(key)
    return row_lengths


def draw_seg_kinds(key, part):
    row_lengths, row_kinds = layout_rows(key)
    return row_kinds


def touch_ends(values, stream_key, smallest, high):
    longest = values.shape.index(max(values.shape))
    spots = []
    for shift in (0, 1):
        where = [jax.random.randint(jax.random.fold_in(stream_key, axis), (), 0, length) for axis, length in enumerate(values.shape)]
        where[longest] = (where[longest] + shift) % values.shape[longest]
        spots.append(tuple(where))
    return values.at[spots[0]].set(smallest).at[spots[1]].set(high)


def block_levels(rng, extent, shards, low, largest):
    factor_of, own = 1.0, jax.random.fold_in(rng, 6)
    for position, blocks in shards:
        steps = jnp.exp(jax.random.uniform(jax.random.fold_in(own, position), (blocks,), jnp.float32, low / len(shards), largest / len(shards)))
        factor_of = factor_of * jnp.repeat(steps, extent[position] // blocks).reshape([-1 if axis == position else 1 for axis in range(len(extent))])
    return factor_of


def scatter_about(stream_key, extent, spread, limit, cuts=(), kind=jnp.bfloat16):
    values = spread * jax.random.normal(stream_key, extent, jnp.float32)
    if cuts:
        values = values * block_levels(stream_key, extent, cuts, -0.22, 0.18)
    return jnp.clip(values, -limit, limit).astype(kind)


def setup_inputs(seed: int = 0) -> dict:
    key_list = jax.random.split(jax.random.key(seed), 14)
    return {
        "tokens": scatter_about(key_list[0], (ROWS, ROW_LEN, D), 1.0, 6.0, ((0, 4), (1, 8))),
        "attn_in": scatter_about(key_list[1], (LAYERS, D, 3 * D), D ** -0.5, 0.1875, ((1, 32),)),
        "attn_out": scatter_about(key_list[2], (LAYERS, D, D), (max(8, D * 64 // ROW_LEN)) ** -0.5, 0.75, ((1, 32),)),
        "ffn_up": scatter_about(key_list[3], (LAYERS, D, FF), D ** -0.5, 0.1875, ((1, 32),)),
        "ffn_down": scatter_about(key_list[4], (LAYERS, FF, D), FF ** -0.5, 0.09375, ((1, 32),)),
        "norm_gains": jnp.clip(1.0 + 0.1 * jax.random.normal(key_list[5], (LAYERS, 2 * D), jnp.float32), 0.5, 1.5).astype(jnp.bfloat16),
        "biases": scatter_about(key_list[6], (LAYERS, BIAS), 0.2, 1.0, ((1, 32),)),
        "colbert": scatter_about(key_list[7], (D, CB), D ** -0.5, 0.1875, ((0, 32),)),
        "log_scale": jnp.clip(jax.random.uniform(key_list[8], (1,), jnp.float32, 1.1, 2.1), 1.1, 2.1),
        "cotangent": scatter_about(key_list[9], (ROWS, ROW_LEN, D), 1.0, 6.0, ((0, 4), (1, 8))),
        "seg_lengths": draw_seg_lengths(jax.random.fold_in(key_list[13], 71), 0),
        "seg_kinds": draw_seg_kinds(jax.random.fold_in(key_list[13], 71), 0),
        "pairing": touch_ends(jax.random.randint(key_list[12], (ROWS, NQ), 0, NDOC), jax.random.fold_in(key_list[12], 1), 0, NDOC - 1).astype(jnp.int32),
    }


@jax.custom_vjp
def low(v):
    return lax.optimization_barrier(v.astype(jnp.bfloat16)).astype(jnp.float32)

@jax.custom_vjp
def low_back(v):
    return v

def low_keep(v):
    return (low(v), None)

def low_pass(kept, grad):
    return (grad,)

def back_keep(v):
    return (v, None)

def back_low(kept, grad):
    return (low(grad),)
low.defvjp(low_keep, low_pass)
low_back.defvjp(back_keep, back_low)
NEG_FILL = -1e+30
SHARPNESS = 16.0
HIGHEST = lax.Precision.HIGHEST

def matmul(left, right):
    return jnp.dot(left, right, precision=HIGHEST, preferred_element_type=jnp.float32)

def token_info(positions, lengths, kinds):
    ends = jnp.cumsum(lengths).astype(jnp.int32)
    starts = (ends - lengths).astype(jnp.int32)
    query_count = (jnp.cumsum(kinds) - kinds).astype(jnp.int32)
    doc_count = (jnp.cumsum(1 - kinds) - (1 - kinds)).astype(jnp.int32)
    segment = lax.optimization_barrier(jnp.sum((positions[:, None] >= ends[None, :]).astype(jnp.int32), axis=1)).astype(jnp.int32)
    onehot = segment[:, None] == jnp.arange(lengths.shape[0], dtype=jnp.int32)[None, :]
    nothing = jnp.zeros((), jnp.int32)
    seg_start = lax.optimization_barrier(jnp.sum(jnp.where(onehot, starts[None, :], nothing), axis=1))
    is_query = lax.optimization_barrier(jnp.sum(jnp.where(onehot, kinds[None, :], nothing), axis=1))
    query_num = lax.optimization_barrier(jnp.sum(jnp.where(onehot, query_count[None, :], nothing), axis=1))
    doc_num = lax.optimization_barrier(jnp.sum(jnp.where(onehot, doc_count[None, :], nothing), axis=1))
    offset = (positions - seg_start).astype(jnp.int32)
    return (segment, offset, is_query, (query_num * QLEN + offset).astype(jnp.int32), doc_num)

def rope_tables(offset, head_dim):
    half = head_dim // 2
    inverse = jnp.exp(jnp.arange(half, dtype=jnp.float32) * (-2.0 * math.log(10000.0) / head_dim))
    angle = offset.astype(jnp.float32)[:, None] * inverse[None, :]
    return (jnp.cos(angle), jnp.sin(angle))

def rotate(flat, cos_table, sin_table):
    length = flat.shape[0]
    head_dim = flat.shape[1] // HEADS
    half = head_dim // 2
    shaped = flat.reshape(length, HEADS, head_dim)
    first_half = shaped[..., :half]
    second_half = shaped[..., half:]
    cos_three = cos_table[:, None, :]
    sin_three = sin_table[:, None, :]
    turned = jnp.concatenate([first_half * cos_three - second_half * sin_three, second_half * cos_three + first_half * sin_three], axis=-1)
    return turned.reshape(length, flat.shape[1])

def layer_norm(rows, gain, shift):
    center = rows - lax.optimization_barrier(jnp.mean(rows, axis=-1, keepdims=True))
    variance = lax.optimization_barrier(jnp.mean(center * center, axis=-1, keepdims=True))
    return center * lax.rsqrt(variance + 1e-05) * gain + shift

def unit_rows(rows):
    return rows * lax.rsqrt(lax.optimization_barrier(jnp.sum(rows * rows, axis=-1, keepdims=True)) + 1e-06)

def ref_attention(queries, keys, values, segment):
    length, model_width = queries.shape
    head_dim = model_width // HEADS
    scale = head_dim ** (-0.5)
    block = 512 if length % 512 == 0 else length
    query_blocks = queries.reshape(length // block, block, HEADS, head_dim)
    seg_blocks = segment.reshape(length // block, block)
    key_three = keys.reshape(length, HEADS, head_dim)
    value_three = values.reshape(length, HEADS, head_dim)

    def one_block(item):
        query_blk, seg_blk = item
        scores = low_back(jnp.einsum('qhd,khd->hqk', query_blk, key_three, precision=HIGHEST) * scale)
        allowed = (seg_blk[:, None] == segment[None, :])[None]
        scores = jnp.where(allowed, scores, NEG_FILL)
        probs = jax.nn.softmax(scores, axis=-1)
        return jnp.einsum('hqk,khd->qhd', low(probs), value_three, precision=HIGHEST)
    result = lax.map(jax.checkpoint(one_block), (query_blocks, seg_blocks))
    return result.reshape(length, model_width)

def ref_layer(hidden, weights, info):
    w_in, w_out, w_up, w_down, gains, bias = weights
    segment, offset = (info[0], info[1])
    model_width = w_out.shape[0]
    hidden_units = w_up.shape[1]
    cos_table, sin_table = rope_tables(offset, model_width // HEADS)
    mixed = low_back(matmul(low(hidden), w_in) + bias[:3 * model_width])
    queries = low(rotate(mixed[:, :model_width], cos_table, sin_table))
    keys = low(rotate(mixed[:, model_width:2 * model_width], cos_table, sin_table))
    values = low(mixed[:, 2 * model_width:])
    context = low(low_back(ref_attention(queries, keys, values, segment)))
    branch = low_back(matmul(context, w_out) + bias[3 * model_width:4 * model_width])
    shift_one = bias[5 * model_width + hidden_units:6 * model_width + hidden_units]
    shift_two = bias[6 * model_width + hidden_units:]
    normed = layer_norm(hidden + branch, gains[:model_width], shift_one)
    pre_act = low_back(matmul(low(normed), w_up) + bias[4 * model_width:4 * model_width + hidden_units])
    act = low(jax.nn.gelu(pre_act, approximate=False))
    branch_two = low_back(matmul(act, w_down) + bias[4 * model_width + hidden_units:5 * model_width + hidden_units])
    return layer_norm(normed + branch_two, gains[model_width:], shift_two)

def ref_colbert(final, w_col, log_scale, info, pairs):
    segment, offset, is_query, query_slot, doc_num = info
    col = low_back(matmul(low(final), w_col))
    selector = ((is_query == 1)[None, :] & (query_slot[None, :] == jnp.arange(NQ * QLEN, dtype=jnp.int32)[:, None])).astype(jnp.float32)
    doc_mask = (is_query == 0)[:, None] & (doc_num[:, None] == jnp.arange(NSD + 1, dtype=jnp.int32)[None, :])
    positive = pairs[:, None] == jnp.arange(NSD + 1, dtype=jnp.int32)[None, :]
    scale = jnp.exp(log_scale[0])
    total = jnp.zeros((), jnp.float32)
    full_width = w_col.shape[1]
    for part_width in (full_width, full_width * 3 // 4, full_width // 2):
        embeds = low(unit_rows(col[:, :part_width]))
        query_emb = matmul(selector, embeds)
        sims = low_back(matmul(query_emb, embeds.T))
        scaled = jnp.where(doc_mask[None], SHARPNESS * sims[:, :, None], NEG_FILL)
        soft = jax.nn.logsumexp(scaled, axis=1) / SHARPNESS
        pair_sum = lax.optimization_barrier(jnp.sum(soft.reshape(NQ, QLEN, NSD + 1), axis=1))
        logits = pair_sum * scale / QLEN
        losses = jax.nn.logsumexp(logits, axis=-1) - lax.optimization_barrier(jnp.sum(jnp.where(positive, logits, 0.0), axis=-1))
        total = total + jnp.sum(losses)
    return total

def row_forward(params, inputs, info, pairs):
    attn_in, attn_out, ffn_up, ffn_down, norm_gains, biases, colbert, log_scale = params
    hidden = inputs
    for layer_index in range(LAYERS):
        weights = (attn_in[layer_index], attn_out[layer_index], ffn_up[layer_index], ffn_down[layer_index], norm_gains[layer_index], biases[layer_index])
        hidden = ref_layer(hidden, weights, info)
    return (hidden, ref_colbert(hidden, colbert, log_scale, info, pairs))

def reference(tokens, attn_in, attn_out, ffn_up, ffn_down, norm_gains, biases, colbert, log_scale, cotangent, seg_lengths, seg_kinds, pairing):
    params = tuple((item.astype(jnp.float32) for item in (attn_in, attn_out, ffn_up, ffn_down, norm_gains, biases, colbert))) + (log_scale.astype(jnp.float32),)
    positions = jnp.arange(ROW_LEN, dtype=jnp.int32)
    loss_weight = 1.0 / (3 * NQ * ROWS)
    grad_sum = None
    loss_total = jnp.zeros((), jnp.float32)
    outputs = []
    input_grads = []
    for row in range(ROWS):
        info = token_info(positions, seg_lengths[row], seg_kinds[row])
        pairs = pairing[row]

        def forward(weights, inputs):
            return row_forward(weights, inputs, info, pairs)
        (final, row_loss), pull = jax.vjp(forward, params, tokens[row].astype(jnp.float32))
        weight_grads, grad_inputs = pull((cotangent[row].astype(jnp.float32), jnp.ones_like(row_loss) * loss_weight))
        grad_sum = weight_grads if grad_sum is None else jax.tree.map(lambda left, right: left + right, grad_sum, weight_grads)
        loss_total = loss_total + row_loss * loss_weight
        outputs.append(final.astype(jnp.bfloat16))
        input_grads.append(grad_inputs)
    return (jnp.stack(outputs), loss_total.reshape(1), jnp.stack(input_grads), grad_sum[0], grad_sum[1], grad_sum[2], grad_sum[3], grad_sum[4], grad_sum[5], grad_sum[6], grad_sum[7])
```

```python
import math

import jax
import jax.numpy as jnp
from jax import lax
from jax.experimental import pallas as pl
from jax.experimental.pallas import tpu as pltpu
from jax.sharding import PartitionSpec as P

HEADS = 16
QLEN = 32
NQ = 4
NSD = 3

NEG_FILL = -1e30
SHARPNESS = 16.0
HIGHEST = lax.Precision.HIGHEST
BF = jnp.bfloat16
F32 = jnp.float32

def dot(left, right):
    return jnp.dot(left, right, preferred_element_type=F32)


def dot_lt(left, right):
    return lax.dot_general(left, right, (((0,), (0,)), ((), ())), preferred_element_type=F32)


def dot_rt(left, right):
    return lax.dot_general(left, right, (((1,), (1,)), ((), ())), preferred_element_type=F32)


PLANE = 8
BOTH = ("seq", "row")


def across(x, mask):
    size = lax.axis_size("seq") * lax.axis_size("row")
    return lax.ppermute(x, BOTH, [(d, d ^ mask) for d in range(size)])


def turned(x):
    size = lax.axis_size("seq") * lax.axis_size("row")
    rows = lax.axis_size("row")
    pairs = []
    for d in range(size):
        o, i, r = d // PLANE, d % PLANE // rows, d % rows
        pairs.append((d, r * PLANE + i * rows + o))
    return lax.ppermute(x, BOTH, pairs)


def plane_gather(x):
    other = {0: x, 2: across(x, 2), 4: across(x, 4), 6: across(x, 6)}
    return jnp.stack([other[k & 6] if k % 2 == 0 else across(other[k & 6], 1) for k in range(PLANE)])


def plane_scatter(parts):
    parts = parts.astype(BF)
    core = across(parts[1::2], 1).astype(F32) + parts[0::2].astype(F32)
    sent = core[1:].astype(BF)
    return core[0] + sum(across(sent[k - 1], 2 * k).astype(F32) for k in (1, 2, 3))


def plane_exchange(x, relative):
    x = jnp.take(x, relative, axis=0)
    core = across(x[1::2], 1)
    mine = [x[0], core[0]]
    for k in (1, 2, 3):
        got = across(jnp.stack([x[2 * k], core[k]]), 2 * k)
        mine += [got[0], got[1]]
    return jnp.take(jnp.stack(mine), relative, axis=0)


def tie(*values):
    return lax.optimization_barrier(values)


def token_info(positions, lengths, kinds):
    ends = jnp.cumsum(lengths)
    starts = ends - lengths
    query_count = jnp.cumsum(kinds) - kinds
    doc_count = jnp.cumsum(1 - kinds) - (1 - kinds)
    segment = jnp.sum((positions[:, None] >= ends[None, :]).astype(jnp.int32), axis=1)
    onehot = segment[:, None] == jnp.arange(lengths.shape[0], dtype=jnp.int32)[None, :]
    nothing = jnp.zeros((), jnp.int32)
    seg_start = jnp.sum(jnp.where(onehot, starts[None, :], nothing), axis=1)
    is_query = jnp.sum(jnp.where(onehot, kinds[None, :], nothing), axis=1)
    query_num = jnp.sum(jnp.where(onehot, query_count[None, :], nothing), axis=1)
    doc_num = jnp.sum(jnp.where(onehot, doc_count[None, :], nothing), axis=1)
    offset = positions - seg_start
    return (segment, offset, is_query, query_num * QLEN + offset, doc_num)


def rope_lanes(offset, head_dim):
    half = head_dim // 2
    inverse = jnp.exp(jnp.arange(half, dtype=F32) * (-2.0 * math.log(10000.0) / head_dim))
    angle = offset.astype(F32)[:, None] * inverse[None, :]
    cos, sin = jnp.cos(angle), jnp.sin(angle)
    return (
        jnp.concatenate([cos, cos, cos, cos], axis=1),
        jnp.concatenate([-sin, -sin, sin, sin], axis=1),
    )


def swap_halves(x):
    half = x.shape[-1] // 2
    return jnp.concatenate([x[..., half:], x[..., :half]], axis=-1)


def layer_norm(rows, gain, shift):
    center = rows - jnp.mean(rows, axis=-1, keepdims=True)
    variance = jnp.mean(center * center, axis=-1, keepdims=True)
    return center * lax.rsqrt(variance + 1e-05) * gain + shift


def unit_rows(rows):
    return rows * lax.rsqrt(jnp.sum(rows * rows, axis=-1, keepdims=True) + 1e-06)


def exact_gelu(values):
    return jax.nn.gelu(values, approximate=False)


def head_masks(width):
    lane = lax.broadcasted_iota(jnp.int32, (1, width), 1)
    first_qk = (lane % (width // 2)) < (width // 4)
    first_v = lane < (width // 2)
    return first_qk, first_v


def pair_probs(query, keys, allowed, scale):
    scores = dot_rt(query, keys) * scale
    scores = jnp.where(allowed, scores, NEG_FILL)
    top = jnp.max(scores, axis=-1, keepdims=True)
    weights = jnp.exp(scores - top)
    return weights / jnp.sum(weights, axis=-1, keepdims=True)


def pair_forward(query, keys, values, allowed, scale):
    first_qk, first_v = head_masks(query.shape[1])
    zero = jnp.zeros((), query.dtype)
    outs = []
    for head in range(2):
        mine = first_qk if head == 0 else jnp.logical_not(first_qk)
        probs = pair_probs(jnp.where(mine, query, zero), keys, allowed, scale)
        outs.append(dot(probs.astype(BF), values))
    return jnp.where(first_v, outs[0], outs[1])


def pair_backward(query, keys, values, grad, allowed, scale):
    first_qk, first_v = head_masks(query.shape[1])
    zero = jnp.zeros((), query.dtype)
    grad_query, grad_keys, grad_values = [], 0.0, 0.0
    for head in range(2):
        mine = first_qk if head == 0 else jnp.logical_not(first_qk)
        mine_v = first_v if head == 0 else jnp.logical_not(first_v)
        query_h = jnp.where(mine, query, zero)
        grad_h = jnp.where(mine_v, grad, zero)
        probs = pair_probs(query_h, keys, allowed, scale)
        grad_probs = dot_rt(grad_h, values)
        delta = jnp.sum(probs * grad_probs, axis=-1, keepdims=True)
        grad_scores = (probs * (grad_probs - delta)).astype(BF)
        grad_query.append(dot(grad_scores, keys))
        grad_keys = grad_keys + dot_lt(grad_scores, query_h)
        grad_values = grad_values + dot_lt(probs.astype(BF), grad_h)
    return (
        jnp.where(first_qk, grad_query[0], grad_query[1]) * scale,
        grad_keys * scale,
        grad_values,
    )


def block_of(count):
    for blocks in (3, 4, 2):
        if count % (blocks * 128) == 0 and count // blocks <= 512:
            return count // blocks
    return 128


def attend_kernel(scale, seg_q, seg_k, query, keys, values, out):
    allowed = seg_q[...] == seg_k[...]
    out[...] = pair_forward(query[...], keys[...], values[...], allowed, scale).astype(out.dtype)


def attend(qkv, seg_col, seg_row, scale):
    count = qkv.shape[0]
    wide = qkv.shape[1] // 3
    block = block_of(count)

    def kernel(seg_q, seg_k, query, keys, values, out):
        attend_kernel(scale, seg_q, seg_k, query, keys, values, out)

    return pl.pallas_call(
        kernel,
        grid=(count // block,),
        in_specs=[
            pl.BlockSpec((block, 1), lambda i: (i, 0)),
            pl.BlockSpec((1, count), lambda i: (0, 0)),
            pl.BlockSpec((block, wide), lambda i: (i, 0)),
            pl.BlockSpec((count, wide), lambda i: (0, 1)),
            pl.BlockSpec((count, wide), lambda i: (0, 2)),
        ],
        out_specs=pl.BlockSpec((block, wide), lambda i: (i, 0)),
        out_shape=jax.ShapeDtypeStruct((count, wide), BF),
        compiler_params=pltpu.CompilerParams(vmem_limit_bytes=40 * 1024 * 1024),
        cost_estimate=pl.CostEstimate(
            flops=8 * count * count * wide, bytes_accessed=8 * count * wide, transcendentals=2 * count * count
        ),
    )(seg_col, seg_row, qkv, qkv, qkv)


def attend_back(qkv, grad, seg_col, seg_row, cos, sin, scale):
    count = qkv.shape[0]
    wide = qkv.shape[1] // 3
    block = block_of(count)
    steps = count // block

    def kernel(seg_q, seg_k, query, keys, values, grad_ref, cos_b, sin_b, cos_all, sin_all, dq, dk, dv, acc_k, acc_v):
        step = pl.program_id(0)
        allowed = seg_q[...] == seg_k[...]
        grad_query, grad_keys, grad_values = pair_backward(
            query[...], keys[...], values[...], grad_ref[...], allowed, scale
        )
        dq[...] = (grad_query * cos_b[...] - swap_halves(grad_query) * sin_b[...]).astype(BF)

        @pl.when(step == 0)
        def _():
            acc_k[...] = grad_keys
            acc_v[...] = grad_values

        @pl.when(step > 0)
        def _():
            acc_k[...] += grad_keys
            acc_v[...] += grad_values

        @pl.when(step == steps - 1)
        def _():
            total = acc_k[...]
            dk[...] = (total * cos_all[...] - swap_halves(total) * sin_all[...]).astype(BF)
            dv[...] = acc_v[...].astype(BF)

    whole = pl.BlockSpec((count, wide), lambda i: (0, 0))
    part = pl.BlockSpec((block, wide), lambda i: (i, 0))
    return pl.pallas_call(
        kernel,
        grid=(steps,),
        in_specs=[
            pl.BlockSpec((block, 1), lambda i: (i, 0)),
            pl.BlockSpec((1, count), lambda i: (0, 0)),
            part,
            pl.BlockSpec((count, wide), lambda i: (0, 1)),
            pl.BlockSpec((count, wide), lambda i: (0, 2)),
            part,
            part,
            part,
            whole,
            whole,
        ],
        out_specs=(part, whole, whole),
        out_shape=tuple(jax.ShapeDtypeStruct((count, wide), BF) for _ in range(3)),
        scratch_shapes=[pltpu.VMEM((count, wide), F32), pltpu.VMEM((count, wide), F32)],
        compiler_params=pltpu.CompilerParams(vmem_limit_bytes=48 * 1024 * 1024),
        cost_estimate=pl.CostEstimate(
            flops=20 * count * count * wide, bytes_accessed=20 * count * wide, transcendentals=2 * count * count
        ),
    )(seg_col, seg_row, qkv, qkv, qkv, grad, cos, sin, cos, sin)


def body(
    tokens,
    attn_in,
    attn_out,
    ffn_up,
    ffn_down,
    norm_gains,
    biases,
    colbert,
    log_scale,
    cotangent,
    seg_lengths,
    seg_kinds,
    pairing,
):
    S = lax.axis_size("seq")
    R = lax.axis_size("row")
    O = S * R // PLANE
    place = lax.axis_index("seq") * R + lax.axis_index("row")
    plane, far = place % PLANE, place // PLANE
    relative = jnp.bitwise_xor(plane, jnp.arange(PLANE, dtype=jnp.int32))
    T = tokens.shape[1]
    D = tokens.shape[2]
    N = PLANE * T
    L = attn_in.shape[0]
    head_dim = D // HEADS
    half = head_dim // 2
    scale = head_dim ** (-0.5)
    wide = 2 * head_dim
    in_cols = 3 * wide
    in_rows = attn_in.shape[1]
    rows_in = PLANE * in_rows
    FF = ffn_up.shape[2]
    up_cols = FF // (S * R)
    hidden_cols = O * up_cols
    gain_part = norm_gains.shape[1]
    bias_part = biases.shape[1]
    part = gain_part + bias_part
    along_z = [[o * (S // O) + i for o in range(O)] for i in range(S // O)]
    is_mine = jnp.arange(PLANE, dtype=jnp.int32) == plane

    def padded_rows(vector, width=D):
        rows = -(-vector.shape[0] // (16 * width)) * 16
        return jnp.pad(vector, (0, rows * width - vector.shape[0])).reshape(rows, width)

    def pack_columns(w):
        lead = w.shape[:-1]
        n = len(lead)
        qk = w[..., : 2 * D].reshape(*lead, 2, PLANE, 2, 2, half)
        qk = qk.transpose((n + 1,) + tuple(range(n)) + (n, n + 3, n + 2, n + 4)).reshape(PLANE, *lead, 2 * wide)
        v = w[..., 2 * D :].reshape(*lead, PLANE, wide)
        v = v.transpose((n,) + tuple(range(n)) + (n + 1,))
        return jnp.concatenate([qk, v], axis=-1)

    def unpack_columns(w):
        rows = w.shape[1]
        qk = w[:, :, : 2 * wide].reshape(PLANE, rows, 2, 2, 2, half)
        qk = qk.transpose(1, 2, 0, 4, 3, 5).reshape(rows, 2 * D)
        v = w[:, :, 2 * wide :].transpose(1, 0, 2).reshape(rows, D)
        return jnp.concatenate([qk, v], axis=1)

    def pack_hidden(w):
        rows = w.shape[0]
        return w.reshape(rows, O, PLANE, up_cols).transpose(2, 0, 1, 3).reshape(PLANE, rows, hidden_cols)

    def unpack_hidden(w):
        rows = w.shape[1]
        return w.reshape(PLANE, rows, O, up_cols).transpose(1, 2, 0, 3).reshape(rows, FF)

    def fold(w):
        n = w.shape[-2] // 2
        return jnp.concatenate([w[..., :n, :], w[..., n:, :]], axis=-1)

    def unfold(w):
        n = w.shape[-1] // 2
        return jnp.concatenate([w[..., :n], w[..., n:]], axis=-2)

    shard_in = [plane_exchange(pack_columns(attn_in[0]), relative).reshape(rows_in, in_cols)]
    small = jnp.concatenate(
        [norm_gains.reshape(-1), biases.reshape(-1), colbert.reshape(-1)]
    )
    count_small = L * part
    small = jnp.take(plane_gather(small), relative, axis=0)
    params_plane = jnp.concatenate(
        [
            small[:, : L * gain_part].reshape(PLANE, L, gain_part),
            small[:, L * gain_part : count_small].reshape(PLANE, L, bias_part),
        ],
        axis=2,
    ).reshape(-1)
    col_plane = small[:, count_small:].reshape(-1)
    to_group = [(b, (b % O) * PLANE + b // O) for b in range(O * PLANE)]
    from_group = [(d, b) for b, d in to_group]
    shard_out = lax.ppermute(attn_out, BOTH, to_group)
    table = turned(jnp.concatenate([seg_lengths[0], seg_kinds[0], pairing[0]]))
    seg_count = seg_lengths.shape[1]
    lengths, kinds = table[:seg_count], table[seg_count : 2 * seg_count]
    pairs_of = table[2 * seg_count :]
    hidden_low = turned(tokens[0])

    def gather_far(parts):
        return lax.all_gather(jnp.concatenate(parts, axis=0), "seq", axis=0, axis_index_groups=along_z)

    rest = jnp.concatenate(
        [pack_hidden(ffn_up[0])]
        + [piece for layer in range(1, L) for piece in (pack_columns(attn_in[layer]), pack_hidden(ffn_up[layer]))],
        axis=-1,
    )
    rest = plane_exchange(rest, relative).reshape(rows_in, -1)
    shard_up = [rest[:, :hidden_cols]]
    at = hidden_cols
    for layer in range(1, L):
        shard_in.append(rest[:, at : at + in_cols])
        shard_up.append(rest[:, at + in_cols : at + in_cols + hidden_cols])
        at += in_cols + hidden_cols

    def attn_block(layer):
        out = shard_out[layer].reshape(in_rows, PLANE, wide).transpose(1, 0, 2).reshape(rows_in, wide)
        return jnp.concatenate([shard_in[layer], out], axis=1)

    w_ins, w_outs, w_ups, w_downs = [], [], [], []
    for layer in range(L):
        own = [attn_block(layer)]
        if layer == 0:
            own.append(padded_rows(params_plane, in_cols + wide))
        full = gather_far(own)
        w_ins.append(full[:, :rows_in, :in_cols].reshape(D, in_cols))
        w_out = full[:, :rows_in, in_cols:].reshape(O, PLANE, in_rows, wide).transpose(0, 2, 1, 3)
        w_outs.append(w_out.reshape(wide, D))
        if layer == 0:
            params = full[:, rows_in:].reshape(O, -1)[:, : PLANE * L * part].reshape(O, PLANE, L, part)
        own = [fold(shard_up[layer]), ffn_down[layer]]
        if layer == L - 1:
            own.append(padded_rows(col_plane))
        full = gather_far(own)
        w_ups.append(unfold(full[:, : rows_in // 2]).reshape(D, hidden_cols))
        w_downs.append(full[:, rows_in // 2 : rows_in // 2 + up_cols].reshape(hidden_cols, D))
        if layer == L - 1:
            w_col = full[:, rows_in // 2 + up_cols :].reshape(O, -1)[:, : col_plane.size]
            w_col = w_col.reshape(D, colbert.shape[1])
    params = params.transpose(2, 0, 1, 3).astype(F32)
    gains_all = params[..., :gain_part].reshape(L, D * 2)
    bias_all = params[..., gain_part:].reshape(L, S * R * bias_part)

    block_at = (relative % R) * (PLANE // R) + relative // R
    positions = (block_at[:, None] * T + jnp.arange(T, dtype=jnp.int32)[None, :]).reshape(N)
    held_segment, held_offset = token_info(positions, lengths, kinds)[:2]
    cos, sin = rope_lanes(held_offset, head_dim)
    seg_col, seg_row = held_segment[:, None], held_segment[None, :]

    def layer_params(layer):
        bias = bias_all[layer]
        gains = gains_all[layer]
        bias_in = jnp.take(pack_columns(bias[: 3 * D]), plane, axis=0)
        bias_up = jnp.take(pack_hidden(bias[None, 4 * D : 4 * D + FF]), plane, axis=0)[0]
        rest_at = 4 * D + FF
        return (
            gains[:D],
            gains[D:],
            bias_in,
            bias[3 * D : 4 * D],
            bias_up,
            bias[rest_at : rest_at + D],
            bias[rest_at + D : rest_at + 2 * D],
            bias[rest_at + 2 * D :],
        )

    def gathered(x):
        return plane_gather(x).reshape(N, x.shape[1])

    def scattered(x):
        return plane_scatter(x.reshape(PLANE, T, D))

    hidden = hidden_low.astype(F32)
    records = []
    for layer in range(L):
        gain_one, gain_two, bias_in, bias_out, bias_up, bias_down, shift_one, shift_two = layer_params(layer)
        x_all = gathered(hidden_low)
        mixed = (dot(x_all, w_ins[layer]) + bias_in).reshape(N, 3, wide)
        qk = mixed[:, :2]
        qk = qk * cos[:, None] + swap_halves(qk) * sin[:, None]
        qkv = jnp.concatenate([qk, mixed[:, 2:]], axis=1).astype(BF).reshape(N, in_cols)
        context = attend(qkv, seg_col, seg_row, scale)
        first = hidden + scattered(dot(context, w_outs[layer])) + bias_out
        normed = layer_norm(first, gain_one, shift_one)
        normed_all = gathered(normed.astype(BF))
        pre = dot(normed_all, w_ups[layer]) + bias_up
        act = exact_gelu(pre).astype(BF)
        second = normed + scattered(dot(act, w_downs[layer])) + bias_down
        records.append((x_all, qkv, context, first, normed_all, pre, act, second))
        hidden = layer_norm(second, gain_two, shift_two)
        hidden_low = hidden.astype(BF)
    hidden_out = turned(hidden_low)

    full_width = w_col.shape[1]
    part_widths = (full_width, full_width * 3 // 4, full_width // 2)
    query_total = NQ * QLEN
    doc_total = NSD + 1
    col = dot(hidden_low, w_col)
    in_order = jnp.arange(PLANE, dtype=jnp.int32)
    in_order = jnp.bitwise_xor((in_order % (PLANE // R)) * R + in_order // (PLANE // R), plane)
    col_row = jnp.take(plane_gather(col.astype(BF)), in_order, axis=0).reshape(N, full_width).astype(F32)
    own_at = block_at[0] * T
    row_positions = jnp.arange(N, dtype=jnp.int32)
    segment, offset, is_query, query_slot, doc_num = token_info(row_positions, lengths, kinds)
    slots = jnp.arange(query_total, dtype=jnp.int32)[:, None]
    selector = (is_query == 1)[None, :] & (query_slot[None, :] == slots)
    selector_low = selector.astype(BF)
    own_selector = lax.dynamic_slice(selector.astype(F32), (0, own_at), (query_total, T))
    embeds = [unit_rows(col_row[:, :width]).astype(BF) for width in part_widths]
    query_emb = [dot(selector_low, embed).astype(BF) for embed in embeds]
    powers = jnp.exp(SHARPNESS * jnp.stack([dot_rt(query_emb[m], embeds[m]) for m in range(3)]))
    doc_code = jnp.where(is_query == 0, doc_num, -1)[None, None, :]
    totals = jnp.stack([jnp.sum(jnp.where(doc_code == d, powers, 0.0), axis=2) for d in range(doc_total)], axis=2)
    soft = jnp.log(totals) / SHARPNESS
    pair_sum = jnp.sum(soft.reshape(3, NQ, QLEN, doc_total), axis=2)
    inverse_temp = jnp.exp(log_scale[0])
    logits = pair_sum * inverse_temp / QLEN
    positive = pairs_of[None, :, None] == jnp.arange(doc_total, dtype=jnp.int32)[None, None, :]
    losses = jax.nn.logsumexp(logits, axis=-1) - jnp.sum(jnp.where(positive, logits, 0.0), axis=-1)
    loss_weight = 1.0 / (3 * NQ * R)
    grad_logits = loss_weight * (jax.nn.softmax(logits, axis=-1) - positive.astype(F32))
    loss_terms = jnp.stack([jnp.sum(losses) * loss_weight, jnp.sum(grad_logits * logits)])
    loss_terms = loss_terms + across(loss_terms, PLANE)
    loss_terms = loss_terms + across(loss_terms, 2 * PLANE)
    grad_pairs = grad_logits * inverse_temp / QLEN
    grad_soft = jnp.broadcast_to(grad_pairs[:, :, None, :], (3, NQ, QLEN, doc_total)).reshape(
        3, query_total, doc_total
    )
    ratio = grad_soft / totals
    weight = sum(jnp.where(doc_code == d, ratio[:, :, d : d + 1], 0.0) for d in range(doc_total))
    grad_sims = (powers * weight).astype(BF)
    own_sims = lax.dynamic_slice(grad_sims, (0, 0, own_at), (3, query_total, T))
    grad_col = jnp.zeros((T, full_width), F32)
    for m in range(3):
        width = part_widths[m]
        grad_query = dot(grad_sims[m], embeds[m])
        grad_embed = dot_lt(own_sims[m], query_emb[m]) + lax.dot_general(
            own_selector, grad_query, (((0,), (0,)), ((), ())), precision=HIGHEST, preferred_element_type=F32
        )
        pull_unit = jax.vjp(unit_rows, col[:, :width])[1]
        grad_col = grad_col + jnp.pad(pull_unit(grad_embed)[0], ((0, 0), (0, full_width - width)))
    grad_col_low = grad_col.astype(BF)
    col_parts = dot_lt(hidden_low, grad_col_low).reshape(O, PLANE, in_rows, full_width).transpose(1, 0, 2, 3)
    col_parts = plane_scatter(jnp.take(col_parts.reshape(PLANE, O * in_rows, full_width), relative, axis=0))
    col_rows = jax.vmap(padded_rows)(col_parts.reshape(O, in_rows * full_width)).astype(BF)
    grad_hidden = turned(cotangent[0]).astype(F32) + dot_rt(grad_col_low, w_col)

    def joined_blocks(parts):
        return jnp.concatenate([item.astype(BF) for item in parts], axis=1)

    def scatter_far(whole):
        whole = whole.reshape(-1, whole.shape[-1])
        return lax.psum_scatter(whole, "seq", scatter_dimension=0, tiled=True, axis_index_groups=along_z)

    def scatter_far_direct(whole):
        total = jnp.take(whole, far, axis=0).astype(F32)
        for step in range(1, O):
            total = total + across(jnp.take(whole, far ^ step, axis=0), PLANE * step).astype(F32)
        return total

    outs = [[None] * L for _ in range(7)]

    def finish_ffn(layer, shares):
        back_up = plane_exchange(unfold(shares[: rows_in // 2]).reshape(PLANE, in_rows, hidden_cols), relative)
        outs[2][layer] = unpack_hidden(back_up).astype(F32)
        at = rows_in // 2 + up_cols
        outs[3][layer] = shares[rows_in // 2 : at].astype(F32)
        outs[1][layer] = lax.ppermute(shares[at : at + in_rows], BOTH, from_group).astype(F32)
        if layer == L - 1:
            col_share = shares[at + in_rows :].reshape(-1)[: in_rows * full_width]
            outs[6][layer] = col_share.reshape(in_rows, full_width).astype(F32)

    def finish_in(layer, shares):
        vector = shares[rows_in:].reshape(-1)[: PLANE * part].reshape(PLANE, part)
        vector = plane_scatter(jnp.take(vector, relative, axis=0))
        outs[4][layer] = vector[:gain_part]
        outs[5][layer] = vector[gain_part:]
        back_in = plane_exchange(shares[:rows_in].astype(BF).reshape(PLANE, in_rows, in_cols), relative)
        outs[0][layer] = unpack_columns(back_in).astype(F32)

    shares_in = None
    for layer in reversed(range(L)):
        gain_one, gain_two, bias_in, bias_out, bias_up, bias_down, shift_one, shift_two = layer_params(layer)
        x_all, qkv, context, first, normed_all, pre, act, second = records[layer]
        pull_two = jax.vjp(layer_norm, second, gain_two, shift_two)[1]
        grad_second, grad_gain_two, grad_shift_two = pull_two(grad_hidden)
        grad_ffo = grad_second.astype(BF)
        grad_bias_down = jnp.sum(grad_ffo.astype(F32), axis=0)
        ffo_all = gathered(grad_ffo)
        grad_act = dot_rt(ffo_all, w_downs[layer])
        pull_gelu = jax.vjp(exact_gelu, pre)[1]
        grad_pre = pull_gelu(grad_act)[0].astype(BF)
        grad_bias_up = jnp.sum(grad_pre.astype(F32), axis=0)
        grad_normed = grad_second + scattered(dot_rt(grad_pre, w_ups[layer]))
        pull_one = jax.vjp(layer_norm, first, gain_one, shift_one)[1]
        grad_first, grad_gain_one, grad_shift_one = pull_one(grad_normed)
        grad_branch = grad_first.astype(BF)
        grad_bias_out = jnp.sum(grad_branch.astype(F32), axis=0)
        branch_all = gathered(grad_branch)
        grad_context = dot_rt(branch_all, w_outs[layer]).astype(BF)
        blocks = [
            fold(dot_lt(normed_all, grad_pre).reshape(O, rows_in, hidden_cols)),
            dot_lt(act, ffo_all).reshape(O, up_cols, D),
            dot_lt(context, branch_all).reshape(O, in_rows, D),
        ]
        if layer == L - 1:
            blocks.append(col_rows)
        grad_context, blocks = tie(grad_context, joined_blocks(blocks))
        shares_ffn = scatter_far(blocks)
        if shares_in is not None:
            grad_context, shares_in = tie(grad_context, shares_in)
            finish_in(layer + 1, shares_in)
        dq, dk, dv = attend_back(qkv, grad_context, seg_col, seg_row, cos, sin, scale)
        grad_mixed = jnp.concatenate([dq, dk, dv], axis=1)
        grad_hidden = grad_first + scattered(dot_rt(grad_mixed, w_ins[layer]))
        grad_bias_in = jnp.sum(grad_mixed.astype(F32), axis=0)
        if layer > 0:
            grad_hidden, shares_ffn = tie(grad_hidden, shares_ffn)
        finish_ffn(layer, shares_ffn)

        spot = is_mine[:, None, None].astype(F32)
        natural = unpack_columns(spot * grad_bias_in.reshape(1, 1, in_cols))[0]
        spread_up = unpack_hidden(spot * grad_bias_up.reshape(1, 1, hidden_cols))[0]
        vector_gain = jnp.concatenate([grad_gain_one, grad_gain_two]).reshape(O, PLANE, gain_part)
        vector_bias = jnp.concatenate(
            [natural, grad_bias_out, spread_up, grad_bias_down, grad_shift_one, grad_shift_two]
        ).reshape(O, PLANE, bias_part)
        vector = jnp.concatenate([vector_gain, vector_bias], axis=2).reshape(O, PLANE * part)
        grad_in = dot_lt(x_all, grad_mixed).reshape(O, rows_in, in_cols)
        blocks = joined_blocks([grad_in, jax.vmap(lambda row: padded_rows(row, in_cols))(vector)])
        grad_hidden, blocks = tie(grad_hidden, blocks)
        if layer > 0:
            shares_in = scatter_far(blocks)
    finish_in(0, scatter_far_direct(blocks))
    col_share = outs.pop()[L - 1]
    stacked = [jnp.stack(items) for items in outs]
    return (
        hidden_out[None],
        loss_terms[:1],
        turned(grad_hidden.astype(BF)).astype(F32)[None],
        stacked[0],
        stacked[1],
        stacked[2],
        stacked[3],
        stacked[4],
        stacked[5],
        col_share,
        loss_terms[1:],
    )


def joined_2(value, axis, join):
    pieces = jax.tree.map(lambda part: lax.all_gather(part, axis), value)
    head = jax.tree.map(lambda part: part[0], pieces)
    tail = jax.tree.map(lambda part: part[1:], pieces)
    so_far, _ = lax.scan(lambda so_far, section: (join(so_far, section), None), head, tail)
    return so_far


def rope_tables(offset, head_dim):
    half = head_dim // 2
    inverse = jnp.exp(jnp.arange(half, dtype=jnp.float32) * (-2.0 * math.log(10000.0) / head_dim))
    angle = offset.astype(jnp.float32)[:, None] * inverse[None, :]
    return (jnp.cos(angle), jnp.sin(angle))


def rotate(flat, cos_table, sin_table):
    length = flat.shape[0]
    head_dim = flat.shape[1] // HEADS
    half = head_dim // 2
    shaped = flat.reshape(length, HEADS, head_dim)
    first_half = shaped[..., :half]
    second_half = shaped[..., half:]
    cos_three = cos_table[:, None, :]
    sin_three = sin_table[:, None, :]
    turned = jnp.concatenate(
        [
            first_half * cos_three - second_half * sin_three,
            second_half * cos_three + first_half * sin_three,
        ],
        axis=-1,
    )
    return turned.reshape(length, flat.shape[1])


def block_for(count):
    blocks = count
    while blocks > 1024 and blocks % 2 == 0:
        blocks = blocks // 2
    return blocks


def merge_pair(first, second):
    max_first, sum_first = first
    max_second, sum_second = second
    top = jnp.maximum(max_first, max_second)
    return (top, sum_first * jnp.exp(max_first - top) + sum_second * jnp.exp(max_second - top))


def matmul_left_t(left, right):
    return jnp.einsum("ti,to->io", left, right, preferred_element_type=jnp.float32)


def matmul_right_t(left, right):
    return jnp.einsum("to,io->ti", left, right, preferred_element_type=jnp.float32)


def body_wide(
    tokens,
    attn_in,
    attn_out,
    ffn_up,
    ffn_down,
    norm_gains,
    biases,
    colbert,
    log_scale,
    cotangent,
    seg_lengths,
    seg_kinds,
    pairing,
):
    rank = lax.axis_index("seq")
    local_len = tokens.shape[1]
    model_width = tokens.shape[2]
    head_dim = model_width // HEADS
    scale = head_dim ** (-0.5)
    lengths = seg_lengths[0]
    kinds = seg_kinds[0]
    positions = rank * local_len + jnp.arange(local_len, dtype=jnp.int32)
    segment, offset, is_query, query_slot, doc_num = token_info(positions, lengths, kinds)
    cos_table, sin_table = rope_tables(offset, head_dim)
    layer_count = attn_in.shape[0]

    def split_pieces(key_piece, value_piece):
        count = key_piece.shape[0]
        blocks = block_for(count)
        key_seg = token_info(jnp.arange(count, dtype=jnp.int32), lengths, kinds)[0]
        key_blocks = key_piece.reshape(count // blocks, blocks, HEADS, head_dim)
        value_blocks = value_piece.reshape(count // blocks, blocks, HEADS, head_dim)
        seg_blocks = key_seg.reshape(count // blocks, blocks)
        return (count, blocks, key_blocks, value_blocks, seg_blocks)

    def attend_back(queries, keys, values, context, log_total, grad_context):
        query_three = queries.reshape(local_len, HEADS, head_dim)
        grad_three = grad_context.reshape(local_len, HEADS, head_dim)
        delta = jnp.sum(
            grad_three.astype(jnp.float32) * context.reshape(local_len, HEADS, head_dim), axis=-1
        ).T

        def score_grads(
            query_blk, grad_blk, key_blk, value_blk, query_seg, key_seg, total_blk, delta_blk
        ):
            scores = (
                jnp.einsum("qhd,khd->hqk", query_blk, key_blk, preferred_element_type=jnp.float32)
                * scale
            )
            allowed = (query_seg[:, None] == key_seg[None, :])[None]
            probs = jnp.where(allowed, jnp.exp(scores - total_blk[..., None]), 0.0)
            grad_probs = jnp.einsum(
                "qhd,khd->hqk", grad_blk, value_blk, preferred_element_type=jnp.float32
            )
            grad_scores = (probs * (grad_probs - delta_blk[..., None])).astype(jnp.bfloat16)
            return (probs, grad_scores)

        grad_query = jnp.zeros((local_len, HEADS, head_dim), jnp.float32)
        count, blocks, key_blocks, value_blocks, seg_blocks = split_pieces(
            lax.all_gather(keys, "seq", axis=0, tiled=True),
            lax.all_gather(values, "seq", axis=0, tiled=True),
        )

        def advance(grad_acc, item):
            key_blk, value_blk, seg_blk = item
            probs, grad_scores = score_grads(
                query_three, grad_three, key_blk, value_blk, segment, seg_blk, log_total, delta
            )
            grad_acc = grad_acc + scale * jnp.einsum(
                "hqk,khd->qhd", grad_scores, key_blk, preferred_element_type=jnp.float32
            )
            grad_key = scale * jnp.einsum(
                "hqk,qhd->khd", grad_scores, query_three, preferred_element_type=jnp.float32
            )
            grad_value = jnp.einsum(
                "hqk,qhd->khd",
                probs.astype(jnp.bfloat16),
                grad_three,
                preferred_element_type=jnp.float32,
            )
            joined = jnp.concatenate(
                [grad_key.reshape(blocks, model_width), grad_value.reshape(blocks, model_width)],
                axis=1,
            )
            return (grad_acc, joined)

        grad_query, pieces_out = lax.scan(
            advance, grad_query, (key_blocks, value_blocks, seg_blocks)
        )
        grad_rows = pieces_out.reshape(count, 2 * model_width)
        grad_query, grad_rows = (grad_query, grad_rows)
        summed = lax.psum_scatter(
            grad_rows.astype(jnp.bfloat16), "seq", scatter_dimension=0, tiled=True
        ).astype(jnp.float32)
        grad_key_out = summed[:, :model_width]
        grad_value_out = summed[:, model_width:]
        return (grad_query.reshape(local_len, model_width), grad_key_out, grad_value_out)

    def unpack(full):
        w_in, w_out, w_up, w_down, gains, bias = full[:6]
        hidden_units = w_up.shape[1]
        gains_f = gains.astype(jnp.float32)
        bias_f = bias.astype(jnp.float32)
        width_three = 3 * model_width
        return (
            w_in,
            w_out,
            w_up,
            w_down,
            hidden_units,
            gains_f[:model_width],
            gains_f[model_width:],
            bias_f[:width_three],
            bias_f[width_three : 4 * model_width],
            bias_f[4 * model_width : 4 * model_width + hidden_units],
            bias_f[4 * model_width + hidden_units : 5 * model_width + hidden_units],
            bias_f[5 * model_width + hidden_units : 6 * model_width + hidden_units],
            bias_f[6 * model_width + hidden_units :],
        )

    def layer_backward(grad_out, full, record):
        (
            w_in,
            w_out,
            w_up,
            w_down,
            hidden_units,
            gain_one,
            gain_two,
            bias_in,
            bias_out,
            bias_up,
            bias_down,
            shift_one,
            shift_two,
        ) = unpack(full)
        (
            inputs_low,
            queries,
            keys,
            values,
            context,
            context_low,
            log_total,
            first,
            normed,
            normed_low,
            pre_act,
            act_low,
            second,
        ) = record
        unused, pull_two = jax.vjp(layer_norm, second, gain_two, shift_two)
        grad_second, grad_gain_two, grad_shift_two = pull_two(grad_out)
        grad_branch_two = grad_second.astype(jnp.bfloat16)
        grad_bias_down = jnp.sum(grad_branch_two.astype(jnp.float32), axis=0)
        grad_w_down = matmul_left_t(act_low, grad_branch_two)
        grad_act = matmul_right_t(grad_branch_two, w_down)
        unused, pull_gelu = jax.vjp(exact_gelu, pre_act)
        grad_pre = pull_gelu(grad_act)[0].astype(jnp.bfloat16)
        grad_bias_up = jnp.sum(grad_pre.astype(jnp.float32), axis=0)
        grad_w_up = matmul_left_t(normed_low, grad_pre)
        grad_normed = grad_second + matmul_right_t(grad_pre, w_up)
        unused, pull_one = jax.vjp(layer_norm, first, gain_one, shift_one)
        grad_first, grad_gain_one, grad_shift_one = pull_one(grad_normed)
        grad_branch = grad_first.astype(jnp.bfloat16)
        grad_bias_out = jnp.sum(grad_branch.astype(jnp.float32), axis=0)
        grad_w_out = matmul_left_t(context_low, grad_branch)
        grad_context = matmul_right_t(grad_branch, w_out).astype(jnp.bfloat16)
        grad_query, grad_key, grad_value = attend_back(
            queries, keys, values, context, log_total, grad_context
        )
        grad_mixed = jnp.concatenate(
            [
                rotate(grad_query, cos_table, -sin_table),
                rotate(grad_key, cos_table, -sin_table),
                grad_value,
            ],
            axis=1,
        ).astype(jnp.bfloat16)
        grad_bias_in = jnp.sum(grad_mixed.astype(jnp.float32), axis=0)
        grad_w_in = matmul_left_t(inputs_low, grad_mixed)
        grad_hidden = grad_first + matmul_right_t(grad_mixed, w_in)
        grad_gains = jnp.concatenate([grad_gain_one, grad_gain_two])
        grad_bias = jnp.concatenate(
            [
                grad_bias_in,
                grad_bias_out,
                grad_bias_up,
                grad_bias_down,
                grad_shift_one,
                grad_shift_two,
            ]
        )
        return (grad_hidden, (grad_w_in, grad_w_out, grad_w_up, grad_w_down, grad_gains, grad_bias))

    hidden = tokens[0].astype(jnp.float32)
    records = []
    gathered = []
    for layer_index in range(layer_count):
        full = (
            lax.all_gather(attn_in[layer_index], ("seq", "row"), axis=0, tiled=True),
            lax.all_gather(attn_out[layer_index], ("seq", "row"), axis=0, tiled=True),
            lax.all_gather(ffn_up[layer_index], ("seq", "row"), axis=0, tiled=True),
            lax.all_gather(ffn_down[layer_index], ("seq", "row"), axis=0, tiled=True),
            lax.all_gather(norm_gains[layer_index], ("seq", "row"), axis=0, tiled=True),
            lax.all_gather(biases[layer_index], ("seq", "row"), axis=0, tiled=True),
            lax.all_gather(colbert, ("seq", "row"), axis=0, tiled=True),
        )
        gathered.append(full)
        (
            layer_w_in,
            layer_w_out,
            layer_w_up,
            layer_w_down,
            layer_hidden_units,
            layer_gain_one,
            layer_gain_two,
            layer_bias_in,
            layer_bias_out,
            layer_bias_up,
            layer_bias_down,
            layer_shift_one,
            layer_shift_two,
        ) = unpack(full)
        layer_inputs_low = hidden.astype(jnp.bfloat16)
        mixed = (
            jnp.dot(layer_inputs_low, layer_w_in, preferred_element_type=jnp.float32)
            + layer_bias_in
        )
        layer_queries = rotate(mixed[:, :model_width], cos_table, sin_table).astype(jnp.bfloat16)
        layer_keys = rotate(mixed[:, model_width : 2 * model_width], cos_table, sin_table).astype(
            jnp.bfloat16
        )
        layer_values = mixed[:, 2 * model_width :].astype(jnp.bfloat16)
        attend_query_three = layer_queries.reshape(local_len, HEADS, head_dim)
        attend_initial = (
            jnp.full((HEADS, local_len), NEG_FILL, jnp.float32),
            jnp.zeros((HEADS, local_len), jnp.float32),
            jnp.zeros((local_len, HEADS, head_dim), jnp.float32),
        )
        absorb_carry = attend_initial
        absorb_count, absorb_blocks, absorb_key_blocks, absorb_value_blocks, absorb_seg_blocks = (
            split_pieces(
                lax.all_gather(layer_keys, "seq", axis=0, tiled=True),
                lax.all_gather(layer_values, "seq", axis=0, tiled=True),
            )
        )

        def absorb_advance(state, item):
            run_max, run_sum, accum = state
            key_blk, value_blk, seg_blk = item
            scores = (
                jnp.einsum(
                    "qhd,khd->hqk", attend_query_three, key_blk, preferred_element_type=jnp.float32
                )
                * scale
            )
            allowed = (segment[:, None] == seg_blk[None, :])[None]
            scores = jnp.where(allowed, scores, NEG_FILL)
            new_max = jnp.maximum(run_max, jnp.max(scores, axis=-1))
            weights = jnp.where(allowed, jnp.exp(scores - new_max[..., None]), 0.0)
            factor = jnp.exp(run_max - new_max)
            run_sum = run_sum * factor + jnp.sum(weights, axis=-1)
            accum = accum * factor.T[:, :, None] + jnp.einsum(
                "hqk,khd->qhd",
                weights.astype(jnp.bfloat16),
                value_blk,
                preferred_element_type=jnp.float32,
            )
            return ((new_max, run_sum, accum), None)

        absorb_carry, absorb_unused = lax.scan(
            absorb_advance,
            absorb_carry,
            (absorb_key_blocks, absorb_value_blocks, absorb_seg_blocks),
        )
        run_max, run_sum, accum = absorb_carry
        attend_context = (accum / run_sum.T[:, :, None]).reshape(local_len, model_width)
        attend_log_total = run_max + jnp.log(run_sum)
        layer_context_low = attend_context.astype(jnp.bfloat16)
        layer_first = (
            hidden
            + jnp.dot(layer_context_low, layer_w_out, preferred_element_type=jnp.float32)
            + layer_bias_out
        )
        layer_normed = layer_norm(layer_first, layer_gain_one, layer_shift_one)
        layer_normed_low = layer_normed.astype(jnp.bfloat16)
        layer_pre_act = (
            jnp.dot(layer_normed_low, layer_w_up, preferred_element_type=jnp.float32)
            + layer_bias_up
        )
        layer_act_low = exact_gelu(layer_pre_act).astype(jnp.bfloat16)
        layer_second = (
            layer_normed
            + jnp.dot(layer_act_low, layer_w_down, preferred_element_type=jnp.float32)
            + layer_bias_down
        )
        output = layer_norm(layer_second, layer_gain_two, layer_shift_two)
        layer_record = (
            layer_inputs_low,
            layer_queries,
            layer_keys,
            layer_values,
            attend_context,
            layer_context_low,
            attend_log_total,
            layer_first,
            layer_normed,
            layer_normed_low,
            layer_pre_act,
            layer_act_low,
            layer_second,
        )
        hidden = output
        record = layer_record
        records.append(record)
    w_col = gathered[layer_count - 1][6]
    final_low = hidden.astype(jnp.bfloat16)
    col = jnp.dot(final_low, w_col, preferred_element_type=jnp.float32)
    full_width = w_col.shape[1]
    part_widths = (full_width, full_width * 3 // 4, full_width // 2)
    query_total = NQ * QLEN
    doc_total = NSD + 1
    selector = (is_query == 1)[None, :] & (
        query_slot[None, :] == jnp.arange(query_total, dtype=jnp.int32)[:, None]
    )
    selector_low = selector.astype(jnp.bfloat16)
    embeds = [unit_rows(col[:, :part_width]).astype(jnp.bfloat16) for part_width in part_widths]
    picked = (
        lax.psum(
            jnp.dot(selector_low, embeds[0], preferred_element_type=jnp.float32).astype(
                jnp.bfloat16
            ),
            "seq",
        ).astype(jnp.float32),
        lax.psum(
            jnp.dot(selector_low, embeds[1], preferred_element_type=jnp.float32).astype(
                jnp.bfloat16
            ),
            "seq",
        ).astype(jnp.float32),
        lax.psum(
            jnp.dot(selector_low, embeds[2], preferred_element_type=jnp.float32).astype(
                jnp.bfloat16
            ),
            "seq",
        ).astype(jnp.float32),
    )
    query_emb = [item.astype(jnp.bfloat16) for item in picked]
    sims = jnp.stack(
        [
            jnp.einsum(
                "qc,tc->qt", query_emb[part], embeds[part], preferred_element_type=jnp.float32
            )
            for part in range(3)
        ]
    )
    doc_mask = (
        (is_query == 0)[:, None]
        & (doc_num[:, None] == jnp.arange(doc_total, dtype=jnp.int32)[None, :])
    )[None, None]
    scaled = jnp.where(doc_mask, SHARPNESS * sims[..., None], NEG_FILL)
    part_max = jnp.max(scaled, axis=2)
    part_sum = jnp.sum(jnp.where(doc_mask, jnp.exp(scaled - part_max[:, :, None, :]), 0.0), axis=2)
    top, total = joined_2((part_max, part_sum), "seq", merge_pair)
    soft = (top + jnp.log(total)) / SHARPNESS
    pair_sum = jnp.sum(soft.reshape(3, NQ, QLEN, doc_total), axis=2)
    inverse_temp = jnp.exp(log_scale[0])
    logits = pair_sum * inverse_temp / QLEN
    positive = pairing[0][None, :, None] == jnp.arange(doc_total, dtype=jnp.int32)[None, None, :]
    losses = jax.nn.logsumexp(logits, axis=-1) - jnp.sum(jnp.where(positive, logits, 0.0), axis=-1)
    loss_weight = 1.0 / (3 * NQ * lax.axis_size("row"))
    grad_logits = loss_weight * (jax.nn.softmax(logits, axis=-1) - positive.astype(jnp.float32))
    loss_total, temp_grad = lax.psum(
        (jnp.sum(losses).reshape(1) * loss_weight, jnp.sum(grad_logits * logits).reshape(1)), "row"
    )
    grad_pairs = grad_logits * inverse_temp / QLEN
    grad_soft = jnp.broadcast_to(grad_pairs[:, :, None, :], (3, NQ, QLEN, doc_total)).reshape(
        3, query_total, doc_total
    )
    shares = jnp.where(doc_mask, jnp.exp(scaled - top[:, :, None, :]), 0.0) / total[:, :, None, :]
    grad_sims = jnp.sum(shares * grad_soft[:, :, None, :], axis=-1).astype(jnp.bfloat16)
    grad_query_emb = (
        lax.psum(
            jnp.dot(grad_sims[0], embeds[0], preferred_element_type=jnp.float32).astype(
                jnp.bfloat16
            ),
            "seq",
        ).astype(jnp.float32),
        lax.psum(
            jnp.dot(grad_sims[1], embeds[1], preferred_element_type=jnp.float32).astype(
                jnp.bfloat16
            ),
            "seq",
        ).astype(jnp.float32),
        lax.psum(
            jnp.dot(grad_sims[2], embeds[2], preferred_element_type=jnp.float32).astype(
                jnp.bfloat16
            ),
            "seq",
        ).astype(jnp.float32),
    )
    selector_f = selector.astype(jnp.float32)
    grad_col = jnp.zeros((local_len, full_width), jnp.float32)
    for part in range(3):
        part_width = part_widths[part]
        grad_embed = jnp.einsum(
            "qt,qc->tc", grad_sims[part], query_emb[part], preferred_element_type=jnp.float32
        )
        grad_embed = grad_embed + jnp.einsum(
            "qt,qc->tc",
            selector_f,
            grad_query_emb[part],
            precision=HIGHEST,
            preferred_element_type=jnp.float32,
        )
        unused, pull_unit = jax.vjp(unit_rows, col[:, :part_width])
        grad_col = grad_col.at[:, :part_width].add(pull_unit(grad_embed)[0])
    grad_col_low = grad_col.astype(jnp.bfloat16)
    grad_w_col = matmul_left_t(final_low, grad_col_low)
    grad_hidden = cotangent[0].astype(jnp.float32) + matmul_right_t(grad_col_low, w_col)
    shard_lists = [[] for unused_slot in range(6)]
    col_share = None
    for layer_index in reversed(range(layer_count)):
        full = (
            lax.all_gather(attn_in[layer_index], ("seq", "row"), axis=0, tiled=True),
            lax.all_gather(attn_out[layer_index], ("seq", "row"), axis=0, tiled=True),
            lax.all_gather(ffn_up[layer_index], ("seq", "row"), axis=0, tiled=True),
            lax.all_gather(ffn_down[layer_index], ("seq", "row"), axis=0, tiled=True),
            lax.all_gather(norm_gains[layer_index], ("seq", "row"), axis=0, tiled=True),
            lax.all_gather(biases[layer_index], ("seq", "row"), axis=0, tiled=True),
            lax.all_gather(colbert, ("seq", "row"), axis=0, tiled=True),
        )
        grad_hidden, layer_grads = layer_backward(grad_hidden, full, records[layer_index])
        col_term = grad_w_col if layer_index == layer_count - 1 else jnp.zeros_like(grad_w_col)
        shares_out = (
            lax.psum_scatter(layer_grads[0], ("seq", "row"), scatter_dimension=0, tiled=True),
            lax.psum_scatter(layer_grads[1], ("seq", "row"), scatter_dimension=0, tiled=True),
            lax.psum_scatter(layer_grads[2], ("seq", "row"), scatter_dimension=0, tiled=True),
            lax.psum_scatter(layer_grads[3], ("seq", "row"), scatter_dimension=0, tiled=True),
            lax.psum_scatter(layer_grads[4], ("seq", "row"), scatter_dimension=0, tiled=True),
            lax.psum_scatter(layer_grads[5], ("seq", "row"), scatter_dimension=0, tiled=True),
            lax.psum_scatter(col_term, ("seq", "row"), scatter_dimension=0, tiled=True),
        )
        for slot in range(6):
            shard_lists[slot].insert(0, shares_out[slot])
        if layer_index == layer_count - 1:
            col_share = shares_out[6]
    stacked = [jnp.stack(items) for items in shard_lists]
    return (
        hidden.astype(jnp.bfloat16)[None],
        loss_total,
        grad_hidden[None],
        stacked[0],
        stacked[1],
        stacked[2],
        stacked[3],
        stacked[4],
        stacked[5],
        col_share,
        temp_grad,
    )


def solution(mesh):
    placed = (
        P("row", "seq", None),
        P(None, ("seq", "row"), None),
        P(None, ("seq", "row"), None),
        P(None, ("seq", "row"), None),
        P(None, ("seq", "row"), None),
        P(None, ("seq", "row")),
        P(None, ("seq", "row")),
        P(("seq", "row"), None),
        P(),
        P("row", "seq", None),
        P("row", None),
        P("row", None),
        P("row", None),
    )
    planes = mesh.shape["row"] == 4 and mesh.shape["seq"] * 4 == 4 * PLANE and HEADS == 2 * PLANE
    return jax.shard_map(
        body if planes else body_wide,
        mesh=mesh,
        in_specs=placed,
        out_specs=(
            P("row", "seq", None),
            P(),
            P("row", "seq", None),
            P(None, ("seq", "row"), None),
            P(None, ("seq", "row"), None),
            P(None, ("seq", "row"), None),
            P(None, ("seq", "row"), None),
            P(None, ("seq", "row")),
            P(None, ("seq", "row")),
            P(("seq", "row"), None),
            P(),
        ),
        check_vma=False,
    )
```

```python
import math

import jax
import jax.numpy as jnp
from jax import lax
from jax.experimental import pallas as pl
from jax.experimental.pallas import tpu as pltpu
from jax.sharding import PartitionSpec as P

HEADS = 16
QLEN = 32
NQ = 4
NSD = 3

NEG_FILL = -1e30
SHARPNESS = 16.0
HIGHEST = lax.Precision.HIGHEST
BF = jnp.bfloat16
F32 = jnp.float32

def dot(left, right):
    return jnp.dot(left, right, preferred_element_type=F32)


def dot_lt(left, right):
    return lax.dot_general(left, right, (((0,), (0,)), ((), ())), preferred_element_type=F32)


def dot_rt(left, right):
    return lax.dot_general(left, right, (((1,), (1,)), ((), ())), preferred_element_type=F32)


PLANE = 8
BOTH = ("seq", "row")


def across(x, mask):
    size = lax.axis_size("seq") * lax.axis_size("row")
    return lax.ppermute(x, BOTH, [(d, d ^ mask) for d in range(size)])


def turned(x):
    size = lax.axis_size("seq") * lax.axis_size("row")
    rows = lax.axis_size("row")
    pairs = []
    for d in range(size):
        o, i, r = d // PLANE, d % PLANE // rows, d % rows
        pairs.append((d, r * PLANE + i * rows + o))
    return lax.ppermute(x, BOTH, pairs)


def plane_gather(x):
    blocks = [x, None, across(x, 2), None, across(x, 4), None, across(x, 6), None]
    for k in range(0, PLANE, 2):
        blocks[k + 1] = across(blocks[k], 1)
    return blocks


def plane_scatter(even, odd, beside=None, first=False):
    core = across(odd, 1)
    if first:
        core, beside = tie(core, beside)
    parts = core_add(even, core)
    got = [across(parts[j], 2 * j) for j in (1, 2, 3)]
    if beside is not None:
        got, beside = tie(got, beside)
    return [parts[0]] + got, beside


def plane_sum(parts):
    parts = parts.astype(BF)
    core = across(parts[1::2], 1).astype(F32) + parts[0::2].astype(F32)
    sent = core[1:].astype(BF)
    return core[0] + sum(across(sent[k - 1], 2 * k).astype(F32) for k in (1, 2, 3))


def plane_exchange(x, relative):
    x = pick(x, relative)
    core = across(x[1::2], 1)
    got = tie(*[across(jnp.stack([x[2 * k], core[k]]), 2 * k) for k in (1, 2, 3)])
    return pick(jnp.concatenate([x[:1], core[:1], *got]), relative)


def pick(x, index, axis=0):
    return x.at[(slice(None),) * axis + (index,)].get(mode="promise_in_bounds")


def tie(*values):
    return lax.optimization_barrier(values)


def token_info(positions, lengths, kinds):
    ends = jnp.cumsum(lengths)
    starts = ends - lengths
    query_count = jnp.cumsum(kinds) - kinds
    doc_count = jnp.cumsum(1 - kinds) - (1 - kinds)
    segment = jnp.sum((positions[:, None] >= ends[None, :]).astype(jnp.int32), axis=1)
    onehot = segment[:, None] == jnp.arange(lengths.shape[0], dtype=jnp.int32)[None, :]
    nothing = jnp.zeros((), jnp.int32)
    seg_start = jnp.sum(jnp.where(onehot, starts[None, :], nothing), axis=1)
    is_query = jnp.sum(jnp.where(onehot, kinds[None, :], nothing), axis=1)
    query_num = jnp.sum(jnp.where(onehot, query_count[None, :], nothing), axis=1)
    doc_num = jnp.sum(jnp.where(onehot, doc_count[None, :], nothing), axis=1)
    offset = positions - seg_start
    return (segment, offset, is_query, query_num * QLEN + offset, doc_num)


def rope_angles(offset, head_dim):
    half = head_dim // 2
    inverse = jnp.exp(jnp.arange(half, dtype=F32) * (-2.0 * math.log(10000.0) / head_dim))
    angle = offset.astype(F32)[:, None] * inverse[None, :]
    return jnp.cos(angle), jnp.sin(angle)


def layer_norm(rows, gain, shift):
    center = rows - jnp.mean(rows, axis=-1, keepdims=True)
    variance = jnp.mean(center * center, axis=-1, keepdims=True)
    return center * lax.rsqrt(variance + 1e-05) * gain + shift


def unit_rows(rows):
    return rows * lax.rsqrt(jnp.sum(rows * rows, axis=-1, keepdims=True) + 1e-06)


def exact_gelu(values):
    return jax.nn.gelu(values, approximate=False)


def head_masks(width):
    lane = lax.broadcasted_iota(jnp.int32, (1, width), 1)
    first_qk = (lane % (width // 2)) < (width // 4)
    first_v = lane < (width // 2)
    return first_qk, first_v


BIG, SMALL = 62, 16

IN_VMEM = pl.BlockSpec(memory_space=pltpu.VMEM)
IN_HBM = pl.BlockSpec(memory_space=pltpu.HBM)


def near(x):
    return (x, "near")


def held(x):
    return (x, "held")


def raw(x):
    return (x, "raw")


def call(kernel, ins, outs, scratch, flops, limit=BIG):
    arrays = [a for a, _ in ins]
    kept = [i for i, (_, kind) in enumerate(ins) if kind == "held"]
    left = [i for i, out in enumerate(outs) if len(out) == 3]
    pieces = [1 if outs[i][2] is True else outs[i][2] for i in left]
    moved = sum(a.size * a.dtype.itemsize for a in arrays)
    moved += sum(math.prod(out[0]) * jnp.dtype(out[1]).itemsize for out in outs)

    def wrapped(*refs):
        in_refs = list(refs[: len(ins)])
        out_refs = list(refs[len(ins) : len(ins) + len(outs)])
        rest = refs[len(ins) + len(outs) :]
        own, rest = rest[: len(scratch)], rest[len(scratch) :]
        in_bufs, out_bufs = rest[: len(kept)], rest[len(kept) : len(kept) + len(left)]
        sems = rest[len(kept) + len(left)] if kept or left else None
        pending = {}
        for k, i in enumerate(kept):
            pending[i] = pltpu.make_async_copy(in_refs[i], in_bufs[k], sems.at[k])
            pending[i].start()

        def getter(i, buf):
            def get():
                if i in pending:
                    pending.pop(i).wait()
                return buf

            return get

        for k, i in enumerate(kept):
            in_refs[i] = getter(i, in_bufs[k])
        leaving = {}

        def flusher(i, k, target):
            def flush(j=0):
                buf = out_bufs[k]
                if pieces[k] > 1:
                    buf, target_j = buf.at[j], target.at[j]
                else:
                    target_j = target
                leaving[i, j] = pltpu.make_async_copy(buf, target_j, sems.at[len(kept) + sum(pieces[:k]) + j])
                leaving[i, j].start()

            return flush

        for k, i in enumerate(left):
            out_refs[i] = (out_bufs[k], flusher(i, k, out_refs[i]))
        kernel(in_refs, out_refs, own)
        assert not pending and len(leaving) == sum(pieces)
        for copy in leaving.values():
            copy.wait()

    buffers = [pltpu.VMEM(*item) if isinstance(item, tuple) else item for item in scratch]
    buffers += [pltpu.VMEM(arrays[i].shape, arrays[i].dtype) for i in kept]
    buffers += [pltpu.VMEM(*outs[i][:2]) for i in left]
    if kept or left:
        buffers.append(pltpu.SemaphoreType.DMA((len(kept) + sum(pieces),)))
    return pl.pallas_call(
        wrapped,
        in_specs=[IN_VMEM if kind == "near" else IN_HBM for _, kind in ins],
        out_specs=tuple(IN_HBM if len(out) == 3 else IN_VMEM for out in outs),
        out_shape=tuple(jax.ShapeDtypeStruct(out[0], out[1]) for out in outs),
        scratch_shapes=buffers,
        compiler_params=pltpu.CompilerParams(vmem_limit_bytes=limit * 1024 * 1024),
        cost_estimate=pl.CostEstimate(flops=flops, bytes_accessed=moved, transcendentals=0),
    )(*arrays)


def core_add(even, got):
    count, T, D = even.shape

    def kernel(ins, outs, _):
        for j in range(count):
            outs[j][...] = (ins[0][j].astype(F32) + ins[1][j].astype(F32)).astype(outs[j].dtype)

    outs = [((T, D), F32)] + [((T, D), BF)] * (count - 1)
    return call(kernel, [near(even), near(got)], outs, [], even.size, SMALL)


def add_norm(parts, params, bias_at, gain_at, shift_at):
    T, D = parts[0].shape

    def kernel(ins, outs, _):
        params = ins[-1]
        (total, leave), normed, low = outs
        rows = params[:, bias_at : bias_at + D]
        for ref in ins[:-1]:
            rows = rows + ref[...].astype(F32)
        total[...] = rows
        leave()
        result = layer_norm(rows, params[:, gain_at : gain_at + D], params[:, shift_at : shift_at + D])
        normed[...] = result
        low[...] = result.astype(BF)

    outs = [((T, D), F32, True), ((T, D), F32), ((T, D), BF)]
    return call(kernel, [near(item) for item in (*parts, params)], outs, [], 10 * T * D, SMALL)


def norm_back(parts, rows, params, gain_at):
    T, D = rows.shape

    def kernel(ins, outs, _):
        rows, params = ins[-2:]
        wide_out, low_out, sums = outs
        grad = ins[0][...].astype(F32)
        for ref in ins[1:-2]:
            grad = grad + ref[...].astype(F32)
        rows = rows()[...]
        center = rows - jnp.mean(rows, axis=-1, keepdims=True)
        inverse = lax.rsqrt(jnp.mean(center * center, axis=-1, keepdims=True) + 1e-05)
        unit = center * inverse
        sums[:, :D] = jnp.sum(grad * unit, axis=0, keepdims=True)
        sums[:, D : 2 * D] = jnp.sum(grad, axis=0, keepdims=True)
        grad = grad * params[:, gain_at : gain_at + D]
        along = jnp.mean(grad * unit, axis=-1, keepdims=True)
        grad = inverse * (grad - jnp.mean(grad, axis=-1, keepdims=True) - unit * along)
        wide_out[...] = grad
        low = grad.astype(BF)
        low_out[...] = low
        sums[:, 2 * D :] = jnp.sum(low.astype(F32), axis=0, keepdims=True)

    outs = [((T, D), F32), ((T, D), BF), ((1, 3 * D), F32)]
    return call(kernel, [near(item) for item in parts] + [held(rows), near(params)], outs, [], 20 * T * D, SMALL)


def roll_halves(x):
    return pltpu.roll(x, x.shape[1] // 2, 1)


def load_attn(full, w_in, w_out):
    far = full.shape[0]
    D, cols = w_in.shape
    rows, wide = D // far, w_out.shape[0]
    part = wide // far
    for o in range(far):
        w_in[o * rows : (o + 1) * rows] = full[o, :rows, :cols]
        for j in range(rows // part):
            w_out[o * part : (o + 1) * part, j * wide : (j + 1) * wide] = full[o, j * part : (j + 1) * part, cols:]


def load_ffn(full, w_up, w_down):
    far = full.shape[0]
    D, H = w_up.shape
    up, down = D // far, H // far
    for o in range(far):
        w_up[o * up : o * up + up // 2] = full[o, : up // 2, :H]
        w_up[o * up + up // 2 : (o + 1) * up] = full[o, : up // 2, H:]
        w_down[o * down : (o + 1) * down] = full[o, up // 2 : up // 2 + down]


def rotary(table, rows, half):
    cos, sin = table[rows, :half], table[rows, half : 2 * half]
    return jnp.concatenate([cos, cos, cos, cos], axis=1), jnp.concatenate([-sin, -sin, sin, sin], axis=1)


def attn_forward(blocks, full, bias, bias_at, table, seg_row, half, scale):
    n = len(blocks)
    T, D = blocks[0].shape
    wide = 4 * half
    N = n * T
    step = 4
    across_block = N

    def kernel(ins, outs, scratch):
        full, table, bias, seg_row = ins[n:]
        (qkv, leave_qkv), (context, leave_context), (logs, leave_logs), even, odd = outs
        w_in, w_out, x, values_t, context_t, x_sems = scratch
        copies = block_copies(ins[:n], x, x_sems)
        start_all(copies)
        load_attn(full(), w_in, w_out)
        table = table()
        for k in range(0, n, step):
            wait_all(copies[k : k + step])
            rows = slice(k * T, (k + step) * T)
            mixed = dot(x[rows], w_in[...]) + bias[:, bias_at : bias_at + 3 * wide]
            cos, sin = rotary(table, rows, half)
            for t, factor in ((0, scale), (1, 1.0)):
                part = mixed[:, t * wide : (t + 1) * wide]
                part = (part * cos + roll_halves(part) * sin).astype(BF)
                qkv[rows, t * wide : (t + 1) * wide] = part * jnp.asarray(factor, BF)
            qkv[rows, 2 * wide :] = mixed[:, 2 * wide :].astype(BF)
        leave_qkv()
        values_t[...] = qkv[:, 2 * wide :].T
        first_qk, _ = head_masks(wide)
        zero = jnp.zeros((), BF)

        def part(c, carry):
            at = pl.ds(pl.multiple_of(c * across_block, 128), across_block)
            allowed = table[:, 2 * half : 2 * half + 1] == seg_row[:, at]
            for head in range(2):
                mine = first_qk if head == 0 else jnp.logical_not(first_qk)
                query = jnp.where(mine, qkv[at, :wide], zero)
                scores = jnp.where(allowed, dot_rt(qkv[:, wide : 2 * wide], query), NEG_FILL)
                top = jnp.max(scores, axis=0, keepdims=True)
                weights = jnp.exp(scores - top)
                total = jnp.sum(weights, axis=0, keepdims=True)
                heads = slice(head * 2 * half, (head + 1) * 2 * half)
                context_t[heads, at] = dot(values_t[heads, :], weights.astype(BF)) * (1.0 / total)
                logs[head : head + 1, at] = top + jnp.log(total)
            return carry

        lax.fori_loop(0, N // across_block, part, 0)
        leave_logs()
        context[...] = context_t[...].T.astype(BF)
        leave_context()
        for k in range(0, n, step):
            put_blocks(dot(context[k * T : (k + step) * T], w_out[...]).astype(BF), k, (even, odd), T)

    outs = [((N, 3 * wide), BF, True), ((N, wide), BF, True), ((2, N), F32, True)]
    outs += [((n // 2, T, D), BF, n // 2), ((n // 2, T, D), BF, n // 2)]
    flops = 2 * N * D * 4 * wide + 8 * N * N * wide
    sems = pltpu.SemaphoreType.DMA
    scratch = [((D, 3 * wide), BF), ((wide, D), BF), ((N, D), BF), ((wide, N), BF), ((wide, N), F32), sems((n,))]
    ins = [raw(item) for item in blocks] + [held(full), held(table), near(bias), near(seg_row)]
    return call(kernel, ins, outs, scratch, flops)


def lanes_of(count):
    return max(w for w in (384, 256, 128) if count % w == 0)


def fetch_ffn(full, w_up, w_down, sems):
    far = full.shape[0]
    D, H = w_up.shape
    up, down = D // far, H // far
    first, second = [], []
    for o in range(far):
        for part in range(2):
            first.append(
                pltpu.make_async_copy(
                    full.at[o, pl.ds(0, up // 2), pl.ds(part * H, H)],
                    w_up.at[pl.ds(o * up + part * (up // 2), up // 2)],
                    sems.at[3 * o + part],
                )
            )
        second.append(
            pltpu.make_async_copy(
                full.at[o, pl.ds(up // 2, down)], w_down.at[pl.ds(o * down, down)], sems.at[3 * o + 2]
            )
        )
    return first, second


def start_all(copies):
    for copy in copies:
        copy.start()


def wait_all(copies):
    for copy in copies:
        copy.wait()


def block_copies(blocks, whole, sems):
    T = blocks[0].shape[0]
    return [pltpu.make_async_copy(block, whole.at[pl.ds(k * T, T)], sems.at[k]) for k, block in enumerate(blocks)]


def ffn_forward(blocks, full, bias, bias_at, H):
    n = len(blocks)
    T, D = blocks[0].shape
    step = 4

    def kernel(ins, outs, scratch):
        full, bias = ins[n:]
        (act, leave_act), (slope, leave_slope), even, odd = outs
        w_up, w_down, x, w_sems, x_sems = scratch
        first, second = fetch_ffn(full, w_up, w_down, w_sems)
        copies = block_copies(ins[:n], x, x_sems)
        start_all(first)
        start_all(copies)
        start_all(second)
        wait_all(first)
        for k in range(0, n, step):
            wait_all(copies[k : k + step])
            rows = slice(k * T, (k + step) * T)
            pre = dot(x[rows], w_up[...]) + bias[:, bias_at : bias_at + H]
            below = 0.5 * (1.0 + lax.erf(pre * math.sqrt(0.5)))
            result = (pre * below).astype(BF)
            act[rows] = result
            slope[rows] = (below + pre * (math.sqrt(0.5 / math.pi) * jnp.exp(-0.5 * pre * pre))).astype(BF)
            if k == 0:
                wait_all(second)
            back = dot(act[rows], w_down[...]).astype(BF)
            put_blocks(back, k, (even, odd), T)
        leave_act()
        leave_slope()

    outs = [((n * T, H), BF, True), ((n * T, H), BF, True), ((n // 2, T, D), BF, n // 2), ((n // 2, T, D), BF, n // 2)]
    ins = [raw(item) for item in blocks] + [raw(full), near(bias)]
    sems = pltpu.SemaphoreType.DMA
    scratch = [((D, H), BF), ((H, D), BF), ((n * T, D), BF), sems((3 * full.shape[0],)), sems((n,))]
    return call(kernel, ins, outs, scratch, 4 * n * T * D * H)


def put_blocks(rows, first, halves, T):
    for i in range(rows.shape[0] // T):
        out, leave = halves[(first + i) % 2]
        out[(first + i) // 2] = rows[i * T : (i + 1) * T]
        leave((first + i) // 2)


def ffn_back(blocks, full, slope):
    n = len(blocks)
    T, D = blocks[0].shape
    H = slope.shape[1]
    step = 4

    def kernel(ins, outs, scratch):
        full, slope = ins[n:]
        grad_pre, bias_grad, even, odd = outs
        w_up, w_down, x, w_sems, x_sems = scratch
        first, second = fetch_ffn(full, w_up, w_down, w_sems)
        copies = block_copies(ins[:n], x, x_sems)
        start_all(second)
        start_all(copies)
        start_all(first)
        wait_all(second)
        total = jnp.zeros((1, H), F32)
        for k in range(0, n, step):
            wait_all(copies[k : k + step])
            rows = slice(k * T, (k + step) * T)
            grad = (dot_rt(x[rows], w_down[...]) * slope()[rows].astype(F32)).astype(BF)
            grad_pre[rows] = grad
            total = total + jnp.sum(grad.astype(F32), axis=0, keepdims=True)
            if k == 0:
                wait_all(first)
            put_blocks(dot_rt(grad_pre[rows], w_up[...]).astype(BF), k, (even, odd), T)
        bias_grad[...] = total

    outs = [((n * T, H), BF), ((1, H), F32), ((n // 2, T, D), BF, n // 2), ((n // 2, T, D), BF, n // 2)]
    ins = [raw(item) for item in blocks] + [raw(full), held(slope)]
    sems = pltpu.SemaphoreType.DMA
    scratch = [((D, H), BF), ((H, D), BF), ((n * T, D), BF), sems((3 * full.shape[0],)), sems((n,))]
    return call(kernel, ins, outs, scratch, 4 * n * T * D * H)


def ffn_weights(normed, grads, act, grad_pre, far, extra):
    n = len(normed)
    T, D = normed[0].shape
    N = n * T
    H = act.shape[1]
    up, down = D // far, H // far
    more = [] if extra is None else [near(extra)]
    count = up // 2 + down + (0 if extra is None else extra.shape[1])

    def kernel(ins, outs, scratch):
        act, grad_pre = ins[2 * n : 2 * n + 2]
        left, right, left_sems, right_sems = scratch
        out = outs[0]
        copies = block_copies(ins[:n], left, left_sems)
        later = block_copies(ins[n : 2 * n], right, right_sems)
        start_all(copies)
        start_all(later)
        wait_all(copies)
        for o in range(far):
            block = dot_lt(left[:, o * up : (o + 1) * up], grad_pre[...]).astype(BF)
            out[o, : up // 2, :H] = block[: up // 2]
            out[o, : up // 2, H:] = block[up // 2 :]
        wait_all(later)
        act = act()
        for o in range(far):
            block = dot_lt(act[:, o * down : (o + 1) * down], right[...]).astype(BF)
            out[o, up // 2 : up // 2 + down] = block
            if more:
                out[o, up // 2 + down :] = ins[2 * n + 2][o]

    sems = pltpu.SemaphoreType.DMA
    scratch = [((N, D), BF), ((N, D), BF), sems((n,)), sems((n,))]
    ins = [raw(item) for item in (*normed, *grads)] + [held(act), near(grad_pre)] + more
    return call(kernel, ins, [((far, count, D), BF)], scratch, 4 * N * D * H)[0]


def attn_back(blocks, full, qkv, context, logs, table, seg_row, half, scale):
    n = len(blocks)
    T, D = blocks[0].shape
    wide = 4 * half
    N = n * T
    step = 4
    across_block = lanes_of(N)

    def kernel(ins, outs, scratch):
        full, table, qkv, context, logs, seg_row = ins[n:]
        mixed, bias_grad, even, odd = outs
        w_in, w_out, x, grad, delta, cos, sin, acc_k, acc_v, x_sems = scratch
        copies = block_copies(ins[:n], x, x_sems)
        start_all(copies)
        load_attn(full(), w_in, w_out)
        for k in range(0, n, step):
            wait_all(copies[k : k + step])
            rows = slice(k * T, (k + step) * T)
            grad[rows] = dot_rt(x[rows], w_out[...]).astype(BF)
        table = table()
        cos[...], sin[...] = rotary(table, slice(None), half)
        acc_k[...] = jnp.zeros_like(acc_k)
        acc_v[...] = jnp.zeros_like(acc_v)
        qkv, logs = qkv(), logs()
        product = (grad[...].astype(F32) * context()[...].astype(F32)).T
        delta[0:1] = jnp.sum(product[: 2 * half], axis=0, keepdims=True)
        delta[1:2] = jnp.sum(product[2 * half :], axis=0, keepdims=True)
        first_qk, first_v = head_masks(wide)
        zero = jnp.zeros((), BF)

        def part(c, carry):
            at = pl.ds(pl.multiple_of(c * across_block, 128), across_block)
            allowed = table[:, 2 * half : 2 * half + 1] == seg_row[:, at]
            grad_query = []
            for head in range(2):
                mine = first_qk if head == 0 else jnp.logical_not(first_qk)
                mine_v = first_v if head == 0 else jnp.logical_not(first_v)
                query = jnp.where(mine, qkv[at, :wide], zero)
                grad_h = jnp.where(mine_v, grad[at, :], zero)
                scores = dot_rt(qkv[:, wide : 2 * wide], query) - logs[head : head + 1, at]
                probs = jnp.exp(jnp.where(allowed, scores, NEG_FILL))
                grad_probs = dot_rt(qkv[:, 2 * wide :], grad_h)
                grad_scores = (probs * (grad_probs - delta[head : head + 1, at])).astype(BF)
                acc_k[...] += dot(grad_scores, query)
                acc_v[...] += dot(probs.astype(BF), grad_h)
                grad_query.append(dot_lt(grad_scores, qkv[:, wide : 2 * wide]))
            result = jnp.where(first_qk, grad_query[0], grad_query[1]) * scale
            mixed[at, :wide] = (result * cos[at, :] - roll_halves(result) * sin[at, :]).astype(BF)
            return carry

        lax.fori_loop(0, N // across_block, part, 0)
        total = acc_k[...]
        mixed[:, wide : 2 * wide] = (total * cos[...] - roll_halves(total) * sin[...]).astype(BF)
        mixed[:, 2 * wide :] = acc_v[...].astype(BF)
        sums = jnp.zeros((1, 3 * wide), F32)
        for k in range(0, n, step):
            rows = slice(k * T, (k + step) * T)
            sums = sums + jnp.sum(mixed[rows].astype(F32), axis=0, keepdims=True)
            put_blocks(dot_rt(mixed[rows], w_in[...]).astype(BF), k, (even, odd), T)
        bias_grad[...] = sums

    outs = [((N, 3 * wide), BF), ((1, 3 * wide), F32), ((n // 2, T, D), BF, n // 2), ((n // 2, T, D), BF, n // 2)]
    scratch = [((D, 3 * wide), BF), ((wide, D), BF), ((N, D), BF), ((N, wide), BF), ((2, N), F32)]
    scratch += [((N, wide), F32)] * 4 + [pltpu.SemaphoreType.DMA((n,))]
    flops = 2 * N * D * 4 * wide + 20 * N * N * wide
    ins = [raw(item) for item in blocks] + [held(item) for item in (full, table, qkv, context, logs)] + [near(seg_row)]
    return call(kernel, ins, outs, scratch, flops)


def attn_weights(inputs, grads, context, mixed, bias_grad, far, relative):
    n = len(inputs)
    T, D = inputs[0].shape
    N = n * T
    wide = context.shape[1]
    rows = D // far
    part = wide // far
    size = lax.axis_size("row")

    def kernel(ins, outs, scratch):
        context, mixed, bias_grad = ins[2 * n :]
        left, right, left_sems, right_sems = scratch
        here = (lax.axis_index("seq") * size + lax.axis_index("row")) // PLANE
        copies = block_copies(ins[:n], left, left_sems)
        later = block_copies(ins[n : 2 * n], right, right_sems)
        start_all(copies)
        start_all(later)
        wait_all(copies)
        for k in range(far):
            if relative:
                lanes = pl.ds(pl.multiple_of((here ^ k) * rows, 128), rows)
                outs[k][:rows, : 3 * wide] = dot_lt(left[:, lanes], mixed[...]).astype(BF)
            else:
                outs[0][k, :rows, : 3 * wide] = dot_lt(left[:, k * rows : (k + 1) * rows], mixed[...]).astype(BF)
        wait_all(later)
        whole = dot_lt(context()[...], right[...]).astype(BF)
        extra = jnp.broadcast_to(bias_grad[...], (16, 3 * wide)).astype(BF)
        if relative:
            right[:wide, :D] = whole
        for k in range(far):
            out = outs[k] if relative else outs[0].at[k]
            if relative:
                block = right[pl.ds(pl.multiple_of((here ^ k) * part, 16), part), :]
            else:
                block = whole[k * part : (k + 1) * part]
            for j in range(rows // part):
                out[j * part : (j + 1) * part, 3 * wide :] = block[:, j * wide : (j + 1) * wide]
            out[rows:, : 3 * wide] = extra
            out[rows:, 3 * wide :] = jnp.zeros((16, wide), BF)

    sems = pltpu.SemaphoreType.DMA
    scratch = [((N, D), BF), ((N, D), BF), sems((n,)), sems((n,))]
    ins = [raw(item) for item in (*inputs, *grads)] + [held(context), near(mixed), near(bias_grad)]
    if relative:
        outs = [((rows + 16, 4 * wide), BF)] * far
    else:
        outs = [((far, rows + 16, 4 * wide), BF)]
    return call(kernel, ins, outs, scratch, 8 * N * D * wide)


def body(
    tokens,
    attn_in,
    attn_out,
    ffn_up,
    ffn_down,
    norm_gains,
    biases,
    colbert,
    log_scale,
    cotangent,
    seg_lengths,
    seg_kinds,
    pairing,
):
    S = lax.axis_size("seq")
    R = lax.axis_size("row")
    O = S * R // PLANE
    place = lax.axis_index("seq") * R + lax.axis_index("row")
    plane, far = place % PLANE, place // PLANE
    relative = jnp.bitwise_xor(plane, jnp.arange(PLANE, dtype=jnp.int32))
    T = tokens.shape[1]
    D = tokens.shape[2]
    N = PLANE * T
    L = attn_in.shape[0]
    head_dim = D // HEADS
    half = head_dim // 2
    scale = head_dim ** (-0.5)
    wide = 2 * head_dim
    in_cols = 3 * wide
    in_rows = attn_in.shape[1]
    rows_in = PLANE * in_rows
    FF = ffn_up.shape[2]
    up_cols = FF // (S * R)
    hidden_cols = O * up_cols
    gain_part = norm_gains.shape[1]
    bias_part = biases.shape[1]
    part = gain_part + bias_part
    along_z = [[o * (S // O) + i for o in range(O)] for i in range(S // O)]
    is_mine = jnp.arange(PLANE, dtype=jnp.int32) == plane

    def padded_rows(vector, width=D):
        rows = -(-vector.shape[0] // (16 * width)) * 16
        return jnp.pad(vector, (0, rows * width - vector.shape[0])).reshape(rows, width)

    def pack_columns(w):
        lead = w.shape[:-1]
        n = len(lead)
        qk = w[..., : 2 * D].reshape(*lead, 2, PLANE, 2, 2, half)
        qk = qk.transpose((n + 1,) + tuple(range(n)) + (n, n + 3, n + 2, n + 4)).reshape(PLANE, *lead, 2 * wide)
        v = w[..., 2 * D :].reshape(*lead, PLANE, wide)
        v = v.transpose((n,) + tuple(range(n)) + (n + 1,))
        return jnp.concatenate([qk, v], axis=-1)

    def unpack_columns(w):
        rows = w.shape[1]
        qk = w[:, :, : 2 * wide].reshape(PLANE, rows, 2, 2, 2, half)
        qk = qk.transpose(1, 2, 0, 4, 3, 5).reshape(rows, 2 * D)
        v = w[:, :, 2 * wide :].transpose(1, 0, 2).reshape(rows, D)
        return jnp.concatenate([qk, v], axis=1)

    def pack_hidden(w):
        rows = w.shape[0]
        return w.reshape(rows, O, PLANE, up_cols).transpose(2, 0, 1, 3).reshape(PLANE, rows, hidden_cols)

    def unpack_hidden(w):
        rows = w.shape[1]
        return w.reshape(PLANE, rows, O, up_cols).transpose(1, 2, 0, 3).reshape(rows, FF)

    def fold(w):
        n = w.shape[-2] // 2
        return jnp.concatenate([w[..., :n, :], w[..., n:, :]], axis=-1)

    def unfold(w):
        n = w.shape[-1] // 2
        return jnp.concatenate([w[..., :n], w[..., n:]], axis=-2)

    to_group = [(b, (b % O) * PLANE + b // O) for b in range(O * PLANE)]
    from_group = [(d, b) for b, d in to_group]
    small = jnp.concatenate([norm_gains.reshape(-1), biases.reshape(-1), colbert.reshape(-1)])
    small = jnp.broadcast_to(padded_rows(small, in_cols), (PLANE, *padded_rows(small, in_cols).shape))
    first_in = plane_exchange(jnp.concatenate([pack_columns(attn_in[0]), small], axis=1), relative)
    first_in, small = first_in[:, :in_rows].reshape(rows_in, in_cols), first_in[:, in_rows:].reshape(PLANE, -1)
    shard_out = lax.ppermute(attn_out, BOTH, to_group)
    table = turned(jnp.concatenate([seg_lengths[0], seg_kinds[0], pairing[0]]))
    seg_count = seg_lengths.shape[1]
    lengths, kinds = table[:seg_count], table[seg_count : 2 * seg_count]
    pairs_of = table[2 * seg_count :]
    hidden_low = turned(tokens[0])
    cot = turned(cotangent[0])

    def attn_block(layer, shard):
        out = shard_out[layer].reshape(in_rows, PLANE, wide).transpose(1, 0, 2).reshape(rows_in, wide)
        return jnp.concatenate([shard, out], axis=1)

    def gather_far(x):
        return lax.all_gather(x, "seq", axis=0, axis_index_groups=along_z)

    own = attn_block(0, first_in)
    full_attn = [gather_far(own)]

    count_small = L * part
    col_plane = small[:, count_small : count_small + colbert.size].reshape(-1)
    params = small[None, :, :count_small]
    step = 1
    while step < O:
        other = across(params, PLANE * step)
        low_side = (far & step) == 0
        params = jnp.concatenate([jnp.where(low_side, params, other), jnp.where(low_side, other, params)], axis=0)
        step *= 2
    params = params.reshape(O * PLANE, count_small).astype(F32)
    gains_all = params[:, : L * gain_part].reshape(O * PLANE, L, gain_part).transpose(1, 0, 2).reshape(L, 2 * D)
    bias_all = params[:, L * gain_part :].reshape(O * PLANE, L, bias_part).transpose(1, 0, 2).reshape(L, -1)
    in_biases = pick(pack_columns(bias_all[:, : 3 * D]), plane, axis=0).reshape(1, L * in_cols)
    up_biases = pick(pack_hidden(bias_all[:, 4 * D : 4 * D + FF]), plane, axis=0).reshape(1, L * hidden_cols)
    rest_at = 4 * D + FF
    params = jnp.concatenate([gains_all, bias_all[:, 3 * D : 4 * D], bias_all[:, rest_at:]], axis=1).reshape(1, -1)
    GAIN_ONE, GAIN_TWO, BIAS_OUT, BIAS_DOWN, SHIFT_ONE, SHIFT_TWO = range(6)

    def at(layer, which):
        return (layer * 6 + which) * D

    rest = jnp.concatenate(
        [pack_hidden(ffn_up[0])]
        + [piece for layer in range(1, L) for piece in (pack_columns(attn_in[layer]), pack_hidden(ffn_up[layer]))],
        axis=-1,
    )
    rest = plane_exchange(rest, relative).reshape(rows_in, -1)
    full_ffn = []
    start = 0
    for layer in range(L):
        if layer > 0:
            full_attn.append(gather_far(attn_block(layer, rest[:, start : start + in_cols])))
            start += in_cols
        own = [fold(rest[:, start : start + hidden_cols]), ffn_down[layer]]
        start += hidden_cols
        if layer == L - 1:
            own.append(padded_rows(col_plane))
        full_ffn.append(gather_far(jnp.concatenate(own, axis=0)))
    w_col = full_ffn[L - 1][:, rows_in // 2 + up_cols :].reshape(O, -1)[:, : col_plane.size]
    w_col = w_col.reshape(D, colbert.shape[1])

    block_at = (relative % R) * (PLANE // R) + relative // R
    positions = (block_at[:, None] * T + jnp.arange(T, dtype=jnp.int32)[None, :]).reshape(N)
    held_segment, held_offset = token_info(positions, lengths, kinds)[:2]
    cos, sin = rope_angles(held_offset, head_dim)
    seg_row = held_segment.astype(F32)[None, :]
    table = jnp.concatenate([cos, sin, jnp.broadcast_to(seg_row.T, (N, wide - 2 * half))], axis=1)

    hidden = hidden_low
    records = []
    for layer in range(L):
        x_all = plane_gather(hidden_low)
        if layer == 0:
            x_all, cot = tie(x_all, cot)
        qkv, context, logs, even, odd = attn_forward(
            x_all, full_attn[layer], in_biases, layer * in_cols, table, seg_row, half, scale
        )
        terms, _ = plane_scatter(even, odd)
        first, normed, normed_low = add_norm(
            [hidden] + terms, params, at(layer, BIAS_OUT), at(layer, GAIN_ONE), at(layer, SHIFT_ONE)
        )
        normed_all = plane_gather(normed_low)
        act, slope, even, odd = ffn_forward(
            normed_all, full_ffn[layer], up_biases, layer * hidden_cols, hidden_cols
        )
        terms, _ = plane_scatter(even, odd)
        second, hidden, hidden_low = add_norm(
            [normed] + terms, params, at(layer, BIAS_DOWN), at(layer, GAIN_TWO), at(layer, SHIFT_TWO)
        )
        records.append((x_all, qkv, context, logs, first, normed_all, act, slope, second))
    hidden_out = turned(hidden_low)

    full_width = w_col.shape[1]
    part_widths = (full_width, full_width * 3 // 4, full_width // 2)
    query_total = NQ * QLEN
    doc_total = NSD + 1
    col = dot(hidden_low, w_col)
    in_order = jnp.arange(PLANE, dtype=jnp.int32)
    in_order = jnp.bitwise_xor((in_order % (PLANE // R)) * R + in_order // (PLANE // R), plane)
    col_row = pick(jnp.stack(plane_gather(col.astype(BF))), in_order, axis=0).reshape(N, full_width).astype(F32)
    own_at = block_at[0] * T
    row_positions = jnp.arange(N, dtype=jnp.int32)
    segment, offset, is_query, query_slot, doc_num = token_info(row_positions, lengths, kinds)
    slots = jnp.arange(query_total, dtype=jnp.int32)[:, None]
    selector = (is_query == 1)[None, :] & (query_slot[None, :] == slots)
    selector_low = selector.astype(BF)
    own_selector = lax.dynamic_slice(selector.astype(F32), (0, own_at), (query_total, T))
    embeds = [unit_rows(col_row[:, :width]).astype(BF) for width in part_widths]
    query_emb = [dot(selector_low, embed).astype(BF) for embed in embeds]
    powers = jnp.exp(SHARPNESS * jnp.stack([dot_rt(query_emb[m], embeds[m]) for m in range(3)]))
    doc_code = jnp.where(is_query == 0, doc_num, -1)[None, None, :]
    totals = jnp.stack([jnp.sum(jnp.where(doc_code == d, powers, 0.0), axis=2) for d in range(doc_total)], axis=2)
    soft = jnp.log(totals) / SHARPNESS
    pair_sum = jnp.sum(soft.reshape(3, NQ, QLEN, doc_total), axis=2)
    inverse_temp = jnp.exp(log_scale[0])
    logits = pair_sum * inverse_temp / QLEN
    positive = pairs_of[None, :, None] == jnp.arange(doc_total, dtype=jnp.int32)[None, None, :]
    losses = jax.nn.logsumexp(logits, axis=-1) - jnp.sum(jnp.where(positive, logits, 0.0), axis=-1)
    loss_weight = 1.0 / (3 * NQ * R)
    grad_logits = loss_weight * (jax.nn.softmax(logits, axis=-1) - positive.astype(F32))
    loss_terms = jnp.stack([jnp.sum(losses) * loss_weight, jnp.sum(grad_logits * logits)])
    grad_pairs = grad_logits * inverse_temp / QLEN
    grad_soft = jnp.broadcast_to(grad_pairs[:, :, None, :], (3, NQ, QLEN, doc_total)).reshape(
        3, query_total, doc_total
    )
    ratio = grad_soft / totals
    weight = sum(jnp.where(doc_code == d, ratio[:, :, d : d + 1], 0.0) for d in range(doc_total))
    grad_sims = (powers * weight).astype(BF)
    own_sims = lax.dynamic_slice(grad_sims, (0, 0, own_at), (3, query_total, T))
    grad_col = jnp.zeros((T, full_width), F32)
    for m in range(3):
        width = part_widths[m]
        grad_query = dot(grad_sims[m], embeds[m])
        grad_embed = dot_lt(own_sims[m], query_emb[m]) + lax.dot_general(
            own_selector, grad_query, (((0,), (0,)), ((), ())), precision=HIGHEST, preferred_element_type=F32
        )
        pull_unit = jax.vjp(unit_rows, col[:, :width])[1]
        grad_col = grad_col + jnp.pad(pull_unit(grad_embed)[0], ((0, 0), (0, full_width - width)))
    grad_col_low = grad_col.astype(BF)
    col_parts = dot_lt(hidden_low, grad_col_low).reshape(O, PLANE, in_rows, full_width).transpose(1, 0, 2, 3)
    col_parts = plane_sum(pick(col_parts.reshape(PLANE, O * in_rows, full_width), relative, axis=0))
    col_rows = jax.vmap(padded_rows)(col_parts.reshape(O, in_rows * full_width)).astype(BF)
    grad_parts = [cot, dot_rt(grad_col_low, w_col)]

    def scatter_far(whole):
        whole = whole.reshape(-1, whole.shape[-1])
        return lax.psum_scatter(whole, "seq", scatter_dimension=0, tiled=True, axis_index_groups=along_z)

    outs = [[None] * L for _ in range(6)]

    def up_share(shares):
        return unfold(shares[: rows_in // 2]).reshape(PLANE, in_rows, hidden_cols)

    def in_share(shares):
        return shares[:rows_in, :in_cols].reshape(PLANE, in_rows, in_cols)

    def finish_out(layer, shares):
        share_out = shares[:rows_in, in_cols:].astype(BF).reshape(PLANE, in_rows, wide)
        share_out = share_out.transpose(1, 0, 2).reshape(in_rows, D)
        outs[1][layer] = lax.ppermute(share_out, BOTH, from_group).astype(F32)

    def bias_in_entries(rows):
        natural = jnp.pad(unpack_columns(rows[:, None].astype(F32))[0], (0, O * PLANE * bias_part - 3 * D))
        return pick(natural.reshape(O * PLANE, bias_part), place)

    def as_rows(x, width):
        return jax.vmap(lambda row: padded_rows(row, width))(x)

    shares_ffn, shares_attn = [None] * L, [None] * L
    vectors = [None] * L
    for layer in reversed(range(L)):
        x_all, qkv, context, logs, first, normed_all, act, slope, second = records[layer]
        grad_second, grad_ffo, sums_two = norm_back(grad_parts, second, params, at(layer, GAIN_TWO))
        ffo_all = plane_gather(grad_ffo)
        if layer == L - 1:
            ffo_all, hidden_out = tie(ffo_all, hidden_out)
        grad_pre, grad_bias_up, even, odd = ffn_back(ffo_all, full_ffn[layer], slope)
        blocks = ffn_weights(normed_all, ffo_all, act, grad_pre, O, col_rows if layer == L - 1 else None)
        terms, blocks = plane_scatter(even, odd, blocks)
        shares_ffn[layer] = scatter_far(blocks)
        grad_first, grad_branch, sums_one = norm_back([grad_second] + terms, first, params, at(layer, GAIN_ONE))
        branch_all = plane_gather(grad_branch)
        if layer < L - 1:
            branch_all, shares_attn[layer + 1] = tie(branch_all, shares_attn[layer + 1])
        grad_mixed, grad_bias_in, even, odd = attn_back(
            branch_all, full_attn[layer], qkv, context, logs, table, seg_row, half, scale
        )

        gain_two, shift_two, down, gain_one, shift_one, out = [
            sums[0, k * D : (k + 1) * D] for sums in (sums_two, sums_one) for k in range(3)
        ]
        own_up = unpack_hidden(is_mine[:, None, None].astype(F32) * grad_bias_up[None])[0]
        gains = jnp.concatenate([gain_one, gain_two]).reshape(O, PLANE, gain_part)
        bias = jnp.concatenate([jnp.zeros((3 * D,), F32), out, own_up, down, shift_one, shift_two])
        vectors[layer] = jnp.concatenate([gains, bias.reshape(O, PLANE, bias_part)], axis=2)

        blocks = attn_weights(x_all, branch_all, context, grad_mixed, grad_bias_in, O, layer == 0)
        terms, blocks = plane_scatter(even, odd, blocks, layer == 0)
        terms, shares_ffn[layer] = tie(terms, shares_ffn[layer])
        if layer > 0:
            shares_attn[layer] = scatter_far(blocks[0])
            grad_parts = [grad_first] + terms

    got = [across(blocks[step], PLANE * step) for step in range(1, O)]
    entries = jnp.concatenate(vectors, axis=2).transpose(1, 0, 2).reshape(PLANE, O * L * part).astype(BF)
    pieces = [in_share(shares_attn[layer]) for layer in range(1, L)] + [up_share(item) for item in shares_ffn]
    pieces = jnp.concatenate(pieces, axis=2)
    got, terms, entries, pieces = tie(got, terms, entries, pieces)
    grad_tokens = turned((grad_first + sum(item.astype(F32) for item in terms)).astype(BF))
    shares_attn[0] = (blocks[0].astype(F32) + sum(item.astype(F32) for item in got)).astype(BF)
    pieces = jnp.concatenate([in_share(shares_attn[0]), pieces], axis=2)
    bias_rows = [jnp.broadcast_to(item[None, rows_in, :in_cols], (PLANE, in_cols)) for item in shares_attn]
    more = as_rows(jnp.concatenate([entries] + bias_rows, axis=1), pieces.shape[2])
    back = plane_exchange(jnp.concatenate([pieces, more], axis=1), relative)
    more = back[:, in_rows:].reshape(PLANE, -1)
    entries = jnp.sum(more[:, : O * L * part].astype(F32), axis=0).reshape(O, L * part)
    entries = jnp.concatenate([entries, jnp.broadcast_to(loss_terms[None], (O, 2))], axis=1)
    mine = pick(entries, far)
    for step in range(1, O):
        mine = mine + across(pick(entries, far ^ step), PLANE * step)
    start = 0
    for layer in range(L):
        outs[0][layer] = unpack_columns(back[:, :in_rows, start : start + in_cols])
        start += in_cols
    for layer in range(L):
        outs[2][layer] = unpack_hidden(back[:, :in_rows, start : start + hidden_cols])
        start += hidden_cols
        at_row = rows_in // 2
        outs[3][layer] = shares_ffn[layer][at_row : at_row + up_cols]
        finish_out(layer, shares_attn[layer])
        at_row = O * L * part + layer * in_cols
        bias_in = bias_in_entries(more[:, at_row : at_row + in_cols])
        outs[4][layer] = mine[layer * part : layer * part + gain_part]
        outs[5][layer] = mine[layer * part + gain_part : (layer + 1) * part] + bias_in
    col_share = shares_ffn[L - 1][rows_in // 2 + up_cols :].reshape(-1)[: in_rows * full_width]
    col_share = col_share.reshape(in_rows, full_width).astype(F32)
    loss_terms = mine[L * part :]
    stacked = [jnp.stack(items).astype(F32) for items in outs]
    return (
        hidden_out[None],
        loss_terms[:1],
        grad_tokens.astype(F32)[None],
        stacked[0],
        stacked[1],
        stacked[2],
        stacked[3],
        stacked[4],
        stacked[5],
        col_share,
        loss_terms[1:],
    )


def joined_2(value, axis, join):
    pieces = jax.tree.map(lambda part: lax.all_gather(part, axis), value)
    head = jax.tree.map(lambda part: part[0], pieces)
    tail = jax.tree.map(lambda part: part[1:], pieces)
    so_far, _ = lax.scan(lambda so_far, section: (join(so_far, section), None), head, tail)
    return so_far


def rope_tables(offset, head_dim):
    half = head_dim // 2
    inverse = jnp.exp(jnp.arange(half, dtype=jnp.float32) * (-2.0 * math.log(10000.0) / head_dim))
    angle = offset.astype(jnp.float32)[:, None] * inverse[None, :]
    return (jnp.cos(angle), jnp.sin(angle))


def rotate(flat, cos_table, sin_table):
    length = flat.shape[0]
    head_dim = flat.shape[1] // HEADS
    half = head_dim // 2
    shaped = flat.reshape(length, HEADS, head_dim)
    first_half = shaped[..., :half]
    second_half = shaped[..., half:]
    cos_three = cos_table[:, None, :]
    sin_three = sin_table[:, None, :]
    turned = jnp.concatenate(
        [
            first_half * cos_three - second_half * sin_three,
            second_half * cos_three + first_half * sin_three,
        ],
        axis=-1,
    )
    return turned.reshape(length, flat.shape[1])


def block_for(count):
    blocks = count
    while blocks > 1024 and blocks % 2 == 0:
        blocks = blocks // 2
    return blocks


def merge_pair(first, second):
    max_first, sum_first = first
    max_second, sum_second = second
    top = jnp.maximum(max_first, max_second)
    return (top, sum_first * jnp.exp(max_first - top) + sum_second * jnp.exp(max_second - top))


def matmul_left_t(left, right):
    return jnp.einsum("ti,to->io", left, right, preferred_element_type=jnp.float32)


def matmul_right_t(left, right):
    return jnp.einsum("to,io->ti", left, right, preferred_element_type=jnp.float32)


def body_wide(
    tokens,
    attn_in,
    attn_out,
    ffn_up,
    ffn_down,
    norm_gains,
    biases,
    colbert,
    log_scale,
    cotangent,
    seg_lengths,
    seg_kinds,
    pairing,
):
    rank = lax.axis_index("seq")
    local_len = tokens.shape[1]
    model_width = tokens.shape[2]
    head_dim = model_width // HEADS
    scale = head_dim ** (-0.5)
    lengths = seg_lengths[0]
    kinds = seg_kinds[0]
    positions = rank * local_len + jnp.arange(local_len, dtype=jnp.int32)
    segment, offset, is_query, query_slot, doc_num = token_info(positions, lengths, kinds)
    cos_table, sin_table = rope_tables(offset, head_dim)
    layer_count = attn_in.shape[0]

    def split_pieces(key_piece, value_piece):
        count = key_piece.shape[0]
        blocks = block_for(count)
        key_seg = token_info(jnp.arange(count, dtype=jnp.int32), lengths, kinds)[0]
        key_blocks = key_piece.reshape(count // blocks, blocks, HEADS, head_dim)
        value_blocks = value_piece.reshape(count // blocks, blocks, HEADS, head_dim)
        seg_blocks = key_seg.reshape(count // blocks, blocks)
        return (count, blocks, key_blocks, value_blocks, seg_blocks)

    def attend_back(queries, keys, values, context, log_total, grad_context):
        query_three = queries.reshape(local_len, HEADS, head_dim)
        grad_three = grad_context.reshape(local_len, HEADS, head_dim)
        delta = jnp.sum(
            grad_three.astype(jnp.float32) * context.reshape(local_len, HEADS, head_dim), axis=-1
        ).T

        def score_grads(
            query_blk, grad_blk, key_blk, value_blk, query_seg, key_seg, total_blk, delta_blk
        ):
            scores = (
                jnp.einsum("qhd,khd->hqk", query_blk, key_blk, preferred_element_type=jnp.float32)
                * scale
            )
            allowed = (query_seg[:, None] == key_seg[None, :])[None]
            probs = jnp.where(allowed, jnp.exp(scores - total_blk[..., None]), 0.0)
            grad_probs = jnp.einsum(
                "qhd,khd->hqk", grad_blk, value_blk, preferred_element_type=jnp.float32
            )
            grad_scores = (probs * (grad_probs - delta_blk[..., None])).astype(jnp.bfloat16)
            return (probs, grad_scores)

        grad_query = jnp.zeros((local_len, HEADS, head_dim), jnp.float32)
        count, blocks, key_blocks, value_blocks, seg_blocks = split_pieces(
            lax.all_gather(keys, "seq", axis=0, tiled=True),
            lax.all_gather(values, "seq", axis=0, tiled=True),
        )

        def advance(grad_acc, item):
            key_blk, value_blk, seg_blk = item
            probs, grad_scores = score_grads(
                query_three, grad_three, key_blk, value_blk, segment, seg_blk, log_total, delta
            )
            grad_acc = grad_acc + scale * jnp.einsum(
                "hqk,khd->qhd", grad_scores, key_blk, preferred_element_type=jnp.float32
            )
            grad_key = scale * jnp.einsum(
                "hqk,qhd->khd", grad_scores, query_three, preferred_element_type=jnp.float32
            )
            grad_value = jnp.einsum(
                "hqk,qhd->khd",
                probs.astype(jnp.bfloat16),
                grad_three,
                preferred_element_type=jnp.float32,
            )
            joined = jnp.concatenate(
                [grad_key.reshape(blocks, model_width), grad_value.reshape(blocks, model_width)],
                axis=1,
            )
            return (grad_acc, joined)

        grad_query, pieces_out = lax.scan(
            advance, grad_query, (key_blocks, value_blocks, seg_blocks)
        )
        grad_rows = pieces_out.reshape(count, 2 * model_width)
        grad_query, grad_rows = (grad_query, grad_rows)
        summed = lax.psum_scatter(
            grad_rows.astype(jnp.bfloat16), "seq", scatter_dimension=0, tiled=True
        ).astype(jnp.float32)
        grad_key_out = summed[:, :model_width]
        grad_value_out = summed[:, model_width:]
        return (grad_query.reshape(local_len, model_width), grad_key_out, grad_value_out)

    def unpack(full):
        w_in, w_out, w_up, w_down, gains, bias = full[:6]
        hidden_units = w_up.shape[1]
        gains_f = gains.astype(jnp.float32)
        bias_f = bias.astype(jnp.float32)
        width_three = 3 * model_width
        return (
            w_in,
            w_out,
            w_up,
            w_down,
            hidden_units,
            gains_f[:model_width],
            gains_f[model_width:],
            bias_f[:width_three],
            bias_f[width_three : 4 * model_width],
            bias_f[4 * model_width : 4 * model_width + hidden_units],
            bias_f[4 * model_width + hidden_units : 5 * model_width + hidden_units],
            bias_f[5 * model_width + hidden_units : 6 * model_width + hidden_units],
            bias_f[6 * model_width + hidden_units :],
        )

    def layer_backward(grad_out, full, record):
        (
            w_in,
            w_out,
            w_up,
            w_down,
            hidden_units,
            gain_one,
            gain_two,
            bias_in,
            bias_out,
            bias_up,
            bias_down,
            shift_one,
            shift_two,
        ) = unpack(full)
        (
            inputs_low,
            queries,
            keys,
            values,
            context,
            context_low,
            log_total,
            first,
            normed,
            normed_low,
            pre_act,
            act_low,
            second,
        ) = record
        unused, pull_two = jax.vjp(layer_norm, second, gain_two, shift_two)
        grad_second, grad_gain_two, grad_shift_two = pull_two(grad_out)
        grad_branch_two = grad_second.astype(jnp.bfloat16)
        grad_bias_down = jnp.sum(grad_branch_two.astype(jnp.float32), axis=0)
        grad_w_down = matmul_left_t(act_low, grad_branch_two)
        grad_act = matmul_right_t(grad_branch_two, w_down)
        unused, pull_gelu = jax.vjp(exact_gelu, pre_act)
        grad_pre = pull_gelu(grad_act)[0].astype(jnp.bfloat16)
        grad_bias_up = jnp.sum(grad_pre.astype(jnp.float32), axis=0)
        grad_w_up = matmul_left_t(normed_low, grad_pre)
        grad_normed = grad_second + matmul_right_t(grad_pre, w_up)
        unused, pull_one = jax.vjp(layer_norm, first, gain_one, shift_one)
        grad_first, grad_gain_one, grad_shift_one = pull_one(grad_normed)
        grad_branch = grad_first.astype(jnp.bfloat16)
        grad_bias_out = jnp.sum(grad_branch.astype(jnp.float32), axis=0)
        grad_w_out = matmul_left_t(context_low, grad_branch)
        grad_context = matmul_right_t(grad_branch, w_out).astype(jnp.bfloat16)
        grad_query, grad_key, grad_value = attend_back(
            queries, keys, values, context, log_total, grad_context
        )
        grad_mixed = jnp.concatenate(
            [
                rotate(grad_query, cos_table, -sin_table),
                rotate(grad_key, cos_table, -sin_table),
                grad_value,
            ],
            axis=1,
        ).astype(jnp.bfloat16)
        grad_bias_in = jnp.sum(grad_mixed.astype(jnp.float32), axis=0)
        grad_w_in = matmul_left_t(inputs_low, grad_mixed)
        grad_hidden = grad_first + matmul_right_t(grad_mixed, w_in)
        grad_gains = jnp.concatenate([grad_gain_one, grad_gain_two])
        grad_bias = jnp.concatenate(
            [
                grad_bias_in,
                grad_bias_out,
                grad_bias_up,
                grad_bias_down,
                grad_shift_one,
                grad_shift_two,
            ]
        )
        return (grad_hidden, (grad_w_in, grad_w_out, grad_w_up, grad_w_down, grad_gains, grad_bias))

    hidden = tokens[0].astype(jnp.float32)
    records = []
    gathered = []
    for layer_index in range(layer_count):
        full = (
            lax.all_gather(attn_in[layer_index], ("seq", "row"), axis=0, tiled=True),
            lax.all_gather(attn_out[layer_index], ("seq", "row"), axis=0, tiled=True),
            lax.all_gather(ffn_up[layer_index], ("seq", "row"), axis=0, tiled=True),
            lax.all_gather(ffn_down[layer_index], ("seq", "row"), axis=0, tiled=True),
            lax.all_gather(norm_gains[layer_index], ("seq", "row"), axis=0, tiled=True),
            lax.all_gather(biases[layer_index], ("seq", "row"), axis=0, tiled=True),
            lax.all_gather(colbert, ("seq", "row"), axis=0, tiled=True),
        )
        gathered.append(full)
        (
            layer_w_in,
            layer_w_out,
            layer_w_up,
            layer_w_down,
            layer_hidden_units,
            layer_gain_one,
            layer_gain_two,
            layer_bias_in,
            layer_bias_out,
            layer_bias_up,
            layer_bias_down,
            layer_shift_one,
            layer_shift_two,
        ) = unpack(full)
        layer_inputs_low = hidden.astype(jnp.bfloat16)
        mixed = (
            jnp.dot(layer_inputs_low, layer_w_in, preferred_element_type=jnp.float32)
            + layer_bias_in
        )
        layer_queries = rotate(mixed[:, :model_width], cos_table, sin_table).astype(jnp.bfloat16)
        layer_keys = rotate(mixed[:, model_width : 2 * model_width], cos_table, sin_table).astype(
            jnp.bfloat16
        )
        layer_values = mixed[:, 2 * model_width :].astype(jnp.bfloat16)
        attend_query_three = layer_queries.reshape(local_len, HEADS, head_dim)
        attend_initial = (
            jnp.full((HEADS, local_len), NEG_FILL, jnp.float32),
            jnp.zeros((HEADS, local_len), jnp.float32),
            jnp.zeros((local_len, HEADS, head_dim), jnp.float32),
        )
        absorb_carry = attend_initial
        absorb_count, absorb_blocks, absorb_key_blocks, absorb_value_blocks, absorb_seg_blocks = (
            split_pieces(
                lax.all_gather(layer_keys, "seq", axis=0, tiled=True),
                lax.all_gather(layer_values, "seq", axis=0, tiled=True),
            )
        )

        def absorb_advance(state, item):
            run_max, run_sum, accum = state
            key_blk, value_blk, seg_blk = item
            scores = (
                jnp.einsum(
                    "qhd,khd->hqk", attend_query_three, key_blk, preferred_element_type=jnp.float32
                )
                * scale
            )
            allowed = (segment[:, None] == seg_blk[None, :])[None]
            scores = jnp.where(allowed, scores, NEG_FILL)
            new_max = jnp.maximum(run_max, jnp.max(scores, axis=-1))
            weights = jnp.where(allowed, jnp.exp(scores - new_max[..., None]), 0.0)
            factor = jnp.exp(run_max - new_max)
            run_sum = run_sum * factor + jnp.sum(weights, axis=-1)
            accum = accum * factor.T[:, :, None] + jnp.einsum(
                "hqk,khd->qhd",
                weights.astype(jnp.bfloat16),
                value_blk,
                preferred_element_type=jnp.float32,
            )
            return ((new_max, run_sum, accum), None)

        absorb_carry, absorb_unused = lax.scan(
            absorb_advance,
            absorb_carry,
            (absorb_key_blocks, absorb_value_blocks, absorb_seg_blocks),
        )
        run_max, run_sum, accum = absorb_carry
        attend_context = (accum / run_sum.T[:, :, None]).reshape(local_len, model_width)
        attend_log_total = run_max + jnp.log(run_sum)
        layer_context_low = attend_context.astype(jnp.bfloat16)
        layer_first = (
            hidden
            + jnp.dot(layer_context_low, layer_w_out, preferred_element_type=jnp.float32)
            + layer_bias_out
        )
        layer_normed = layer_norm(layer_first, layer_gain_one, layer_shift_one)
        layer_normed_low = layer_normed.astype(jnp.bfloat16)
        layer_pre_act = (
            jnp.dot(layer_normed_low, layer_w_up, preferred_element_type=jnp.float32)
            + layer_bias_up
        )
        layer_act_low = exact_gelu(layer_pre_act).astype(jnp.bfloat16)
        layer_second = (
            layer_normed
            + jnp.dot(layer_act_low, layer_w_down, preferred_element_type=jnp.float32)
            + layer_bias_down
        )
        output = layer_norm(layer_second, layer_gain_two, layer_shift_two)
        layer_record = (
            layer_inputs_low,
            layer_queries,
            layer_keys,
            layer_values,
            attend_context,
            layer_context_low,
            attend_log_total,
            layer_first,
            layer_normed,
            layer_normed_low,
            layer_pre_act,
            layer_act_low,
            layer_second,
        )
        hidden = output
        record = layer_record
        records.append(record)
    w_col = gathered[layer_count - 1][6]
    final_low = hidden.astype(jnp.bfloat16)
    col = jnp.dot(final_low, w_col, preferred_element_type=jnp.float32)
    full_width = w_col.shape[1]
    part_widths = (full_width, full_width * 3 // 4, full_width // 2)
    query_total = NQ * QLEN
    doc_total = NSD + 1
    selector = (is_query == 1)[None, :] & (
        query_slot[None, :] == jnp.arange(query_total, dtype=jnp.int32)[:, None]
    )
    selector_low = selector.astype(jnp.bfloat16)
    embeds = [unit_rows(col[:, :part_width]).astype(jnp.bfloat16) for part_width in part_widths]
    picked = (
        lax.psum(
            jnp.dot(selector_low, embeds[0], preferred_element_type=jnp.float32).astype(
                jnp.bfloat16
            ),
            "seq",
        ).astype(jnp.float32),
        lax.psum(
            jnp.dot(selector_low, embeds[1], preferred_element_type=jnp.float32).astype(
                jnp.bfloat16
            ),
            "seq",
        ).astype(jnp.float32),
        lax.psum(
            jnp.dot(selector_low, embeds[2], preferred_element_type=jnp.float32).astype(
                jnp.bfloat16
            ),
            "seq",
        ).astype(jnp.float32),
    )
    query_emb = [item.astype(jnp.bfloat16) for item in picked]
    sims = jnp.stack(
        [
            jnp.einsum(
                "qc,tc->qt", query_emb[part], embeds[part], preferred_element_type=jnp.float32
            )
            for part in range(3)
        ]
    )
    doc_mask = (
        (is_query == 0)[:, None]
        & (doc_num[:, None] == jnp.arange(doc_total, dtype=jnp.int32)[None, :])
    )[None, None]
    scaled = jnp.where(doc_mask, SHARPNESS * sims[..., None], NEG_FILL)
    part_max = jnp.max(scaled, axis=2)
    part_sum = jnp.sum(jnp.where(doc_mask, jnp.exp(scaled - part_max[:, :, None, :]), 0.0), axis=2)
    top, total = joined_2((part_max, part_sum), "seq", merge_pair)
    soft = (top + jnp.log(total)) / SHARPNESS
    pair_sum = jnp.sum(soft.reshape(3, NQ, QLEN, doc_total), axis=2)
    inverse_temp = jnp.exp(log_scale[0])
    logits = pair_sum * inverse_temp / QLEN
    positive = pairing[0][None, :, None] == jnp.arange(doc_total, dtype=jnp.int32)[None, None, :]
    losses = jax.nn.logsumexp(logits, axis=-1) - jnp.sum(jnp.where(positive, logits, 0.0), axis=-1)
    loss_weight = 1.0 / (3 * NQ * lax.axis_size("row"))
    grad_logits = loss_weight * (jax.nn.softmax(logits, axis=-1) - positive.astype(jnp.float32))
    loss_total, temp_grad = lax.psum(
        (jnp.sum(losses).reshape(1) * loss_weight, jnp.sum(grad_logits * logits).reshape(1)), "row"
    )
    grad_pairs = grad_logits * inverse_temp / QLEN
    grad_soft = jnp.broadcast_to(grad_pairs[:, :, None, :], (3, NQ, QLEN, doc_total)).reshape(
        3, query_total, doc_total
    )
    shares = jnp.where(doc_mask, jnp.exp(scaled - top[:, :, None, :]), 0.0) / total[:, :, None, :]
    grad_sims = jnp.sum(shares * grad_soft[:, :, None, :], axis=-1).astype(jnp.bfloat16)
    grad_query_emb = (
        lax.psum(
            jnp.dot(grad_sims[0], embeds[0], preferred_element_type=jnp.float32).astype(
                jnp.bfloat16
            ),
            "seq",
        ).astype(jnp.float32),
        lax.psum(
            jnp.dot(grad_sims[1], embeds[1], preferred_element_type=jnp.float32).astype(
                jnp.bfloat16
            ),
            "seq",
        ).astype(jnp.float32),
        lax.psum(
            jnp.dot(grad_sims[2], embeds[2], preferred_element_type=jnp.float32).astype(
                jnp.bfloat16
            ),
            "seq",
        ).astype(jnp.float32),
    )
    selector_f = selector.astype(jnp.float32)
    grad_col = jnp.zeros((local_len, full_width), jnp.float32)
    for part in range(3):
        part_width = part_widths[part]
        grad_embed = jnp.einsum(
            "qt,qc->tc", grad_sims[part], query_emb[part], preferred_element_type=jnp.float32
        )
        grad_embed = grad_embed + jnp.einsum(
            "qt,qc->tc",
            selector_f,
            grad_query_emb[part],
            precision=HIGHEST,
            preferred_element_type=jnp.float32,
        )
        unused, pull_unit = jax.vjp(unit_rows, col[:, :part_width])
        grad_col = grad_col.at[:, :part_width].add(pull_unit(grad_embed)[0])
    grad_col_low = grad_col.astype(jnp.bfloat16)
    grad_w_col = matmul_left_t(final_low, grad_col_low)
    grad_hidden = cotangent[0].astype(jnp.float32) + matmul_right_t(grad_col_low, w_col)
    shard_lists = [[] for unused_slot in range(6)]
    col_share = None
    for layer_index in reversed(range(layer_count)):
        full = (
            lax.all_gather(attn_in[layer_index], ("seq", "row"), axis=0, tiled=True),
            lax.all_gather(attn_out[layer_index], ("seq", "row"), axis=0, tiled=True),
            lax.all_gather(ffn_up[layer_index], ("seq", "row"), axis=0, tiled=True),
            lax.all_gather(ffn_down[layer_index], ("seq", "row"), axis=0, tiled=True),
            lax.all_gather(norm_gains[layer_index], ("seq", "row"), axis=0, tiled=True),
            lax.all_gather(biases[layer_index], ("seq", "row"), axis=0, tiled=True),
            lax.all_gather(colbert, ("seq", "row"), axis=0, tiled=True),
        )
        grad_hidden, layer_grads = layer_backward(grad_hidden, full, records[layer_index])
        col_term = grad_w_col if layer_index == layer_count - 1 else jnp.zeros_like(grad_w_col)
        shares_out = (
            lax.psum_scatter(layer_grads[0], ("seq", "row"), scatter_dimension=0, tiled=True),
            lax.psum_scatter(layer_grads[1], ("seq", "row"), scatter_dimension=0, tiled=True),
            lax.psum_scatter(layer_grads[2], ("seq", "row"), scatter_dimension=0, tiled=True),
            lax.psum_scatter(layer_grads[3], ("seq", "row"), scatter_dimension=0, tiled=True),
            lax.psum_scatter(layer_grads[4], ("seq", "row"), scatter_dimension=0, tiled=True),
            lax.psum_scatter(layer_grads[5], ("seq", "row"), scatter_dimension=0, tiled=True),
            lax.psum_scatter(col_term, ("seq", "row"), scatter_dimension=0, tiled=True),
        )
        for slot in range(6):
            shard_lists[slot].insert(0, shares_out[slot])
        if layer_index == layer_count - 1:
            col_share = shares_out[6]
    stacked = [jnp.stack(items) for items in shard_lists]
    return (
        hidden.astype(jnp.bfloat16)[None],
        loss_total,
        grad_hidden[None],
        stacked[0],
        stacked[1],
        stacked[2],
        stacked[3],
        stacked[4],
        stacked[5],
        col_share,
        temp_grad,
    )


def solution(mesh):
    placed = (
        P("row", "seq", None),
        P(None, ("seq", "row"), None),
        P(None, ("seq", "row"), None),
        P(None, ("seq", "row"), None),
        P(None, ("seq", "row"), None),
        P(None, ("seq", "row")),
        P(None, ("seq", "row")),
        P(("seq", "row"), None),
        P(),
        P("row", "seq", None),
        P("row", None),
        P("row", None),
        P("row", None),
    )
    planes = mesh.shape["row"] == 4 and mesh.shape["seq"] * 4 == 4 * PLANE and HEADS == 2 * PLANE
    return jax.shard_map(
        body if planes else body_wide,
        mesh=mesh,
        in_specs=placed,
        out_specs=(
            P("row", "seq", None),
            P(),
            P("row", "seq", None),
            P(None, ("seq", "row"), None),
            P(None, ("seq", "row"), None),
            P(None, ("seq", "row"), None),
            P(None, ("seq", "row"), None),
            P(None, ("seq", "row")),
            P(None, ("seq", "row")),
            P(("seq", "row"), None),
            P(),
        ),
        check_vma=False,
    )
```

```python
import math

import jax
import jax.numpy as jnp
from jax import lax
from jax.experimental import pallas as pl
from jax.experimental.pallas import tpu as pltpu
from jax.sharding import PartitionSpec as P

HEADS = 16
QLEN = 32
NQ = 4
NSD = 3

NEG_FILL = -1e30
SHARPNESS = 16.0
HIGHEST = lax.Precision.HIGHEST
BF = jnp.bfloat16
F32 = jnp.float32

def dot(left, right):
    return jnp.dot(left, right, preferred_element_type=F32)


def dot_lt(left, right):
    return lax.dot_general(left, right, (((0,), (0,)), ((), ())), preferred_element_type=F32)


def dot_rt(left, right):
    return lax.dot_general(left, right, (((1,), (1,)), ((), ())), preferred_element_type=F32)


PLANE = 8
BOTH = ("seq", "row")


def across(x, mask):
    size = lax.axis_size("seq") * lax.axis_size("row")
    return lax.ppermute(x, BOTH, [(d, d ^ mask) for d in range(size)])


def turned(x, back=False):
    size = lax.axis_size("seq") * lax.axis_size("row")
    pairs = []
    for d in range(size):
        z, y, column, core = d // PLANE, d // 4 % 2, d // 2 % 2, d % 2
        to = (2 * core + column) * PLANE + 4 * y + 2 * (column ^ (z // 2)) + z % 2
        pairs.append((to, d) if back else (d, to))
    return lax.ppermute(x, BOTH, pairs)


def plane_gather(x):
    blocks = [x, None, across(x, 2), None, across(x, 4), None, across(x, 6), None]
    for k in range(0, PLANE, 2):
        blocks[k + 1] = across(blocks[k], 1)
    return blocks


def plane_scatter(even, odd, beside=None, first=False):
    core = across(odd, 1)
    if first:
        core, beside = tie(core, beside)
    parts = core_add(even, core)
    got = [across(parts[j], 2 * j) for j in (1, 2, 3)]
    if beside is not None and not first:
        got, beside = tie(got, beside)
    return [parts[0]] + got, beside


def plane_sum(parts):
    parts = parts.astype(BF)
    core = across(parts[1::2], 1).astype(F32) + parts[0::2].astype(F32)
    sent = core[1:].astype(BF)
    return core[0] + sum(across(sent[k - 1], 2 * k).astype(F32) for k in (1, 2, 3))


def plane_exchange(x, relative, before=None):
    x = pick(x, relative)
    core = across(x[1::2], 1)
    if before is not None:
        core, before = tie(core, before)
    got = tie(*[across(jnp.stack([x[2 * k], core[k]]), 2 * k) for k in (1, 2, 3)])
    x = pick(jnp.concatenate([x[:1], core[:1], *got]), relative)
    return x if before is None else (x, before)


def pick(x, index, axis=0):
    return x.at[(slice(None),) * axis + (index,)].get(mode="promise_in_bounds")


def tie(*values):
    return lax.optimization_barrier(values)


def token_info(positions, lengths, kinds):
    ends = jnp.cumsum(lengths)
    starts = ends - lengths
    query_count = jnp.cumsum(kinds) - kinds
    doc_count = jnp.cumsum(1 - kinds) - (1 - kinds)
    segment = jnp.sum((positions[:, None] >= ends[None, :]).astype(jnp.int32), axis=1)
    onehot = segment[:, None] == jnp.arange(lengths.shape[0], dtype=jnp.int32)[None, :]
    nothing = jnp.zeros((), jnp.int32)
    seg_start = jnp.sum(jnp.where(onehot, starts[None, :], nothing), axis=1)
    is_query = jnp.sum(jnp.where(onehot, kinds[None, :], nothing), axis=1)
    query_num = jnp.sum(jnp.where(onehot, query_count[None, :], nothing), axis=1)
    doc_num = jnp.sum(jnp.where(onehot, doc_count[None, :], nothing), axis=1)
    offset = positions - seg_start
    return (segment, offset, is_query, query_num * QLEN + offset, doc_num)


def rope_angles(offset, head_dim):
    half = head_dim // 2
    inverse = jnp.exp(jnp.arange(half, dtype=F32) * (-2.0 * math.log(10000.0) / head_dim))
    angle = offset.astype(F32)[:, None] * inverse[None, :]
    return jnp.cos(angle), jnp.sin(angle)


def layer_norm(rows, gain, shift):
    center = rows - jnp.mean(rows, axis=-1, keepdims=True)
    variance = jnp.mean(center * center, axis=-1, keepdims=True)
    return center * lax.rsqrt(variance + 1e-05) * gain + shift


def unit_rows(rows):
    return rows * lax.rsqrt(jnp.sum(rows * rows, axis=-1, keepdims=True) + 1e-06)


def exact_gelu(values):
    return jax.nn.gelu(values, approximate=False)


def head_masks(width):
    lane = lax.broadcasted_iota(jnp.int32, (1, width), 1)
    first_qk = (lane % (width // 2)) < (width // 4)
    first_v = lane < (width // 2)
    return first_qk, first_v


BIG, SMALL = 62, 16

IN_VMEM = pl.BlockSpec(memory_space=pltpu.VMEM)
IN_HBM = pl.BlockSpec(memory_space=pltpu.HBM)


def near(x):
    return (x, "near")


def held(x):
    return (x, "held")


def raw(x):
    return (x, "raw")


def call(kernel, ins, outs, scratch, flops, limit=BIG):
    arrays = [a for a, _ in ins]
    kept = [i for i, (_, kind) in enumerate(ins) if kind == "held"]
    left = [i for i, out in enumerate(outs) if len(out) == 3]
    pieces = [1 if outs[i][2] is True else outs[i][2] for i in left]
    moved = sum(a.size * a.dtype.itemsize for a in arrays)
    moved += sum(math.prod(out[0]) * jnp.dtype(out[1]).itemsize for out in outs)

    def wrapped(*refs):
        in_refs = list(refs[: len(ins)])
        out_refs = list(refs[len(ins) : len(ins) + len(outs)])
        rest = refs[len(ins) + len(outs) :]
        own, rest = rest[: len(scratch)], rest[len(scratch) :]
        in_bufs, out_bufs = rest[: len(kept)], rest[len(kept) : len(kept) + len(left)]
        sems = rest[len(kept) + len(left)] if kept or left else None
        pending = {}
        for k, i in enumerate(kept):
            pending[i] = pltpu.make_async_copy(in_refs[i], in_bufs[k], sems.at[k])
            pending[i].start()

        def getter(i, buf):
            def get():
                if i in pending:
                    pending.pop(i).wait()
                return buf

            return get

        for k, i in enumerate(kept):
            in_refs[i] = getter(i, in_bufs[k])
        leaving = {}

        def flusher(i, k, target):
            def flush(j=0):
                buf = out_bufs[k]
                if pieces[k] > 1:
                    buf, target_j = buf.at[j], target.at[j]
                else:
                    target_j = target
                leaving[i, j] = pltpu.make_async_copy(buf, target_j, sems.at[len(kept) + sum(pieces[:k]) + j])
                leaving[i, j].start()

            return flush

        for k, i in enumerate(left):
            out_refs[i] = (out_bufs[k], flusher(i, k, out_refs[i]))
        kernel(in_refs, out_refs, own)
        assert not pending and len(leaving) == sum(pieces)
        for copy in leaving.values():
            copy.wait()

    buffers = [pltpu.VMEM(*item) if isinstance(item, tuple) else item for item in scratch]
    buffers += [pltpu.VMEM(arrays[i].shape, arrays[i].dtype) for i in kept]
    buffers += [pltpu.VMEM(*outs[i][:2]) for i in left]
    if kept or left:
        buffers.append(pltpu.SemaphoreType.DMA((len(kept) + sum(pieces),)))
    return pl.pallas_call(
        wrapped,
        in_specs=[IN_VMEM if kind == "near" else IN_HBM for _, kind in ins],
        out_specs=tuple(IN_HBM if len(out) == 3 else IN_VMEM for out in outs),
        out_shape=tuple(jax.ShapeDtypeStruct(out[0], out[1]) for out in outs),
        scratch_shapes=buffers,
        compiler_params=pltpu.CompilerParams(vmem_limit_bytes=limit * 1024 * 1024),
        cost_estimate=pl.CostEstimate(flops=flops, bytes_accessed=moved, transcendentals=0),
    )(*arrays)


def core_add(even, got):
    count, T, D = even.shape

    def kernel(ins, outs, _):
        for j in range(count):
            outs[j][...] = (ins[0][j].astype(F32) + ins[1][j].astype(F32)).astype(outs[j].dtype)

    outs = [((T, D), F32)] + [((T, D), BF)] * (count - 1)
    return call(kernel, [near(even), near(got)], outs, [], even.size, SMALL)


def add_norm(parts, params, bias_at, gain_at, shift_at):
    T, D = parts[0].shape

    def kernel(ins, outs, _):
        params = ins[-1]
        (total, leave), normed, low = outs
        rows = params[:, bias_at : bias_at + D]
        for ref in ins[:-1]:
            rows = rows + ref[...].astype(F32)
        total[...] = rows
        leave()
        result = layer_norm(rows, params[:, gain_at : gain_at + D], params[:, shift_at : shift_at + D])
        normed[...] = result
        low[...] = result.astype(BF)

    outs = [((T, D), F32, True), ((T, D), F32), ((T, D), BF)]
    return call(kernel, [near(item) for item in (*parts, params)], outs, [], 10 * T * D, SMALL)


def norm_back(parts, rows, params, gain_at):
    T, D = rows.shape

    def kernel(ins, outs, _):
        rows, params = ins[-2:]
        wide_out, low_out, sums = outs
        grad = ins[0][...].astype(F32)
        for ref in ins[1:-2]:
            grad = grad + ref[...].astype(F32)
        rows = rows()[...]
        center = rows - jnp.mean(rows, axis=-1, keepdims=True)
        inverse = lax.rsqrt(jnp.mean(center * center, axis=-1, keepdims=True) + 1e-05)
        unit = center * inverse
        sums[:, :D] = jnp.sum(grad * unit, axis=0, keepdims=True)
        sums[:, D : 2 * D] = jnp.sum(grad, axis=0, keepdims=True)
        grad = grad * params[:, gain_at : gain_at + D]
        along = jnp.mean(grad * unit, axis=-1, keepdims=True)
        grad = inverse * (grad - jnp.mean(grad, axis=-1, keepdims=True) - unit * along)
        wide_out[...] = grad
        low = grad.astype(BF)
        low_out[...] = low
        sums[:, 2 * D :] = jnp.sum(low.astype(F32), axis=0, keepdims=True)

    outs = [((T, D), F32), ((T, D), BF), ((1, 3 * D), F32)]
    return call(kernel, [near(item) for item in parts] + [held(rows), near(params)], outs, [], 20 * T * D, SMALL)


def roll_halves(x):
    return pltpu.roll(x, x.shape[1] // 2, 1)


def load_attn(full, w_in, w_out):
    far = full.shape[0]
    D, cols = w_in.shape
    rows, wide = D // far, w_out.shape[0]
    part = wide // far
    for o in range(far):
        w_in[o * rows : (o + 1) * rows] = full[o, :rows, :cols]
        for j in range(rows // part):
            w_out[o * part : (o + 1) * part, j * wide : (j + 1) * wide] = full[o, j * part : (j + 1) * part, cols:]


def load_ffn(full, w_up, w_down):
    far = full.shape[0]
    D, H = w_up.shape
    up, down = D // far, H // far
    for o in range(far):
        w_up[o * up : o * up + up // 2] = full[o, : up // 2, :H]
        w_up[o * up + up // 2 : (o + 1) * up] = full[o, : up // 2, H:]
        w_down[o * down : (o + 1) * down] = full[o, up // 2 : up // 2 + down]


def rotary(table, rows, half):
    cos, sin = table[rows, :half], table[rows, half : 2 * half]
    return jnp.concatenate([cos, cos, cos, cos], axis=1), jnp.concatenate([-sin, -sin, sin, sin], axis=1)


def attn_forward(blocks, full, bias, bias_at, table, seg_row, half, scale):
    n = len(blocks)
    T, D = blocks[0].shape
    wide = 4 * half
    N = n * T
    step = 4
    across_block = N

    def kernel(ins, outs, scratch):
        full, table, bias, seg_row = ins[n:]
        (qkv, leave_qkv), (context, leave_context), (logs, leave_logs), even, odd = outs
        w_in, w_out, x, values_t, context_t, x_sems = scratch
        copies = block_copies(ins[:n], x, x_sems)
        start_all(copies)
        load_attn(full(), w_in, w_out)
        table = table()
        for k in range(0, n, step):
            wait_all(copies[k : k + step])
            rows = slice(k * T, (k + step) * T)
            mixed = dot(x[rows], w_in[...]) + bias[:, bias_at : bias_at + 3 * wide]
            cos, sin = rotary(table, rows, half)
            for t, factor in ((0, scale), (1, 1.0)):
                part = mixed[:, t * wide : (t + 1) * wide]
                part = (part * cos + roll_halves(part) * sin).astype(BF)
                qkv[rows, t * wide : (t + 1) * wide] = part * jnp.asarray(factor, BF)
            qkv[rows, 2 * wide :] = mixed[:, 2 * wide :].astype(BF)
        leave_qkv()
        values_t[...] = qkv[:, 2 * wide :].T
        first_qk, _ = head_masks(wide)
        zero = jnp.zeros((), BF)

        def part(c, carry):
            at = pl.ds(pl.multiple_of(c * across_block, 128), across_block)
            allowed = table[:, 2 * half : 2 * half + 1] == seg_row[:, at]
            for head in range(2):
                mine = first_qk if head == 0 else jnp.logical_not(first_qk)
                query = jnp.where(mine, qkv[at, :wide], zero)
                scores = jnp.where(allowed, dot_rt(qkv[:, wide : 2 * wide], query), NEG_FILL)
                top = jnp.max(scores, axis=0, keepdims=True)
                weights = jnp.exp(scores - top)
                total = jnp.sum(weights, axis=0, keepdims=True)
                heads = slice(head * 2 * half, (head + 1) * 2 * half)
                context_t[heads, at] = dot(values_t[heads, :], weights.astype(BF)) * (1.0 / total)
                logs[head : head + 1, at] = top + jnp.log(total)
            return carry

        lax.fori_loop(0, N // across_block, part, 0)
        leave_logs()
        context[...] = context_t[...].T.astype(BF)
        leave_context()
        for k in range(0, n, step):
            put_blocks(dot(context[k * T : (k + step) * T], w_out[...]).astype(BF), k, (even, odd), T)

    outs = [((N, 3 * wide), BF, True), ((N, wide), BF, True), ((2, N), F32, True)]
    outs += [((n // 2, T, D), BF, n // 2), ((n // 2, T, D), BF, n // 2)]
    flops = 2 * N * D * 4 * wide + 8 * N * N * wide
    sems = pltpu.SemaphoreType.DMA
    scratch = [((D, 3 * wide), BF), ((wide, D), BF), ((N, D), BF), ((wide, N), BF), ((wide, N), F32), sems((n,))]
    ins = [raw(item) for item in blocks] + [held(full), held(table), near(bias), near(seg_row)]
    return call(kernel, ins, outs, scratch, flops)


def lanes_of(count):
    return max(w for w in (384, 256, 128) if count % w == 0)


def fetch_ffn(full, w_up, w_down, sems):
    far = full.shape[0]
    D, H = w_up.shape
    up, down = D // far, H // far
    first, second = [], []
    for o in range(far):
        for part in range(2):
            first.append(
                pltpu.make_async_copy(
                    full.at[o, pl.ds(0, up // 2), pl.ds(part * H, H)],
                    w_up.at[pl.ds(o * up + part * (up // 2), up // 2)],
                    sems.at[3 * o + part],
                )
            )
        second.append(
            pltpu.make_async_copy(
                full.at[o, pl.ds(up // 2, down)], w_down.at[pl.ds(o * down, down)], sems.at[3 * o + 2]
            )
        )
    return first, second


def start_all(copies):
    for copy in copies:
        copy.start()


def wait_all(copies):
    for copy in copies:
        copy.wait()


def block_copies(blocks, whole, sems):
    T = blocks[0].shape[0]
    return [pltpu.make_async_copy(block, whole.at[pl.ds(k * T, T)], sems.at[k]) for k, block in enumerate(blocks)]


def ffn_forward(blocks, full, bias, bias_at, H):
    n = len(blocks)
    T, D = blocks[0].shape
    step = 4

    def kernel(ins, outs, scratch):
        full, bias = ins[n:]
        (act, leave_act), (slope, leave_slope), even, odd = outs
        w_up, w_down, x, w_sems, x_sems = scratch
        first, second = fetch_ffn(full, w_up, w_down, w_sems)
        copies = block_copies(ins[:n], x, x_sems)
        start_all(first)
        start_all(copies)
        start_all(second)
        wait_all(first)
        for k in range(0, n, step):
            wait_all(copies[k : k + step])
            rows = slice(k * T, (k + step) * T)
            pre = dot(x[rows], w_up[...]) + bias[:, bias_at : bias_at + H]
            below = 0.5 * (1.0 + lax.erf(pre * math.sqrt(0.5)))
            result = (pre * below).astype(BF)
            act[rows] = result
            slope[rows] = (below + pre * (math.sqrt(0.5 / math.pi) * jnp.exp(-0.5 * pre * pre))).astype(BF)
            if k == 0:
                wait_all(second)
            back = dot(act[rows], w_down[...]).astype(BF)
            put_blocks(back, k, (even, odd), T)
        leave_act()
        leave_slope()

    outs = [((n * T, H), BF, True), ((n * T, H), BF, True), ((n // 2, T, D), BF, n // 2), ((n // 2, T, D), BF, n // 2)]
    ins = [raw(item) for item in blocks] + [raw(full), near(bias)]
    sems = pltpu.SemaphoreType.DMA
    scratch = [((D, H), BF), ((H, D), BF), ((n * T, D), BF), sems((3 * full.shape[0],)), sems((n,))]
    return call(kernel, ins, outs, scratch, 4 * n * T * D * H)


def put_blocks(rows, first, halves, T):
    for i in range(rows.shape[0] // T):
        out, leave = halves[(first + i) % 2]
        out[(first + i) // 2] = rows[i * T : (i + 1) * T]
        leave((first + i) // 2)


def ffn_back(blocks, full, slope):
    n = len(blocks)
    T, D = blocks[0].shape
    H = slope.shape[1]
    step = 4

    def kernel(ins, outs, scratch):
        full, slope = ins[n:]
        grad_pre, bias_grad, even, odd = outs
        w_up, w_down, x, w_sems, x_sems = scratch
        first, second = fetch_ffn(full, w_up, w_down, w_sems)
        copies = block_copies(ins[:n], x, x_sems)
        start_all(second)
        start_all(copies)
        start_all(first)
        wait_all(second)
        total = jnp.zeros((1, H), F32)
        for k in range(0, n, step):
            wait_all(copies[k : k + step])
            rows = slice(k * T, (k + step) * T)
            grad = (dot_rt(x[rows], w_down[...]) * slope()[rows].astype(F32)).astype(BF)
            grad_pre[rows] = grad
            total = total + jnp.sum(grad.astype(F32), axis=0, keepdims=True)
            if k == 0:
                wait_all(first)
            put_blocks(dot_rt(grad_pre[rows], w_up[...]).astype(BF), k, (even, odd), T)
        bias_grad[...] = total

    outs = [((n * T, H), BF), ((1, H), F32), ((n // 2, T, D), BF, n // 2), ((n // 2, T, D), BF, n // 2)]
    ins = [raw(item) for item in blocks] + [raw(full), held(slope)]
    sems = pltpu.SemaphoreType.DMA
    scratch = [((D, H), BF), ((H, D), BF), ((n * T, D), BF), sems((3 * full.shape[0],)), sems((n,))]
    return call(kernel, ins, outs, scratch, 4 * n * T * D * H)


def ffn_weights(normed, grads, act, grad_pre, far, extra):
    n = len(normed)
    T, D = normed[0].shape
    N = n * T
    H = act.shape[1]
    up, down = D // far, H // far
    more = [] if extra is None else [near(extra)]
    count = up // 2 + down + (0 if extra is None else extra.shape[1])

    def kernel(ins, outs, scratch):
        act, grad_pre = ins[2 * n : 2 * n + 2]
        left, right, left_sems, right_sems = scratch
        out = outs[0]
        copies = block_copies(ins[:n], left, left_sems)
        later = block_copies(ins[n : 2 * n], right, right_sems)
        start_all(copies)
        start_all(later)
        wait_all(copies)
        for o in range(far):
            block = dot_lt(left[:, o * up : (o + 1) * up], grad_pre[...]).astype(BF)
            out[o, : up // 2, :H] = block[: up // 2]
            out[o, : up // 2, H:] = block[up // 2 :]
        wait_all(later)
        act = act()
        for o in range(far):
            block = dot_lt(act[:, o * down : (o + 1) * down], right[...]).astype(BF)
            out[o, up // 2 : up // 2 + down] = block
            if more:
                out[o, up // 2 + down :] = ins[2 * n + 2][o]

    sems = pltpu.SemaphoreType.DMA
    scratch = [((N, D), BF), ((N, D), BF), sems((n,)), sems((n,))]
    ins = [raw(item) for item in (*normed, *grads)] + [held(act), near(grad_pre)] + more
    return call(kernel, ins, [((far, count, D), BF)], scratch, 4 * N * D * H)[0]


def attn_back(blocks, full, qkv, context, logs, table, seg_row, half, scale):
    n = len(blocks)
    T, D = blocks[0].shape
    wide = 4 * half
    N = n * T
    step = 4
    across_block = lanes_of(N)

    def kernel(ins, outs, scratch):
        full, table, qkv, context, logs, seg_row = ins[n:]
        mixed, bias_grad, even, odd = outs
        w_in, w_out, x, grad, delta, cos, sin, acc_k, acc_v, x_sems = scratch
        copies = block_copies(ins[:n], x, x_sems)
        start_all(copies)
        load_attn(full(), w_in, w_out)
        for k in range(0, n, step):
            wait_all(copies[k : k + step])
            rows = slice(k * T, (k + step) * T)
            grad[rows] = dot_rt(x[rows], w_out[...]).astype(BF)
        table = table()
        cos[...], sin[...] = rotary(table, slice(None), half)
        acc_k[...] = jnp.zeros_like(acc_k)
        acc_v[...] = jnp.zeros_like(acc_v)
        qkv, logs = qkv(), logs()
        product = (grad[...].astype(F32) * context()[...].astype(F32)).T
        delta[0:1] = jnp.sum(product[: 2 * half], axis=0, keepdims=True)
        delta[1:2] = jnp.sum(product[2 * half :], axis=0, keepdims=True)
        first_qk, first_v = head_masks(wide)
        zero = jnp.zeros((), BF)

        def part(c, carry):
            at = pl.ds(pl.multiple_of(c * across_block, 128), across_block)
            allowed = table[:, 2 * half : 2 * half + 1] == seg_row[:, at]
            grad_query = []
            for head in range(2):
                mine = first_qk if head == 0 else jnp.logical_not(first_qk)
                mine_v = first_v if head == 0 else jnp.logical_not(first_v)
                query = jnp.where(mine, qkv[at, :wide], zero)
                grad_h = jnp.where(mine_v, grad[at, :], zero)
                scores = dot_rt(qkv[:, wide : 2 * wide], query) - logs[head : head + 1, at]
                probs = jnp.exp(jnp.where(allowed, scores, NEG_FILL))
                grad_probs = dot_rt(qkv[:, 2 * wide :], grad_h)
                grad_scores = (probs * (grad_probs - delta[head : head + 1, at])).astype(BF)
                acc_k[...] += dot(grad_scores, query)
                acc_v[...] += dot(probs.astype(BF), grad_h)
                grad_query.append(dot_lt(grad_scores, qkv[:, wide : 2 * wide]))
            result = jnp.where(first_qk, grad_query[0], grad_query[1]) * scale
            mixed[at, :wide] = (result * cos[at, :] - roll_halves(result) * sin[at, :]).astype(BF)
            return carry

        lax.fori_loop(0, N // across_block, part, 0)
        total = acc_k[...]
        mixed[:, wide : 2 * wide] = (total * cos[...] - roll_halves(total) * sin[...]).astype(BF)
        mixed[:, 2 * wide :] = acc_v[...].astype(BF)
        sums = jnp.zeros((1, 3 * wide), F32)
        for k in range(0, n, step):
            rows = slice(k * T, (k + step) * T)
            sums = sums + jnp.sum(mixed[rows].astype(F32), axis=0, keepdims=True)
            put_blocks(dot_rt(mixed[rows], w_in[...]).astype(BF), k, (even, odd), T)
        bias_grad[...] = sums

    outs = [((N, 3 * wide), BF), ((1, 3 * wide), F32), ((n // 2, T, D), BF, n // 2), ((n // 2, T, D), BF, n // 2)]
    scratch = [((D, 3 * wide), BF), ((wide, D), BF), ((N, D), BF), ((N, wide), BF), ((2, N), F32)]
    scratch += [((N, wide), F32)] * 4 + [pltpu.SemaphoreType.DMA((n,))]
    flops = 2 * N * D * 4 * wide + 20 * N * N * wide
    ins = [raw(item) for item in blocks] + [held(item) for item in (full, table, qkv, context, logs)] + [near(seg_row)]
    return call(kernel, ins, outs, scratch, flops)


def attn_weights(inputs, grads, context, mixed, bias_grad, far, relative):
    n = len(inputs)
    T, D = inputs[0].shape
    N = n * T
    wide = context.shape[1]
    rows = D // far
    part = wide // far
    size = lax.axis_size("row")

    def kernel(ins, outs, scratch):
        context, mixed, bias_grad = ins[2 * n :]
        left, right, left_sems, right_sems = scratch
        here = (lax.axis_index("seq") * size + lax.axis_index("row")) // PLANE
        copies = block_copies(ins[:n], left, left_sems)
        later = block_copies(ins[n : 2 * n], right, right_sems)
        start_all(copies)
        start_all(later)
        wait_all(copies)
        for k in range(far):
            if relative:
                lanes = pl.ds(pl.multiple_of((here ^ k) * rows, 128), rows)
                outs[k][:rows, : 3 * wide] = dot_lt(left[:, lanes], mixed[...]).astype(BF)
            else:
                outs[0][k, :rows, : 3 * wide] = dot_lt(left[:, k * rows : (k + 1) * rows], mixed[...]).astype(BF)
        wait_all(later)
        whole = dot_lt(context()[...], right[...]).astype(BF)
        extra = jnp.broadcast_to(bias_grad[...], (16, 3 * wide)).astype(BF)
        if relative:
            right[:wide, :D] = whole
        for k in range(far):
            out = outs[k] if relative else outs[0].at[k]
            if relative:
                block = right[pl.ds(pl.multiple_of((here ^ k) * part, 16), part), :]
            else:
                block = whole[k * part : (k + 1) * part]
            for j in range(rows // part):
                out[j * part : (j + 1) * part, 3 * wide :] = block[:, j * wide : (j + 1) * wide]
            out[rows:, : 3 * wide] = extra
            out[rows:, 3 * wide :] = jnp.zeros((16, wide), BF)

    sems = pltpu.SemaphoreType.DMA
    scratch = [((N, D), BF), ((N, D), BF), sems((n,)), sems((n,))]
    ins = [raw(item) for item in (*inputs, *grads)] + [held(context), near(mixed), near(bias_grad)]
    if relative:
        outs = [((rows + 16, 4 * wide), BF)] * far
    else:
        outs = [((far, rows + 16, 4 * wide), BF)]
    return call(kernel, ins, outs, scratch, 8 * N * D * wide)


def plane_index():
    return lax.axis_index("seq") % (PLANE // lax.axis_size("row")) * lax.axis_size("row") + lax.axis_index("row")


def pack_shares(sums, others, ffn, lines, in_cols, hidden_cols):
    rows, width = sums[0].shape[0] - 16, sums[0].shape[1]
    part = rows // PLANE
    L = len(ffn)
    count = L * (in_cols + hidden_cols) + 128
    bias_lines = in_cols // 128
    first_line = part - L * bias_lines

    def kernel(ins, outs, scratch):
        even, odd, last = outs
        attn = scratch[0]
        n = len(sums)
        total = ins[0][...].astype(F32)
        for ref in ins[1:n]:
            total = total + ref[...].astype(F32)
        attn[0] = total.astype(BF)
        for layer in range(1, L):
            attn[layer] = ins[n + layer - 1][...]
        last[...] = attn[0, :rows, in_cols:]
        ups = ins[n + L - 1 : n + 2 * L - 1]
        lines = ins[n + 2 * L - 1]
        here = plane_index()
        line = lax.broadcasted_iota(jnp.int32, (part, 128), 0)
        for k in range(PLANE):
            to = here ^ k
            out = (odd if k % 2 else even).at[k // 2]
            at = pl.ds(pl.multiple_of(to * part, 16), part)
            half = pl.ds(pl.multiple_of(lax.rem(to, PLANE // 2) * part, 16), part)
            for layer in range(L):
                out[:, layer * in_cols : (layer + 1) * in_cols] = attn[layer, at, :in_cols]
                folded = ups[layer][half, :]
                own = jnp.where(to < PLANE // 2, folded[:, :hidden_cols], folded[:, hidden_cols:])
                start = L * in_cols + layer * hidden_cols
                out[:, start : start + hidden_cols] = own
            block = lines[to]
            for layer in range(L):
                bias = attn[layer, rows : rows + 16, :in_cols].astype(F32)[:1]
                for j in range(bias_lines):
                    spot = line == first_line + layer * bias_lines + j
                    block = jnp.where(spot, bias[:, j * 128 : (j + 1) * 128], block)
            out[:, count - 128 :] = block.astype(BF)

    half = PLANE // 2
    outs = [((half, part, count), BF), ((half, part, count), BF), ((rows, width - in_cols), BF)]
    ins = [near(item) for item in (*sums, *others, *ffn, lines)]
    return call(kernel, ins, outs, [((L, rows + 16, width), BF)], rows * count, SMALL)


def unpack_shares(even, core, got, L, in_cols, hidden_cols):
    part, count = even.shape[1:]
    wide = in_cols // 3
    D, far = PLANE * wide, hidden_cols // 128
    bias_lines = in_cols // 128
    first_line = part - L * bias_lines

    def natural(x):
        q = wide // 4
        return jnp.concatenate([x[:, :q], x[:, 2 * q : 3 * q], x[:, q : 2 * q], x[:, 3 * q :]], axis=1)

    def kernel(ins, outs, scratch):
        even, core, *got = ins
        w_in, w_up, lines, bias = outs
        here = plane_index()
        blocks = [even.at[0], core.at[0]] + [ref.at[j] for ref in got for j in range(2)]
        total = jnp.zeros((part, 128), F32)
        for k in range(PLANE):
            block = blocks[k][...].astype(F32)
            of = here ^ k
            own_lines = block[:, count - 128 :]
            total = total + own_lines
            for layer in range(L):
                for t in range(3):
                    at = pl.ds(pl.multiple_of(t * D + of * wide, 128), wide)
                    start = layer * in_cols + t * wide
                    columns = block[:, start : start + wide]
                    row = first_line + layer * bias_lines + t
                    line = own_lines[row : row + 1]
                    if t < 2:
                        columns, line = natural(columns), natural(line)
                    w_in[layer, :, at] = columns
                    bias[layer, :, at] = line
                for o in range(far):
                    at = pl.ds(pl.multiple_of(o * PLANE * 128 + of * 128, 128), 128)
                    start = L * in_cols + layer * hidden_cols + o * 128
                    w_up[layer, :, at] = block[:, start : start + 128]
        lines[...] = total

    outs = [((L, part, 3 * D), F32), ((L, part, far * PLANE * 128), F32), ((part, 128), F32), ((L, 1, 3 * D), F32)]
    ins = [near(item) for item in (even, core, *got)]
    return call(kernel, ins, outs, [], part * count * PLANE, SMALL)


def body(
    tokens,
    attn_in,
    attn_out,
    ffn_up,
    ffn_down,
    norm_gains,
    biases,
    colbert,
    log_scale,
    cotangent,
    seg_lengths,
    seg_kinds,
    pairing,
):
    S = lax.axis_size("seq")
    R = lax.axis_size("row")
    O = S * R // PLANE
    place = lax.axis_index("seq") * R + lax.axis_index("row")
    plane, far = place % PLANE, place // PLANE
    relative = jnp.bitwise_xor(plane, jnp.arange(PLANE, dtype=jnp.int32))
    T = tokens.shape[1]
    D = tokens.shape[2]
    N = PLANE * T
    L = attn_in.shape[0]
    head_dim = D // HEADS
    half = head_dim // 2
    scale = head_dim ** (-0.5)
    wide = 2 * head_dim
    in_cols = 3 * wide
    in_rows = attn_in.shape[1]
    rows_in = PLANE * in_rows
    FF = ffn_up.shape[2]
    up_cols = FF // (S * R)
    hidden_cols = O * up_cols
    gain_part = norm_gains.shape[1]
    bias_part = biases.shape[1]
    part = gain_part + bias_part
    along_z = [[o * (S // O) + i for o in range(O)] for i in range(S // O)]
    is_mine = jnp.arange(PLANE, dtype=jnp.int32) == plane

    def padded_rows(vector, width=D):
        rows = -(-vector.shape[0] // (16 * width)) * 16
        return jnp.pad(vector, (0, rows * width - vector.shape[0])).reshape(rows, width)

    def pack_columns(w):
        lead = w.shape[:-1]
        n = len(lead)
        qk = w[..., : 2 * D].reshape(*lead, 2, PLANE, 2, 2, half)
        qk = qk.transpose((n + 1,) + tuple(range(n)) + (n, n + 3, n + 2, n + 4)).reshape(PLANE, *lead, 2 * wide)
        v = w[..., 2 * D :].reshape(*lead, PLANE, wide)
        v = v.transpose((n,) + tuple(range(n)) + (n + 1,))
        return jnp.concatenate([qk, v], axis=-1)

    def unpack_columns(w):
        rows = w.shape[1]
        qk = w[:, :, : 2 * wide].reshape(PLANE, rows, 2, 2, 2, half)
        qk = qk.transpose(1, 2, 0, 4, 3, 5).reshape(rows, 2 * D)
        v = w[:, :, 2 * wide :].transpose(1, 0, 2).reshape(rows, D)
        return jnp.concatenate([qk, v], axis=1)

    def pack_hidden(w):
        rows = w.shape[0]
        return w.reshape(rows, O, PLANE, up_cols).transpose(2, 0, 1, 3).reshape(PLANE, rows, hidden_cols)

    def unpack_hidden(w):
        rows = w.shape[1]
        return w.reshape(PLANE, rows, O, up_cols).transpose(1, 2, 0, 3).reshape(rows, FF)

    def fold(w):
        n = w.shape[-2] // 2
        return jnp.concatenate([w[..., :n, :], w[..., n:, :]], axis=-1)

    def unfold(w):
        n = w.shape[-1] // 2
        return jnp.concatenate([w[..., :n], w[..., n:]], axis=-2)

    to_group = [(b, (b % O) * PLANE + b // O) for b in range(O * PLANE)]
    from_group = [(d, b) for b, d in to_group]
    small = jnp.concatenate([norm_gains.reshape(-1), biases.reshape(-1), colbert.reshape(-1)])
    small = jnp.broadcast_to(padded_rows(small, in_cols), (PLANE, *padded_rows(small, in_cols).shape))
    first_in = plane_exchange(jnp.concatenate([pack_columns(attn_in[0]), small], axis=1), relative)
    first_in, small = first_in[:, :in_rows].reshape(rows_in, in_cols), first_in[:, in_rows:].reshape(PLANE, -1)
    shard_out = lax.ppermute(attn_out, BOTH, to_group)
    table = turned(jnp.concatenate([seg_lengths[0], seg_kinds[0], pairing[0]]))
    seg_count = seg_lengths.shape[1]
    lengths, kinds = table[:seg_count], table[seg_count : 2 * seg_count]
    pairs_of = table[2 * seg_count :]
    hidden_low = turned(tokens[0])

    def attn_block(layer, shard):
        out = shard_out[layer].reshape(in_rows, PLANE, wide).transpose(1, 0, 2).reshape(rows_in, wide)
        return jnp.concatenate([shard, out], axis=1)

    def gather_far(x):
        return lax.all_gather(x, "seq", axis=0, axis_index_groups=along_z)

    own = attn_block(0, first_in)
    full_attn = [gather_far(own)]

    count_small = L * part
    col_plane = small[:, count_small : count_small + colbert.size].reshape(-1)
    params = small[None, :, :count_small]
    step = 1
    while step < O:
        other = across(params, PLANE * step)
        low_side = (far & step) == 0
        params = jnp.concatenate([jnp.where(low_side, params, other), jnp.where(low_side, other, params)], axis=0)
        step *= 2
    params = params.reshape(O * PLANE, count_small).astype(F32)
    gains_all = params[:, : L * gain_part].reshape(O * PLANE, L, gain_part).transpose(1, 0, 2).reshape(L, 2 * D)
    bias_all = params[:, L * gain_part :].reshape(O * PLANE, L, bias_part).transpose(1, 0, 2).reshape(L, -1)
    in_biases = pick(pack_columns(bias_all[:, : 3 * D]), plane, axis=0).reshape(1, L * in_cols)
    up_biases = pick(pack_hidden(bias_all[:, 4 * D : 4 * D + FF]), plane, axis=0).reshape(1, L * hidden_cols)
    rest_at = 4 * D + FF
    params = jnp.concatenate([gains_all, bias_all[:, 3 * D : 4 * D], bias_all[:, rest_at:]], axis=1).reshape(1, -1)
    GAIN_ONE, GAIN_TWO, BIAS_OUT, BIAS_DOWN, SHIFT_ONE, SHIFT_TWO = range(6)

    def at(layer, which):
        return (layer * 6 + which) * D

    rest = jnp.concatenate(
        [pack_hidden(ffn_up[0])]
        + [piece for layer in range(1, L) for piece in (pack_columns(attn_in[layer]), pack_hidden(ffn_up[layer]))],
        axis=-1,
    )
    rest = plane_exchange(rest, relative).reshape(rows_in, -1)
    full_ffn = []
    start = 0
    for layer in range(L):
        if layer > 0:
            full_attn.append(gather_far(attn_block(layer, rest[:, start : start + in_cols])))
            start += in_cols
        own = [fold(rest[:, start : start + hidden_cols]), ffn_down[layer]]
        start += hidden_cols
        if layer == L - 1:
            own.append(padded_rows(col_plane))
        full_ffn.append(gather_far(jnp.concatenate(own, axis=0)))
    w_col = full_ffn[L - 1][:, rows_in // 2 + up_cols :].reshape(O, -1)[:, : col_plane.size]
    w_col = w_col.reshape(D, colbert.shape[1])

    block_at = 4 * ((relative // 2 % 2) ^ (far % 2)) + 2 * (relative % 2) + relative // 4
    positions = (block_at[:, None] * T + jnp.arange(T, dtype=jnp.int32)[None, :]).reshape(N)
    held_segment, held_offset = token_info(positions, lengths, kinds)[:2]
    cos, sin = rope_angles(held_offset, head_dim)
    seg_row = held_segment.astype(F32)[None, :]
    table = jnp.concatenate([cos, sin, jnp.broadcast_to(seg_row.T, (N, wide - 2 * half))], axis=1)

    hidden = hidden_low
    records = []
    for layer in range(L):
        x_all = plane_gather(hidden_low)
        qkv, context, logs, even, odd = attn_forward(
            x_all, full_attn[layer], in_biases, layer * in_cols, table, seg_row, half, scale
        )
        terms, _ = plane_scatter(even, odd)
        first, normed, normed_low = add_norm(
            [hidden] + terms, params, at(layer, BIAS_OUT), at(layer, GAIN_ONE), at(layer, SHIFT_ONE)
        )
        normed_all = plane_gather(normed_low)
        act, slope, even, odd = ffn_forward(
            normed_all, full_ffn[layer], up_biases, layer * hidden_cols, hidden_cols
        )
        terms, _ = plane_scatter(even, odd)
        second, hidden, hidden_low = add_norm(
            [normed] + terms, params, at(layer, BIAS_DOWN), at(layer, GAIN_TWO), at(layer, SHIFT_TWO)
        )
        records.append((x_all, qkv, context, logs, first, normed_all, act, slope, second))
    hidden_out = turned(hidden_low, True)

    full_width = w_col.shape[1]
    part_widths = (full_width, full_width * 3 // 4, full_width // 2)
    query_total = NQ * QLEN
    doc_total = NSD + 1
    hidden_low, cot = tie(hidden_low, cotangent[0])
    cot = turned(cot)
    col = dot(hidden_low, w_col)
    in_order = jnp.arange(PLANE, dtype=jnp.int32)
    in_order = 4 * (in_order % 2) + 2 * ((in_order // 4) ^ (far % 2)) + in_order // 2 % 2
    in_order = jnp.bitwise_xor(in_order, plane)
    col_row = pick(jnp.stack(plane_gather(col.astype(BF))), in_order, axis=0).reshape(N, full_width).astype(F32)
    own_at = block_at[0] * T
    row_positions = jnp.arange(N, dtype=jnp.int32)
    segment, offset, is_query, query_slot, doc_num = token_info(row_positions, lengths, kinds)
    slots = jnp.arange(query_total, dtype=jnp.int32)[:, None]
    selector = (is_query == 1)[None, :] & (query_slot[None, :] == slots)
    selector_low = selector.astype(BF)
    own_selector = lax.dynamic_slice(selector.astype(F32), (0, own_at), (query_total, T))
    embeds = [unit_rows(col_row[:, :width]).astype(BF) for width in part_widths]
    query_emb = [dot(selector_low, embed).astype(BF) for embed in embeds]
    powers = jnp.exp(SHARPNESS * jnp.stack([dot_rt(query_emb[m], embeds[m]) for m in range(3)]))
    doc_code = jnp.where(is_query == 0, doc_num, -1)[None, None, :]
    totals = jnp.stack([jnp.sum(jnp.where(doc_code == d, powers, 0.0), axis=2) for d in range(doc_total)], axis=2)
    soft = jnp.log(totals) / SHARPNESS
    pair_sum = jnp.sum(soft.reshape(3, NQ, QLEN, doc_total), axis=2)
    inverse_temp = jnp.exp(log_scale[0])
    logits = pair_sum * inverse_temp / QLEN
    positive = pairs_of[None, :, None] == jnp.arange(doc_total, dtype=jnp.int32)[None, None, :]
    losses = jax.nn.logsumexp(logits, axis=-1) - jnp.sum(jnp.where(positive, logits, 0.0), axis=-1)
    loss_weight = 1.0 / (3 * NQ * R)
    grad_logits = loss_weight * (jax.nn.softmax(logits, axis=-1) - positive.astype(F32))
    loss_terms = jnp.stack([jnp.sum(losses) * loss_weight, jnp.sum(grad_logits * logits)])
    grad_pairs = grad_logits * inverse_temp / QLEN
    grad_soft = jnp.broadcast_to(grad_pairs[:, :, None, :], (3, NQ, QLEN, doc_total)).reshape(
        3, query_total, doc_total
    )
    ratio = grad_soft / totals
    weight = sum(jnp.where(doc_code == d, ratio[:, :, d : d + 1], 0.0) for d in range(doc_total))
    grad_sims = (powers * weight).astype(BF)
    own_sims = lax.dynamic_slice(grad_sims, (0, 0, own_at), (3, query_total, T))
    grad_col = jnp.zeros((T, full_width), F32)
    for m in range(3):
        width = part_widths[m]
        grad_query = dot(grad_sims[m], embeds[m])
        grad_embed = dot_lt(own_sims[m], query_emb[m]) + lax.dot_general(
            own_selector, grad_query, (((0,), (0,)), ((), ())), precision=HIGHEST, preferred_element_type=F32
        )
        pull_unit = jax.vjp(unit_rows, col[:, :width])[1]
        grad_col = grad_col + jnp.pad(pull_unit(grad_embed)[0], ((0, 0), (0, full_width - width)))
    grad_col_low, cot = tie(grad_col.astype(BF), cot)
    col_parts = dot_lt(hidden_low, grad_col_low).reshape(O, PLANE, in_rows, full_width).transpose(1, 0, 2, 3)
    col_parts = plane_sum(pick(col_parts.reshape(PLANE, O * in_rows, full_width), relative, axis=0))
    col_rows = jax.vmap(padded_rows)(col_parts.reshape(O, in_rows * full_width)).astype(BF)
    grad_parts = [cot, dot_rt(grad_col_low, w_col)]

    def scatter_far(whole):
        whole = whole.reshape(-1, whole.shape[-1])
        return lax.psum_scatter(whole, "seq", scatter_dimension=0, tiled=True, axis_index_groups=along_z)

    outs = [[None] * L for _ in range(6)]

    def finish_out(layer, share_out):
        share_out = share_out.reshape(PLANE, in_rows, wide).transpose(1, 0, 2).reshape(in_rows, D)
        outs[1][layer] = lax.ppermute(share_out, BOTH, from_group).astype(F32)

    shares_ffn, shares_attn = [None] * L, [None] * L
    vectors = [None] * L
    for layer in reversed(range(L)):
        x_all, qkv, context, logs, first, normed_all, act, slope, second = records[layer]
        grad_second, grad_ffo, sums_two = norm_back(grad_parts, second, params, at(layer, GAIN_TWO))
        ffo_all = plane_gather(grad_ffo)
        if layer == L - 1:
            ffo_all, hidden_out = tie(ffo_all, hidden_out)
        grad_pre, grad_bias_up, even, odd = ffn_back(ffo_all, full_ffn[layer], slope)
        blocks = ffn_weights(normed_all, ffo_all, act, grad_pre, O, col_rows if layer == L - 1 else None)
        terms, blocks = plane_scatter(even, odd, blocks)
        shares_ffn[layer] = scatter_far(blocks)
        grad_first, grad_branch, sums_one = norm_back([grad_second] + terms, first, params, at(layer, GAIN_ONE))
        branch_all = plane_gather(grad_branch)
        if layer < L - 1:
            branch_all, shares_attn[layer + 1] = tie(branch_all, shares_attn[layer + 1])
        grad_mixed, grad_bias_in, even, odd = attn_back(
            branch_all, full_attn[layer], qkv, context, logs, table, seg_row, half, scale
        )

        gain_two, shift_two, down, gain_one, shift_one, out = [
            sums[0, k * D : (k + 1) * D] for sums in (sums_two, sums_one) for k in range(3)
        ]
        own_up = unpack_hidden(is_mine[:, None, None].astype(F32) * grad_bias_up[None])[0]
        gains = jnp.concatenate([gain_one, gain_two]).reshape(O, PLANE, gain_part)
        bias = jnp.concatenate([jnp.zeros((3 * D,), F32), out, own_up, down, shift_one, shift_two])
        vectors[layer] = jnp.concatenate([gains, bias.reshape(O, PLANE, bias_part)], axis=2)

        blocks = attn_weights(x_all, branch_all, context, grad_mixed, grad_bias_in, O, layer == 0)
        terms, blocks = plane_scatter(even, odd, blocks, layer == 0)
        terms, shares_ffn[layer] = tie(terms, shares_ffn[layer])
        if layer > 0:
            shares_attn[layer] = scatter_far(blocks[0])
            grad_parts = [grad_first] + terms

    got = [across(blocks[step], PLANE * step) for step in range(1, O)]
    entries = jnp.concatenate(vectors, axis=2).transpose(1, 0, 2).reshape(PLANE, O * L * part)
    lines = jnp.pad(entries, ((0, 0), (0, in_rows * 128 - O * L * part))).reshape(PLANE, in_rows, 128)
    got, lines = tie(got, lines)
    grad_tokens = turned((grad_first + sum(item.astype(F32) for item in terms)).astype(BF), True)
    even, odd, last_out = pack_shares([blocks[0]] + got, shares_attn[1:], shares_ffn, lines, in_cols, hidden_cols)
    core, grad_tokens = tie(across(odd, 1), grad_tokens)
    got = tie(*[across(jnp.stack([even[k], core[k]]), 2 * k) for k in (1, 2, 3)])
    w_in_grad, w_up_grad, lines, bias_in_grad = unpack_shares(even, core, got, L, in_cols, hidden_cols)
    entries = lines.reshape(-1)[: O * L * part].reshape(O, L * part)
    entries = jnp.concatenate([entries, jnp.broadcast_to(loss_terms[None], (O, 2))], axis=1)
    mine = pick(entries, far)
    for step in range(1, O):
        mine = mine + across(pick(entries, far ^ step), PLANE * step)
    bias_in_grad = jnp.pad(bias_in_grad[:, 0], ((0, 0), (0, O * PLANE * bias_part - 3 * D)))
    bias_in_grad = pick(bias_in_grad.reshape(L, O * PLANE, bias_part), place, axis=1)
    for layer in range(L):
        outs[3][layer] = shares_ffn[layer][rows_in // 2 : rows_in // 2 + up_cols]
        finish_out(layer, shares_attn[layer][:rows_in, in_cols:] if layer > 0 else last_out)
        outs[4][layer] = mine[layer * part : layer * part + gain_part]
        outs[5][layer] = mine[layer * part + gain_part : (layer + 1) * part] + bias_in_grad[layer]
    col_share = shares_ffn[L - 1][rows_in // 2 + up_cols :].reshape(-1)[: in_rows * full_width]
    col_share = col_share.reshape(in_rows, full_width).astype(F32)
    loss_terms = mine[L * part :]
    outs[0], outs[2] = w_in_grad, w_up_grad
    stacked = [jnp.stack(items).astype(F32) if isinstance(items, list) else items for items in outs]
    return (
        hidden_out[None],
        loss_terms[:1],
        grad_tokens.astype(F32)[None],
        stacked[0],
        stacked[1],
        stacked[2],
        stacked[3],
        stacked[4],
        stacked[5],
        col_share,
        loss_terms[1:],
    )


def joined_2(value, axis, join):
    pieces = jax.tree.map(lambda part: lax.all_gather(part, axis), value)
    head = jax.tree.map(lambda part: part[0], pieces)
    tail = jax.tree.map(lambda part: part[1:], pieces)
    so_far, _ = lax.scan(lambda so_far, section: (join(so_far, section), None), head, tail)
    return so_far


def rope_tables(offset, head_dim):
    half = head_dim // 2
    inverse = jnp.exp(jnp.arange(half, dtype=jnp.float32) * (-2.0 * math.log(10000.0) / head_dim))
    angle = offset.astype(jnp.float32)[:, None] * inverse[None, :]
    return (jnp.cos(angle), jnp.sin(angle))


def rotate(flat, cos_table, sin_table):
    length = flat.shape[0]
    head_dim = flat.shape[1] // HEADS
    half = head_dim // 2
    shaped = flat.reshape(length, HEADS, head_dim)
    first_half = shaped[..., :half]
    second_half = shaped[..., half:]
    cos_three = cos_table[:, None, :]
    sin_three = sin_table[:, None, :]
    turned = jnp.concatenate(
        [
            first_half * cos_three - second_half * sin_three,
            second_half * cos_three + first_half * sin_three,
        ],
        axis=-1,
    )
    return turned.reshape(length, flat.shape[1])


def block_for(count):
    blocks = count
    while blocks > 1024 and blocks % 2 == 0:
        blocks = blocks // 2
    return blocks


def merge_pair(first, second):
    max_first, sum_first = first
    max_second, sum_second = second
    top = jnp.maximum(max_first, max_second)
    return (top, sum_first * jnp.exp(max_first - top) + sum_second * jnp.exp(max_second - top))


def matmul_left_t(left, right):
    return jnp.einsum("ti,to->io", left, right, preferred_element_type=jnp.float32)


def matmul_right_t(left, right):
    return jnp.einsum("to,io->ti", left, right, preferred_element_type=jnp.float32)


def body_wide(
    tokens,
    attn_in,
    attn_out,
    ffn_up,
    ffn_down,
    norm_gains,
    biases,
    colbert,
    log_scale,
    cotangent,
    seg_lengths,
    seg_kinds,
    pairing,
):
    rank = lax.axis_index("seq")
    local_len = tokens.shape[1]
    model_width = tokens.shape[2]
    head_dim = model_width // HEADS
    scale = head_dim ** (-0.5)
    lengths = seg_lengths[0]
    kinds = seg_kinds[0]
    positions = rank * local_len + jnp.arange(local_len, dtype=jnp.int32)
    segment, offset, is_query, query_slot, doc_num = token_info(positions, lengths, kinds)
    cos_table, sin_table = rope_tables(offset, head_dim)
    layer_count = attn_in.shape[0]

    def split_pieces(key_piece, value_piece):
        count = key_piece.shape[0]
        blocks = block_for(count)
        key_seg = token_info(jnp.arange(count, dtype=jnp.int32), lengths, kinds)[0]
        key_blocks = key_piece.reshape(count // blocks, blocks, HEADS, head_dim)
        value_blocks = value_piece.reshape(count // blocks, blocks, HEADS, head_dim)
        seg_blocks = key_seg.reshape(count // blocks, blocks)
        return (count, blocks, key_blocks, value_blocks, seg_blocks)

    def attend_back(queries, keys, values, context, log_total, grad_context):
        query_three = queries.reshape(local_len, HEADS, head_dim)
        grad_three = grad_context.reshape(local_len, HEADS, head_dim)
        delta = jnp.sum(
            grad_three.astype(jnp.float32) * context.reshape(local_len, HEADS, head_dim), axis=-1
        ).T

        def score_grads(
            query_blk, grad_blk, key_blk, value_blk, query_seg, key_seg, total_blk, delta_blk
        ):
            scores = (
                jnp.einsum("qhd,khd->hqk", query_blk, key_blk, preferred_element_type=jnp.float32)
                * scale
            )
            allowed = (query_seg[:, None] == key_seg[None, :])[None]
            probs = jnp.where(allowed, jnp.exp(scores - total_blk[..., None]), 0.0)
            grad_probs = jnp.einsum(
                "qhd,khd->hqk", grad_blk, value_blk, preferred_element_type=jnp.float32
            )
            grad_scores = (probs * (grad_probs - delta_blk[..., None])).astype(jnp.bfloat16)
            return (probs, grad_scores)

        grad_query = jnp.zeros((local_len, HEADS, head_dim), jnp.float32)
        count, blocks, key_blocks, value_blocks, seg_blocks = split_pieces(
            lax.all_gather(keys, "seq", axis=0, tiled=True),
            lax.all_gather(values, "seq", axis=0, tiled=True),
        )

        def advance(grad_acc, item):
            key_blk, value_blk, seg_blk = item
            probs, grad_scores = score_grads(
                query_three, grad_three, key_blk, value_blk, segment, seg_blk, log_total, delta
            )
            grad_acc = grad_acc + scale * jnp.einsum(
                "hqk,khd->qhd", grad_scores, key_blk, preferred_element_type=jnp.float32
            )
            grad_key = scale * jnp.einsum(
                "hqk,qhd->khd", grad_scores, query_three, preferred_element_type=jnp.float32
            )
            grad_value = jnp.einsum(
                "hqk,qhd->khd",
                probs.astype(jnp.bfloat16),
                grad_three,
                preferred_element_type=jnp.float32,
            )
            joined = jnp.concatenate(
                [grad_key.reshape(blocks, model_width), grad_value.reshape(blocks, model_width)],
                axis=1,
            )
            return (grad_acc, joined)

        grad_query, pieces_out = lax.scan(
            advance, grad_query, (key_blocks, value_blocks, seg_blocks)
        )
        grad_rows = pieces_out.reshape(count, 2 * model_width)
        grad_query, grad_rows = (grad_query, grad_rows)
        summed = lax.psum_scatter(
            grad_rows.astype(jnp.bfloat16), "seq", scatter_dimension=0, tiled=True
        ).astype(jnp.float32)
        grad_key_out = summed[:, :model_width]
        grad_value_out = summed[:, model_width:]
        return (grad_query.reshape(local_len, model_width), grad_key_out, grad_value_out)

    def unpack(full):
        w_in, w_out, w_up, w_down, gains, bias = full[:6]
        hidden_units = w_up.shape[1]
        gains_f = gains.astype(jnp.float32)
        bias_f = bias.astype(jnp.float32)
        width_three = 3 * model_width
        return (
            w_in,
            w_out,
            w_up,
            w_down,
            hidden_units,
            gains_f[:model_width],
            gains_f[model_width:],
            bias_f[:width_three],
            bias_f[width_three : 4 * model_width],
            bias_f[4 * model_width : 4 * model_width + hidden_units],
            bias_f[4 * model_width + hidden_units : 5 * model_width + hidden_units],
            bias_f[5 * model_width + hidden_units : 6 * model_width + hidden_units],
            bias_f[6 * model_width + hidden_units :],
        )

    def layer_backward(grad_out, full, record):
        (
            w_in,
            w_out,
            w_up,
            w_down,
            hidden_units,
            gain_one,
            gain_two,
            bias_in,
            bias_out,
            bias_up,
            bias_down,
            shift_one,
            shift_two,
        ) = unpack(full)
        (
            inputs_low,
            queries,
            keys,
            values,
            context,
            context_low,
            log_total,
            first,
            normed,
            normed_low,
            pre_act,
            act_low,
            second,
        ) = record
        unused, pull_two = jax.vjp(layer_norm, second, gain_two, shift_two)
        grad_second, grad_gain_two, grad_shift_two = pull_two(grad_out)
        grad_branch_two = grad_second.astype(jnp.bfloat16)
        grad_bias_down = jnp.sum(grad_branch_two.astype(jnp.float32), axis=0)
        grad_w_down = matmul_left_t(act_low, grad_branch_two)
        grad_act = matmul_right_t(grad_branch_two, w_down)
        unused, pull_gelu = jax.vjp(exact_gelu, pre_act)
        grad_pre = pull_gelu(grad_act)[0].astype(jnp.bfloat16)
        grad_bias_up = jnp.sum(grad_pre.astype(jnp.float32), axis=0)
        grad_w_up = matmul_left_t(normed_low, grad_pre)
        grad_normed = grad_second + matmul_right_t(grad_pre, w_up)
        unused, pull_one = jax.vjp(layer_norm, first, gain_one, shift_one)
        grad_first, grad_gain_one, grad_shift_one = pull_one(grad_normed)
        grad_branch = grad_first.astype(jnp.bfloat16)
        grad_bias_out = jnp.sum(grad_branch.astype(jnp.float32), axis=0)
        grad_w_out = matmul_left_t(context_low, grad_branch)
        grad_context = matmul_right_t(grad_branch, w_out).astype(jnp.bfloat16)
        grad_query, grad_key, grad_value = attend_back(
            queries, keys, values, context, log_total, grad_context
        )
        grad_mixed = jnp.concatenate(
            [
                rotate(grad_query, cos_table, -sin_table),
                rotate(grad_key, cos_table, -sin_table),
                grad_value,
            ],
            axis=1,
        ).astype(jnp.bfloat16)
        grad_bias_in = jnp.sum(grad_mixed.astype(jnp.float32), axis=0)
        grad_w_in = matmul_left_t(inputs_low, grad_mixed)
        grad_hidden = grad_first + matmul_right_t(grad_mixed, w_in)
        grad_gains = jnp.concatenate([grad_gain_one, grad_gain_two])
        grad_bias = jnp.concatenate(
            [
                grad_bias_in,
                grad_bias_out,
                grad_bias_up,
                grad_bias_down,
                grad_shift_one,
                grad_shift_two,
            ]
        )
        return (grad_hidden, (grad_w_in, grad_w_out, grad_w_up, grad_w_down, grad_gains, grad_bias))

    hidden = tokens[0].astype(jnp.float32)
    records = []
    gathered = []
    for layer_index in range(layer_count):
        full = (
            lax.all_gather(attn_in[layer_index], ("seq", "row"), axis=0, tiled=True),
            lax.all_gather(attn_out[layer_index], ("seq", "row"), axis=0, tiled=True),
            lax.all_gather(ffn_up[layer_index], ("seq", "row"), axis=0, tiled=True),
            lax.all_gather(ffn_down[layer_index], ("seq", "row"), axis=0, tiled=True),
            lax.all_gather(norm_gains[layer_index], ("seq", "row"), axis=0, tiled=True),
            lax.all_gather(biases[layer_index], ("seq", "row"), axis=0, tiled=True),
            lax.all_gather(colbert, ("seq", "row"), axis=0, tiled=True),
        )
        gathered.append(full)
        (
            layer_w_in,
            layer_w_out,
            layer_w_up,
            layer_w_down,
            layer_hidden_units,
            layer_gain_one,
            layer_gain_two,
            layer_bias_in,
            layer_bias_out,
            layer_bias_up,
            layer_bias_down,
            layer_shift_one,
            layer_shift_two,
        ) = unpack(full)
        layer_inputs_low = hidden.astype(jnp.bfloat16)
        mixed = (
            jnp.dot(layer_inputs_low, layer_w_in, preferred_element_type=jnp.float32)
            + layer_bias_in
        )
        layer_queries = rotate(mixed[:, :model_width], cos_table, sin_table).astype(jnp.bfloat16)
        layer_keys = rotate(mixed[:, model_width : 2 * model_width], cos_table, sin_table).astype(
            jnp.bfloat16
        )
        layer_values = mixed[:, 2 * model_width :].astype(jnp.bfloat16)
        attend_query_three = layer_queries.reshape(local_len, HEADS, head_dim)
        attend_initial = (
            jnp.full((HEADS, local_len), NEG_FILL, jnp.float32),
            jnp.zeros((HEADS, local_len), jnp.float32),
            jnp.zeros((local_len, HEADS, head_dim), jnp.float32),
        )
        absorb_carry = attend_initial
        absorb_count, absorb_blocks, absorb_key_blocks, absorb_value_blocks, absorb_seg_blocks = (
            split_pieces(
                lax.all_gather(layer_keys, "seq", axis=0, tiled=True),
                lax.all_gather(layer_values, "seq", axis=0, tiled=True),
            )
        )

        def absorb_advance(state, item):
            run_max, run_sum, accum = state
            key_blk, value_blk, seg_blk = item
            scores = (
                jnp.einsum(
                    "qhd,khd->hqk", attend_query_three, key_blk, preferred_element_type=jnp.float32
                )
                * scale
            )
            allowed = (segment[:, None] == seg_blk[None, :])[None]
            scores = jnp.where(allowed, scores, NEG_FILL)
            new_max = jnp.maximum(run_max, jnp.max(scores, axis=-1))
            weights = jnp.where(allowed, jnp.exp(scores - new_max[..., None]), 0.0)
            factor = jnp.exp(run_max - new_max)
            run_sum = run_sum * factor + jnp.sum(weights, axis=-1)
            accum = accum * factor.T[:, :, None] + jnp.einsum(
                "hqk,khd->qhd",
                weights.astype(jnp.bfloat16),
                value_blk,
                preferred_element_type=jnp.float32,
            )
            return ((new_max, run_sum, accum), None)

        absorb_carry, absorb_unused = lax.scan(
            absorb_advance,
            absorb_carry,
            (absorb_key_blocks, absorb_value_blocks, absorb_seg_blocks),
        )
        run_max, run_sum, accum = absorb_carry
        attend_context = (accum / run_sum.T[:, :, None]).reshape(local_len, model_width)
        attend_log_total = run_max + jnp.log(run_sum)
        layer_context_low = attend_context.astype(jnp.bfloat16)
        layer_first = (
            hidden
            + jnp.dot(layer_context_low, layer_w_out, preferred_element_type=jnp.float32)
            + layer_bias_out
        )
        layer_normed = layer_norm(layer_first, layer_gain_one, layer_shift_one)
        layer_normed_low = layer_normed.astype(jnp.bfloat16)
        layer_pre_act = (
            jnp.dot(layer_normed_low, layer_w_up, preferred_element_type=jnp.float32)
            + layer_bias_up
        )
        layer_act_low = exact_gelu(layer_pre_act).astype(jnp.bfloat16)
        layer_second = (
            layer_normed
            + jnp.dot(layer_act_low, layer_w_down, preferred_element_type=jnp.float32)
            + layer_bias_down
        )
        output = layer_norm(layer_second, layer_gain_two, layer_shift_two)
        layer_record = (
            layer_inputs_low,
            layer_queries,
            layer_keys,
            layer_values,
            attend_context,
            layer_context_low,
            attend_log_total,
            layer_first,
            layer_normed,
            layer_normed_low,
            layer_pre_act,
            layer_act_low,
            layer_second,
        )
        hidden = output
        record = layer_record
        records.append(record)
    w_col = gathered[layer_count - 1][6]
    final_low = hidden.astype(jnp.bfloat16)
    col = jnp.dot(final_low, w_col, preferred_element_type=jnp.float32)
    full_width = w_col.shape[1]
    part_widths = (full_width, full_width * 3 // 4, full_width // 2)
    query_total = NQ * QLEN
    doc_total = NSD + 1
    selector = (is_query == 1)[None, :] & (
        query_slot[None, :] == jnp.arange(query_total, dtype=jnp.int32)[:, None]
    )
    selector_low = selector.astype(jnp.bfloat16)
    embeds = [unit_rows(col[:, :part_width]).astype(jnp.bfloat16) for part_width in part_widths]
    picked = (
        lax.psum(
            jnp.dot(selector_low, embeds[0], preferred_element_type=jnp.float32).astype(
                jnp.bfloat16
            ),
            "seq",
        ).astype(jnp.float32),
        lax.psum(
            jnp.dot(selector_low, embeds[1], preferred_element_type=jnp.float32).astype(
                jnp.bfloat16
            ),
            "seq",
        ).astype(jnp.float32),
        lax.psum(
            jnp.dot(selector_low, embeds[2], preferred_element_type=jnp.float32).astype(
                jnp.bfloat16
            ),
            "seq",
        ).astype(jnp.float32),
    )
    query_emb = [item.astype(jnp.bfloat16) for item in picked]
    sims = jnp.stack(
        [
            jnp.einsum(
                "qc,tc->qt", query_emb[part], embeds[part], preferred_element_type=jnp.float32
            )
            for part in range(3)
        ]
    )
    doc_mask = (
        (is_query == 0)[:, None]
        & (doc_num[:, None] == jnp.arange(doc_total, dtype=jnp.int32)[None, :])
    )[None, None]
    scaled = jnp.where(doc_mask, SHARPNESS * sims[..., None], NEG_FILL)
    part_max = jnp.max(scaled, axis=2)
    part_sum = jnp.sum(jnp.where(doc_mask, jnp.exp(scaled - part_max[:, :, None, :]), 0.0), axis=2)
    top, total = joined_2((part_max, part_sum), "seq", merge_pair)
    soft = (top + jnp.log(total)) / SHARPNESS
    pair_sum = jnp.sum(soft.reshape(3, NQ, QLEN, doc_total), axis=2)
    inverse_temp = jnp.exp(log_scale[0])
    logits = pair_sum * inverse_temp / QLEN
    positive = pairing[0][None, :, None] == jnp.arange(doc_total, dtype=jnp.int32)[None, None, :]
    losses = jax.nn.logsumexp(logits, axis=-1) - jnp.sum(jnp.where(positive, logits, 0.0), axis=-1)
    loss_weight = 1.0 / (3 * NQ * lax.axis_size("row"))
    grad_logits = loss_weight * (jax.nn.softmax(logits, axis=-1) - positive.astype(jnp.float32))
    loss_total, temp_grad = lax.psum(
        (jnp.sum(losses).reshape(1) * loss_weight, jnp.sum(grad_logits * logits).reshape(1)), "row"
    )
    grad_pairs = grad_logits * inverse_temp / QLEN
    grad_soft = jnp.broadcast_to(grad_pairs[:, :, None, :], (3, NQ, QLEN, doc_total)).reshape(
        3, query_total, doc_total
    )
    shares = jnp.where(doc_mask, jnp.exp(scaled - top[:, :, None, :]), 0.0) / total[:, :, None, :]
    grad_sims = jnp.sum(shares * grad_soft[:, :, None, :], axis=-1).astype(jnp.bfloat16)
    grad_query_emb = (
        lax.psum(
            jnp.dot(grad_sims[0], embeds[0], preferred_element_type=jnp.float32).astype(
                jnp.bfloat16
            ),
            "seq",
        ).astype(jnp.float32),
        lax.psum(
            jnp.dot(grad_sims[1], embeds[1], preferred_element_type=jnp.float32).astype(
                jnp.bfloat16
            ),
            "seq",
        ).astype(jnp.float32),
        lax.psum(
            jnp.dot(grad_sims[2], embeds[2], preferred_element_type=jnp.float32).astype(
                jnp.bfloat16
            ),
            "seq",
        ).astype(jnp.float32),
    )
    selector_f = selector.astype(jnp.float32)
    grad_col = jnp.zeros((local_len, full_width), jnp.float32)
    for part in range(3):
        part_width = part_widths[part]
        grad_embed = jnp.einsum(
            "qt,qc->tc", grad_sims[part], query_emb[part], preferred_element_type=jnp.float32
        )
        grad_embed = grad_embed + jnp.einsum(
            "qt,qc->tc",
            selector_f,
            grad_query_emb[part],
            precision=HIGHEST,
            preferred_element_type=jnp.float32,
        )
        unused, pull_unit = jax.vjp(unit_rows, col[:, :part_width])
        grad_col = grad_col.at[:, :part_width].add(pull_unit(grad_embed)[0])
    grad_col_low = grad_col.astype(jnp.bfloat16)
    grad_w_col = matmul_left_t(final_low, grad_col_low)
    grad_hidden = cotangent[0].astype(jnp.float32) + matmul_right_t(grad_col_low, w_col)
    shard_lists = [[] for unused_slot in range(6)]
    col_share = None
    for layer_index in reversed(range(layer_count)):
        full = (
            lax.all_gather(attn_in[layer_index], ("seq", "row"), axis=0, tiled=True),
            lax.all_gather(attn_out[layer_index], ("seq", "row"), axis=0, tiled=True),
            lax.all_gather(ffn_up[layer_index], ("seq", "row"), axis=0, tiled=True),
            lax.all_gather(ffn_down[layer_index], ("seq", "row"), axis=0, tiled=True),
            lax.all_gather(norm_gains[layer_index], ("seq", "row"), axis=0, tiled=True),
            lax.all_gather(biases[layer_index], ("seq", "row"), axis=0, tiled=True),
            lax.all_gather(colbert, ("seq", "row"), axis=0, tiled=True),
        )
        grad_hidden, layer_grads = layer_backward(grad_hidden, full, records[layer_index])
        col_term = grad_w_col if layer_index == layer_count - 1 else jnp.zeros_like(grad_w_col)
        shares_out = (
            lax.psum_scatter(layer_grads[0], ("seq", "row"), scatter_dimension=0, tiled=True),
            lax.psum_scatter(layer_grads[1], ("seq", "row"), scatter_dimension=0, tiled=True),
            lax.psum_scatter(layer_grads[2], ("seq", "row"), scatter_dimension=0, tiled=True),
            lax.psum_scatter(layer_grads[3], ("seq", "row"), scatter_dimension=0, tiled=True),
            lax.psum_scatter(layer_grads[4], ("seq", "row"), scatter_dimension=0, tiled=True),
            lax.psum_scatter(layer_grads[5], ("seq", "row"), scatter_dimension=0, tiled=True),
            lax.psum_scatter(col_term, ("seq", "row"), scatter_dimension=0, tiled=True),
        )
        for slot in range(6):
            shard_lists[slot].insert(0, shares_out[slot])
        if layer_index == layer_count - 1:
            col_share = shares_out[6]
    stacked = [jnp.stack(items) for items in shard_lists]
    return (
        hidden.astype(jnp.bfloat16)[None],
        loss_total,
        grad_hidden[None],
        stacked[0],
        stacked[1],
        stacked[2],
        stacked[3],
        stacked[4],
        stacked[5],
        col_share,
        temp_grad,
    )


def solution(mesh):
    placed = (
        P("row", "seq", None),
        P(None, ("seq", "row"), None),
        P(None, ("seq", "row"), None),
        P(None, ("seq", "row"), None),
        P(None, ("seq", "row"), None),
        P(None, ("seq", "row")),
        P(None, ("seq", "row")),
        P(("seq", "row"), None),
        P(),
        P("row", "seq", None),
        P("row", None),
        P("row", None),
        P("row", None),
    )
    planes = mesh.shape["row"] == 4 and mesh.shape["seq"] * 4 == 4 * PLANE and HEADS == 2 * PLANE
    return jax.shard_map(
        body if planes else body_wide,
        mesh=mesh,
        in_specs=placed,
        out_specs=(
            P("row", "seq", None),
            P(),
            P("row", "seq", None),
            P(None, ("seq", "row"), None),
            P(None, ("seq", "row"), None),
            P(None, ("seq", "row"), None),
            P(None, ("seq", "row"), None),
            P(None, ("seq", "row")),
            P(None, ("seq", "row")),
            P(("seq", "row"), None),
            P(),
        ),
        check_vma=False,
    )
```

```python
import math

import jax
import jax.numpy as jnp
from jax import lax
from jax.experimental import pallas as pl
from jax.experimental.pallas import tpu as pltpu
from jax.sharding import PartitionSpec as P

HEADS = 16
QLEN = 32
NQ = 4
NSD = 3

NEG_FILL = -1e30
SHARPNESS = 16.0
HIGHEST = lax.Precision.HIGHEST
BF = jnp.bfloat16
F32 = jnp.float32

def dot(left, right):
    return jnp.dot(left, right, preferred_element_type=F32)


def dot_lt(left, right):
    return lax.dot_general(left, right, (((0,), (0,)), ((), ())), preferred_element_type=F32)


def dot_rt(left, right):
    return lax.dot_general(left, right, (((1,), (1,)), ((), ())), preferred_element_type=F32)


PLANE = 8
BOTH = ("seq", "row")


def across(x, mask):
    size = lax.axis_size("seq") * lax.axis_size("row")
    return lax.ppermute(x, BOTH, [(d, d ^ mask) for d in range(size)])


def turned(x, back=False):
    size = lax.axis_size("seq") * lax.axis_size("row")
    pairs = []
    for d in range(size):
        z, y, column, core = d // PLANE, d // 4 % 2, d // 2 % 2, d % 2
        to = (2 * core + column) * PLANE + 4 * y + 2 * (column ^ (z // 2)) + z % 2
        pairs.append((to, d) if back else (d, to))
    return lax.ppermute(x, BOTH, pairs)


def plane_gather(x):
    blocks = [x, None, across(x, 2), None, across(x, 4), None, across(x, 6), None]
    for k in range(0, PLANE, 2):
        blocks[k + 1] = across(blocks[k], 1)
    return blocks


def plane_scatter(even, odd, beside=None, first=False):
    core = across(odd, 1)
    if first:
        core, beside = tie(core, beside)
    parts = core_add(even, core)
    got = [across(parts[j], 2 * j) for j in (1, 2, 3)]
    if beside is not None and not first:
        got, beside = tie(got, beside)
    return [parts[0]] + got, beside


def plane_sum(parts):
    parts = parts.astype(BF)
    core = across(parts[1::2], 1).astype(F32) + parts[0::2].astype(F32)
    sent = core[1:].astype(BF)
    return core[0] + sum(across(sent[k - 1], 2 * k).astype(F32) for k in (1, 2, 3))


def plane_exchange(x, relative, before=None):
    x = pick(x, relative)
    core = across(x[1::2], 1)
    if before is not None:
        core, before = tie(core, before)
    got = tie(*[across(jnp.stack([x[2 * k], core[k]]), 2 * k) for k in (1, 2, 3)])
    x = pick(jnp.concatenate([x[:1], core[:1], *got]), relative)
    return x if before is None else (x, before)


def pick(x, index, axis=0):
    return x.at[(slice(None),) * axis + (index,)].get(mode="promise_in_bounds")


def tie(*values):
    return lax.optimization_barrier(values)


def token_info(positions, lengths, kinds):
    ends = jnp.cumsum(lengths)
    starts = ends - lengths
    query_count = jnp.cumsum(kinds) - kinds
    doc_count = jnp.cumsum(1 - kinds) - (1 - kinds)
    segment = jnp.sum((positions[:, None] >= ends[None, :]).astype(jnp.int32), axis=1)
    onehot = segment[:, None] == jnp.arange(lengths.shape[0], dtype=jnp.int32)[None, :]
    nothing = jnp.zeros((), jnp.int32)
    seg_start = jnp.sum(jnp.where(onehot, starts[None, :], nothing), axis=1)
    is_query = jnp.sum(jnp.where(onehot, kinds[None, :], nothing), axis=1)
    query_num = jnp.sum(jnp.where(onehot, query_count[None, :], nothing), axis=1)
    doc_num = jnp.sum(jnp.where(onehot, doc_count[None, :], nothing), axis=1)
    offset = positions - seg_start
    return (segment, offset, is_query, query_num * QLEN + offset, doc_num)


def rope_angles(offset, head_dim):
    half = head_dim // 2
    inverse = jnp.exp(jnp.arange(half, dtype=F32) * (-2.0 * math.log(10000.0) / head_dim))
    angle = offset.astype(F32)[:, None] * inverse[None, :]
    return jnp.cos(angle), jnp.sin(angle)


def layer_norm(rows, gain, shift):
    center = rows - jnp.mean(rows, axis=-1, keepdims=True)
    variance = jnp.mean(center * center, axis=-1, keepdims=True)
    return center * lax.rsqrt(variance + 1e-05) * gain + shift


def unit_rows(rows):
    return rows * lax.rsqrt(jnp.sum(rows * rows, axis=-1, keepdims=True) + 1e-06)


def exact_gelu(values):
    return jax.nn.gelu(values, approximate=False)


def head_masks(width):
    lane = lax.broadcasted_iota(jnp.int32, (1, width), 1)
    first_qk = (lane % (width // 2)) < (width // 4)
    first_v = lane < (width // 2)
    return first_qk, first_v


BIG, SMALL = 62, 16

IN_VMEM = pl.BlockSpec(memory_space=pltpu.VMEM)
IN_HBM = pl.BlockSpec(memory_space=pltpu.HBM)


def near(x):
    return (x, "near")


def held(x):
    return (x, "held")


def raw(x):
    return (x, "raw")


def call(kernel, ins, outs, scratch, flops, limit=BIG):
    arrays = [a for a, _ in ins]
    kept = [i for i, (_, kind) in enumerate(ins) if kind == "held"]
    left = [i for i, out in enumerate(outs) if len(out) == 3]
    pieces = [1 if outs[i][2] is True else outs[i][2] for i in left]
    moved = sum(a.size * a.dtype.itemsize for a in arrays)
    moved += sum(math.prod(out[0]) * jnp.dtype(out[1]).itemsize for out in outs)

    def wrapped(*refs):
        in_refs = list(refs[: len(ins)])
        out_refs = list(refs[len(ins) : len(ins) + len(outs)])
        rest = refs[len(ins) + len(outs) :]
        own, rest = rest[: len(scratch)], rest[len(scratch) :]
        in_bufs, out_bufs = rest[: len(kept)], rest[len(kept) : len(kept) + len(left)]
        sems = rest[len(kept) + len(left)] if kept or left else None
        pending = {}
        for k, i in enumerate(kept):
            pending[i] = pltpu.make_async_copy(in_refs[i], in_bufs[k], sems.at[k])
            pending[i].start()

        def getter(i, buf):
            def get():
                if i in pending:
                    pending.pop(i).wait()
                return buf

            return get

        for k, i in enumerate(kept):
            in_refs[i] = getter(i, in_bufs[k])
        leaving = {}

        def flusher(i, k, target):
            def flush(j=0):
                buf = out_bufs[k]
                if pieces[k] > 1:
                    buf, target_j = buf.at[j], target.at[j]
                else:
                    target_j = target
                leaving[i, j] = pltpu.make_async_copy(buf, target_j, sems.at[len(kept) + sum(pieces[:k]) + j])
                leaving[i, j].start()

            return flush

        for k, i in enumerate(left):
            out_refs[i] = (out_bufs[k], flusher(i, k, out_refs[i]))
        kernel(in_refs, out_refs, own)
        assert not pending and len(leaving) == sum(pieces)
        for copy in leaving.values():
            copy.wait()

    buffers = [pltpu.VMEM(*item) if isinstance(item, tuple) else item for item in scratch]
    buffers += [pltpu.VMEM(arrays[i].shape, arrays[i].dtype) for i in kept]
    buffers += [pltpu.VMEM(*outs[i][:2]) for i in left]
    if kept or left:
        buffers.append(pltpu.SemaphoreType.DMA((len(kept) + sum(pieces),)))
    return pl.pallas_call(
        wrapped,
        in_specs=[IN_VMEM if kind == "near" else IN_HBM for _, kind in ins],
        out_specs=tuple(IN_HBM if len(out) == 3 else IN_VMEM for out in outs),
        out_shape=tuple(jax.ShapeDtypeStruct(out[0], out[1]) for out in outs),
        scratch_shapes=buffers,
        compiler_params=pltpu.CompilerParams(vmem_limit_bytes=limit * 1024 * 1024),
        cost_estimate=pl.CostEstimate(flops=flops, bytes_accessed=moved, transcendentals=0),
    )(*arrays)


def core_add(even, got):
    count, T, D = even.shape

    def kernel(ins, outs, _):
        for j in range(count):
            outs[j][...] = (ins[0][j].astype(F32) + ins[1][j].astype(F32)).astype(outs[j].dtype)

    outs = [((T, D), F32)] + [((T, D), BF)] * (count - 1)
    return call(kernel, [near(even), near(got)], outs, [], even.size, SMALL)


def add_norm(parts, params, bias_at, gain_at, shift_at):
    T, D = parts[0].shape

    def kernel(ins, outs, _):
        params = ins[-1]
        (total, leave), normed, low = outs
        rows = params[:, bias_at : bias_at + D]
        for ref in ins[:-1]:
            rows = rows + ref[...].astype(F32)
        total[...] = rows
        leave()
        result = layer_norm(rows, params[:, gain_at : gain_at + D], params[:, shift_at : shift_at + D])
        normed[...] = result
        low[...] = result.astype(BF)

    outs = [((T, D), F32, True), ((T, D), F32), ((T, D), BF)]
    return call(kernel, [near(item) for item in (*parts, params)], outs, [], 10 * T * D, SMALL)


def norm_back(parts, rows, params, gain_at):
    T, D = rows.shape

    def kernel(ins, outs, _):
        rows, params = ins[-2:]
        wide_out, low_out, sums = outs
        grad = ins[0][...].astype(F32)
        for ref in ins[1:-2]:
            grad = grad + ref[...].astype(F32)
        rows = rows()[...]
        center = rows - jnp.mean(rows, axis=-1, keepdims=True)
        inverse = lax.rsqrt(jnp.mean(center * center, axis=-1, keepdims=True) + 1e-05)
        unit = center * inverse
        sums[:, :D] = jnp.sum(grad * unit, axis=0, keepdims=True)
        sums[:, D : 2 * D] = jnp.sum(grad, axis=0, keepdims=True)
        grad = grad * params[:, gain_at : gain_at + D]
        along = jnp.mean(grad * unit, axis=-1, keepdims=True)
        grad = inverse * (grad - jnp.mean(grad, axis=-1, keepdims=True) - unit * along)
        wide_out[...] = grad
        low = grad.astype(BF)
        low_out[...] = low
        sums[:, 2 * D :] = jnp.sum(low.astype(F32), axis=0, keepdims=True)

    outs = [((T, D), F32), ((T, D), BF), ((1, 3 * D), F32)]
    return call(kernel, [near(item) for item in parts] + [held(rows), near(params)], outs, [], 20 * T * D, SMALL)


def roll_halves(x):
    return pltpu.roll(x, x.shape[1] // 2, 1)


def load_attn(full, w_in, w_out):
    far = full.shape[0]
    D, cols = w_in.shape
    rows, wide = D // far, w_out.shape[0]
    part = wide // far
    for o in range(far):
        w_in[o * rows : (o + 1) * rows] = full[o, :rows, :cols]
        for j in range(rows // part):
            w_out[o * part : (o + 1) * part, j * wide : (j + 1) * wide] = full[o, j * part : (j + 1) * part, cols:]


def load_ffn(full, w_up, w_down):
    far = full.shape[0]
    D, H = w_up.shape
    up, down = D // far, H // far
    for o in range(far):
        w_up[o * up : o * up + up // 2] = full[o, : up // 2, :H]
        w_up[o * up + up // 2 : (o + 1) * up] = full[o, : up // 2, H:]
        w_down[o * down : (o + 1) * down] = full[o, up // 2 : up // 2 + down]


def rotary(table, rows, half):
    cos, sin = table[rows, :half], table[rows, half : 2 * half]
    return jnp.concatenate([cos, cos, cos, cos], axis=1), jnp.concatenate([-sin, -sin, sin, sin], axis=1)


def attn_forward(blocks, full, bias, bias_at, table, seg_row, half, scale):
    n = len(blocks)
    T, D = blocks[0].shape
    wide = 4 * half
    N = n * T
    step = 4
    across_block = N

    def kernel(ins, outs, scratch):
        full, table, bias, seg_row = ins[n:]
        (qkv, leave_qkv), (context, leave_context), (logs, leave_logs), even, odd = outs
        w_in, w_out, x, values_t, context_t, x_sems = scratch
        copies = block_copies(ins[:n], x, x_sems)
        start_all(copies)
        load_attn(full(), w_in, w_out)
        table = table()
        for k in range(0, n, step):
            wait_all(copies[k : k + step])
            rows = slice(k * T, (k + step) * T)
            mixed = dot(x[rows], w_in[...]) + bias[:, bias_at : bias_at + 3 * wide]
            cos, sin = rotary(table, rows, half)
            for t, factor in ((0, scale), (1, 1.0)):
                part = mixed[:, t * wide : (t + 1) * wide]
                part = (part * cos + roll_halves(part) * sin).astype(BF)
                qkv[rows, t * wide : (t + 1) * wide] = part * jnp.asarray(factor, BF)
            qkv[rows, 2 * wide :] = mixed[:, 2 * wide :].astype(BF)
        leave_qkv()
        values_t[...] = qkv[:, 2 * wide :].T
        first_qk, _ = head_masks(wide)
        zero = jnp.zeros((), BF)

        def part(c, carry):
            at = pl.ds(pl.multiple_of(c * across_block, 128), across_block)
            allowed = table[:, 2 * half : 2 * half + 1] == seg_row[:, at]
            for head in range(2):
                mine = first_qk if head == 0 else jnp.logical_not(first_qk)
                query = jnp.where(mine, qkv[at, :wide], zero)
                scores = jnp.where(allowed, dot_rt(qkv[:, wide : 2 * wide], query), NEG_FILL)
                top = jnp.max(scores, axis=0, keepdims=True)
                weights = jnp.exp(scores - top)
                total = jnp.sum(weights, axis=0, keepdims=True)
                heads = slice(head * 2 * half, (head + 1) * 2 * half)
                context_t[heads, at] = dot(values_t[heads, :], weights.astype(BF)) * (1.0 / total)
                logs[head : head + 1, at] = top + jnp.log(total)
            return carry

        lax.fori_loop(0, N // across_block, part, 0)
        leave_logs()
        context[...] = context_t[...].T.astype(BF)
        leave_context()
        for k in range(0, n, step):
            put_blocks(dot(context[k * T : (k + step) * T], w_out[...]).astype(BF), k, (even, odd), T)

    outs = [((N, 3 * wide), BF, True), ((N, wide), BF, True), ((2, N), F32, True)]
    outs += [((n // 2, T, D), BF, n // 2), ((n // 2, T, D), BF, n // 2)]
    flops = 2 * N * D * 4 * wide + 8 * N * N * wide
    sems = pltpu.SemaphoreType.DMA
    scratch = [((D, 3 * wide), BF), ((wide, D), BF), ((N, D), BF), ((wide, N), BF), ((wide, N), F32), sems((n,))]
    ins = [raw(item) for item in blocks] + [held(full), held(table), near(bias), near(seg_row)]
    return call(kernel, ins, outs, scratch, flops)


def lanes_of(count):
    return max(w for w in (384, 256, 128) if count % w == 0)


def fetch_ffn(full, w_up, w_down, sems):
    far = full.shape[0]
    D, H = w_up.shape
    up, down = D // far, H // far
    first, second = [], []
    for o in range(far):
        for part in range(2):
            first.append(
                pltpu.make_async_copy(
                    full.at[o, pl.ds(0, up // 2), pl.ds(part * H, H)],
                    w_up.at[pl.ds(o * up + part * (up // 2), up // 2)],
                    sems.at[3 * o + part],
                )
            )
        second.append(
            pltpu.make_async_copy(
                full.at[o, pl.ds(up // 2, down)], w_down.at[pl.ds(o * down, down)], sems.at[3 * o + 2]
            )
        )
    return first, second


def start_all(copies):
    for copy in copies:
        copy.start()


def wait_all(copies):
    for copy in copies:
        copy.wait()


def block_copies(blocks, whole, sems):
    T = blocks[0].shape[0]
    return [pltpu.make_async_copy(block, whole.at[pl.ds(k * T, T)], sems.at[k]) for k, block in enumerate(blocks)]


def ffn_forward(blocks, full, bias, bias_at, H):
    n = len(blocks)
    T, D = blocks[0].shape
    step = 4

    def kernel(ins, outs, scratch):
        full, bias = ins[n:]
        (act, leave_act), (slope, leave_slope), even, odd = outs
        w_up, w_down, x, w_sems, x_sems = scratch
        first, second = fetch_ffn(full, w_up, w_down, w_sems)
        copies = block_copies(ins[:n], x, x_sems)
        start_all(first)
        start_all(copies)
        start_all(second)
        wait_all(first)
        for k in range(0, n, step):
            wait_all(copies[k : k + step])
            rows = slice(k * T, (k + step) * T)
            pre = dot(x[rows], w_up[...]) + bias[:, bias_at : bias_at + H]
            below = 0.5 * (1.0 + lax.erf(pre * math.sqrt(0.5)))
            result = (pre * below).astype(BF)
            act[rows] = result
            slope[rows] = (below + pre * (math.sqrt(0.5 / math.pi) * jnp.exp(-0.5 * pre * pre))).astype(BF)
            if k == 0:
                wait_all(second)
            back = dot(act[rows], w_down[...]).astype(BF)
            put_blocks(back, k, (even, odd), T)
        leave_act()
        leave_slope()

    outs = [((n * T, H), BF, True), ((n * T, H), BF, True), ((n // 2, T, D), BF, n // 2), ((n // 2, T, D), BF, n // 2)]
    ins = [raw(item) for item in blocks] + [raw(full), near(bias)]
    sems = pltpu.SemaphoreType.DMA
    scratch = [((D, H), BF), ((H, D), BF), ((n * T, D), BF), sems((3 * full.shape[0],)), sems((n,))]
    return call(kernel, ins, outs, scratch, 4 * n * T * D * H)


def put_blocks(rows, first, halves, T):
    for i in range(rows.shape[0] // T):
        out, leave = halves[(first + i) % 2]
        out[(first + i) // 2] = rows[i * T : (i + 1) * T]
        leave((first + i) // 2)


def ffn_back(blocks, full, slope):
    n = len(blocks)
    T, D = blocks[0].shape
    H = slope.shape[1]
    step = 4

    def kernel(ins, outs, scratch):
        full, slope = ins[n:]
        grad_pre, bias_grad, even, odd = outs
        w_up, w_down, x, w_sems, x_sems = scratch
        first, second = fetch_ffn(full, w_up, w_down, w_sems)
        copies = block_copies(ins[:n], x, x_sems)
        start_all(second)
        start_all(copies)
        start_all(first)
        wait_all(second)
        total = jnp.zeros((1, H), F32)
        for k in range(0, n, step):
            wait_all(copies[k : k + step])
            rows = slice(k * T, (k + step) * T)
            grad = (dot_rt(x[rows], w_down[...]) * slope()[rows].astype(F32)).astype(BF)
            grad_pre[rows] = grad
            total = total + jnp.sum(grad.astype(F32), axis=0, keepdims=True)
            if k == 0:
                wait_all(first)
            put_blocks(dot_rt(grad_pre[rows], w_up[...]).astype(BF), k, (even, odd), T)
        bias_grad[...] = total

    outs = [((n * T, H), BF), ((1, H), F32), ((n // 2, T, D), BF, n // 2), ((n // 2, T, D), BF, n // 2)]
    ins = [raw(item) for item in blocks] + [raw(full), held(slope)]
    sems = pltpu.SemaphoreType.DMA
    scratch = [((D, H), BF), ((H, D), BF), ((n * T, D), BF), sems((3 * full.shape[0],)), sems((n,))]
    return call(kernel, ins, outs, scratch, 4 * n * T * D * H)


def ffn_weights(normed, grads, act, grad_pre, far, extra):
    n = len(normed)
    T, D = normed[0].shape
    N = n * T
    H = act.shape[1]
    up, down = D // far, H // far
    more = [] if extra is None else [near(extra)]
    count = up // 2 + down + (0 if extra is None else extra.shape[1])

    def kernel(ins, outs, scratch):
        act, grad_pre = ins[2 * n : 2 * n + 2]
        left, right, left_sems, right_sems = scratch
        out = outs[0]
        copies = block_copies(ins[:n], left, left_sems)
        later = block_copies(ins[n : 2 * n], right, right_sems)
        start_all(copies)
        start_all(later)
        wait_all(copies)
        for o in range(far):
            block = dot_lt(left[:, o * up : (o + 1) * up], grad_pre[...]).astype(BF)
            out[o, : up // 2, :H] = block[: up // 2]
            out[o, : up // 2, H:] = block[up // 2 :]
        wait_all(later)
        act = act()
        for o in range(far):
            block = dot_lt(act[:, o * down : (o + 1) * down], right[...]).astype(BF)
            out[o, up // 2 : up // 2 + down] = block
            if more:
                out[o, up // 2 + down :] = ins[2 * n + 2][o]

    sems = pltpu.SemaphoreType.DMA
    scratch = [((N, D), BF), ((N, D), BF), sems((n,)), sems((n,))]
    ins = [raw(item) for item in (*normed, *grads)] + [held(act), near(grad_pre)] + more
    return call(kernel, ins, [((far, count, D), BF)], scratch, 4 * N * D * H)[0]


def attn_back(blocks, full, qkv, context, logs, table, seg_row, half, scale):
    n = len(blocks)
    T, D = blocks[0].shape
    wide = 4 * half
    N = n * T
    step = 4
    across_block = lanes_of(N)

    def kernel(ins, outs, scratch):
        full, table, qkv, context, logs, seg_row = ins[n:]
        mixed, bias_grad, even, odd = outs
        w_in, w_out, x, grad, delta, cos, sin, acc_k, acc_v, x_sems = scratch
        copies = block_copies(ins[:n], x, x_sems)
        start_all(copies)
        load_attn(full(), w_in, w_out)
        for k in range(0, n, step):
            wait_all(copies[k : k + step])
            rows = slice(k * T, (k + step) * T)
            grad[rows] = dot_rt(x[rows], w_out[...]).astype(BF)
        table = table()
        cos[...], sin[...] = rotary(table, slice(None), half)
        acc_k[...] = jnp.zeros_like(acc_k)
        acc_v[...] = jnp.zeros_like(acc_v)
        qkv, logs = qkv(), logs()
        product = (grad[...].astype(F32) * context()[...].astype(F32)).T
        delta[0:1] = jnp.sum(product[: 2 * half], axis=0, keepdims=True)
        delta[1:2] = jnp.sum(product[2 * half :], axis=0, keepdims=True)
        first_qk, first_v = head_masks(wide)
        zero = jnp.zeros((), BF)

        def part(c, carry):
            at = pl.ds(pl.multiple_of(c * across_block, 128), across_block)
            allowed = table[:, 2 * half : 2 * half + 1] == seg_row[:, at]
            grad_query = []
            for head in range(2):
                mine = first_qk if head == 0 else jnp.logical_not(first_qk)
                mine_v = first_v if head == 0 else jnp.logical_not(first_v)
                query = jnp.where(mine, qkv[at, :wide], zero)
                grad_h = jnp.where(mine_v, grad[at, :], zero)
                scores = dot_rt(qkv[:, wide : 2 * wide], query) - logs[head : head + 1, at]
                probs = jnp.exp(jnp.where(allowed, scores, NEG_FILL))
                grad_probs = dot_rt(qkv[:, 2 * wide :], grad_h)
                grad_scores = (probs * (grad_probs - delta[head : head + 1, at])).astype(BF)
                acc_k[...] += dot(grad_scores, query)
                acc_v[...] += dot(probs.astype(BF), grad_h)
                grad_query.append(dot_lt(grad_scores, qkv[:, wide : 2 * wide]))
            result = jnp.where(first_qk, grad_query[0], grad_query[1]) * scale
            mixed[at, :wide] = (result * cos[at, :] - roll_halves(result) * sin[at, :]).astype(BF)
            return carry

        lax.fori_loop(0, N // across_block, part, 0)
        total = acc_k[...]
        mixed[:, wide : 2 * wide] = (total * cos[...] - roll_halves(total) * sin[...]).astype(BF)
        mixed[:, 2 * wide :] = acc_v[...].astype(BF)
        sums = jnp.zeros((1, 3 * wide), F32)
        for k in range(0, n, step):
            rows = slice(k * T, (k + step) * T)
            sums = sums + jnp.sum(mixed[rows].astype(F32), axis=0, keepdims=True)
            put_blocks(dot_rt(mixed[rows], w_in[...]).astype(BF), k, (even, odd), T)
        bias_grad[...] = sums

    outs = [((N, 3 * wide), BF), ((1, 3 * wide), F32), ((n // 2, T, D), BF, n // 2), ((n // 2, T, D), BF, n // 2)]
    scratch = [((D, 3 * wide), BF), ((wide, D), BF), ((N, D), BF), ((N, wide), BF), ((2, N), F32)]
    scratch += [((N, wide), F32)] * 4 + [pltpu.SemaphoreType.DMA((n,))]
    flops = 2 * N * D * 4 * wide + 20 * N * N * wide
    ins = [raw(item) for item in blocks] + [held(item) for item in (full, table, qkv, context, logs)] + [near(seg_row)]
    return call(kernel, ins, outs, scratch, flops)


def attn_weights(inputs, grads, context, mixed, bias_grad, far, relative):
    n = len(inputs)
    T, D = inputs[0].shape
    N = n * T
    wide = context.shape[1]
    rows = D // far
    part = wide // far
    size = lax.axis_size("row")

    def kernel(ins, outs, scratch):
        context, mixed, bias_grad = ins[2 * n :]
        left, right, left_sems, right_sems = scratch
        here = (lax.axis_index("seq") * size + lax.axis_index("row")) // PLANE
        copies = block_copies(ins[:n], left, left_sems)
        later = block_copies(ins[n : 2 * n], right, right_sems)
        start_all(copies)
        start_all(later)
        wait_all(copies)
        for k in range(far):
            if relative:
                lanes = pl.ds(pl.multiple_of((here ^ k) * rows, 128), rows)
                outs[k][:rows, : 3 * wide] = dot_lt(left[:, lanes], mixed[...]).astype(BF)
            else:
                outs[0][k, :rows, : 3 * wide] = dot_lt(left[:, k * rows : (k + 1) * rows], mixed[...]).astype(BF)
        wait_all(later)
        whole = dot_lt(context()[...], right[...]).astype(BF)
        extra = jnp.broadcast_to(bias_grad[...], (16, 3 * wide)).astype(BF)
        if relative:
            right[:wide, :D] = whole
        for k in range(far):
            out = outs[k] if relative else outs[0].at[k]
            if relative:
                block = right[pl.ds(pl.multiple_of((here ^ k) * part, 16), part), :]
            else:
                block = whole[k * part : (k + 1) * part]
            for j in range(rows // part):
                out[j * part : (j + 1) * part, 3 * wide :] = block[:, j * wide : (j + 1) * wide]
            out[rows:, : 3 * wide] = extra
            out[rows:, 3 * wide :] = jnp.zeros((16, wide), BF)

    sems = pltpu.SemaphoreType.DMA
    scratch = [((N, D), BF), ((N, D), BF), sems((n,)), sems((n,))]
    ins = [raw(item) for item in (*inputs, *grads)] + [held(context), near(mixed), near(bias_grad)]
    if relative:
        outs = [((rows + 16, 4 * wide), BF)] * far
    else:
        outs = [((far, rows + 16, 4 * wide), BF)]
    return call(kernel, ins, outs, scratch, 8 * N * D * wide)


def plane_index():
    return lax.axis_index("seq") % (PLANE // lax.axis_size("row")) * lax.axis_size("row") + lax.axis_index("row")


def head_kernel(blocks, own, codes, own_codes, positive, temp, w_col, loss_weight):
    n = len(blocks)
    T, C = own.shape
    N = n * T
    D = w_col.shape[0]
    slots = NQ * QLEN

    def kernel(ins, outs, scratch):
        own, codes, own_codes, positive, temp, w_col = ins[n:]
        grad, low, terms = outs
        held, embeds = scratch
        here = plane_index()
        upper = lax.rem(lax.axis_index("seq") // (PLANE // lax.axis_size("row")), 2)

        def place(c):
            column = lax.rem(c // 2, 2) ^ upper
            return pl.ds(pl.multiple_of((4 * column + 2 * lax.rem(c, 2) + c // 4) * T, 16), T)

        for k in range(n):
            held[place(here ^ k), :] = ins[k][...]
        lane = lax.broadcasted_iota(jnp.int32, (1, C), 1)
        slot = lax.broadcasted_iota(jnp.int32, (slots, 1), 0)
        doc, own_doc = codes[0:1, :], own_codes[0:1, :]
        select = jnp.where(codes[1:2, :] == slot, 1.0, 0.0).astype(BF)
        own_select = jnp.where(own_codes[1:2, :] == slot, 1.0, 0.0).astype(BF)
        rows = held[...].astype(F32)
        mine = own[...]
        heat = temp[...]
        wanted = lane == positive[...]
        valid = lane <= NSD
        loss = jnp.zeros((1, 1), F32)
        heat_grad = jnp.zeros((1, 1), F32)
        total = jnp.zeros((T, C), F32)
        for width in (C, C * 3 // 4, C // 2):
            inside = lane < width
            size = jnp.sum(jnp.where(inside, rows * rows, 0.0), axis=1, keepdims=True)
            embed = jnp.where(inside, rows * lax.rsqrt(size + 1e-06), 0.0).astype(BF)
            embeds[...] = embed
            query = dot(select, embed).astype(BF)
            powers = jnp.exp(SHARPNESS * dot_rt(query, embed))
            soft = jnp.zeros((slots, C), F32)
            sums = []
            for d in range(NSD + 1):
                sums.append(jnp.sum(jnp.where(doc == d, powers, 0.0), axis=1, keepdims=True))
                soft = jnp.where(lane == d, jnp.log(sums[d]) / SHARPNESS, soft)
            pair = jnp.sum(soft.reshape(NQ, QLEN, C), axis=1, keepdims=True)
            pair = jnp.broadcast_to(pair, (NQ, QLEN, C)).reshape(slots, C)
            logits = pair * heat / QLEN
            masked = jnp.where(valid, logits, NEG_FILL)
            top = jnp.max(masked, axis=1, keepdims=True)
            shares = jnp.exp(masked - top)
            share_sum = jnp.sum(shares, axis=1, keepdims=True)
            chosen = jnp.sum(jnp.where(wanted, logits, 0.0), axis=1, keepdims=True)
            losses = top + jnp.log(share_sum) - chosen
            loss = loss + jnp.sum(losses, axis=0, keepdims=True) * (loss_weight / QLEN)
            grad_logits = loss_weight * (shares / share_sum - jnp.where(wanted, 1.0, 0.0))
            along = jnp.sum(jnp.where(valid, grad_logits * logits, 0.0), axis=1, keepdims=True)
            heat_grad = heat_grad + jnp.sum(along, axis=0, keepdims=True) / QLEN
            grad_soft = grad_logits * heat / QLEN
            weight = jnp.zeros((slots, N), F32)
            own_weight = jnp.zeros((slots, T), F32)
            for d in range(NSD + 1):
                ratio = grad_soft[:, d : d + 1] / sums[d]
                weight = jnp.where(doc == d, ratio, weight)
                own_weight = jnp.where(own_doc == d, ratio, own_weight)
            grad_query = dot((powers * weight).astype(BF), embed)
            own_embed = embeds[place(here), :]
            own_powers = jnp.exp(SHARPNESS * dot_rt(query, own_embed))
            grad_embed = dot_lt((own_powers * own_weight).astype(BF), query)
            high = grad_query.astype(BF)
            rest = (grad_query - high.astype(F32)).astype(BF)
            grad_embed = grad_embed + dot_lt(own_select, high) + dot_lt(own_select, rest)
            size = jnp.sum(jnp.where(inside, mine * mine, 0.0), axis=1, keepdims=True)
            inverse = lax.rsqrt(size + 1e-06)
            along = jnp.sum(jnp.where(inside, grad_embed * mine, 0.0), axis=1, keepdims=True)
            part = inverse * grad_embed - mine * (inverse * inverse * inverse * along)
            total = total + jnp.where(inside, part, 0.0)
        low[...] = total.astype(BF)
        grad[...] = dot_rt(total.astype(BF), w_col[...])
        terms[...] = jnp.where(lane == 0, loss, jnp.where(lane == 1, heat_grad, 0.0))

    outs = [((T, D), F32), ((T, C), BF), ((1, C), F32)]
    ins = [near(item) for item in (*blocks, own, codes, own_codes, positive, temp, w_col)]
    return call(kernel, ins, outs, [((N, C), BF), ((N, C), BF)], 24 * slots * N * C, 40)


def swap_quarters(x):
    q = x.shape[1] // 4
    return jnp.concatenate([x[:, :q], x[:, 2 * q : 3 * q], x[:, q : 2 * q], x[:, 3 * q :]], axis=1)


def pack_first(w, small):
    rows, width = w.shape
    D, wide = width // 3, width // 3 // PLANE
    count = rows + small.shape[0]

    def kernel(ins, outs, _):
        w, small = ins
        here = plane_index()
        for k in range(PLANE):
            out = outs[k % 2].at[k // 2]
            for t in range(3):
                columns = w[:, pl.ds(pl.multiple_of(t * D + (here ^ k) * wide, 128), wide)]
                out[:rows, t * wide : (t + 1) * wide] = swap_quarters(columns) if t < 2 else columns
            out[rows:] = small[...]

    outs = [((PLANE // 2, count, 3 * wide), BF)] * 2
    return call(kernel, [near(w), near(small)], outs, [], w.size, SMALL)


def unpack_first(even, core, got, out_rows):
    rows, D = out_rows.shape
    count, cols = even.shape[1:]
    wide = cols // 3

    def kernel(ins, outs, _):
        even, core, *got, out_rows = ins
        block, below = outs
        here = plane_index()
        blocks = [even.at[0], core.at[0]] + [ref.at[j] for ref in got for j in range(2)]
        for k in range(PLANE):
            of = here ^ k
            block[pl.ds(pl.multiple_of(of * rows, 16), rows), :cols] = blocks[k][:rows]
            below[of] = blocks[k][rows:]
            block[k * rows : (k + 1) * rows, cols:] = out_rows[:, k * wide : (k + 1) * wide]

    outs = [((PLANE * rows, cols + wide), BF), ((PLANE, count - rows, cols), BF)]
    return call(kernel, [near(item) for item in (even, core, *got, out_rows)], outs, [], even.size, SMALL)


def pack_shares(sums, others, ffn, lines, in_cols, hidden_cols):
    rows, width = sums[0].shape[0] - 16, sums[0].shape[1]
    part = rows // PLANE
    L = len(ffn)
    count = L * (in_cols + hidden_cols) + 128
    bias_lines = in_cols // 128
    first_line = part - L * bias_lines

    def kernel(ins, outs, scratch):
        even, odd, last = outs
        attn = scratch[0]
        n = len(sums)
        total = ins[0][...].astype(F32)
        for ref in ins[1:n]:
            total = total + ref[...].astype(F32)
        attn[0] = total.astype(BF)
        for layer in range(1, L):
            attn[layer] = ins[n + layer - 1][...]
        last[...] = attn[0, :rows, in_cols:]
        ups = ins[n + L - 1 : n + 2 * L - 1]
        lines = ins[n + 2 * L - 1]
        here = plane_index()
        line = lax.broadcasted_iota(jnp.int32, (part, 128), 0)
        for k in range(PLANE):
            to = here ^ k
            out = (odd if k % 2 else even).at[k // 2]
            at = pl.ds(pl.multiple_of(to * part, 16), part)
            half = pl.ds(pl.multiple_of(lax.rem(to, PLANE // 2) * part, 16), part)
            for layer in range(L):
                out[:, layer * in_cols : (layer + 1) * in_cols] = attn[layer, at, :in_cols]
                folded = ups[layer][half, :]
                own = jnp.where(to < PLANE // 2, folded[:, :hidden_cols], folded[:, hidden_cols:])
                start = L * in_cols + layer * hidden_cols
                out[:, start : start + hidden_cols] = own
            block = lines[to]
            for layer in range(L):
                bias = attn[layer, rows : rows + 16, :in_cols].astype(F32)[:1]
                for j in range(bias_lines):
                    spot = line == first_line + layer * bias_lines + j
                    block = jnp.where(spot, bias[:, j * 128 : (j + 1) * 128], block)
            out[:, count - 128 :] = block.astype(BF)

    half = PLANE // 2
    outs = [((half, part, count), BF), ((half, part, count), BF), ((rows, width - in_cols), BF)]
    ins = [near(item) for item in (*sums, *others, *ffn, lines)]
    return call(kernel, ins, outs, [((L, rows + 16, width), BF)], rows * count, SMALL)


def unpack_shares(even, core, got, L, in_cols, hidden_cols):
    part, count = even.shape[1:]
    wide = in_cols // 3
    D, far = PLANE * wide, hidden_cols // 128
    bias_lines = in_cols // 128
    first_line = part - L * bias_lines

    def natural(x):
        q = wide // 4
        return jnp.concatenate([x[:, :q], x[:, 2 * q : 3 * q], x[:, q : 2 * q], x[:, 3 * q :]], axis=1)

    def kernel(ins, outs, scratch):
        even, core, *got = ins
        w_in, w_up, lines, bias = outs
        here = plane_index()
        blocks = [even.at[0], core.at[0]] + [ref.at[j] for ref in got for j in range(2)]
        total = jnp.zeros((part, 128), F32)
        for k in range(PLANE):
            block = blocks[k][...].astype(F32)
            of = here ^ k
            own_lines = block[:, count - 128 :]
            total = total + own_lines
            for layer in range(L):
                for t in range(3):
                    at = pl.ds(pl.multiple_of(t * D + of * wide, 128), wide)
                    start = layer * in_cols + t * wide
                    columns = block[:, start : start + wide]
                    row = first_line + layer * bias_lines + t
                    line = own_lines[row : row + 1]
                    if t < 2:
                        columns, line = natural(columns), natural(line)
                    w_in[layer, :, at] = columns
                    bias[layer, :, at] = line
                for o in range(far):
                    at = pl.ds(pl.multiple_of(o * PLANE * 128 + of * 128, 128), 128)
                    start = L * in_cols + layer * hidden_cols + o * 128
                    w_up[layer, :, at] = block[:, start : start + 128]
        lines[...] = total

    outs = [((L, part, 3 * D), F32), ((L, part, far * PLANE * 128), F32), ((part, 128), F32), ((L, 1, 3 * D), F32)]
    ins = [near(item) for item in (even, core, *got)]
    return call(kernel, ins, outs, [], part * count * PLANE, SMALL)


def body(
    tokens,
    attn_in,
    attn_out,
    ffn_up,
    ffn_down,
    norm_gains,
    biases,
    colbert,
    log_scale,
    cotangent,
    seg_lengths,
    seg_kinds,
    pairing,
):
    S = lax.axis_size("seq")
    R = lax.axis_size("row")
    O = S * R // PLANE
    place = lax.axis_index("seq") * R + lax.axis_index("row")
    plane, far = place % PLANE, place // PLANE
    relative = jnp.bitwise_xor(plane, jnp.arange(PLANE, dtype=jnp.int32))
    T = tokens.shape[1]
    D = tokens.shape[2]
    N = PLANE * T
    L = attn_in.shape[0]
    head_dim = D // HEADS
    half = head_dim // 2
    scale = head_dim ** (-0.5)
    wide = 2 * head_dim
    in_cols = 3 * wide
    in_rows = attn_in.shape[1]
    rows_in = PLANE * in_rows
    FF = ffn_up.shape[2]
    up_cols = FF // (S * R)
    hidden_cols = O * up_cols
    gain_part = norm_gains.shape[1]
    bias_part = biases.shape[1]
    part = gain_part + bias_part
    along_z = [[o * (S // O) + i for o in range(O)] for i in range(S // O)]
    is_mine = jnp.arange(PLANE, dtype=jnp.int32) == plane

    def padded_rows(vector, width=D):
        rows = -(-vector.shape[0] // (16 * width)) * 16
        return jnp.pad(vector, (0, rows * width - vector.shape[0])).reshape(rows, width)

    def pack_columns(w):
        lead = w.shape[:-1]
        n = len(lead)
        qk = w[..., : 2 * D].reshape(*lead, 2, PLANE, 2, 2, half)
        qk = qk.transpose((n + 1,) + tuple(range(n)) + (n, n + 3, n + 2, n + 4)).reshape(PLANE, *lead, 2 * wide)
        v = w[..., 2 * D :].reshape(*lead, PLANE, wide)
        v = v.transpose((n,) + tuple(range(n)) + (n + 1,))
        return jnp.concatenate([qk, v], axis=-1)

    def unpack_columns(w):
        rows = w.shape[1]
        qk = w[:, :, : 2 * wide].reshape(PLANE, rows, 2, 2, 2, half)
        qk = qk.transpose(1, 2, 0, 4, 3, 5).reshape(rows, 2 * D)
        v = w[:, :, 2 * wide :].transpose(1, 0, 2).reshape(rows, D)
        return jnp.concatenate([qk, v], axis=1)

    def pack_hidden(w):
        rows = w.shape[0]
        return w.reshape(rows, O, PLANE, up_cols).transpose(2, 0, 1, 3).reshape(PLANE, rows, hidden_cols)

    def unpack_hidden(w):
        rows = w.shape[1]
        return w.reshape(PLANE, rows, O, up_cols).transpose(1, 2, 0, 3).reshape(rows, FF)

    def fold(w):
        n = w.shape[-2] // 2
        return jnp.concatenate([w[..., :n, :], w[..., n:, :]], axis=-1)

    def unfold(w):
        n = w.shape[-1] // 2
        return jnp.concatenate([w[..., :n], w[..., n:]], axis=-2)

    to_group = [(b, (b % O) * PLANE + b // O) for b in range(O * PLANE)]
    from_group = [(d, b) for b, d in to_group]
    small = jnp.concatenate([norm_gains.reshape(-1), biases.reshape(-1), colbert.reshape(-1)])
    even, odd = pack_first(attn_in[0], padded_rows(small, in_cols))
    core = across(odd, 1)
    got = tie(*[across(jnp.stack([even[k], core[k]]), 2 * k) for k in (1, 2, 3)])
    shard_out = lax.ppermute(attn_out, BOTH, to_group)
    table = turned(jnp.concatenate([seg_lengths[0], seg_kinds[0], pairing[0]]))
    seg_count = seg_lengths.shape[1]
    lengths, kinds = table[:seg_count], table[seg_count : 2 * seg_count]
    pairs_of = table[2 * seg_count :]
    hidden_low = turned(tokens[0])

    def attn_block(layer, shard):
        out = shard_out[layer].reshape(in_rows, PLANE, wide).transpose(1, 0, 2).reshape(rows_in, wide)
        return jnp.concatenate([shard, out], axis=1)

    def gather_far(x):
        return lax.all_gather(x, "seq", axis=0, axis_index_groups=along_z)

    own, small = unpack_first(even, core, got, shard_out[0])
    small = small.reshape(PLANE, -1)
    full_attn = [gather_far(own)]
    count_small = L * part
    col_plane = small[:, count_small : count_small + colbert.size].reshape(-1)
    params = small[None, :, :count_small]
    step = 1
    while step < O:
        other = across(params, PLANE * step)
        low_side = (far & step) == 0
        params = jnp.concatenate([jnp.where(low_side, params, other), jnp.where(low_side, other, params)], axis=0)
        step *= 2
    params = params.reshape(O * PLANE, count_small).astype(F32)
    gains_all = params[:, : L * gain_part].reshape(O * PLANE, L, gain_part).transpose(1, 0, 2).reshape(L, 2 * D)
    bias_all = params[:, L * gain_part :].reshape(O * PLANE, L, bias_part).transpose(1, 0, 2).reshape(L, -1)
    in_biases = pick(pack_columns(bias_all[:, : 3 * D]), plane, axis=0).reshape(1, L * in_cols)
    up_biases = pick(pack_hidden(bias_all[:, 4 * D : 4 * D + FF]), plane, axis=0).reshape(1, L * hidden_cols)
    rest_at = 4 * D + FF
    params = jnp.concatenate([gains_all, bias_all[:, 3 * D : 4 * D], bias_all[:, rest_at:]], axis=1).reshape(1, -1)
    GAIN_ONE, GAIN_TWO, BIAS_OUT, BIAS_DOWN, SHIFT_ONE, SHIFT_TWO = range(6)

    def at(layer, which):
        return (layer * 6 + which) * D

    rest = jnp.concatenate(
        [pack_hidden(ffn_up[0])]
        + [piece for layer in range(1, L) for piece in (pack_columns(attn_in[layer]), pack_hidden(ffn_up[layer]))],
        axis=-1,
    )
    rest = plane_exchange(rest, relative).reshape(rows_in, -1)
    full_ffn = []
    start = 0
    for layer in range(L):
        if layer > 0:
            full_attn.append(gather_far(attn_block(layer, rest[:, start : start + in_cols])))
            start += in_cols
        own = [fold(rest[:, start : start + hidden_cols]), ffn_down[layer]]
        start += hidden_cols
        if layer == L - 1:
            own.append(padded_rows(col_plane))
        full_ffn.append(gather_far(jnp.concatenate(own, axis=0)))
    w_col = full_ffn[L - 1][:, rows_in // 2 + up_cols :].reshape(O, -1)[:, : col_plane.size]
    w_col = w_col.reshape(D, colbert.shape[1])

    block_at = 4 * ((relative // 2 % 2) ^ (far % 2)) + 2 * (relative % 2) + relative // 4
    positions = (block_at[:, None] * T + jnp.arange(T, dtype=jnp.int32)[None, :]).reshape(N)
    held_segment, held_offset = token_info(positions, lengths, kinds)[:2]
    cos, sin = rope_angles(held_offset, head_dim)
    seg_row = held_segment.astype(F32)[None, :]
    table = jnp.concatenate([cos, sin, jnp.broadcast_to(seg_row.T, (N, wide - 2 * half))], axis=1)

    hidden = hidden_low
    records = []
    for layer in range(L):
        x_all = plane_gather(hidden_low)
        qkv, context, logs, even, odd = attn_forward(
            x_all, full_attn[layer], in_biases, layer * in_cols, table, seg_row, half, scale
        )
        terms, _ = plane_scatter(even, odd)
        first, normed, normed_low = add_norm(
            [hidden] + terms, params, at(layer, BIAS_OUT), at(layer, GAIN_ONE), at(layer, SHIFT_ONE)
        )
        normed_all = plane_gather(normed_low)
        act, slope, even, odd = ffn_forward(
            normed_all, full_ffn[layer], up_biases, layer * hidden_cols, hidden_cols
        )
        terms, _ = plane_scatter(even, odd)
        second, hidden, hidden_low = add_norm(
            [normed] + terms, params, at(layer, BIAS_DOWN), at(layer, GAIN_TWO), at(layer, SHIFT_TWO)
        )
        records.append((x_all, qkv, context, logs, first, normed_all, act, slope, second))
    hidden_out = turned(hidden_low, True)

    full_width = w_col.shape[1]
    row_positions = jnp.arange(N, dtype=jnp.int32)
    segment, offset, is_query, query_slot, doc_num = token_info(row_positions, lengths, kinds)
    codes = jnp.stack([jnp.where(is_query == 0, doc_num, -1), jnp.where(is_query == 1, query_slot, -1)])
    own_codes = lax.dynamic_slice(codes, (0, block_at[0] * T), (2, T))
    positive = jnp.repeat(pairs_of, QLEN)[:, None]
    temp = jnp.exp(log_scale)[None]
    hidden_low, cot = tie(hidden_low, cotangent[0])
    cot = turned(cot)
    col = dot(hidden_low, w_col)
    col_blocks = plane_gather(col.astype(BF))
    grad_out, grad_col_low, terms = head_kernel(
        col_blocks, col, codes, own_codes, positive, temp, w_col, 1.0 / (3 * NQ * R)
    )
    loss_terms = terms[0, :2]
    col_parts = dot_lt(hidden_low, grad_col_low).reshape(O, PLANE, in_rows, full_width).transpose(1, 0, 2, 3)
    col_parts = plane_sum(pick(col_parts.reshape(PLANE, O * in_rows, full_width), relative, axis=0))
    col_rows = jax.vmap(padded_rows)(col_parts.reshape(O, in_rows * full_width)).astype(BF)
    grad_parts = [cot, grad_out]

    def scatter_far(whole):
        whole = whole.reshape(-1, whole.shape[-1])
        return lax.psum_scatter(whole, "seq", scatter_dimension=0, tiled=True, axis_index_groups=along_z)

    outs = [[None] * L for _ in range(6)]

    def finish_out(layer, share_out):
        share_out = share_out.reshape(PLANE, in_rows, wide).transpose(1, 0, 2).reshape(in_rows, D)
        outs[1][layer] = lax.ppermute(share_out, BOTH, from_group).astype(F32)

    shares_ffn, shares_attn = [None] * L, [None] * L
    vectors = [None] * L
    for layer in reversed(range(L)):
        x_all, qkv, context, logs, first, normed_all, act, slope, second = records[layer]
        grad_second, grad_ffo, sums_two = norm_back(grad_parts, second, params, at(layer, GAIN_TWO))
        ffo_all = plane_gather(grad_ffo)
        if layer == L - 1:
            ffo_all, hidden_out = tie(ffo_all, hidden_out)
        grad_pre, grad_bias_up, even, odd = ffn_back(ffo_all, full_ffn[layer], slope)
        blocks = ffn_weights(normed_all, ffo_all, act, grad_pre, O, col_rows if layer == L - 1 else None)
        terms, blocks = plane_scatter(even, odd, blocks)
        shares_ffn[layer] = scatter_far(blocks)
        grad_first, grad_branch, sums_one = norm_back([grad_second] + terms, first, params, at(layer, GAIN_ONE))
        branch_all = plane_gather(grad_branch)
        if layer < L - 1:
            branch_all, shares_attn[layer + 1] = tie(branch_all, shares_attn[layer + 1])
        grad_mixed, grad_bias_in, even, odd = attn_back(
            branch_all, full_attn[layer], qkv, context, logs, table, seg_row, half, scale
        )

        gain_two, shift_two, down, gain_one, shift_one, out = [
            sums[0, k * D : (k + 1) * D] for sums in (sums_two, sums_one) for k in range(3)
        ]
        own_up = unpack_hidden(is_mine[:, None, None].astype(F32) * grad_bias_up[None])[0]
        gains = jnp.concatenate([gain_one, gain_two]).reshape(O, PLANE, gain_part)
        bias = jnp.concatenate([jnp.zeros((3 * D,), F32), out, own_up, down, shift_one, shift_two])
        vectors[layer] = jnp.concatenate([gains, bias.reshape(O, PLANE, bias_part)], axis=2)

        blocks = attn_weights(x_all, branch_all, context, grad_mixed, grad_bias_in, O, layer == 0)
        terms, blocks = plane_scatter(even, odd, blocks, layer == 0)
        terms, shares_ffn[layer] = tie(terms, shares_ffn[layer])
        if layer > 0:
            shares_attn[layer] = scatter_far(blocks[0])
            grad_parts = [grad_first] + terms

    got = [across(blocks[step], PLANE * step) for step in range(1, O)]
    entries = jnp.concatenate(vectors, axis=2).transpose(1, 0, 2).reshape(PLANE, O * L * part)
    lines = jnp.pad(entries, ((0, 0), (0, in_rows * 128 - O * L * part))).reshape(PLANE, in_rows, 128)
    got, lines = tie(got, lines)
    grad_tokens = turned((grad_first + sum(item.astype(F32) for item in terms)).astype(BF), True)
    even, odd, last_out = pack_shares([blocks[0]] + got, shares_attn[1:], shares_ffn, lines, in_cols, hidden_cols)
    core, grad_tokens = tie(across(odd, 1), grad_tokens)
    got = tie(*[across(jnp.stack([even[k], core[k]]), 2 * k) for k in (1, 2, 3)])
    w_in_grad, w_up_grad, lines, bias_in_grad = unpack_shares(even, core, got, L, in_cols, hidden_cols)
    entries = lines.reshape(-1)[: O * L * part].reshape(O, L * part)
    entries = jnp.concatenate([entries, jnp.broadcast_to(loss_terms[None], (O, 2))], axis=1)
    mine = pick(entries, far)
    for step in range(1, O):
        mine = mine + across(pick(entries, far ^ step), PLANE * step)
    bias_in_grad = jnp.pad(bias_in_grad[:, 0], ((0, 0), (0, O * PLANE * bias_part - 3 * D)))
    bias_in_grad = pick(bias_in_grad.reshape(L, O * PLANE, bias_part), place, axis=1)
    for layer in range(L):
        outs[3][layer] = shares_ffn[layer][rows_in // 2 : rows_in // 2 + up_cols]
        finish_out(layer, shares_attn[layer][:rows_in, in_cols:] if layer > 0 else last_out)
        outs[4][layer] = mine[layer * part : layer * part + gain_part]
        outs[5][layer] = mine[layer * part + gain_part : (layer + 1) * part] + bias_in_grad[layer]
    col_share = shares_ffn[L - 1][rows_in // 2 + up_cols :].reshape(-1)[: in_rows * full_width]
    col_share = col_share.reshape(in_rows, full_width).astype(F32)
    loss_terms = mine[L * part :]
    outs[0], outs[2] = w_in_grad, w_up_grad
    stacked = [jnp.stack(items).astype(F32) if isinstance(items, list) else items for items in outs]
    return (
        hidden_out[None],
        loss_terms[:1],
        grad_tokens.astype(F32)[None],
        stacked[0],
        stacked[1],
        stacked[2],
        stacked[3],
        stacked[4],
        stacked[5],
        col_share,
        loss_terms[1:],
    )


def joined_2(value, axis, join):
    pieces = jax.tree.map(lambda part: lax.all_gather(part, axis), value)
    head = jax.tree.map(lambda part: part[0], pieces)
    tail = jax.tree.map(lambda part: part[1:], pieces)
    so_far, _ = lax.scan(lambda so_far, section: (join(so_far, section), None), head, tail)
    return so_far


def rope_tables(offset, head_dim):
    half = head_dim // 2
    inverse = jnp.exp(jnp.arange(half, dtype=jnp.float32) * (-2.0 * math.log(10000.0) / head_dim))
    angle = offset.astype(jnp.float32)[:, None] * inverse[None, :]
    return (jnp.cos(angle), jnp.sin(angle))


def rotate(flat, cos_table, sin_table):
    length = flat.shape[0]
    head_dim = flat.shape[1] // HEADS
    half = head_dim // 2
    shaped = flat.reshape(length, HEADS, head_dim)
    first_half = shaped[..., :half]
    second_half = shaped[..., half:]
    cos_three = cos_table[:, None, :]
    sin_three = sin_table[:, None, :]
    turned = jnp.concatenate(
        [
            first_half * cos_three - second_half * sin_three,
            second_half * cos_three + first_half * sin_three,
        ],
        axis=-1,
    )
    return turned.reshape(length, flat.shape[1])


def block_for(count):
    blocks = count
    while blocks > 1024 and blocks % 2 == 0:
        blocks = blocks // 2
    return blocks


def merge_pair(first, second):
    max_first, sum_first = first
    max_second, sum_second = second
    top = jnp.maximum(max_first, max_second)
    return (top, sum_first * jnp.exp(max_first - top) + sum_second * jnp.exp(max_second - top))


def matmul_left_t(left, right):
    return jnp.einsum("ti,to->io", left, right, preferred_element_type=jnp.float32)


def matmul_right_t(left, right):
    return jnp.einsum("to,io->ti", left, right, preferred_element_type=jnp.float32)


def body_wide(
    tokens,
    attn_in,
    attn_out,
    ffn_up,
    ffn_down,
    norm_gains,
    biases,
    colbert,
    log_scale,
    cotangent,
    seg_lengths,
    seg_kinds,
    pairing,
):
    rank = lax.axis_index("seq")
    local_len = tokens.shape[1]
    model_width = tokens.shape[2]
    head_dim = model_width // HEADS
    scale = head_dim ** (-0.5)
    lengths = seg_lengths[0]
    kinds = seg_kinds[0]
    positions = rank * local_len + jnp.arange(local_len, dtype=jnp.int32)
    segment, offset, is_query, query_slot, doc_num = token_info(positions, lengths, kinds)
    cos_table, sin_table = rope_tables(offset, head_dim)
    layer_count = attn_in.shape[0]

    def split_pieces(key_piece, value_piece):
        count = key_piece.shape[0]
        blocks = block_for(count)
        key_seg = token_info(jnp.arange(count, dtype=jnp.int32), lengths, kinds)[0]
        key_blocks = key_piece.reshape(count // blocks, blocks, HEADS, head_dim)
        value_blocks = value_piece.reshape(count // blocks, blocks, HEADS, head_dim)
        seg_blocks = key_seg.reshape(count // blocks, blocks)
        return (count, blocks, key_blocks, value_blocks, seg_blocks)

    def attend_back(queries, keys, values, context, log_total, grad_context):
        query_three = queries.reshape(local_len, HEADS, head_dim)
        grad_three = grad_context.reshape(local_len, HEADS, head_dim)
        delta = jnp.sum(
            grad_three.astype(jnp.float32) * context.reshape(local_len, HEADS, head_dim), axis=-1
        ).T

        def score_grads(
            query_blk, grad_blk, key_blk, value_blk, query_seg, key_seg, total_blk, delta_blk
        ):
            scores = (
                jnp.einsum("qhd,khd->hqk", query_blk, key_blk, preferred_element_type=jnp.float32)
                * scale
            )
            allowed = (query_seg[:, None] == key_seg[None, :])[None]
            probs = jnp.where(allowed, jnp.exp(scores - total_blk[..., None]), 0.0)
            grad_probs = jnp.einsum(
                "qhd,khd->hqk", grad_blk, value_blk, preferred_element_type=jnp.float32
            )
            grad_scores = (probs * (grad_probs - delta_blk[..., None])).astype(jnp.bfloat16)
            return (probs, grad_scores)

        grad_query = jnp.zeros((local_len, HEADS, head_dim), jnp.float32)
        count, blocks, key_blocks, value_blocks, seg_blocks = split_pieces(
            lax.all_gather(keys, "seq", axis=0, tiled=True),
            lax.all_gather(values, "seq", axis=0, tiled=True),
        )

        def advance(grad_acc, item):
            key_blk, value_blk, seg_blk = item
            probs, grad_scores = score_grads(
                query_three, grad_three, key_blk, value_blk, segment, seg_blk, log_total, delta
            )
            grad_acc = grad_acc + scale * jnp.einsum(
                "hqk,khd->qhd", grad_scores, key_blk, preferred_element_type=jnp.float32
            )
            grad_key = scale * jnp.einsum(
                "hqk,qhd->khd", grad_scores, query_three, preferred_element_type=jnp.float32
            )
            grad_value = jnp.einsum(
                "hqk,qhd->khd",
                probs.astype(jnp.bfloat16),
                grad_three,
                preferred_element_type=jnp.float32,
            )
            joined = jnp.concatenate(
                [grad_key.reshape(blocks, model_width), grad_value.reshape(blocks, model_width)],
                axis=1,
            )
            return (grad_acc, joined)

        grad_query, pieces_out = lax.scan(
            advance, grad_query, (key_blocks, value_blocks, seg_blocks)
        )
        grad_rows = pieces_out.reshape(count, 2 * model_width)
        grad_query, grad_rows = (grad_query, grad_rows)
        summed = lax.psum_scatter(
            grad_rows.astype(jnp.bfloat16), "seq", scatter_dimension=0, tiled=True
        ).astype(jnp.float32)
        grad_key_out = summed[:, :model_width]
        grad_value_out = summed[:, model_width:]
        return (grad_query.reshape(local_len, model_width), grad_key_out, grad_value_out)

    def unpack(full):
        w_in, w_out, w_up, w_down, gains, bias = full[:6]
        hidden_units = w_up.shape[1]
        gains_f = gains.astype(jnp.float32)
        bias_f = bias.astype(jnp.float32)
        width_three = 3 * model_width
        return (
            w_in,
            w_out,
            w_up,
            w_down,
            hidden_units,
            gains_f[:model_width],
            gains_f[model_width:],
            bias_f[:width_three],
            bias_f[width_three : 4 * model_width],
            bias_f[4 * model_width : 4 * model_width + hidden_units],
            bias_f[4 * model_width + hidden_units : 5 * model_width + hidden_units],
            bias_f[5 * model_width + hidden_units : 6 * model_width + hidden_units],
            bias_f[6 * model_width + hidden_units :],
        )

    def layer_backward(grad_out, full, record):
        (
            w_in,
            w_out,
            w_up,
            w_down,
            hidden_units,
            gain_one,
            gain_two,
            bias_in,
            bias_out,
            bias_up,
            bias_down,
            shift_one,
            shift_two,
        ) = unpack(full)
        (
            inputs_low,
            queries,
            keys,
            values,
            context,
            context_low,
            log_total,
            first,
            normed,
            normed_low,
            pre_act,
            act_low,
            second,
        ) = record
        unused, pull_two = jax.vjp(layer_norm, second, gain_two, shift_two)
        grad_second, grad_gain_two, grad_shift_two = pull_two(grad_out)
        grad_branch_two = grad_second.astype(jnp.bfloat16)
        grad_bias_down = jnp.sum(grad_branch_two.astype(jnp.float32), axis=0)
        grad_w_down = matmul_left_t(act_low, grad_branch_two)
        grad_act = matmul_right_t(grad_branch_two, w_down)
        unused, pull_gelu = jax.vjp(exact_gelu, pre_act)
        grad_pre = pull_gelu(grad_act)[0].astype(jnp.bfloat16)
        grad_bias_up = jnp.sum(grad_pre.astype(jnp.float32), axis=0)
        grad_w_up = matmul_left_t(normed_low, grad_pre)
        grad_normed = grad_second + matmul_right_t(grad_pre, w_up)
        unused, pull_one = jax.vjp(layer_norm, first, gain_one, shift_one)
        grad_first, grad_gain_one, grad_shift_one = pull_one(grad_normed)
        grad_branch = grad_first.astype(jnp.bfloat16)
        grad_bias_out = jnp.sum(grad_branch.astype(jnp.float32), axis=0)
        grad_w_out = matmul_left_t(context_low, grad_branch)
        grad_context = matmul_right_t(grad_branch, w_out).astype(jnp.bfloat16)
        grad_query, grad_key, grad_value = attend_back(
            queries, keys, values, context, log_total, grad_context
        )
        grad_mixed = jnp.concatenate(
            [
                rotate(grad_query, cos_table, -sin_table),
                rotate(grad_key, cos_table, -sin_table),
                grad_value,
            ],
            axis=1,
        ).astype(jnp.bfloat16)
        grad_bias_in = jnp.sum(grad_mixed.astype(jnp.float32), axis=0)
        grad_w_in = matmul_left_t(inputs_low, grad_mixed)
        grad_hidden = grad_first + matmul_right_t(grad_mixed, w_in)
        grad_gains = jnp.concatenate([grad_gain_one, grad_gain_two])
        grad_bias = jnp.concatenate(
            [
                grad_bias_in,
                grad_bias_out,
                grad_bias_up,
                grad_bias_down,
                grad_shift_one,
                grad_shift_two,
            ]
        )
        return (grad_hidden, (grad_w_in, grad_w_out, grad_w_up, grad_w_down, grad_gains, grad_bias))

    hidden = tokens[0].astype(jnp.float32)
    records = []
    gathered = []
    for layer_index in range(layer_count):
        full = (
            lax.all_gather(attn_in[layer_index], ("seq", "row"), axis=0, tiled=True),
            lax.all_gather(attn_out[layer_index], ("seq", "row"), axis=0, tiled=True),
            lax.all_gather(ffn_up[layer_index], ("seq", "row"), axis=0, tiled=True),
            lax.all_gather(ffn_down[layer_index], ("seq", "row"), axis=0, tiled=True),
            lax.all_gather(norm_gains[layer_index], ("seq", "row"), axis=0, tiled=True),
            lax.all_gather(biases[layer_index], ("seq", "row"), axis=0, tiled=True),
            lax.all_gather(colbert, ("seq", "row"), axis=0, tiled=True),
        )
        gathered.append(full)
        (
            layer_w_in,
            layer_w_out,
            layer_w_up,
            layer_w_down,
            layer_hidden_units,
            layer_gain_one,
            layer_gain_two,
            layer_bias_in,
            layer_bias_out,
            layer_bias_up,
            layer_bias_down,
            layer_shift_one,
            layer_shift_two,
        ) = unpack(full)
        layer_inputs_low = hidden.astype(jnp.bfloat16)
        mixed = (
            jnp.dot(layer_inputs_low, layer_w_in, preferred_element_type=jnp.float32)
            + layer_bias_in
        )
        layer_queries = rotate(mixed[:, :model_width], cos_table, sin_table).astype(jnp.bfloat16)
        layer_keys = rotate(mixed[:, model_width : 2 * model_width], cos_table, sin_table).astype(
            jnp.bfloat16
        )
        layer_values = mixed[:, 2 * model_width :].astype(jnp.bfloat16)
        attend_query_three = layer_queries.reshape(local_len, HEADS, head_dim)
        attend_initial = (
            jnp.full((HEADS, local_len), NEG_FILL, jnp.float32),
            jnp.zeros((HEADS, local_len), jnp.float32),
            jnp.zeros((local_len, HEADS, head_dim), jnp.float32),
        )
        absorb_carry = attend_initial
        absorb_count, absorb_blocks, absorb_key_blocks, absorb_value_blocks, absorb_seg_blocks = (
            split_pieces(
                lax.all_gather(layer_keys, "seq", axis=0, tiled=True),
                lax.all_gather(layer_values, "seq", axis=0, tiled=True),
            )
        )

        def absorb_advance(state, item):
            run_max, run_sum, accum = state
            key_blk, value_blk, seg_blk = item
            scores = (
                jnp.einsum(
                    "qhd,khd->hqk", attend_query_three, key_blk, preferred_element_type=jnp.float32
                )
                * scale
            )
            allowed = (segment[:, None] == seg_blk[None, :])[None]
            scores = jnp.where(allowed, scores, NEG_FILL)
            new_max = jnp.maximum(run_max, jnp.max(scores, axis=-1))
            weights = jnp.where(allowed, jnp.exp(scores - new_max[..., None]), 0.0)
            factor = jnp.exp(run_max - new_max)
            run_sum = run_sum * factor + jnp.sum(weights, axis=-1)
            accum = accum * factor.T[:, :, None] + jnp.einsum(
                "hqk,khd->qhd",
                weights.astype(jnp.bfloat16),
                value_blk,
                preferred_element_type=jnp.float32,
            )
            return ((new_max, run_sum, accum), None)

        absorb_carry, absorb_unused = lax.scan(
            absorb_advance,
            absorb_carry,
            (absorb_key_blocks, absorb_value_blocks, absorb_seg_blocks),
        )
        run_max, run_sum, accum = absorb_carry
        attend_context = (accum / run_sum.T[:, :, None]).reshape(local_len, model_width)
        attend_log_total = run_max + jnp.log(run_sum)
        layer_context_low = attend_context.astype(jnp.bfloat16)
        layer_first = (
            hidden
            + jnp.dot(layer_context_low, layer_w_out, preferred_element_type=jnp.float32)
            + layer_bias_out
        )
        layer_normed = layer_norm(layer_first, layer_gain_one, layer_shift_one)
        layer_normed_low = layer_normed.astype(jnp.bfloat16)
        layer_pre_act = (
            jnp.dot(layer_normed_low, layer_w_up, preferred_element_type=jnp.float32)
            + layer_bias_up
        )
        layer_act_low = exact_gelu(layer_pre_act).astype(jnp.bfloat16)
        layer_second = (
            layer_normed
            + jnp.dot(layer_act_low, layer_w_down, preferred_element_type=jnp.float32)
            + layer_bias_down
        )
        output = layer_norm(layer_second, layer_gain_two, layer_shift_two)
        layer_record = (
            layer_inputs_low,
            layer_queries,
            layer_keys,
            layer_values,
            attend_context,
            layer_context_low,
            attend_log_total,
            layer_first,
            layer_normed,
            layer_normed_low,
            layer_pre_act,
            layer_act_low,
            layer_second,
        )
        hidden = output
        record = layer_record
        records.append(record)
    w_col = gathered[layer_count - 1][6]
    final_low = hidden.astype(jnp.bfloat16)
    col = jnp.dot(final_low, w_col, preferred_element_type=jnp.float32)
    full_width = w_col.shape[1]
    part_widths = (full_width, full_width * 3 // 4, full_width // 2)
    query_total = NQ * QLEN
    doc_total = NSD + 1
    selector = (is_query == 1)[None, :] & (
        query_slot[None, :] == jnp.arange(query_total, dtype=jnp.int32)[:, None]
    )
    selector_low = selector.astype(jnp.bfloat16)
    embeds = [unit_rows(col[:, :part_width]).astype(jnp.bfloat16) for part_width in part_widths]
    picked = (
        lax.psum(
            jnp.dot(selector_low, embeds[0], preferred_element_type=jnp.float32).astype(
                jnp.bfloat16
            ),
            "seq",
        ).astype(jnp.float32),
        lax.psum(
            jnp.dot(selector_low, embeds[1], preferred_element_type=jnp.float32).astype(
                jnp.bfloat16
            ),
            "seq",
        ).astype(jnp.float32),
        lax.psum(
            jnp.dot(selector_low, embeds[2], preferred_element_type=jnp.float32).astype(
                jnp.bfloat16
            ),
            "seq",
        ).astype(jnp.float32),
    )
    query_emb = [item.astype(jnp.bfloat16) for item in picked]
    sims = jnp.stack(
        [
            jnp.einsum(
                "qc,tc->qt", query_emb[part], embeds[part], preferred_element_type=jnp.float32
            )
            for part in range(3)
        ]
    )
    doc_mask = (
        (is_query == 0)[:, None]
        & (doc_num[:, None] == jnp.arange(doc_total, dtype=jnp.int32)[None, :])
    )[None, None]
    scaled = jnp.where(doc_mask, SHARPNESS * sims[..., None], NEG_FILL)
    part_max = jnp.max(scaled, axis=2)
    part_sum = jnp.sum(jnp.where(doc_mask, jnp.exp(scaled - part_max[:, :, None, :]), 0.0), axis=2)
    top, total = joined_2((part_max, part_sum), "seq", merge_pair)
    soft = (top + jnp.log(total)) / SHARPNESS
    pair_sum = jnp.sum(soft.reshape(3, NQ, QLEN, doc_total), axis=2)
    inverse_temp = jnp.exp(log_scale[0])
    logits = pair_sum * inverse_temp / QLEN
    positive = pairing[0][None, :, None] == jnp.arange(doc_total, dtype=jnp.int32)[None, None, :]
    losses = jax.nn.logsumexp(logits, axis=-1) - jnp.sum(jnp.where(positive, logits, 0.0), axis=-1)
    loss_weight = 1.0 / (3 * NQ * lax.axis_size("row"))
    grad_logits = loss_weight * (jax.nn.softmax(logits, axis=-1) - positive.astype(jnp.float32))
    loss_total, temp_grad = lax.psum(
        (jnp.sum(losses).reshape(1) * loss_weight, jnp.sum(grad_logits * logits).reshape(1)), "row"
    )
    grad_pairs = grad_logits * inverse_temp / QLEN
    grad_soft = jnp.broadcast_to(grad_pairs[:, :, None, :], (3, NQ, QLEN, doc_total)).reshape(
        3, query_total, doc_total
    )
    shares = jnp.where(doc_mask, jnp.exp(scaled - top[:, :, None, :]), 0.0) / total[:, :, None, :]
    grad_sims = jnp.sum(shares * grad_soft[:, :, None, :], axis=-1).astype(jnp.bfloat16)
    grad_query_emb = (
        lax.psum(
            jnp.dot(grad_sims[0], embeds[0], preferred_element_type=jnp.float32).astype(
                jnp.bfloat16
            ),
            "seq",
        ).astype(jnp.float32),
        lax.psum(
            jnp.dot(grad_sims[1], embeds[1], preferred_element_type=jnp.float32).astype(
                jnp.bfloat16
            ),
            "seq",
        ).astype(jnp.float32),
        lax.psum(
            jnp.dot(grad_sims[2], embeds[2], preferred_element_type=jnp.float32).astype(
                jnp.bfloat16
            ),
            "seq",
        ).astype(jnp.float32),
    )
    selector_f = selector.astype(jnp.float32)
    grad_col = jnp.zeros((local_len, full_width), jnp.float32)
    for part in range(3):
        part_width = part_widths[part]
        grad_embed = jnp.einsum(
            "qt,qc->tc", grad_sims[part], query_emb[part], preferred_element_type=jnp.float32
        )
        grad_embed = grad_embed + jnp.einsum(
            "qt,qc->tc",
            selector_f,
            grad_query_emb[part],
            precision=HIGHEST,
            preferred_element_type=jnp.float32,
        )
        unused, pull_unit = jax.vjp(unit_rows, col[:, :part_width])
        grad_col = grad_col.at[:, :part_width].add(pull_unit(grad_embed)[0])
    grad_col_low = grad_col.astype(jnp.bfloat16)
    grad_w_col = matmul_left_t(final_low, grad_col_low)
    grad_hidden = cotangent[0].astype(jnp.float32) + matmul_right_t(grad_col_low, w_col)
    shard_lists = [[] for unused_slot in range(6)]
    col_share = None
    for layer_index in reversed(range(layer_count)):
        full = (
            lax.all_gather(attn_in[layer_index], ("seq", "row"), axis=0, tiled=True),
            lax.all_gather(attn_out[layer_index], ("seq", "row"), axis=0, tiled=True),
            lax.all_gather(ffn_up[layer_index], ("seq", "row"), axis=0, tiled=True),
            lax.all_gather(ffn_down[layer_index], ("seq", "row"), axis=0, tiled=True),
            lax.all_gather(norm_gains[layer_index], ("seq", "row"), axis=0, tiled=True),
            lax.all_gather(biases[layer_index], ("seq", "row"), axis=0, tiled=True),
            lax.all_gather(colbert, ("seq", "row"), axis=0, tiled=True),
        )
        grad_hidden, layer_grads = layer_backward(grad_hidden, full, records[layer_index])
        col_term = grad_w_col if layer_index == layer_count - 1 else jnp.zeros_like(grad_w_col)
        shares_out = (
            lax.psum_scatter(layer_grads[0], ("seq", "row"), scatter_dimension=0, tiled=True),
            lax.psum_scatter(layer_grads[1], ("seq", "row"), scatter_dimension=0, tiled=True),
            lax.psum_scatter(layer_grads[2], ("seq", "row"), scatter_dimension=0, tiled=True),
            lax.psum_scatter(layer_grads[3], ("seq", "row"), scatter_dimension=0, tiled=True),
            lax.psum_scatter(layer_grads[4], ("seq", "row"), scatter_dimension=0, tiled=True),
            lax.psum_scatter(layer_grads[5], ("seq", "row"), scatter_dimension=0, tiled=True),
            lax.psum_scatter(col_term, ("seq", "row"), scatter_dimension=0, tiled=True),
        )
        for slot in range(6):
            shard_lists[slot].insert(0, shares_out[slot])
        if layer_index == layer_count - 1:
            col_share = shares_out[6]
    stacked = [jnp.stack(items) for items in shard_lists]
    return (
        hidden.astype(jnp.bfloat16)[None],
        loss_total,
        grad_hidden[None],
        stacked[0],
        stacked[1],
        stacked[2],
        stacked[3],
        stacked[4],
        stacked[5],
        col_share,
        temp_grad,
    )


def solution(mesh):
    placed = (
        P("row", "seq", None),
        P(None, ("seq", "row"), None),
        P(None, ("seq", "row"), None),
        P(None, ("seq", "row"), None),
        P(None, ("seq", "row"), None),
        P(None, ("seq", "row")),
        P(None, ("seq", "row")),
        P(("seq", "row"), None),
        P(),
        P("row", "seq", None),
        P("row", None),
        P("row", None),
        P("row", None),
    )
    planes = mesh.shape["row"] == 4 and mesh.shape["seq"] * 4 == 4 * PLANE and HEADS == 2 * PLANE
    return jax.shard_map(
        body if planes else body_wide,
        mesh=mesh,
        in_specs=placed,
        out_specs=(
            P("row", "seq", None),
            P(),
            P("row", "seq", None),
            P(None, ("seq", "row"), None),
            P(None, ("seq", "row"), None),
            P(None, ("seq", "row"), None),
            P(None, ("seq", "row"), None),
            P(None, ("seq", "row")),
            P(None, ("seq", "row")),
            P(("seq", "row"), None),
            P(),
        ),
        check_vma=False,
    )
```

```python
import math

import jax
import jax.numpy as jnp
from jax import lax
from jax.experimental import pallas as pl
from jax.experimental.pallas import tpu as pltpu
from jax.sharding import PartitionSpec as P

HEADS = 16
QLEN = 32
NQ = 4
NSD = 3

NEG_FILL = -1e30
SHARPNESS = 16.0
HIGHEST = lax.Precision.HIGHEST
BF = jnp.bfloat16
F32 = jnp.float32

def dot(left, right):
    return jnp.dot(left, right, preferred_element_type=F32)


def dot_lt(left, right):
    return lax.dot_general(left, right, (((0,), (0,)), ((), ())), preferred_element_type=F32)


def dot_rt(left, right):
    return lax.dot_general(left, right, (((1,), (1,)), ((), ())), preferred_element_type=F32)


PLANE = 8
BOTH = ("seq", "row")


def across(x, mask):
    size = lax.axis_size("seq") * lax.axis_size("row")
    return lax.ppermute(x, BOTH, [(d, d ^ mask) for d in range(size)])


def turned(x, back=False):
    size = lax.axis_size("seq") * lax.axis_size("row")
    pairs = []
    for d in range(size):
        z, y, column, core = d // PLANE, d // 4 % 2, d // 2 % 2, d % 2
        to = (2 * core + column) * PLANE + 4 * y + 2 * (column ^ (z // 2)) + z % 2
        pairs.append((to, d) if back else (d, to))
    return lax.ppermute(x, BOTH, pairs)


def plane_gather(x):
    blocks = [x, None, across(x, 2), None, across(x, 4), None, across(x, 6), None]
    for k in range(0, PLANE, 2):
        blocks[k + 1] = across(blocks[k], 1)
    return blocks


def plane_scatter(even, odd, beside=None, first=False):
    core = across(odd, 1)
    if first:
        core, beside = tie(core, beside)
    parts = core_add(even, core)
    got = [across(parts[j], 2 * j) for j in (1, 2, 3)]
    if beside is not None and not first:
        got, beside = tie(got, beside)
    return [parts[0]] + got, beside


def plane_sum(parts):
    parts = parts.astype(BF)
    core = across(parts[1::2], 1).astype(F32) + parts[0::2].astype(F32)
    sent = core[1:].astype(BF)
    return core[0] + sum(across(sent[k - 1], 2 * k).astype(F32) for k in (1, 2, 3))


def plane_exchange(x, relative, before=None):
    x = pick(x, relative)
    core = across(x[1::2], 1)
    if before is not None:
        core, before = tie(core, before)
    got = tie(*[across(jnp.stack([x[2 * k], core[k]]), 2 * k) for k in (1, 2, 3)])
    x = pick(jnp.concatenate([x[:1], core[:1], *got]), relative)
    return x if before is None else (x, before)


def pick(x, index, axis=0):
    return x.at[(slice(None),) * axis + (index,)].get(mode="promise_in_bounds")


def tie(*values):
    return lax.optimization_barrier(values)


def token_info(positions, lengths, kinds):
    ends = jnp.cumsum(lengths)
    starts = ends - lengths
    query_count = jnp.cumsum(kinds) - kinds
    doc_count = jnp.cumsum(1 - kinds) - (1 - kinds)
    segment = jnp.sum((positions[:, None] >= ends[None, :]).astype(jnp.int32), axis=1)
    onehot = segment[:, None] == jnp.arange(lengths.shape[0], dtype=jnp.int32)[None, :]
    nothing = jnp.zeros((), jnp.int32)
    seg_start = jnp.sum(jnp.where(onehot, starts[None, :], nothing), axis=1)
    is_query = jnp.sum(jnp.where(onehot, kinds[None, :], nothing), axis=1)
    query_num = jnp.sum(jnp.where(onehot, query_count[None, :], nothing), axis=1)
    doc_num = jnp.sum(jnp.where(onehot, doc_count[None, :], nothing), axis=1)
    offset = positions - seg_start
    return (segment, offset, is_query, query_num * QLEN + offset, doc_num)


def rope_angles(offset, head_dim):
    half = head_dim // 2
    inverse = jnp.exp(jnp.arange(half, dtype=F32) * (-2.0 * math.log(10000.0) / head_dim))
    angle = offset.astype(F32)[:, None] * inverse[None, :]
    return jnp.cos(angle), jnp.sin(angle)


def layer_norm(rows, gain, shift):
    center = rows - jnp.mean(rows, axis=-1, keepdims=True)
    variance = jnp.mean(center * center, axis=-1, keepdims=True)
    return center * lax.rsqrt(variance + 1e-05) * gain + shift


def unit_rows(rows):
    return rows * lax.rsqrt(jnp.sum(rows * rows, axis=-1, keepdims=True) + 1e-06)


def exact_gelu(values):
    return jax.nn.gelu(values, approximate=False)


def head_masks(width):
    lane = lax.broadcasted_iota(jnp.int32, (1, width), 1)
    first_qk = (lane % (width // 2)) < (width // 4)
    first_v = lane < (width // 2)
    return first_qk, first_v


BIG, SMALL = 62, 16

IN_VMEM = pl.BlockSpec(memory_space=pltpu.VMEM)
IN_HBM = pl.BlockSpec(memory_space=pltpu.HBM)


def near(x):
    return (x, "near")


def held(x):
    return (x, "held")


def raw(x):
    return (x, "raw")


def call(kernel, ins, outs, scratch, flops, limit=BIG, light=True):
    arrays = [a for a, _ in ins]
    kept = [i for i, (_, kind) in enumerate(ins) if kind == "held"]
    left = [i for i, out in enumerate(outs) if len(out) == 3]
    pieces = [1 if outs[i][2] is True else outs[i][2] for i in left]
    moved = sum(a.size * a.dtype.itemsize for a in arrays)
    moved += sum(math.prod(out[0]) * jnp.dtype(out[1]).itemsize for out in outs)

    def wrapped(*refs):
        in_refs = list(refs[: len(ins)])
        out_refs = list(refs[len(ins) : len(ins) + len(outs)])
        rest = refs[len(ins) + len(outs) :]
        own, rest = rest[: len(scratch)], rest[len(scratch) :]
        in_bufs, out_bufs = rest[: len(kept)], rest[len(kept) : len(kept) + len(left)]
        sems = rest[len(kept) + len(left)] if kept or left else None
        pending = {}
        for k, i in enumerate(kept):
            pending[i] = pltpu.make_async_copy(in_refs[i], in_bufs[k], sems.at[k])
            pending[i].start()

        def getter(i, buf):
            def get():
                if i in pending:
                    pending.pop(i).wait()
                return buf

            return get

        for k, i in enumerate(kept):
            in_refs[i] = getter(i, in_bufs[k])
        leaving = {}

        def flusher(i, k, target):
            def flush(j=0):
                buf = out_bufs[k]
                if pieces[k] > 1:
                    buf, target_j = buf.at[j], target.at[j]
                else:
                    target_j = target
                leaving[i, j] = pltpu.make_async_copy(buf, target_j, sems.at[len(kept) + sum(pieces[:k]) + j])
                leaving[i, j].start()

            return flush

        for k, i in enumerate(left):
            out_refs[i] = (out_bufs[k], flusher(i, k, out_refs[i]))
        kernel(in_refs, out_refs, own)
        assert not pending and len(leaving) == sum(pieces)
        for copy in leaving.values():
            copy.wait()

    buffers = [pltpu.VMEM(*item) if isinstance(item, tuple) else item for item in scratch]
    buffers += [pltpu.VMEM(arrays[i].shape, arrays[i].dtype) for i in kept]
    buffers += [pltpu.VMEM(*outs[i][:2]) for i in left]
    if kept or left:
        buffers.append(pltpu.SemaphoreType.DMA((len(kept) + sum(pieces),)))
    return pl.pallas_call(
        wrapped,
        in_specs=[IN_VMEM if kind == "near" else IN_HBM for _, kind in ins],
        out_specs=tuple(IN_HBM if len(out) == 3 else IN_VMEM for out in outs),
        out_shape=tuple(jax.ShapeDtypeStruct(out[0], out[1]) for out in outs),
        scratch_shapes=buffers,
        compiler_params=pltpu.CompilerParams(vmem_limit_bytes=limit * 1024 * 1024),
        cost_estimate=pl.CostEstimate(flops=1 if light else flops, bytes_accessed=1 if light else moved, transcendentals=0),
    )(*arrays)


def core_add(even, got):
    count, T, D = even.shape

    def kernel(ins, outs, _):
        for j in range(count):
            outs[j][...] = (ins[0][j].astype(F32) + ins[1][j].astype(F32)).astype(outs[j].dtype)

    outs = [((T, D), F32)] + [((T, D), BF)] * (count - 1)
    return call(kernel, [near(even), near(got)], outs, [], even.size, SMALL)


def add_norm(parts, params, bias_at, gain_at, shift_at):
    T, D = parts[0].shape

    def kernel(ins, outs, _):
        params = ins[-1]
        (total, leave), normed, low = outs
        rows = params[:, bias_at : bias_at + D]
        for ref in ins[:-1]:
            rows = rows + ref[...].astype(F32)
        total[...] = rows
        leave()
        result = layer_norm(rows, params[:, gain_at : gain_at + D], params[:, shift_at : shift_at + D])
        normed[...] = result
        low[...] = result.astype(BF)

    outs = [((T, D), F32, True), ((T, D), F32), ((T, D), BF)]
    return call(kernel, [near(item) for item in (*parts, params)], outs, [], 10 * T * D, SMALL)


def norm_back(parts, rows, params, gain_at):
    T, D = rows.shape

    def kernel(ins, outs, _):
        rows, params = ins[-2:]
        wide_out, low_out, sums = outs
        grad = ins[0][...].astype(F32)
        for ref in ins[1:-2]:
            grad = grad + ref[...].astype(F32)
        rows = rows()[...]
        center = rows - jnp.mean(rows, axis=-1, keepdims=True)
        inverse = lax.rsqrt(jnp.mean(center * center, axis=-1, keepdims=True) + 1e-05)
        unit = center * inverse
        sums[:, :D] = jnp.sum(grad * unit, axis=0, keepdims=True)
        sums[:, D : 2 * D] = jnp.sum(grad, axis=0, keepdims=True)
        grad = grad * params[:, gain_at : gain_at + D]
        along = jnp.mean(grad * unit, axis=-1, keepdims=True)
        grad = inverse * (grad - jnp.mean(grad, axis=-1, keepdims=True) - unit * along)
        wide_out[...] = grad
        low = grad.astype(BF)
        low_out[...] = low
        sums[:, 2 * D :] = jnp.sum(low.astype(F32), axis=0, keepdims=True)

    outs = [((T, D), F32), ((T, D), BF), ((1, 3 * D), F32)]
    return call(kernel, [near(item) for item in parts] + [held(rows), near(params)], outs, [], 20 * T * D, SMALL)


def roll_halves(x):
    return pltpu.roll(x, x.shape[1] // 2, 1)


def load_attn(full, w_in, w_out):
    far = full.shape[0]
    D, cols = w_in.shape
    rows, wide = D // far, w_out.shape[0]
    part = wide // far
    for o in range(far):
        w_in[o * rows : (o + 1) * rows] = full[o, :rows, :cols]
        for j in range(rows // part):
            w_out[o * part : (o + 1) * part, j * wide : (j + 1) * wide] = full[o, j * part : (j + 1) * part, cols:]


def load_ffn(full, w_up, w_down):
    far = full.shape[0]
    D, H = w_up.shape
    up, down = D // far, H // far
    for o in range(far):
        w_up[o * up : o * up + up // 2] = full[o, : up // 2, :H]
        w_up[o * up + up // 2 : (o + 1) * up] = full[o, : up // 2, H:]
        w_down[o * down : (o + 1) * down] = full[o, up // 2 : up // 2 + down]


def rotary(table, rows, half):
    cos, sin = table[rows, :half], table[rows, half : 2 * half]
    return jnp.concatenate([cos, cos, cos, cos], axis=1), jnp.concatenate([-sin, -sin, sin, sin], axis=1)


def attn_forward(blocks, full, bias, bias_at, table, seg_row, half, scale):
    n = len(blocks)
    T, D = blocks[0].shape
    wide = 4 * half
    N = n * T
    step = 4
    across_block = N

    def kernel(ins, outs, scratch):
        full, table, bias, seg_row = ins[n:]
        (qkv, leave_qkv), (context, leave_context), (logs, leave_logs), even, odd = outs
        w_in, w_out, x, values_t, context_t, x_sems = scratch
        copies = block_copies(ins[:n], x, x_sems)
        start_all(copies)
        load_attn(full(), w_in, w_out)
        table = table()
        for k in range(0, n, step):
            wait_all(copies[k : k + step])
            rows = slice(k * T, (k + step) * T)
            mixed = dot(x[rows], w_in[...]) + bias[:, bias_at : bias_at + 3 * wide]
            cos, sin = rotary(table, rows, half)
            for t, factor in ((0, scale), (1, 1.0)):
                part = mixed[:, t * wide : (t + 1) * wide]
                part = (part * cos + roll_halves(part) * sin).astype(BF)
                qkv[rows, t * wide : (t + 1) * wide] = part * jnp.asarray(factor, BF)
            qkv[rows, 2 * wide :] = mixed[:, 2 * wide :].astype(BF)
        leave_qkv()
        values_t[...] = qkv[:, 2 * wide :].T
        first_qk, _ = head_masks(wide)
        zero = jnp.zeros((), BF)

        def part(c, carry):
            at = pl.ds(pl.multiple_of(c * across_block, 128), across_block)
            allowed = table[:, 2 * half : 2 * half + 1] == seg_row[:, at]
            for head in range(2):
                mine = first_qk if head == 0 else jnp.logical_not(first_qk)
                query = jnp.where(mine, qkv[at, :wide], zero)
                scores = jnp.where(allowed, dot_rt(qkv[:, wide : 2 * wide], query), NEG_FILL)
                top = jnp.max(scores, axis=0, keepdims=True)
                weights = jnp.exp(scores - top)
                total = jnp.sum(weights, axis=0, keepdims=True)
                heads = slice(head * 2 * half, (head + 1) * 2 * half)
                context_t[heads, at] = dot(values_t[heads, :], weights.astype(BF)) * (1.0 / total)
                logs[head : head + 1, at] = top + jnp.log(total)
            return carry

        lax.fori_loop(0, N // across_block, part, 0)
        leave_logs()
        context[...] = context_t[...].T.astype(BF)
        leave_context()
        for k in range(0, n, step):
            put_blocks(dot(context[k * T : (k + step) * T], w_out[...]).astype(BF), k, (even, odd), T)

    outs = [((N, 3 * wide), BF, True), ((N, wide), BF, True), ((2, N), F32, True)]
    outs += [((n // 2, T, D), BF, n // 2), ((n // 2, T, D), BF, n // 2)]
    flops = 2 * N * D * 4 * wide + 8 * N * N * wide
    sems = pltpu.SemaphoreType.DMA
    scratch = [((D, 3 * wide), BF), ((wide, D), BF), ((N, D), BF), ((wide, N), BF), ((wide, N), F32), sems((n,))]
    ins = [raw(item) for item in blocks] + [held(full), held(table), near(bias), near(seg_row)]
    return call(kernel, ins, outs, scratch, flops)


def lanes_of(count):
    return max(w for w in (384, 256, 128) if count % w == 0)


def fetch_ffn(full, w_up, w_down, sems):
    far = full.shape[0]
    D, H = w_up.shape
    up, down = D // far, H // far
    first, second = [], []
    for o in range(far):
        for part in range(2):
            first.append(
                pltpu.make_async_copy(
                    full.at[o, pl.ds(0, up // 2), pl.ds(part * H, H)],
                    w_up.at[pl.ds(o * up + part * (up // 2), up // 2)],
                    sems.at[3 * o + part],
                )
            )
        second.append(
            pltpu.make_async_copy(
                full.at[o, pl.ds(up // 2, down)], w_down.at[pl.ds(o * down, down)], sems.at[3 * o + 2]
            )
        )
    return first, second


def start_all(copies):
    for copy in copies:
        copy.start()


def wait_all(copies):
    for copy in copies:
        copy.wait()


def block_copies(blocks, whole, sems):
    T = blocks[0].shape[0]
    return [pltpu.make_async_copy(block, whole.at[pl.ds(k * T, T)], sems.at[k]) for k, block in enumerate(blocks)]


def ffn_forward(blocks, full, bias, bias_at, H):
    n = len(blocks)
    T, D = blocks[0].shape
    step = 4

    def kernel(ins, outs, scratch):
        full, bias = ins[n:]
        (act, leave_act), (slope, leave_slope), even, odd = outs
        w_up, w_down, x, w_sems, x_sems = scratch
        first, second = fetch_ffn(full, w_up, w_down, w_sems)
        copies = block_copies(ins[:n], x, x_sems)
        start_all(first)
        start_all(copies)
        start_all(second)
        wait_all(first)
        for k in range(0, n, step):
            wait_all(copies[k : k + step])
            rows = slice(k * T, (k + step) * T)
            pre = dot(x[rows], w_up[...]) + bias[:, bias_at : bias_at + H]
            below = 0.5 * (1.0 + lax.erf(pre * math.sqrt(0.5)))
            result = (pre * below).astype(BF)
            act[rows] = result
            slope[rows] = (below + pre * (math.sqrt(0.5 / math.pi) * jnp.exp(-0.5 * pre * pre))).astype(BF)
            if k == 0:
                wait_all(second)
            back = dot(act[rows], w_down[...]).astype(BF)
            put_blocks(back, k, (even, odd), T)
        leave_act()
        leave_slope()

    outs = [((n * T, H), BF, True), ((n * T, H), BF, True), ((n // 2, T, D), BF, n // 2), ((n // 2, T, D), BF, n // 2)]
    ins = [raw(item) for item in blocks] + [raw(full), near(bias)]
    sems = pltpu.SemaphoreType.DMA
    scratch = [((D, H), BF), ((H, D), BF), ((n * T, D), BF), sems((3 * full.shape[0],)), sems((n,))]
    return call(kernel, ins, outs, scratch, 4 * n * T * D * H)


def put_blocks(rows, first, halves, T):
    for i in range(rows.shape[0] // T):
        out, leave = halves[(first + i) % 2]
        out[(first + i) // 2] = rows[i * T : (i + 1) * T]
        leave((first + i) // 2)


def ffn_back(blocks, full, slope):
    n = len(blocks)
    T, D = blocks[0].shape
    H = slope.shape[1]
    step = 4

    def kernel(ins, outs, scratch):
        full, slope = ins[n:]
        grad_pre, bias_grad, even, odd = outs
        w_up, w_down, x, w_sems, x_sems = scratch
        first, second = fetch_ffn(full, w_up, w_down, w_sems)
        copies = block_copies(ins[:n], x, x_sems)
        start_all(second)
        start_all(copies)
        start_all(first)
        wait_all(second)
        total = jnp.zeros((1, H), F32)
        for k in range(0, n, step):
            wait_all(copies[k : k + step])
            rows = slice(k * T, (k + step) * T)
            grad = (dot_rt(x[rows], w_down[...]) * slope()[rows].astype(F32)).astype(BF)
            grad_pre[rows] = grad
            total = total + jnp.sum(grad.astype(F32), axis=0, keepdims=True)
            if k == 0:
                wait_all(first)
            put_blocks(dot_rt(grad_pre[rows], w_up[...]).astype(BF), k, (even, odd), T)
        bias_grad[...] = total

    outs = [((n * T, H), BF), ((1, H), F32), ((n // 2, T, D), BF, n // 2), ((n // 2, T, D), BF, n // 2)]
    ins = [raw(item) for item in blocks] + [raw(full), held(slope)]
    sems = pltpu.SemaphoreType.DMA
    scratch = [((D, H), BF), ((H, D), BF), ((n * T, D), BF), sems((3 * full.shape[0],)), sems((n,))]
    return call(kernel, ins, outs, scratch, 4 * n * T * D * H)


def ffn_weights(normed, grads, act, grad_pre, far, extra):
    n = len(normed)
    T, D = normed[0].shape
    N = n * T
    H = act.shape[1]
    up, down = D // far, H // far
    more = [] if extra is None else [near(extra)]
    count = up // 2 + down + (0 if extra is None else extra.shape[1])

    def kernel(ins, outs, scratch):
        act, grad_pre = ins[2 * n : 2 * n + 2]
        left, right, left_sems, right_sems = scratch
        out = outs[0]
        copies = block_copies(ins[:n], left, left_sems)
        later = block_copies(ins[n : 2 * n], right, right_sems)
        start_all(copies)
        start_all(later)
        wait_all(copies)
        for o in range(far):
            block = dot_lt(left[:, o * up : (o + 1) * up], grad_pre[...]).astype(BF)
            out[o, : up // 2, :H] = block[: up // 2]
            out[o, : up // 2, H:] = block[up // 2 :]
        wait_all(later)
        act = act()
        for o in range(far):
            block = dot_lt(act[:, o * down : (o + 1) * down], right[...]).astype(BF)
            out[o, up // 2 : up // 2 + down] = block
            if more:
                out[o, up // 2 + down :] = ins[2 * n + 2][o]

    sems = pltpu.SemaphoreType.DMA
    scratch = [((N, D), BF), ((N, D), BF), sems((n,)), sems((n,))]
    ins = [raw(item) for item in (*normed, *grads)] + [held(act), near(grad_pre)] + more
    return call(kernel, ins, [((far, count, D), BF)], scratch, 4 * N * D * H, light=False)[0]


def attn_back(blocks, full, qkv, context, logs, table, seg_row, half, scale):
    n = len(blocks)
    T, D = blocks[0].shape
    wide = 4 * half
    N = n * T
    step = 4
    across_block = lanes_of(N)

    def kernel(ins, outs, scratch):
        full, table, qkv, context, logs, seg_row = ins[n:]
        mixed, bias_grad, even, odd = outs
        w_in, w_out, x, grad, delta, cos, sin, acc_k, acc_v, x_sems = scratch
        copies = block_copies(ins[:n], x, x_sems)
        start_all(copies)
        load_attn(full(), w_in, w_out)
        for k in range(0, n, step):
            wait_all(copies[k : k + step])
            rows = slice(k * T, (k + step) * T)
            grad[rows] = dot_rt(x[rows], w_out[...]).astype(BF)
        table = table()
        cos[...], sin[...] = rotary(table, slice(None), half)
        acc_k[...] = jnp.zeros_like(acc_k)
        acc_v[...] = jnp.zeros_like(acc_v)
        qkv, logs = qkv(), logs()
        product = (grad[...].astype(F32) * context()[...].astype(F32)).T
        delta[0:1] = jnp.sum(product[: 2 * half], axis=0, keepdims=True)
        delta[1:2] = jnp.sum(product[2 * half :], axis=0, keepdims=True)
        first_qk, first_v = head_masks(wide)
        zero = jnp.zeros((), BF)

        def part(c, carry):
            at = pl.ds(pl.multiple_of(c * across_block, 128), across_block)
            allowed = table[:, 2 * half : 2 * half + 1] == seg_row[:, at]
            grad_query = []
            for head in range(2):
                mine = first_qk if head == 0 else jnp.logical_not(first_qk)
                mine_v = first_v if head == 0 else jnp.logical_not(first_v)
                query = jnp.where(mine, qkv[at, :wide], zero)
                grad_h = jnp.where(mine_v, grad[at, :], zero)
                scores = dot_rt(qkv[:, wide : 2 * wide], query) - logs[head : head + 1, at]
                probs = jnp.exp(jnp.where(allowed, scores, NEG_FILL))
                grad_probs = dot_rt(qkv[:, 2 * wide :], grad_h)
                grad_scores = (probs * (grad_probs - delta[head : head + 1, at])).astype(BF)
                acc_k[...] += dot(grad_scores, query)
                acc_v[...] += dot(probs.astype(BF), grad_h)
                grad_query.append(dot_lt(grad_scores, qkv[:, wide : 2 * wide]))
            result = jnp.where(first_qk, grad_query[0], grad_query[1]) * scale
            mixed[at, :wide] = (result * cos[at, :] - roll_halves(result) * sin[at, :]).astype(BF)
            return carry

        lax.fori_loop(0, N // across_block, part, 0)
        total = acc_k[...]
        mixed[:, wide : 2 * wide] = (total * cos[...] - roll_halves(total) * sin[...]).astype(BF)
        mixed[:, 2 * wide :] = acc_v[...].astype(BF)
        sums = jnp.zeros((1, 3 * wide), F32)
        for k in range(0, n, step):
            rows = slice(k * T, (k + step) * T)
            sums = sums + jnp.sum(mixed[rows].astype(F32), axis=0, keepdims=True)
            put_blocks(dot_rt(mixed[rows], w_in[...]).astype(BF), k, (even, odd), T)
        bias_grad[...] = sums

    outs = [((N, 3 * wide), BF), ((1, 3 * wide), F32), ((n // 2, T, D), BF, n // 2), ((n // 2, T, D), BF, n // 2)]
    scratch = [((D, 3 * wide), BF), ((wide, D), BF), ((N, D), BF), ((N, wide), BF), ((2, N), F32)]
    scratch += [((N, wide), F32)] * 4 + [pltpu.SemaphoreType.DMA((n,))]
    flops = 2 * N * D * 4 * wide + 20 * N * N * wide
    ins = [raw(item) for item in blocks] + [held(item) for item in (full, table, qkv, context, logs)] + [near(seg_row)]
    return call(kernel, ins, outs, scratch, flops)


def attn_weights(inputs, grads, context, mixed, bias_grad, far, relative):
    n = len(inputs)
    T, D = inputs[0].shape
    N = n * T
    wide = context.shape[1]
    rows = D // far
    part = wide // far
    size = lax.axis_size("row")

    def kernel(ins, outs, scratch):
        context, mixed, bias_grad = ins[2 * n :]
        left, right, left_sems, right_sems = scratch
        here = (lax.axis_index("seq") * size + lax.axis_index("row")) // PLANE
        copies = block_copies(ins[:n], left, left_sems)
        later = block_copies(ins[n : 2 * n], right, right_sems)
        start_all(copies)
        start_all(later)
        wait_all(copies)
        for k in range(far):
            if relative:
                lanes = pl.ds(pl.multiple_of((here ^ k) * rows, 128), rows)
                outs[k][:rows, : 3 * wide] = dot_lt(left[:, lanes], mixed[...]).astype(BF)
            else:
                outs[0][k, :rows, : 3 * wide] = dot_lt(left[:, k * rows : (k + 1) * rows], mixed[...]).astype(BF)
        wait_all(later)
        whole = dot_lt(context()[...], right[...]).astype(BF)
        extra = jnp.broadcast_to(bias_grad[...], (16, 3 * wide)).astype(BF)
        if relative:
            right[:wide, :D] = whole
        for k in range(far):
            out = outs[k] if relative else outs[0].at[k]
            if relative:
                block = right[pl.ds(pl.multiple_of((here ^ k) * part, 16), part), :]
            else:
                block = whole[k * part : (k + 1) * part]
            for j in range(rows // part):
                out[j * part : (j + 1) * part, 3 * wide :] = block[:, j * wide : (j + 1) * wide]
            out[rows:, : 3 * wide] = extra
            out[rows:, 3 * wide :] = jnp.zeros((16, wide), BF)

    sems = pltpu.SemaphoreType.DMA
    scratch = [((N, D), BF), ((N, D), BF), sems((n,)), sems((n,))]
    ins = [raw(item) for item in (*inputs, *grads)] + [held(context), near(mixed), near(bias_grad)]
    if relative:
        outs = [((rows + 16, 4 * wide), BF)] * far
    else:
        outs = [((far, rows + 16, 4 * wide), BF)]
    return call(kernel, ins, outs, scratch, 8 * N * D * wide, light=False)


def plane_index():
    return lax.axis_index("seq") % (PLANE // lax.axis_size("row")) * lax.axis_size("row") + lax.axis_index("row")


def head_kernel(blocks, own, codes, own_codes, positive, temp, w_col, loss_weight):
    n = len(blocks)
    T, C = own.shape
    N = n * T
    D = w_col.shape[0]
    slots = NQ * QLEN

    def kernel(ins, outs, scratch):
        own, codes, own_codes, positive, temp, w_col = ins[n:]
        grad, low, terms = outs
        held, embeds = scratch
        here = plane_index()
        upper = lax.rem(lax.axis_index("seq") // (PLANE // lax.axis_size("row")), 2)

        def place(c):
            column = lax.rem(c // 2, 2) ^ upper
            return pl.ds(pl.multiple_of((4 * column + 2 * lax.rem(c, 2) + c // 4) * T, 16), T)

        for k in range(n):
            held[place(here ^ k), :] = ins[k][...]
        lane = lax.broadcasted_iota(jnp.int32, (1, C), 1)
        slot = lax.broadcasted_iota(jnp.int32, (slots, 1), 0)
        doc, own_doc = codes[0:1, :], own_codes[0:1, :]
        select = jnp.where(codes[1:2, :] == slot, 1.0, 0.0).astype(BF)
        own_select = jnp.where(own_codes[1:2, :] == slot, 1.0, 0.0).astype(BF)
        rows = held[...].astype(F32)
        mine = own[...]
        heat = temp[...]
        wanted = lane == positive[...]
        valid = lane <= NSD
        loss = jnp.zeros((1, 1), F32)
        heat_grad = jnp.zeros((1, 1), F32)
        total = jnp.zeros((T, C), F32)
        for width in (C, C * 3 // 4, C // 2):
            inside = lane < width
            size = jnp.sum(jnp.where(inside, rows * rows, 0.0), axis=1, keepdims=True)
            embed = jnp.where(inside, rows * lax.rsqrt(size + 1e-06), 0.0).astype(BF)
            embeds[...] = embed
            query = dot(select, embed).astype(BF)
            powers = jnp.exp(SHARPNESS * dot_rt(query, embed))
            soft = jnp.zeros((slots, C), F32)
            sums = []
            for d in range(NSD + 1):
                sums.append(jnp.sum(jnp.where(doc == d, powers, 0.0), axis=1, keepdims=True))
                soft = jnp.where(lane == d, jnp.log(sums[d]) / SHARPNESS, soft)
            pair = jnp.sum(soft.reshape(NQ, QLEN, C), axis=1, keepdims=True)
            pair = jnp.broadcast_to(pair, (NQ, QLEN, C)).reshape(slots, C)
            logits = pair * heat / QLEN
            masked = jnp.where(valid, logits, NEG_FILL)
            top = jnp.max(masked, axis=1, keepdims=True)
            shares = jnp.exp(masked - top)
            share_sum = jnp.sum(shares, axis=1, keepdims=True)
            chosen = jnp.sum(jnp.where(wanted, logits, 0.0), axis=1, keepdims=True)
            losses = top + jnp.log(share_sum) - chosen
            loss = loss + jnp.sum(losses, axis=0, keepdims=True) * (loss_weight / QLEN)
            grad_logits = loss_weight * (shares / share_sum - jnp.where(wanted, 1.0, 0.0))
            along = jnp.sum(jnp.where(valid, grad_logits * logits, 0.0), axis=1, keepdims=True)
            heat_grad = heat_grad + jnp.sum(along, axis=0, keepdims=True) / QLEN
            grad_soft = grad_logits * heat / QLEN
            weight = jnp.zeros((slots, N), F32)
            own_weight = jnp.zeros((slots, T), F32)
            for d in range(NSD + 1):
                ratio = grad_soft[:, d : d + 1] / sums[d]
                weight = jnp.where(doc == d, ratio, weight)
                own_weight = jnp.where(own_doc == d, ratio, own_weight)
            grad_query = dot((powers * weight).astype(BF), embed)
            own_embed = embeds[place(here), :]
            own_powers = jnp.exp(SHARPNESS * dot_rt(query, own_embed))
            grad_embed = dot_lt((own_powers * own_weight).astype(BF), query)
            high = grad_query.astype(BF)
            rest = (grad_query - high.astype(F32)).astype(BF)
            grad_embed = grad_embed + dot_lt(own_select, high) + dot_lt(own_select, rest)
            size = jnp.sum(jnp.where(inside, mine * mine, 0.0), axis=1, keepdims=True)
            inverse = lax.rsqrt(size + 1e-06)
            along = jnp.sum(jnp.where(inside, grad_embed * mine, 0.0), axis=1, keepdims=True)
            part = inverse * grad_embed - mine * (inverse * inverse * inverse * along)
            total = total + jnp.where(inside, part, 0.0)
        low[...] = total.astype(BF)
        grad[...] = dot_rt(total.astype(BF), w_col[...])
        terms[...] = jnp.where(lane == 0, loss, jnp.where(lane == 1, heat_grad, 0.0))

    outs = [((T, D), F32), ((T, C), BF), ((1, C), F32)]
    ins = [near(item) for item in (*blocks, own, codes, own_codes, positive, temp, w_col)]
    return call(kernel, ins, outs, [((N, C), BF), ((N, C), BF)], 24 * slots * N * C, 40)


def swap_quarters(x):
    q = x.shape[1] // 4
    return jnp.concatenate([x[:, :q], x[:, 2 * q : 3 * q], x[:, q : 2 * q], x[:, 3 * q :]], axis=1)


def pack_first(w, small):
    rows, width = w.shape
    D, wide = width // 3, width // 3 // PLANE
    count = rows + small.shape[0]

    def kernel(ins, outs, _):
        w, small = ins
        here = plane_index()
        for k in range(PLANE):
            out = outs[k % 2].at[k // 2]
            for t in range(3):
                columns = w[:, pl.ds(pl.multiple_of(t * D + (here ^ k) * wide, 128), wide)]
                out[:rows, t * wide : (t + 1) * wide] = swap_quarters(columns) if t < 2 else columns
            out[rows:] = small[...]

    outs = [((PLANE // 2, count, 3 * wide), BF)] * 2
    return call(kernel, [near(w), near(small)], outs, [], w.size, SMALL)


def unpack_first(even, core, got, out_rows):
    rows, D = out_rows.shape
    count, cols = even.shape[1:]
    wide = cols // 3

    def kernel(ins, outs, _):
        even, core, *got, out_rows = ins
        block, below = outs
        here = plane_index()
        blocks = [even.at[0], core.at[0]] + [ref.at[j] for ref in got for j in range(2)]
        for k in range(PLANE):
            of = here ^ k
            block[pl.ds(pl.multiple_of(of * rows, 16), rows), :cols] = blocks[k][:rows]
            below[of] = blocks[k][rows:]
            block[k * rows : (k + 1) * rows, cols:] = out_rows[:, k * wide : (k + 1) * wide]

    outs = [((PLANE * rows, cols + wide), BF), ((PLANE, count - rows, cols), BF)]
    return call(kernel, [near(item) for item in (even, core, *got, out_rows)], outs, [], even.size, SMALL)


def pack_shares(sums, others, ffn, lines, in_cols, hidden_cols):
    rows, width = sums[0].shape[0] - 16, sums[0].shape[1]
    part = rows // PLANE
    L = len(ffn)
    count = L * (in_cols + hidden_cols) + 128
    bias_lines = in_cols // 128
    first_line = part - L * bias_lines

    def kernel(ins, outs, scratch):
        even, odd, last = outs
        attn = scratch[0]
        n = len(sums)
        total = ins[0][...].astype(F32)
        for ref in ins[1:n]:
            total = total + ref[...].astype(F32)
        attn[0] = total.astype(BF)
        for layer in range(1, L):
            attn[layer] = ins[n + layer - 1][...]
        last[...] = attn[0, :rows, in_cols:]
        ups = ins[n + L - 1 : n + 2 * L - 1]
        lines = ins[n + 2 * L - 1]
        here = plane_index()
        line = lax.broadcasted_iota(jnp.int32, (part, 128), 0)
        for k in range(PLANE):
            to = here ^ k
            out = (odd if k % 2 else even).at[k // 2]
            at = pl.ds(pl.multiple_of(to * part, 16), part)
            half = pl.ds(pl.multiple_of(lax.rem(to, PLANE // 2) * part, 16), part)
            for layer in range(L):
                out[:, layer * in_cols : (layer + 1) * in_cols] = attn[layer, at, :in_cols]
                folded = ups[layer][half, :]
                own = jnp.where(to < PLANE // 2, folded[:, :hidden_cols], folded[:, hidden_cols:])
                start = L * in_cols + layer * hidden_cols
                out[:, start : start + hidden_cols] = own
            block = lines[to]
            for layer in range(L):
                bias = attn[layer, rows : rows + 16, :in_cols].astype(F32)[:1]
                for j in range(bias_lines):
                    spot = line == first_line + layer * bias_lines + j
                    block = jnp.where(spot, bias[:, j * 128 : (j + 1) * 128], block)
            out[:, count - 128 :] = block.astype(BF)

    half = PLANE // 2
    outs = [((half, part, count), BF), ((half, part, count), BF), ((rows, width - in_cols), BF)]
    ins = [near(item) for item in (*sums, *others, *ffn, lines)]
    return call(kernel, ins, outs, [((L, rows + 16, width), BF)], rows * count, SMALL)


def unpack_shares(even, core, got, L, in_cols, hidden_cols):
    part, count = even.shape[1:]
    wide = in_cols // 3
    D, far = PLANE * wide, hidden_cols // 128
    bias_lines = in_cols // 128
    first_line = part - L * bias_lines

    def natural(x):
        q = wide // 4
        return jnp.concatenate([x[:, :q], x[:, 2 * q : 3 * q], x[:, q : 2 * q], x[:, 3 * q :]], axis=1)

    def kernel(ins, outs, scratch):
        even, core, *got = ins
        w_in, w_up, lines, bias = outs
        here = plane_index()
        blocks = [even.at[0], core.at[0]] + [ref.at[j] for ref in got for j in range(2)]
        total = jnp.zeros((part, 128), F32)
        for k in range(PLANE):
            block = blocks[k][...].astype(F32)
            of = here ^ k
            own_lines = block[:, count - 128 :]
            total = total + own_lines
            for layer in range(L):
                for t in range(3):
                    at = pl.ds(pl.multiple_of(t * D + of * wide, 128), wide)
                    start = layer * in_cols + t * wide
                    columns = block[:, start : start + wide]
                    row = first_line + layer * bias_lines + t
                    line = own_lines[row : row + 1]
                    if t < 2:
                        columns, line = natural(columns), natural(line)
                    w_in[layer, :, at] = columns
                    bias[layer, :, at] = line
                for o in range(far):
                    at = pl.ds(pl.multiple_of(o * PLANE * 128 + of * 128, 128), 128)
                    start = L * in_cols + layer * hidden_cols + o * 128
                    w_up[layer, :, at] = block[:, start : start + 128]
        lines[...] = total

    outs = [((L, part, 3 * D), F32), ((L, part, far * PLANE * 128), F32), ((part, 128), F32), ((L, 1, 3 * D), F32)]
    ins = [near(item) for item in (even, core, *got)]
    return call(kernel, ins, outs, [], part * count * PLANE, SMALL)


def body(
    tokens,
    attn_in,
    attn_out,
    ffn_up,
    ffn_down,
    norm_gains,
    biases,
    colbert,
    log_scale,
    cotangent,
    seg_lengths,
    seg_kinds,
    pairing,
):
    S = lax.axis_size("seq")
    R = lax.axis_size("row")
    O = S * R // PLANE
    place = lax.axis_index("seq") * R + lax.axis_index("row")
    plane, far = place % PLANE, place // PLANE
    relative = jnp.bitwise_xor(plane, jnp.arange(PLANE, dtype=jnp.int32))
    T = tokens.shape[1]
    D = tokens.shape[2]
    N = PLANE * T
    L = attn_in.shape[0]
    head_dim = D // HEADS
    half = head_dim // 2
    scale = head_dim ** (-0.5)
    wide = 2 * head_dim
    in_cols = 3 * wide
    in_rows = attn_in.shape[1]
    rows_in = PLANE * in_rows
    FF = ffn_up.shape[2]
    up_cols = FF // (S * R)
    hidden_cols = O * up_cols
    gain_part = norm_gains.shape[1]
    bias_part = biases.shape[1]
    part = gain_part + bias_part
    along_z = [[o * (S // O) + i for o in range(O)] for i in range(S // O)]
    is_mine = jnp.arange(PLANE, dtype=jnp.int32) == plane

    def padded_rows(vector, width=D):
        rows = -(-vector.shape[0] // (16 * width)) * 16
        return jnp.pad(vector, (0, rows * width - vector.shape[0])).reshape(rows, width)

    def pack_columns(w):
        lead = w.shape[:-1]
        n = len(lead)
        qk = w[..., : 2 * D].reshape(*lead, 2, PLANE, 2, 2, half)
        qk = qk.transpose((n + 1,) + tuple(range(n)) + (n, n + 3, n + 2, n + 4)).reshape(PLANE, *lead, 2 * wide)
        v = w[..., 2 * D :].reshape(*lead, PLANE, wide)
        v = v.transpose((n,) + tuple(range(n)) + (n + 1,))
        return jnp.concatenate([qk, v], axis=-1)

    def unpack_columns(w):
        rows = w.shape[1]
        qk = w[:, :, : 2 * wide].reshape(PLANE, rows, 2, 2, 2, half)
        qk = qk.transpose(1, 2, 0, 4, 3, 5).reshape(rows, 2 * D)
        v = w[:, :, 2 * wide :].transpose(1, 0, 2).reshape(rows, D)
        return jnp.concatenate([qk, v], axis=1)

    def pack_hidden(w):
        rows = w.shape[0]
        return w.reshape(rows, O, PLANE, up_cols).transpose(2, 0, 1, 3).reshape(PLANE, rows, hidden_cols)

    def unpack_hidden(w):
        rows = w.shape[1]
        return w.reshape(PLANE, rows, O, up_cols).transpose(1, 2, 0, 3).reshape(rows, FF)

    def fold(w):
        n = w.shape[-2] // 2
        return jnp.concatenate([w[..., :n, :], w[..., n:, :]], axis=-1)

    def unfold(w):
        n = w.shape[-1] // 2
        return jnp.concatenate([w[..., :n], w[..., n:]], axis=-2)

    to_group = [(b, (b % O) * PLANE + b // O) for b in range(O * PLANE)]
    from_group = [(d, b) for b, d in to_group]
    small = jnp.concatenate([norm_gains.reshape(-1), biases.reshape(-1), colbert.reshape(-1)])
    even, odd = pack_first(attn_in[0], padded_rows(small, in_cols))
    core = across(odd, 1)
    got = tie(*[across(jnp.stack([even[k], core[k]]), 2 * k) for k in (1, 2, 3)])
    shard_out = lax.ppermute(attn_out, BOTH, to_group)
    table = turned(jnp.concatenate([seg_lengths[0], seg_kinds[0], pairing[0]]))
    seg_count = seg_lengths.shape[1]
    lengths, kinds = table[:seg_count], table[seg_count : 2 * seg_count]
    pairs_of = table[2 * seg_count :]
    hidden_low = turned(tokens[0])

    def attn_block(layer, shard):
        out = shard_out[layer].reshape(in_rows, PLANE, wide).transpose(1, 0, 2).reshape(rows_in, wide)
        return jnp.concatenate([shard, out], axis=1)

    def gather_far(x):
        return lax.all_gather(x, "seq", axis=0, axis_index_groups=along_z)

    own, small = unpack_first(even, core, got, shard_out[0])
    small = small.reshape(PLANE, -1)
    full_attn = [gather_far(own)]
    count_small = L * part
    col_plane = small[:, count_small : count_small + colbert.size].reshape(-1)
    params = small[None, :, :count_small]
    step = 1
    while step < O:
        other = across(params, PLANE * step)
        low_side = (far & step) == 0
        params = jnp.concatenate([jnp.where(low_side, params, other), jnp.where(low_side, other, params)], axis=0)
        step *= 2
    params = params.reshape(O * PLANE, count_small).astype(F32)
    gains_all = params[:, : L * gain_part].reshape(O * PLANE, L, gain_part).transpose(1, 0, 2).reshape(L, 2 * D)
    bias_all = params[:, L * gain_part :].reshape(O * PLANE, L, bias_part).transpose(1, 0, 2).reshape(L, -1)
    in_biases = pick(pack_columns(bias_all[:, : 3 * D]), plane, axis=0).reshape(1, L * in_cols)
    up_biases = pick(pack_hidden(bias_all[:, 4 * D : 4 * D + FF]), plane, axis=0).reshape(1, L * hidden_cols)
    rest_at = 4 * D + FF
    params = jnp.concatenate([gains_all, bias_all[:, 3 * D : 4 * D], bias_all[:, rest_at:]], axis=1).reshape(1, -1)
    GAIN_ONE, GAIN_TWO, BIAS_OUT, BIAS_DOWN, SHIFT_ONE, SHIFT_TWO = range(6)

    def at(layer, which):
        return (layer * 6 + which) * D

    rest = jnp.concatenate(
        [pack_hidden(ffn_up[0])]
        + [piece for layer in range(1, L) for piece in (pack_columns(attn_in[layer]), pack_hidden(ffn_up[layer]))],
        axis=-1,
    )
    rest = plane_exchange(rest, relative).reshape(rows_in, -1)
    full_ffn = []
    start = 0
    for layer in range(L):
        if layer > 0:
            full_attn.append(gather_far(attn_block(layer, rest[:, start : start + in_cols])))
            start += in_cols
        own = [fold(rest[:, start : start + hidden_cols]), ffn_down[layer]]
        start += hidden_cols
        if layer == L - 1:
            own.append(padded_rows(col_plane))
        full_ffn.append(gather_far(jnp.concatenate(own, axis=0)))
    w_col = full_ffn[L - 1][:, rows_in // 2 + up_cols :].reshape(O, -1)[:, : col_plane.size]
    w_col = w_col.reshape(D, colbert.shape[1])

    block_at = 4 * ((relative // 2 % 2) ^ (far % 2)) + 2 * (relative % 2) + relative // 4
    positions = (block_at[:, None] * T + jnp.arange(T, dtype=jnp.int32)[None, :]).reshape(N)
    held_segment, held_offset = token_info(positions, lengths, kinds)[:2]
    cos, sin = rope_angles(held_offset, head_dim)
    seg_row = held_segment.astype(F32)[None, :]
    table = jnp.concatenate([cos, sin, jnp.broadcast_to(seg_row.T, (N, wide - 2 * half))], axis=1)

    hidden = hidden_low
    records = []
    for layer in range(L):
        x_all = plane_gather(hidden_low)
        qkv, context, logs, even, odd = attn_forward(
            x_all, full_attn[layer], in_biases, layer * in_cols, table, seg_row, half, scale
        )
        terms, _ = plane_scatter(even, odd)
        first, normed, normed_low = add_norm(
            [hidden] + terms, params, at(layer, BIAS_OUT), at(layer, GAIN_ONE), at(layer, SHIFT_ONE)
        )
        normed_all = plane_gather(normed_low)
        act, slope, even, odd = ffn_forward(
            normed_all, full_ffn[layer], up_biases, layer * hidden_cols, hidden_cols
        )
        terms, _ = plane_scatter(even, odd)
        second, hidden, hidden_low = add_norm(
            [normed] + terms, params, at(layer, BIAS_DOWN), at(layer, GAIN_TWO), at(layer, SHIFT_TWO)
        )
        records.append((x_all, qkv, context, logs, first, normed_all, act, slope, second))
    hidden_out = turned(hidden_low, True)

    full_width = w_col.shape[1]
    row_positions = jnp.arange(N, dtype=jnp.int32)
    segment, offset, is_query, query_slot, doc_num = token_info(row_positions, lengths, kinds)
    codes = jnp.stack([jnp.where(is_query == 0, doc_num, -1), jnp.where(is_query == 1, query_slot, -1)])
    own_codes = lax.dynamic_slice(codes, (0, block_at[0] * T), (2, T))
    positive = jnp.repeat(pairs_of, QLEN)[:, None]
    temp = jnp.exp(log_scale)[None]
    hidden_low, cot = tie(hidden_low, cotangent[0])
    cot = turned(cot)
    col = dot(hidden_low, w_col)
    col_blocks = plane_gather(col.astype(BF))
    grad_out, grad_col_low, terms = head_kernel(
        col_blocks, col, codes, own_codes, positive, temp, w_col, 1.0 / (3 * NQ * R)
    )
    loss_terms = terms[0, :2]
    col_parts = dot_lt(hidden_low, grad_col_low).reshape(O, PLANE, in_rows, full_width).transpose(1, 0, 2, 3)
    col_parts = plane_sum(pick(col_parts.reshape(PLANE, O * in_rows, full_width), relative, axis=0))
    col_rows = jax.vmap(padded_rows)(col_parts.reshape(O, in_rows * full_width)).astype(BF)
    grad_parts = [cot, grad_out]

    def scatter_far(whole):
        whole = whole.reshape(-1, whole.shape[-1])
        return lax.psum_scatter(whole, "seq", scatter_dimension=0, tiled=True, axis_index_groups=along_z)

    outs = [[None] * L for _ in range(6)]

    def finish_out(layer, share_out):
        share_out = share_out.reshape(PLANE, in_rows, wide).transpose(1, 0, 2).reshape(in_rows, D)
        outs[1][layer] = lax.ppermute(share_out, BOTH, from_group).astype(F32)

    shares_ffn, shares_attn = [None] * L, [None] * L
    vectors = [None] * L
    for layer in reversed(range(L)):
        x_all, qkv, context, logs, first, normed_all, act, slope, second = records[layer]
        grad_second, grad_ffo, sums_two = norm_back(grad_parts, second, params, at(layer, GAIN_TWO))
        ffo_all = plane_gather(grad_ffo)
        if layer == L - 1:
            ffo_all, hidden_out = tie(ffo_all, hidden_out)
        grad_pre, grad_bias_up, even, odd = ffn_back(ffo_all, full_ffn[layer], slope)
        blocks = ffn_weights(normed_all, ffo_all, act, grad_pre, O, col_rows if layer == L - 1 else None)
        terms, blocks = plane_scatter(even, odd, blocks)
        shares_ffn[layer] = scatter_far(blocks)
        grad_first, grad_branch, sums_one = norm_back([grad_second] + terms, first, params, at(layer, GAIN_ONE))
        branch_all = plane_gather(grad_branch)
        if layer < L - 1:
            branch_all, shares_attn[layer + 1] = tie(branch_all, shares_attn[layer + 1])
        grad_mixed, grad_bias_in, even, odd = attn_back(
            branch_all, full_attn[layer], qkv, context, logs, table, seg_row, half, scale
        )

        gain_two, shift_two, down, gain_one, shift_one, out = [
            sums[0, k * D : (k + 1) * D] for sums in (sums_two, sums_one) for k in range(3)
        ]
        own_up = unpack_hidden(is_mine[:, None, None].astype(F32) * grad_bias_up[None])[0]
        gains = jnp.concatenate([gain_one, gain_two]).reshape(O, PLANE, gain_part)
        bias = jnp.concatenate([jnp.zeros((3 * D,), F32), out, own_up, down, shift_one, shift_two])
        vectors[layer] = jnp.concatenate([gains, bias.reshape(O, PLANE, bias_part)], axis=2)

        blocks = attn_weights(x_all, branch_all, context, grad_mixed, grad_bias_in, O, layer == 0)
        terms, blocks = plane_scatter(even, odd, blocks, layer == 0)
        terms, shares_ffn[layer] = tie(terms, shares_ffn[layer])
        if layer > 0:
            shares_attn[layer] = scatter_far(blocks[0])
            grad_parts = [grad_first] + terms

    got = [across(blocks[step], PLANE * step) for step in range(1, O)]
    entries = jnp.concatenate(vectors, axis=2).transpose(1, 0, 2).reshape(PLANE, O * L * part)
    lines = jnp.pad(entries, ((0, 0), (0, in_rows * 128 - O * L * part))).reshape(PLANE, in_rows, 128)
    grad_tokens = turned((grad_first + sum(item.astype(F32) for item in terms)).astype(BF), True)
    got, lines, grad_tokens = tie(got, lines, grad_tokens)
    even, odd, last_out = pack_shares([blocks[0]] + got, shares_attn[1:], shares_ffn, lines, in_cols, hidden_cols)
    core = across(odd, 1)
    got = tie(*[across(jnp.stack([even[k], core[k]]), 2 * k) for k in (1, 2, 3)])
    w_in_grad, w_up_grad, lines, bias_in_grad = unpack_shares(even, core, got, L, in_cols, hidden_cols)
    entries = lines.reshape(-1)[: O * L * part].reshape(O, L * part)
    entries = jnp.concatenate([entries, jnp.broadcast_to(loss_terms[None], (O, 2))], axis=1)
    mine = pick(entries, far)
    for step in range(1, O):
        mine = mine + across(pick(entries, far ^ step), PLANE * step)
    bias_in_grad = jnp.pad(bias_in_grad[:, 0], ((0, 0), (0, O * PLANE * bias_part - 3 * D)))
    bias_in_grad = pick(bias_in_grad.reshape(L, O * PLANE, bias_part), place, axis=1)
    for layer in range(L):
        outs[3][layer] = shares_ffn[layer][rows_in // 2 : rows_in // 2 + up_cols]
        finish_out(layer, shares_attn[layer][:rows_in, in_cols:] if layer > 0 else last_out)
        outs[4][layer] = mine[layer * part : layer * part + gain_part]
        outs[5][layer] = mine[layer * part + gain_part : (layer + 1) * part] + bias_in_grad[layer]
    col_share = shares_ffn[L - 1][rows_in // 2 + up_cols :].reshape(-1)[: in_rows * full_width]
    col_share = col_share.reshape(in_rows, full_width).astype(F32)
    loss_terms = mine[L * part :]
    outs[0], outs[2] = w_in_grad, w_up_grad
    stacked = [jnp.stack(items).astype(F32) if isinstance(items, list) else items for items in outs]
    return (
        hidden_out[None],
        loss_terms[:1],
        grad_tokens.astype(F32)[None],
        stacked[0],
        stacked[1],
        stacked[2],
        stacked[3],
        stacked[4],
        stacked[5],
        col_share,
        loss_terms[1:],
    )


def joined_2(value, axis, join):
    pieces = jax.tree.map(lambda part: lax.all_gather(part, axis), value)
    head = jax.tree.map(lambda part: part[0], pieces)
    tail = jax.tree.map(lambda part: part[1:], pieces)
    so_far, _ = lax.scan(lambda so_far, section: (join(so_far, section), None), head, tail)
    return so_far


def rope_tables(offset, head_dim):
    half = head_dim // 2
    inverse = jnp.exp(jnp.arange(half, dtype=jnp.float32) * (-2.0 * math.log(10000.0) / head_dim))
    angle = offset.astype(jnp.float32)[:, None] * inverse[None, :]
    return (jnp.cos(angle), jnp.sin(angle))


def rotate(flat, cos_table, sin_table):
    length = flat.shape[0]
    head_dim = flat.shape[1] // HEADS
    half = head_dim // 2
    shaped = flat.reshape(length, HEADS, head_dim)
    first_half = shaped[..., :half]
    second_half = shaped[..., half:]
    cos_three = cos_table[:, None, :]
    sin_three = sin_table[:, None, :]
    turned = jnp.concatenate(
        [
            first_half * cos_three - second_half * sin_three,
            second_half * cos_three + first_half * sin_three,
        ],
        axis=-1,
    )
    return turned.reshape(length, flat.shape[1])


def block_for(count):
    blocks = count
    while blocks > 1024 and blocks % 2 == 0:
        blocks = blocks // 2
    return blocks


def merge_pair(first, second):
    max_first, sum_first = first
    max_second, sum_second = second
    top = jnp.maximum(max_first, max_second)
    return (top, sum_first * jnp.exp(max_first - top) + sum_second * jnp.exp(max_second - top))


def matmul_left_t(left, right):
    return jnp.einsum("ti,to->io", left, right, preferred_element_type=jnp.float32)


def matmul_right_t(left, right):
    return jnp.einsum("to,io->ti", left, right, preferred_element_type=jnp.float32)


def body_wide(
    tokens,
    attn_in,
    attn_out,
    ffn_up,
    ffn_down,
    norm_gains,
    biases,
    colbert,
    log_scale,
    cotangent,
    seg_lengths,
    seg_kinds,
    pairing,
):
    rank = lax.axis_index("seq")
    local_len = tokens.shape[1]
    model_width = tokens.shape[2]
    head_dim = model_width // HEADS
    scale = head_dim ** (-0.5)
    lengths = seg_lengths[0]
    kinds = seg_kinds[0]
    positions = rank * local_len + jnp.arange(local_len, dtype=jnp.int32)
    segment, offset, is_query, query_slot, doc_num = token_info(positions, lengths, kinds)
    cos_table, sin_table = rope_tables(offset, head_dim)
    layer_count = attn_in.shape[0]

    def split_pieces(key_piece, value_piece):
        count = key_piece.shape[0]
        blocks = block_for(count)
        key_seg = token_info(jnp.arange(count, dtype=jnp.int32), lengths, kinds)[0]
        key_blocks = key_piece.reshape(count // blocks, blocks, HEADS, head_dim)
        value_blocks = value_piece.reshape(count // blocks, blocks, HEADS, head_dim)
        seg_blocks = key_seg.reshape(count // blocks, blocks)
        return (count, blocks, key_blocks, value_blocks, seg_blocks)

    def attend_back(queries, keys, values, context, log_total, grad_context):
        query_three = queries.reshape(local_len, HEADS, head_dim)
        grad_three = grad_context.reshape(local_len, HEADS, head_dim)
        delta = jnp.sum(
            grad_three.astype(jnp.float32) * context.reshape(local_len, HEADS, head_dim), axis=-1
        ).T

        def score_grads(
            query_blk, grad_blk, key_blk, value_blk, query_seg, key_seg, total_blk, delta_blk
        ):
            scores = (
                jnp.einsum("qhd,khd->hqk", query_blk, key_blk, preferred_element_type=jnp.float32)
                * scale
            )
            allowed = (query_seg[:, None] == key_seg[None, :])[None]
            probs = jnp.where(allowed, jnp.exp(scores - total_blk[..., None]), 0.0)
            grad_probs = jnp.einsum(
                "qhd,khd->hqk", grad_blk, value_blk, preferred_element_type=jnp.float32
            )
            grad_scores = (probs * (grad_probs - delta_blk[..., None])).astype(jnp.bfloat16)
            return (probs, grad_scores)

        grad_query = jnp.zeros((local_len, HEADS, head_dim), jnp.float32)
        count, blocks, key_blocks, value_blocks, seg_blocks = split_pieces(
            lax.all_gather(keys, "seq", axis=0, tiled=True),
            lax.all_gather(values, "seq", axis=0, tiled=True),
        )

        def advance(grad_acc, item):
            key_blk, value_blk, seg_blk = item
            probs, grad_scores = score_grads(
                query_three, grad_three, key_blk, value_blk, segment, seg_blk, log_total, delta
            )
            grad_acc = grad_acc + scale * jnp.einsum(
                "hqk,khd->qhd", grad_scores, key_blk, preferred_element_type=jnp.float32
            )
            grad_key = scale * jnp.einsum(
                "hqk,qhd->khd", grad_scores, query_three, preferred_element_type=jnp.float32
            )
            grad_value = jnp.einsum(
                "hqk,qhd->khd",
                probs.astype(jnp.bfloat16),
                grad_three,
                preferred_element_type=jnp.float32,
            )
            joined = jnp.concatenate(
                [grad_key.reshape(blocks, model_width), grad_value.reshape(blocks, model_width)],
                axis=1,
            )
            return (grad_acc, joined)

        grad_query, pieces_out = lax.scan(
            advance, grad_query, (key_blocks, value_blocks, seg_blocks)
        )
        grad_rows = pieces_out.reshape(count, 2 * model_width)
        grad_query, grad_rows = (grad_query, grad_rows)
        summed = lax.psum_scatter(
            grad_rows.astype(jnp.bfloat16), "seq", scatter_dimension=0, tiled=True
        ).astype(jnp.float32)
        grad_key_out = summed[:, :model_width]
        grad_value_out = summed[:, model_width:]
        return (grad_query.reshape(local_len, model_width), grad_key_out, grad_value_out)

    def unpack(full):
        w_in, w_out, w_up, w_down, gains, bias = full[:6]
        hidden_units = w_up.shape[1]
        gains_f = gains.astype(jnp.float32)
        bias_f = bias.astype(jnp.float32)
        width_three = 3 * model_width
        return (
            w_in,
            w_out,
            w_up,
            w_down,
            hidden_units,
            gains_f[:model_width],
            gains_f[model_width:],
            bias_f[:width_three],
            bias_f[width_three : 4 * model_width],
            bias_f[4 * model_width : 4 * model_width + hidden_units],
            bias_f[4 * model_width + hidden_units : 5 * model_width + hidden_units],
            bias_f[5 * model_width + hidden_units : 6 * model_width + hidden_units],
            bias_f[6 * model_width + hidden_units :],
        )

    def layer_backward(grad_out, full, record):
        (
            w_in,
            w_out,
            w_up,
            w_down,
            hidden_units,
            gain_one,
            gain_two,
            bias_in,
            bias_out,
            bias_up,
            bias_down,
            shift_one,
            shift_two,
        ) = unpack(full)
        (
            inputs_low,
            queries,
            keys,
            values,
            context,
            context_low,
            log_total,
            first,
            normed,
            normed_low,
            pre_act,
            act_low,
            second,
        ) = record
        unused, pull_two = jax.vjp(layer_norm, second, gain_two, shift_two)
        grad_second, grad_gain_two, grad_shift_two = pull_two(grad_out)
        grad_branch_two = grad_second.astype(jnp.bfloat16)
        grad_bias_down = jnp.sum(grad_branch_two.astype(jnp.float32), axis=0)
        grad_w_down = matmul_left_t(act_low, grad_branch_two)
        grad_act = matmul_right_t(grad_branch_two, w_down)
        unused, pull_gelu = jax.vjp(exact_gelu, pre_act)
        grad_pre = pull_gelu(grad_act)[0].astype(jnp.bfloat16)
        grad_bias_up = jnp.sum(grad_pre.astype(jnp.float32), axis=0)
        grad_w_up = matmul_left_t(normed_low, grad_pre)
        grad_normed = grad_second + matmul_right_t(grad_pre, w_up)
        unused, pull_one = jax.vjp(layer_norm, first, gain_one, shift_one)
        grad_first, grad_gain_one, grad_shift_one = pull_one(grad_normed)
        grad_branch = grad_first.astype(jnp.bfloat16)
        grad_bias_out = jnp.sum(grad_branch.astype(jnp.float32), axis=0)
        grad_w_out = matmul_left_t(context_low, grad_branch)
        grad_context = matmul_right_t(grad_branch, w_out).astype(jnp.bfloat16)
        grad_query, grad_key, grad_value = attend_back(
            queries, keys, values, context, log_total, grad_context
        )
        grad_mixed = jnp.concatenate(
            [
                rotate(grad_query, cos_table, -sin_table),
                rotate(grad_key, cos_table, -sin_table),
                grad_value,
            ],
            axis=1,
        ).astype(jnp.bfloat16)
        grad_bias_in = jnp.sum(grad_mixed.astype(jnp.float32), axis=0)
        grad_w_in = matmul_left_t(inputs_low, grad_mixed)
        grad_hidden = grad_first + matmul_right_t(grad_mixed, w_in)
        grad_gains = jnp.concatenate([grad_gain_one, grad_gain_two])
        grad_bias = jnp.concatenate(
            [
                grad_bias_in,
                grad_bias_out,
                grad_bias_up,
                grad_bias_down,
                grad_shift_one,
                grad_shift_two,
            ]
        )
        return (grad_hidden, (grad_w_in, grad_w_out, grad_w_up, grad_w_down, grad_gains, grad_bias))

    hidden = tokens[0].astype(jnp.float32)
    records = []
    gathered = []
    for layer_index in range(layer_count):
        full = (
            lax.all_gather(attn_in[layer_index], ("seq", "row"), axis=0, tiled=True),
            lax.all_gather(attn_out[layer_index], ("seq", "row"), axis=0, tiled=True),
            lax.all_gather(ffn_up[layer_index], ("seq", "row"), axis=0, tiled=True),
            lax.all_gather(ffn_down[layer_index], ("seq", "row"), axis=0, tiled=True),
            lax.all_gather(norm_gains[layer_index], ("seq", "row"), axis=0, tiled=True),
            lax.all_gather(biases[layer_index], ("seq", "row"), axis=0, tiled=True),
            lax.all_gather(colbert, ("seq", "row"), axis=0, tiled=True),
        )
        gathered.append(full)
        (
            layer_w_in,
            layer_w_out,
            layer_w_up,
            layer_w_down,
            layer_hidden_units,
            layer_gain_one,
            layer_gain_two,
            layer_bias_in,
            layer_bias_out,
            layer_bias_up,
            layer_bias_down,
            layer_shift_one,
            layer_shift_two,
        ) = unpack(full)
        layer_inputs_low = hidden.astype(jnp.bfloat16)
        mixed = (
            jnp.dot(layer_inputs_low, layer_w_in, preferred_element_type=jnp.float32)
            + layer_bias_in
        )
        layer_queries = rotate(mixed[:, :model_width], cos_table, sin_table).astype(jnp.bfloat16)
        layer_keys = rotate(mixed[:, model_width : 2 * model_width], cos_table, sin_table).astype(
            jnp.bfloat16
        )
        layer_values = mixed[:, 2 * model_width :].astype(jnp.bfloat16)
        attend_query_three = layer_queries.reshape(local_len, HEADS, head_dim)
        attend_initial = (
            jnp.full((HEADS, local_len), NEG_FILL, jnp.float32),
            jnp.zeros((HEADS, local_len), jnp.float32),
            jnp.zeros((local_len, HEADS, head_dim), jnp.float32),
        )
        absorb_carry = attend_initial
        absorb_count, absorb_blocks, absorb_key_blocks, absorb_value_blocks, absorb_seg_blocks = (
            split_pieces(
                lax.all_gather(layer_keys, "seq", axis=0, tiled=True),
                lax.all_gather(layer_values, "seq", axis=0, tiled=True),
            )
        )

        def absorb_advance(state, item):
            run_max, run_sum, accum = state
            key_blk, value_blk, seg_blk = item
            scores = (
                jnp.einsum(
                    "qhd,khd->hqk", attend_query_three, key_blk, preferred_element_type=jnp.float32
                )
                * scale
            )
            allowed = (segment[:, None] == seg_blk[None, :])[None]
            scores = jnp.where(allowed, scores, NEG_FILL)
            new_max = jnp.maximum(run_max, jnp.max(scores, axis=-1))
            weights = jnp.where(allowed, jnp.exp(scores - new_max[..., None]), 0.0)
            factor = jnp.exp(run_max - new_max)
            run_sum = run_sum * factor + jnp.sum(weights, axis=-1)
            accum = accum * factor.T[:, :, None] + jnp.einsum(
                "hqk,khd->qhd",
                weights.astype(jnp.bfloat16),
                value_blk,
                preferred_element_type=jnp.float32,
            )
            return ((new_max, run_sum, accum), None)

        absorb_carry, absorb_unused = lax.scan(
            absorb_advance,
            absorb_carry,
            (absorb_key_blocks, absorb_value_blocks, absorb_seg_blocks),
        )
        run_max, run_sum, accum = absorb_carry
        attend_context = (accum / run_sum.T[:, :, None]).reshape(local_len, model_width)
        attend_log_total = run_max + jnp.log(run_sum)
        layer_context_low = attend_context.astype(jnp.bfloat16)
        layer_first = (
            hidden
            + jnp.dot(layer_context_low, layer_w_out, preferred_element_type=jnp.float32)
            + layer_bias_out
        )
        layer_normed = layer_norm(layer_first, layer_gain_one, layer_shift_one)
        layer_normed_low = layer_normed.astype(jnp.bfloat16)
        layer_pre_act = (
            jnp.dot(layer_normed_low, layer_w_up, preferred_element_type=jnp.float32)
            + layer_bias_up
        )
        layer_act_low = exact_gelu(layer_pre_act).astype(jnp.bfloat16)
        layer_second = (
            layer_normed
            + jnp.dot(layer_act_low, layer_w_down, preferred_element_type=jnp.float32)
            + layer_bias_down
        )
        output = layer_norm(layer_second, layer_gain_two, layer_shift_two)
        layer_record = (
            layer_inputs_low,
            layer_queries,
            layer_keys,
            layer_values,
            attend_context,
            layer_context_low,
            attend_log_total,
            layer_first,
            layer_normed,
            layer_normed_low,
            layer_pre_act,
            layer_act_low,
            layer_second,
        )
        hidden = output
        record = layer_record
        records.append(record)
    w_col = gathered[layer_count - 1][6]
    final_low = hidden.astype(jnp.bfloat16)
    col = jnp.dot(final_low, w_col, preferred_element_type=jnp.float32)
    full_width = w_col.shape[1]
    part_widths = (full_width, full_width * 3 // 4, full_width // 2)
    query_total = NQ * QLEN
    doc_total = NSD + 1
    selector = (is_query == 1)[None, :] & (
        query_slot[None, :] == jnp.arange(query_total, dtype=jnp.int32)[:, None]
    )
    selector_low = selector.astype(jnp.bfloat16)
    embeds = [unit_rows(col[:, :part_width]).astype(jnp.bfloat16) for part_width in part_widths]
    picked = (
        lax.psum(
            jnp.dot(selector_low, embeds[0], preferred_element_type=jnp.float32).astype(
                jnp.bfloat16
            ),
            "seq",
        ).astype(jnp.float32),
        lax.psum(
            jnp.dot(selector_low, embeds[1], preferred_element_type=jnp.float32).astype(
                jnp.bfloat16
            ),
            "seq",
        ).astype(jnp.float32),
        lax.psum(
            jnp.dot(selector_low, embeds[2], preferred_element_type=jnp.float32).astype(
                jnp.bfloat16
            ),
            "seq",
        ).astype(jnp.float32),
    )
    query_emb = [item.astype(jnp.bfloat16) for item in picked]
    sims = jnp.stack(
        [
            jnp.einsum(
                "qc,tc->qt", query_emb[part], embeds[part], preferred_element_type=jnp.float32
            )
            for part in range(3)
        ]
    )
    doc_mask = (
        (is_query == 0)[:, None]
        & (doc_num[:, None] == jnp.arange(doc_total, dtype=jnp.int32)[None, :])
    )[None, None]
    scaled = jnp.where(doc_mask, SHARPNESS * sims[..., None], NEG_FILL)
    part_max = jnp.max(scaled, axis=2)
    part_sum = jnp.sum(jnp.where(doc_mask, jnp.exp(scaled - part_max[:, :, None, :]), 0.0), axis=2)
    top, total = joined_2((part_max, part_sum), "seq", merge_pair)
    soft = (top + jnp.log(total)) / SHARPNESS
    pair_sum = jnp.sum(soft.reshape(3, NQ, QLEN, doc_total), axis=2)
    inverse_temp = jnp.exp(log_scale[0])
    logits = pair_sum * inverse_temp / QLEN
    positive = pairing[0][None, :, None] == jnp.arange(doc_total, dtype=jnp.int32)[None, None, :]
    losses = jax.nn.logsumexp(logits, axis=-1) - jnp.sum(jnp.where(positive, logits, 0.0), axis=-1)
    loss_weight = 1.0 / (3 * NQ * lax.axis_size("row"))
    grad_logits = loss_weight * (jax.nn.softmax(logits, axis=-1) - positive.astype(jnp.float32))
    loss_total, temp_grad = lax.psum(
        (jnp.sum(losses).reshape(1) * loss_weight, jnp.sum(grad_logits * logits).reshape(1)), "row"
    )
    grad_pairs = grad_logits * inverse_temp / QLEN
    grad_soft = jnp.broadcast_to(grad_pairs[:, :, None, :], (3, NQ, QLEN, doc_total)).reshape(
        3, query_total, doc_total
    )
    shares = jnp.where(doc_mask, jnp.exp(scaled - top[:, :, None, :]), 0.0) / total[:, :, None, :]
    grad_sims = jnp.sum(shares * grad_soft[:, :, None, :], axis=-1).astype(jnp.bfloat16)
    grad_query_emb = (
        lax.psum(
            jnp.dot(grad_sims[0], embeds[0], preferred_element_type=jnp.float32).astype(
                jnp.bfloat16
            ),
            "seq",
        ).astype(jnp.float32),
        lax.psum(
            jnp.dot(grad_sims[1], embeds[1], preferred_element_type=jnp.float32).astype(
                jnp.bfloat16
            ),
            "seq",
        ).astype(jnp.float32),
        lax.psum(
            jnp.dot(grad_sims[2], embeds[2], preferred_element_type=jnp.float32).astype(
                jnp.bfloat16
            ),
            "seq",
        ).astype(jnp.float32),
    )
    selector_f = selector.astype(jnp.float32)
    grad_col = jnp.zeros((local_len, full_width), jnp.float32)
    for part in range(3):
        part_width = part_widths[part]
        grad_embed = jnp.einsum(
            "qt,qc->tc", grad_sims[part], query_emb[part], preferred_element_type=jnp.float32
        )
        grad_embed = grad_embed + jnp.einsum(
            "qt,qc->tc",
            selector_f,
            grad_query_emb[part],
            precision=HIGHEST,
            preferred_element_type=jnp.float32,
        )
        unused, pull_unit = jax.vjp(unit_rows, col[:, :part_width])
        grad_col = grad_col.at[:, :part_width].add(pull_unit(grad_embed)[0])
    grad_col_low = grad_col.astype(jnp.bfloat16)
    grad_w_col = matmul_left_t(final_low, grad_col_low)
    grad_hidden = cotangent[0].astype(jnp.float32) + matmul_right_t(grad_col_low, w_col)
    shard_lists = [[] for unused_slot in range(6)]
    col_share = None
    for layer_index in reversed(range(layer_count)):
        full = (
            lax.all_gather(attn_in[layer_index], ("seq", "row"), axis=0, tiled=True),
            lax.all_gather(attn_out[layer_index], ("seq", "row"), axis=0, tiled=True),
            lax.all_gather(ffn_up[layer_index], ("seq", "row"), axis=0, tiled=True),
            lax.all_gather(ffn_down[layer_index], ("seq", "row"), axis=0, tiled=True),
            lax.all_gather(norm_gains[layer_index], ("seq", "row"), axis=0, tiled=True),
            lax.all_gather(biases[layer_index], ("seq", "row"), axis=0, tiled=True),
            lax.all_gather(colbert, ("seq", "row"), axis=0, tiled=True),
        )
        grad_hidden, layer_grads = layer_backward(grad_hidden, full, records[layer_index])
        col_term = grad_w_col if layer_index == layer_count - 1 else jnp.zeros_like(grad_w_col)
        shares_out = (
            lax.psum_scatter(layer_grads[0], ("seq", "row"), scatter_dimension=0, tiled=True),
            lax.psum_scatter(layer_grads[1], ("seq", "row"), scatter_dimension=0, tiled=True),
            lax.psum_scatter(layer_grads[2], ("seq", "row"), scatter_dimension=0, tiled=True),
            lax.psum_scatter(layer_grads[3], ("seq", "row"), scatter_dimension=0, tiled=True),
            lax.psum_scatter(layer_grads[4], ("seq", "row"), scatter_dimension=0, tiled=True),
            lax.psum_scatter(layer_grads[5], ("seq", "row"), scatter_dimension=0, tiled=True),
            lax.psum_scatter(col_term, ("seq", "row"), scatter_dimension=0, tiled=True),
        )
        for slot in range(6):
            shard_lists[slot].insert(0, shares_out[slot])
        if layer_index == layer_count - 1:
            col_share = shares_out[6]
    stacked = [jnp.stack(items) for items in shard_lists]
    return (
        hidden.astype(jnp.bfloat16)[None],
        loss_total,
        grad_hidden[None],
        stacked[0],
        stacked[1],
        stacked[2],
        stacked[3],
        stacked[4],
        stacked[5],
        col_share,
        temp_grad,
    )


def solution(mesh):
    placed = (
        P("row", "seq", None),
        P(None, ("seq", "row"), None),
        P(None, ("seq", "row"), None),
        P(None, ("seq", "row"), None),
        P(None, ("seq", "row"), None),
        P(None, ("seq", "row")),
        P(None, ("seq", "row")),
        P(("seq", "row"), None),
        P(),
        P("row", "seq", None),
        P("row", None),
        P("row", None),
        P("row", None),
    )
    planes = mesh.shape["row"] == 4 and mesh.shape["seq"] * 4 == 4 * PLANE and HEADS == 2 * PLANE
    return jax.shard_map(
        body if planes else body_wide,
        mesh=mesh,
        in_specs=placed,
        out_specs=(
            P("row", "seq", None),
            P(),
            P("row", "seq", None),
            P(None, ("seq", "row"), None),
            P(None, ("seq", "row"), None),
            P(None, ("seq", "row"), None),
            P(None, ("seq", "row"), None),
            P(None, ("seq", "row")),
            P(None, ("seq", "row")),
            P(("seq", "row"), None),
            P(),
        ),
        check_vma=False,
    )
```

```python
import math

import jax
import jax.numpy as jnp
from jax import lax
from jax.experimental import pallas as pl
from jax.experimental.pallas import tpu as pltpu
from jax.sharding import PartitionSpec as P

HEADS = 16
QLEN = 32
NQ = 4
NSD = 3

NEG_FILL = -1e30
SHARPNESS = 16.0
HIGHEST = lax.Precision.HIGHEST
BF = jnp.bfloat16
F32 = jnp.float32

def dot(left, right):
    return jnp.dot(left, right, preferred_element_type=F32)


def dot_lt(left, right):
    return lax.dot_general(left, right, (((0,), (0,)), ((), ())), preferred_element_type=F32)


def dot_rt(left, right):
    return lax.dot_general(left, right, (((1,), (1,)), ((), ())), preferred_element_type=F32)


PLANE = 8
BOTH = ("seq", "row")


def across(x, mask):
    size = lax.axis_size("seq") * lax.axis_size("row")
    return lax.ppermute(x, BOTH, [(d, d ^ mask) for d in range(size)])


def turned(x, back=False):
    size = lax.axis_size("seq") * lax.axis_size("row")
    pairs = []
    for d in range(size):
        z, y, column, core = d // PLANE, d // 4 % 2, d // 2 % 2, d % 2
        to = (2 * core + column) * PLANE + 4 * y + 2 * (column ^ (z // 2)) + z % 2
        pairs.append((to, d) if back else (d, to))
    return lax.ppermute(x, BOTH, pairs)


def plane_gather(x):
    blocks = [x, None, across(x, 2), None, across(x, 4), None, across(x, 6), None]
    for k in range(0, PLANE, 2):
        blocks[k + 1] = across(blocks[k], 1)
    return blocks


def plane_scatter(even, odd, beside=None, first=False):
    core = across(odd, 1)
    if first:
        core, beside = tie(core, beside)
    parts = core_add(even, core)
    got = [across(parts[j], 2 * j) for j in (1, 2, 3)]
    if beside is not None and not first:
        got, beside = tie(got, beside)
    return [parts[0]] + got, beside


def plane_sum(parts):
    parts = parts.astype(BF)
    core = across(parts[1::2], 1).astype(F32) + parts[0::2].astype(F32)
    sent = core[1:].astype(BF)
    return core[0] + sum(across(sent[k - 1], 2 * k).astype(F32) for k in (1, 2, 3))


def plane_exchange(x, relative, before=None):
    x = pick(x, relative)
    core = across(x[1::2], 1)
    if before is not None:
        core, before = tie(core, before)
    got = tie(*[across(jnp.stack([x[2 * k], core[k]]), 2 * k) for k in (1, 2, 3)])
    x = pick(jnp.concatenate([x[:1], core[:1], *got]), relative)
    return x if before is None else (x, before)


def pick(x, index, axis=0):
    return x.at[(slice(None),) * axis + (index,)].get(mode="promise_in_bounds")


def tie(*values):
    return lax.optimization_barrier(values)


def token_info(positions, lengths, kinds):
    ends = jnp.cumsum(lengths)
    starts = ends - lengths
    query_count = jnp.cumsum(kinds) - kinds
    doc_count = jnp.cumsum(1 - kinds) - (1 - kinds)
    segment = jnp.sum((positions[:, None] >= ends[None, :]).astype(jnp.int32), axis=1)
    onehot = segment[:, None] == jnp.arange(lengths.shape[0], dtype=jnp.int32)[None, :]
    nothing = jnp.zeros((), jnp.int32)
    seg_start = jnp.sum(jnp.where(onehot, starts[None, :], nothing), axis=1)
    is_query = jnp.sum(jnp.where(onehot, kinds[None, :], nothing), axis=1)
    query_num = jnp.sum(jnp.where(onehot, query_count[None, :], nothing), axis=1)
    doc_num = jnp.sum(jnp.where(onehot, doc_count[None, :], nothing), axis=1)
    offset = positions - seg_start
    return (segment, offset, is_query, query_num * QLEN + offset, doc_num)


def rope_angles(offset, head_dim):
    half = head_dim // 2
    inverse = jnp.exp(jnp.arange(half, dtype=F32) * (-2.0 * math.log(10000.0) / head_dim))
    angle = offset.astype(F32)[:, None] * inverse[None, :]
    return jnp.cos(angle), jnp.sin(angle)


def layer_norm(rows, gain, shift):
    center = rows - jnp.mean(rows, axis=-1, keepdims=True)
    variance = jnp.mean(center * center, axis=-1, keepdims=True)
    return center * lax.rsqrt(variance + 1e-05) * gain + shift


def unit_rows(rows):
    return rows * lax.rsqrt(jnp.sum(rows * rows, axis=-1, keepdims=True) + 1e-06)


def exact_gelu(values):
    return jax.nn.gelu(values, approximate=False)


def head_masks(width):
    lane = lax.broadcasted_iota(jnp.int32, (1, width), 1)
    first_qk = (lane % (width // 2)) < (width // 4)
    first_v = lane < (width // 2)
    return first_qk, first_v


BIG, SMALL = 62, 16

IN_VMEM = pl.BlockSpec(memory_space=pltpu.VMEM)
IN_HBM = pl.BlockSpec(memory_space=pltpu.HBM)


def near(x):
    return (x, "near")


def held(x):
    return (x, "held")


def raw(x):
    return (x, "raw")


def call(kernel, ins, outs, scratch, flops, limit=BIG, light=True):
    arrays = [a for a, _ in ins]
    kept = [i for i, (_, kind) in enumerate(ins) if kind == "held"]
    left = [i for i, out in enumerate(outs) if len(out) == 3]
    pieces = [1 if outs[i][2] is True else outs[i][2] for i in left]
    moved = sum(a.size * a.dtype.itemsize for a in arrays)
    moved += sum(math.prod(out[0]) * jnp.dtype(out[1]).itemsize for out in outs)

    def wrapped(*refs):
        in_refs = list(refs[: len(ins)])
        out_refs = list(refs[len(ins) : len(ins) + len(outs)])
        rest = refs[len(ins) + len(outs) :]
        own, rest = rest[: len(scratch)], rest[len(scratch) :]
        in_bufs, out_bufs = rest[: len(kept)], rest[len(kept) : len(kept) + len(left)]
        sems = rest[len(kept) + len(left)] if kept or left else None
        pending = {}
        for k, i in enumerate(kept):
            pending[i] = pltpu.make_async_copy(in_refs[i], in_bufs[k], sems.at[k])
            pending[i].start()

        def getter(i, buf):
            def get():
                if i in pending:
                    pending.pop(i).wait()
                return buf

            return get

        for k, i in enumerate(kept):
            in_refs[i] = getter(i, in_bufs[k])
        leaving = {}

        def flusher(i, k, target):
            def flush(j=0):
                buf = out_bufs[k]
                if pieces[k] > 1:
                    buf, target_j = buf.at[j], target.at[j]
                else:
                    target_j = target
                leaving[i, j] = pltpu.make_async_copy(buf, target_j, sems.at[len(kept) + sum(pieces[:k]) + j])
                leaving[i, j].start()

            return flush

        for k, i in enumerate(left):
            out_refs[i] = (out_bufs[k], flusher(i, k, out_refs[i]))
        kernel(in_refs, out_refs, own)
        assert not pending and len(leaving) == sum(pieces)
        for copy in leaving.values():
            copy.wait()

    buffers = [pltpu.VMEM(*item) if isinstance(item, tuple) else item for item in scratch]
    buffers += [pltpu.VMEM(arrays[i].shape, arrays[i].dtype) for i in kept]
    buffers += [pltpu.VMEM(*outs[i][:2]) for i in left]
    if kept or left:
        buffers.append(pltpu.SemaphoreType.DMA((len(kept) + sum(pieces),)))
    return pl.pallas_call(
        wrapped,
        in_specs=[IN_VMEM if kind == "near" else IN_HBM for _, kind in ins],
        out_specs=tuple(IN_HBM if len(out) == 3 else IN_VMEM for out in outs),
        out_shape=tuple(jax.ShapeDtypeStruct(out[0], out[1]) for out in outs),
        scratch_shapes=buffers,
        compiler_params=pltpu.CompilerParams(vmem_limit_bytes=limit * 1024 * 1024),
        cost_estimate=pl.CostEstimate(flops=1 if light else flops, bytes_accessed=1 if light else moved, transcendentals=0),
    )(*arrays)


def core_add(even, got):
    count, T, D = even.shape

    def kernel(ins, outs, _):
        for j in range(count):
            outs[j][...] = (ins[0][j].astype(F32) + ins[1][j].astype(F32)).astype(outs[j].dtype)

    outs = [((T, D), F32)] + [((T, D), BF)] * (count - 1)
    return call(kernel, [near(even), near(got)], outs, [], even.size, SMALL)


def add_norm(parts, params, bias_at, gain_at, shift_at):
    T, D = parts[0].shape

    def kernel(ins, outs, _):
        params = ins[-1]
        (total, leave), normed, low = outs
        rows = params[:, bias_at : bias_at + D]
        for ref in ins[:-1]:
            rows = rows + ref[...].astype(F32)
        total[...] = rows
        leave()
        result = layer_norm(rows, params[:, gain_at : gain_at + D], params[:, shift_at : shift_at + D])
        normed[...] = result
        low[...] = result.astype(BF)

    outs = [((T, D), F32, True), ((T, D), F32), ((T, D), BF)]
    return call(kernel, [near(item) for item in (*parts, params)], outs, [], 10 * T * D, SMALL)


def norm_back(parts, rows, params, gain_at):
    T, D = rows.shape

    def kernel(ins, outs, _):
        rows, params = ins[-2:]
        wide_out, low_out, sums = outs
        grad = ins[0][...].astype(F32)
        for ref in ins[1:-2]:
            grad = grad + ref[...].astype(F32)
        rows = rows()[...]
        center = rows - jnp.mean(rows, axis=-1, keepdims=True)
        inverse = lax.rsqrt(jnp.mean(center * center, axis=-1, keepdims=True) + 1e-05)
        unit = center * inverse
        sums[:, :D] = jnp.sum(grad * unit, axis=0, keepdims=True)
        sums[:, D : 2 * D] = jnp.sum(grad, axis=0, keepdims=True)
        grad = grad * params[:, gain_at : gain_at + D]
        along = jnp.mean(grad * unit, axis=-1, keepdims=True)
        grad = inverse * (grad - jnp.mean(grad, axis=-1, keepdims=True) - unit * along)
        wide_out[...] = grad
        low = grad.astype(BF)
        low_out[...] = low
        sums[:, 2 * D :] = jnp.sum(low.astype(F32), axis=0, keepdims=True)

    outs = [((T, D), F32), ((T, D), BF), ((1, 3 * D), F32)]
    return call(kernel, [near(item) for item in parts] + [held(rows), near(params)], outs, [], 20 * T * D, SMALL)


def roll_halves(x):
    return pltpu.roll(x, x.shape[1] // 2, 1)


def load_attn(full, w_in, w_out):
    far = full.shape[0]
    D, cols = w_in.shape
    rows, wide = D // far, w_out.shape[0]
    part = wide // far
    for o in range(far):
        w_in[o * rows : (o + 1) * rows] = full[o, :rows, :cols]
        for j in range(rows // part):
            w_out[o * part : (o + 1) * part, j * wide : (j + 1) * wide] = full[o, j * part : (j + 1) * part, cols:]


def load_ffn(full, w_up, w_down):
    far = full.shape[0]
    D, H = w_up.shape
    up, down = D // far, H // far
    for o in range(far):
        w_up[o * up : o * up + up // 2] = full[o, : up // 2, :H]
        w_up[o * up + up // 2 : (o + 1) * up] = full[o, : up // 2, H:]
        w_down[o * down : (o + 1) * down] = full[o, up // 2 : up // 2 + down]


def rotary(table, rows, half):
    cos, sin = table[rows, :half], table[rows, half : 2 * half]
    return jnp.concatenate([cos, cos, cos, cos], axis=1), jnp.concatenate([-sin, -sin, sin, sin], axis=1)


def attn_forward(blocks, full, bias, bias_at, table, seg_row, half, scale):
    n = len(blocks)
    T, D = blocks[0].shape
    wide = 4 * half
    N = n * T
    step = 4
    across_block = N

    def kernel(ins, outs, scratch):
        full, table, bias, seg_row = ins[n:]
        (qkv, leave_qkv), (context, leave_context), (logs, leave_logs), even, odd = outs
        w_in, w_out, x, values_t, context_t, x_sems = scratch
        copies = block_copies(ins[:n], x, x_sems)
        start_all(copies)
        load_attn(full(), w_in, w_out)
        table = table()
        for k in range(0, n, step):
            wait_all(copies[k : k + step])
            rows = slice(k * T, (k + step) * T)
            mixed = dot(x[rows], w_in[...]) + bias[:, bias_at : bias_at + 3 * wide]
            cos, sin = rotary(table, rows, half)
            for t, factor in ((0, scale), (1, 1.0)):
                part = mixed[:, t * wide : (t + 1) * wide]
                part = (part * cos + roll_halves(part) * sin).astype(BF)
                qkv[rows, t * wide : (t + 1) * wide] = part * jnp.asarray(factor, BF)
            qkv[rows, 2 * wide :] = mixed[:, 2 * wide :].astype(BF)
        leave_qkv()
        values_t[...] = qkv[:, 2 * wide :].T
        first_qk, _ = head_masks(wide)
        zero = jnp.zeros((), BF)

        def part(c, carry):
            at = pl.ds(pl.multiple_of(c * across_block, 128), across_block)
            allowed = table[:, 2 * half : 2 * half + 1] == seg_row[:, at]
            for head in range(2):
                mine = first_qk if head == 0 else jnp.logical_not(first_qk)
                query = jnp.where(mine, qkv[at, :wide], zero)
                scores = jnp.where(allowed, dot_rt(qkv[:, wide : 2 * wide], query), NEG_FILL)
                top = jnp.max(scores, axis=0, keepdims=True)
                weights = jnp.exp(scores - top)
                total = jnp.sum(weights, axis=0, keepdims=True)
                heads = slice(head * 2 * half, (head + 1) * 2 * half)
                context_t[heads, at] = dot(values_t[heads, :], weights.astype(BF)) * (1.0 / total)
                logs[head : head + 1, at] = top + jnp.log(total)
            return carry

        lax.fori_loop(0, N // across_block, part, 0)
        leave_logs()
        context[...] = context_t[...].T.astype(BF)
        leave_context()
        for k in range(0, n, step):
            put_blocks(dot(context[k * T : (k + step) * T], w_out[...]).astype(BF), k, (even, odd), T)

    outs = [((N, 3 * wide), BF, True), ((N, wide), BF, True), ((2, N), F32, True)]
    outs += [((n // 2, T, D), BF, n // 2), ((n // 2, T, D), BF, n // 2)]
    flops = 2 * N * D * 4 * wide + 8 * N * N * wide
    sems = pltpu.SemaphoreType.DMA
    scratch = [((D, 3 * wide), BF), ((wide, D), BF), ((N, D), BF), ((wide, N), BF), ((wide, N), F32), sems((n,))]
    ins = [raw(item) for item in blocks] + [held(full), held(table), near(bias), near(seg_row)]
    return call(kernel, ins, outs, scratch, flops)


def lanes_of(count):
    return max(w for w in (384, 256, 128) if count % w == 0)


def fetch_ffn(full, w_up, w_down, sems):
    far = full.shape[0]
    D, H = w_up.shape
    up, down = D // far, H // far
    first, second = [], []
    for o in range(far):
        for part in range(2):
            first.append(
                pltpu.make_async_copy(
                    full.at[o, pl.ds(0, up // 2), pl.ds(part * H, H)],
                    w_up.at[pl.ds(o * up + part * (up // 2), up // 2)],
                    sems.at[3 * o + part],
                )
            )
        second.append(
            pltpu.make_async_copy(
                full.at[o, pl.ds(up // 2, down)], w_down.at[pl.ds(o * down, down)], sems.at[3 * o + 2]
            )
        )
    return first, second


def start_all(copies):
    for copy in copies:
        copy.start()


def wait_all(copies):
    for copy in copies:
        copy.wait()


def block_copies(blocks, whole, sems):
    T = blocks[0].shape[0]
    return [pltpu.make_async_copy(block, whole.at[pl.ds(k * T, T)], sems.at[k]) for k, block in enumerate(blocks)]


def ffn_forward(blocks, full, bias, bias_at, H):
    n = len(blocks)
    T, D = blocks[0].shape
    step = 4

    def kernel(ins, outs, scratch):
        full, bias = ins[n:]
        (act, leave_act), (slope, leave_slope), even, odd = outs
        w_up, w_down, x, w_sems, x_sems = scratch
        first, second = fetch_ffn(full, w_up, w_down, w_sems)
        copies = block_copies(ins[:n], x, x_sems)
        start_all(first)
        start_all(copies)
        start_all(second)
        wait_all(first)
        for k in range(0, n, step):
            wait_all(copies[k : k + step])
            rows = slice(k * T, (k + step) * T)
            pre = dot(x[rows], w_up[...]) + bias[:, bias_at : bias_at + H]
            below = 0.5 * (1.0 + lax.erf(pre * math.sqrt(0.5)))
            result = (pre * below).astype(BF)
            act[rows] = result
            slope[rows] = (below + pre * (math.sqrt(0.5 / math.pi) * jnp.exp(-0.5 * pre * pre))).astype(BF)
            if k == 0:
                wait_all(second)
            back = dot(act[rows], w_down[...]).astype(BF)
            put_blocks(back, k, (even, odd), T)
        leave_act()
        leave_slope()

    outs = [((n * T, H), BF, True), ((n * T, H), BF, True), ((n // 2, T, D), BF, n // 2), ((n // 2, T, D), BF, n // 2)]
    ins = [raw(item) for item in blocks] + [raw(full), near(bias)]
    sems = pltpu.SemaphoreType.DMA
    scratch = [((D, H), BF), ((H, D), BF), ((n * T, D), BF), sems((3 * full.shape[0],)), sems((n,))]
    return call(kernel, ins, outs, scratch, 4 * n * T * D * H)


def put_blocks(rows, first, halves, T):
    for i in range(rows.shape[0] // T):
        out, leave = halves[(first + i) % 2]
        out[(first + i) // 2] = rows[i * T : (i + 1) * T]
        leave((first + i) // 2)


def ffn_back(blocks, full, slope):
    n = len(blocks)
    T, D = blocks[0].shape
    H = slope.shape[1]
    step = 4

    def kernel(ins, outs, scratch):
        full, slope = ins[n:]
        grad_pre, bias_grad, even, odd = outs
        w_up, w_down, x, w_sems, x_sems = scratch
        first, second = fetch_ffn(full, w_up, w_down, w_sems)
        copies = block_copies(ins[:n], x, x_sems)
        start_all(second)
        start_all(copies)
        start_all(first)
        wait_all(second)
        total = jnp.zeros((1, H), F32)
        for k in range(0, n, step):
            wait_all(copies[k : k + step])
            rows = slice(k * T, (k + step) * T)
            grad = (dot_rt(x[rows], w_down[...]) * slope()[rows].astype(F32)).astype(BF)
            grad_pre[rows] = grad
            total = total + jnp.sum(grad.astype(F32), axis=0, keepdims=True)
            if k == 0:
                wait_all(first)
            put_blocks(dot_rt(grad_pre[rows], w_up[...]).astype(BF), k, (even, odd), T)
        bias_grad[...] = total

    outs = [((n * T, H), BF), ((1, H), F32), ((n // 2, T, D), BF, n // 2), ((n // 2, T, D), BF, n // 2)]
    ins = [raw(item) for item in blocks] + [raw(full), held(slope)]
    sems = pltpu.SemaphoreType.DMA
    scratch = [((D, H), BF), ((H, D), BF), ((n * T, D), BF), sems((3 * full.shape[0],)), sems((n,))]
    return call(kernel, ins, outs, scratch, 4 * n * T * D * H)


def ffn_weights(normed, grads, act, grad_pre, far, extra):
    n = len(normed)
    T, D = normed[0].shape
    N = n * T
    H = act.shape[1]
    up, down = D // far, H // far
    more = [] if extra is None else [near(extra)]
    count = up // 2 + down + (0 if extra is None else extra.shape[1])

    def kernel(ins, outs, scratch):
        act, grad_pre = ins[2 * n : 2 * n + 2]
        left, right, left_sems, right_sems = scratch
        out = outs[0]
        copies = block_copies(ins[:n], left, left_sems)
        later = block_copies(ins[n : 2 * n], right, right_sems)
        start_all(copies)
        start_all(later)
        wait_all(copies)
        for o in range(far):
            block = dot_lt(left[:, o * up : (o + 1) * up], grad_pre[...]).astype(BF)
            out[o, : up // 2, :H] = block[: up // 2]
            out[o, : up // 2, H:] = block[up // 2 :]
        wait_all(later)
        act = act()
        for o in range(far):
            block = dot_lt(act[:, o * down : (o + 1) * down], right[...]).astype(BF)
            out[o, up // 2 : up // 2 + down] = block
            if more:
                out[o, up // 2 + down :] = ins[2 * n + 2][o]

    sems = pltpu.SemaphoreType.DMA
    scratch = [((N, D), BF), ((N, D), BF), sems((n,)), sems((n,))]
    ins = [raw(item) for item in (*normed, *grads)] + [held(act), near(grad_pre)] + more
    return call(kernel, ins, [((far, count, D), BF)], scratch, 4 * N * D * H, light=False)[0]


def attn_back(blocks, full, qkv, context, logs, table, seg_row, half, scale):
    n = len(blocks)
    T, D = blocks[0].shape
    wide = 4 * half
    N = n * T
    step = 4
    across_block = lanes_of(N)

    def kernel(ins, outs, scratch):
        full, table, qkv, context, logs, seg_row = ins[n:]
        mixed, bias_grad, even, odd = outs
        w_in, w_out, x, grad, delta, cos, sin, acc_k, acc_v, x_sems = scratch
        copies = block_copies(ins[:n], x, x_sems)
        start_all(copies)
        load_attn(full(), w_in, w_out)
        for k in range(0, n, step):
            wait_all(copies[k : k + step])
            rows = slice(k * T, (k + step) * T)
            grad[rows] = dot_rt(x[rows], w_out[...]).astype(BF)
        table = table()
        cos[...], sin[...] = rotary(table, slice(None), half)
        acc_k[...] = jnp.zeros_like(acc_k)
        acc_v[...] = jnp.zeros_like(acc_v)
        qkv, logs = qkv(), logs()
        product = (grad[...].astype(F32) * context()[...].astype(F32)).T
        delta[0:1] = jnp.sum(product[: 2 * half], axis=0, keepdims=True)
        delta[1:2] = jnp.sum(product[2 * half :], axis=0, keepdims=True)
        first_qk, first_v = head_masks(wide)
        zero = jnp.zeros((), BF)

        def part(c, carry):
            at = pl.ds(pl.multiple_of(c * across_block, 128), across_block)
            allowed = table[:, 2 * half : 2 * half + 1] == seg_row[:, at]
            grad_query = []
            for head in range(2):
                mine = first_qk if head == 0 else jnp.logical_not(first_qk)
                mine_v = first_v if head == 0 else jnp.logical_not(first_v)
                query = jnp.where(mine, qkv[at, :wide], zero)
                grad_h = jnp.where(mine_v, grad[at, :], zero)
                scores = dot_rt(qkv[:, wide : 2 * wide], query) - logs[head : head + 1, at]
                probs = jnp.exp(jnp.where(allowed, scores, NEG_FILL))
                grad_probs = dot_rt(qkv[:, 2 * wide :], grad_h)
                grad_scores = (probs * (grad_probs - delta[head : head + 1, at])).astype(BF)
                acc_k[...] += dot(grad_scores, query)
                acc_v[...] += dot(probs.astype(BF), grad_h)
                grad_query.append(dot_lt(grad_scores, qkv[:, wide : 2 * wide]))
            result = jnp.where(first_qk, grad_query[0], grad_query[1]) * scale
            mixed[at, :wide] = (result * cos[at, :] - roll_halves(result) * sin[at, :]).astype(BF)
            return carry

        lax.fori_loop(0, N // across_block, part, 0)
        total = acc_k[...]
        mixed[:, wide : 2 * wide] = (total * cos[...] - roll_halves(total) * sin[...]).astype(BF)
        mixed[:, 2 * wide :] = acc_v[...].astype(BF)
        sums = jnp.zeros((1, 3 * wide), F32)
        for k in range(0, n, step):
            rows = slice(k * T, (k + step) * T)
            sums = sums + jnp.sum(mixed[rows].astype(F32), axis=0, keepdims=True)
            put_blocks(dot_rt(mixed[rows], w_in[...]).astype(BF), k, (even, odd), T)
        bias_grad[...] = sums

    outs = [((N, 3 * wide), BF), ((1, 3 * wide), F32), ((n // 2, T, D), BF, n // 2), ((n // 2, T, D), BF, n // 2)]
    scratch = [((D, 3 * wide), BF), ((wide, D), BF), ((N, D), BF), ((N, wide), BF), ((2, N), F32)]
    scratch += [((N, wide), F32)] * 4 + [pltpu.SemaphoreType.DMA((n,))]
    flops = 2 * N * D * 4 * wide + 20 * N * N * wide
    ins = [raw(item) for item in blocks] + [held(item) for item in (full, table, qkv, context, logs)] + [near(seg_row)]
    return call(kernel, ins, outs, scratch, flops)


def attn_weights(inputs, grads, context, mixed, bias_grad, far, relative):
    n = len(inputs)
    T, D = inputs[0].shape
    N = n * T
    wide = context.shape[1]
    rows = D // far
    part = wide // far
    size = lax.axis_size("row")

    def kernel(ins, outs, scratch):
        context, mixed, bias_grad = ins[2 * n :]
        left, right, left_sems, right_sems = scratch
        here = (lax.axis_index("seq") * size + lax.axis_index("row")) // PLANE
        copies = block_copies(ins[:n], left, left_sems)
        later = block_copies(ins[n : 2 * n], right, right_sems)
        start_all(copies)
        start_all(later)
        wait_all(copies)
        for k in range(far):
            if relative:
                lanes = pl.ds(pl.multiple_of((here ^ k) * rows, 128), rows)
                outs[k][:rows, : 3 * wide] = dot_lt(left[:, lanes], mixed[...]).astype(BF)
            else:
                outs[0][k, :rows, : 3 * wide] = dot_lt(left[:, k * rows : (k + 1) * rows], mixed[...]).astype(BF)
        wait_all(later)
        whole = dot_lt(context()[...], right[...]).astype(BF)
        extra = jnp.broadcast_to(bias_grad[...], (16, 3 * wide)).astype(BF)
        if relative:
            right[:wide, :D] = whole
        for k in range(far):
            out = outs[k] if relative else outs[0].at[k]
            if relative:
                block = right[pl.ds(pl.multiple_of((here ^ k) * part, 16), part), :]
            else:
                block = whole[k * part : (k + 1) * part]
            for j in range(rows // part):
                out[j * part : (j + 1) * part, 3 * wide :] = block[:, j * wide : (j + 1) * wide]
            out[rows:, : 3 * wide] = extra
            out[rows:, 3 * wide :] = jnp.zeros((16, wide), BF)

    sems = pltpu.SemaphoreType.DMA
    scratch = [((N, D), BF), ((N, D), BF), sems((n,)), sems((n,))]
    ins = [raw(item) for item in (*inputs, *grads)] + [held(context), near(mixed), near(bias_grad)]
    if relative:
        outs = [((rows + 16, 4 * wide), BF)] * far
    else:
        outs = [((far, rows + 16, 4 * wide), BF)]
    return call(kernel, ins, outs, scratch, 8 * N * D * wide, light=False)


def plane_index():
    return lax.axis_index("seq") % (PLANE // lax.axis_size("row")) * lax.axis_size("row") + lax.axis_index("row")


def head_kernel(blocks, own, codes, own_codes, positive, temp, w_col, loss_weight):
    n = len(blocks)
    T, C = own.shape
    N = n * T
    D = w_col.shape[0]
    slots = NQ * QLEN

    def kernel(ins, outs, scratch):
        own, codes, own_codes, positive, temp, w_col = ins[n:]
        grad, low, terms = outs
        held, embeds = scratch
        here = plane_index()
        upper = lax.rem(lax.axis_index("seq") // (PLANE // lax.axis_size("row")), 2)

        def place(c):
            column = lax.rem(c // 2, 2) ^ upper
            return pl.ds(pl.multiple_of((4 * column + 2 * lax.rem(c, 2) + c // 4) * T, 16), T)

        for k in range(n):
            held[place(here ^ k), :] = ins[k][...]
        lane = lax.broadcasted_iota(jnp.int32, (1, C), 1)
        slot = lax.broadcasted_iota(jnp.int32, (slots, 1), 0)
        doc, own_doc = codes[0:1, :], own_codes[0:1, :]
        select = jnp.where(codes[1:2, :] == slot, 1.0, 0.0).astype(BF)
        own_select = jnp.where(own_codes[1:2, :] == slot, 1.0, 0.0).astype(BF)
        rows = held[...].astype(F32)
        mine = own[...]
        heat = temp[...]
        wanted = lane == positive[...]
        valid = lane <= NSD
        loss = jnp.zeros((1, 1), F32)
        heat_grad = jnp.zeros((1, 1), F32)
        total = jnp.zeros((T, C), F32)
        for width in (C, C * 3 // 4, C // 2):
            inside = lane < width
            size = jnp.sum(jnp.where(inside, rows * rows, 0.0), axis=1, keepdims=True)
            embed = jnp.where(inside, rows * lax.rsqrt(size + 1e-06), 0.0).astype(BF)
            embeds[...] = embed
            query = dot(select, embed).astype(BF)
            powers = jnp.exp(SHARPNESS * dot_rt(query, embed))
            soft = jnp.zeros((slots, C), F32)
            sums = []
            for d in range(NSD + 1):
                sums.append(jnp.sum(jnp.where(doc == d, powers, 0.0), axis=1, keepdims=True))
                soft = jnp.where(lane == d, jnp.log(sums[d]) / SHARPNESS, soft)
            pair = jnp.sum(soft.reshape(NQ, QLEN, C), axis=1, keepdims=True)
            pair = jnp.broadcast_to(pair, (NQ, QLEN, C)).reshape(slots, C)
            logits = pair * heat / QLEN
            masked = jnp.where(valid, logits, NEG_FILL)
            top = jnp.max(masked, axis=1, keepdims=True)
            shares = jnp.exp(masked - top)
            share_sum = jnp.sum(shares, axis=1, keepdims=True)
            chosen = jnp.sum(jnp.where(wanted, logits, 0.0), axis=1, keepdims=True)
            losses = top + jnp.log(share_sum) - chosen
            loss = loss + jnp.sum(losses, axis=0, keepdims=True) * (loss_weight / QLEN)
            grad_logits = loss_weight * (shares / share_sum - jnp.where(wanted, 1.0, 0.0))
            along = jnp.sum(jnp.where(valid, grad_logits * logits, 0.0), axis=1, keepdims=True)
            heat_grad = heat_grad + jnp.sum(along, axis=0, keepdims=True) / QLEN
            grad_soft = grad_logits * heat / QLEN
            weight = jnp.zeros((slots, N), F32)
            own_weight = jnp.zeros((slots, T), F32)
            for d in range(NSD + 1):
                ratio = grad_soft[:, d : d + 1] / sums[d]
                weight = jnp.where(doc == d, ratio, weight)
                own_weight = jnp.where(own_doc == d, ratio, own_weight)
            grad_query = dot((powers * weight).astype(BF), embed)
            own_embed = embeds[place(here), :]
            own_powers = jnp.exp(SHARPNESS * dot_rt(query, own_embed))
            grad_embed = dot_lt((own_powers * own_weight).astype(BF), query)
            high = grad_query.astype(BF)
            rest = (grad_query - high.astype(F32)).astype(BF)
            grad_embed = grad_embed + dot_lt(own_select, high) + dot_lt(own_select, rest)
            size = jnp.sum(jnp.where(inside, mine * mine, 0.0), axis=1, keepdims=True)
            inverse = lax.rsqrt(size + 1e-06)
            along = jnp.sum(jnp.where(inside, grad_embed * mine, 0.0), axis=1, keepdims=True)
            part = inverse * grad_embed - mine * (inverse * inverse * inverse * along)
            total = total + jnp.where(inside, part, 0.0)
        low[...] = total.astype(BF)
        grad[...] = dot_rt(total.astype(BF), w_col[...])
        terms[...] = jnp.where(lane == 0, loss, jnp.where(lane == 1, heat_grad, 0.0))

    outs = [((T, D), F32), ((T, C), BF), ((1, C), F32)]
    ins = [near(item) for item in (*blocks, own, codes, own_codes, positive, temp, w_col)]
    return call(kernel, ins, outs, [((N, C), BF), ((N, C), BF)], 24 * slots * N * C, 40)


def swap_quarters(x):
    q = x.shape[1] // 4
    return jnp.concatenate([x[:, :q], x[:, 2 * q : 3 * q], x[:, q : 2 * q], x[:, 3 * q :]], axis=1)


def pack_first(w, small):
    rows, width = w.shape
    D, wide = width // 3, width // 3 // PLANE
    count = rows + small.shape[0]

    def kernel(ins, outs, _):
        w, small = ins
        here = plane_index()
        for k in range(PLANE):
            out = outs[k % 2].at[k // 2]
            for t in range(3):
                columns = w[:, pl.ds(pl.multiple_of(t * D + (here ^ k) * wide, 128), wide)]
                out[:rows, t * wide : (t + 1) * wide] = swap_quarters(columns) if t < 2 else columns
            out[rows:] = small[...]

    outs = [((PLANE // 2, count, 3 * wide), BF)] * 2
    return call(kernel, [near(w), near(small)], outs, [], w.size, SMALL)


def unpack_first(even, core, got, out_rows):
    rows, D = out_rows.shape
    count, cols = even.shape[1:]
    wide = cols // 3

    def kernel(ins, outs, _):
        even, core, *got, out_rows = ins
        block, below = outs
        here = plane_index()
        blocks = [even.at[0], core.at[0]] + [ref.at[j] for ref in got for j in range(2)]
        for k in range(PLANE):
            of = here ^ k
            block[pl.ds(pl.multiple_of(of * rows, 16), rows), :cols] = blocks[k][:rows]
            below[of] = blocks[k][rows:]
            block[k * rows : (k + 1) * rows, cols:] = out_rows[:, k * wide : (k + 1) * wide]

    outs = [((PLANE * rows, cols + wide), BF), ((PLANE, count - rows, cols), BF)]
    return call(kernel, [near(item) for item in (even, core, *got, out_rows)], outs, [], even.size, SMALL)


def pack_shares(sums, others, ffn, lines, in_cols, hidden_cols):
    rows, width = sums[0].shape[0] - 16, sums[0].shape[1]
    part = rows // PLANE
    L = len(ffn)
    count = L * (in_cols + hidden_cols) + 128
    bias_lines = in_cols // 128
    first_line = part - L * bias_lines

    def kernel(ins, outs, scratch):
        even, odd, last = outs
        attn = scratch[0]
        n = len(sums)
        total = ins[0][...].astype(F32)
        for ref in ins[1:n]:
            total = total + ref[...].astype(F32)
        attn[0] = total.astype(BF)
        for layer in range(1, L):
            attn[layer] = ins[n + layer - 1][...]
        last[...] = attn[0, :rows, in_cols:]
        ups = ins[n + L - 1 : n + 2 * L - 1]
        lines = ins[n + 2 * L - 1]
        here = plane_index()
        line = lax.broadcasted_iota(jnp.int32, (part, 128), 0)
        for k in range(PLANE):
            to = here ^ k
            out = (odd if k % 2 else even).at[k // 2]
            at = pl.ds(pl.multiple_of(to * part, 16), part)
            half = pl.ds(pl.multiple_of(lax.rem(to, PLANE // 2) * part, 16), part)
            for layer in range(L):
                out[:, layer * in_cols : (layer + 1) * in_cols] = attn[layer, at, :in_cols]
                folded = ups[layer][half, :]
                own = jnp.where(to < PLANE // 2, folded[:, :hidden_cols], folded[:, hidden_cols:])
                start = L * in_cols + layer * hidden_cols
                out[:, start : start + hidden_cols] = own
            block = lines[to]
            for layer in range(L):
                bias = attn[layer, rows : rows + 16, :in_cols].astype(F32)[:1]
                for j in range(bias_lines):
                    spot = line == first_line + layer * bias_lines + j
                    block = jnp.where(spot, bias[:, j * 128 : (j + 1) * 128], block)
            out[:, count - 128 :] = block.astype(BF)

    half = PLANE // 2
    outs = [((half, part, count), BF), ((half, part, count), BF), ((rows, width - in_cols), BF)]
    ins = [near(item) for item in (*sums, *others, *ffn, lines)]
    return call(kernel, ins, outs, [((L, rows + 16, width), BF)], rows * count, SMALL)


def unpack_shares(even, core, got, L, in_cols, hidden_cols):
    part, count = even.shape[1:]
    wide = in_cols // 3
    D, far = PLANE * wide, hidden_cols // 128
    bias_lines = in_cols // 128
    first_line = part - L * bias_lines

    def natural(x):
        q = wide // 4
        return jnp.concatenate([x[:, :q], x[:, 2 * q : 3 * q], x[:, q : 2 * q], x[:, 3 * q :]], axis=1)

    def kernel(ins, outs, scratch):
        even, core, *got = ins
        w_in, w_up, lines, bias = outs
        here = plane_index()
        blocks = [even.at[0], core.at[0]] + [ref.at[j] for ref in got for j in range(2)]
        total = jnp.zeros((part, 128), F32)
        for k in range(PLANE):
            block = blocks[k][...].astype(F32)
            of = here ^ k
            own_lines = block[:, count - 128 :]
            total = total + own_lines
            for layer in range(L):
                for t in range(3):
                    at = pl.ds(pl.multiple_of(t * D + of * wide, 128), wide)
                    start = layer * in_cols + t * wide
                    columns = block[:, start : start + wide]
                    row = first_line + layer * bias_lines + t
                    line = own_lines[row : row + 1]
                    if t < 2:
                        columns, line = natural(columns), natural(line)
                    w_in[layer, :, at] = columns
                    bias[layer, :, at] = line
                for o in range(far):
                    at = pl.ds(pl.multiple_of(o * PLANE * 128 + of * 128, 128), 128)
                    start = L * in_cols + layer * hidden_cols + o * 128
                    w_up[layer, :, at] = block[:, start : start + 128]
        lines[...] = total

    outs = [((L, part, 3 * D), F32), ((L, part, far * PLANE * 128), F32), ((part, 128), F32), ((L, 1, 3 * D), F32)]
    ins = [near(item) for item in (even, core, *got)]
    return call(kernel, ins, outs, [], part * count * PLANE, SMALL)


def body(
    tokens,
    attn_in,
    attn_out,
    ffn_up,
    ffn_down,
    norm_gains,
    biases,
    colbert,
    log_scale,
    cotangent,
    seg_lengths,
    seg_kinds,
    pairing,
):
    S = lax.axis_size("seq")
    R = lax.axis_size("row")
    O = S * R // PLANE
    place = lax.axis_index("seq") * R + lax.axis_index("row")
    plane, far = place % PLANE, place // PLANE
    relative = jnp.bitwise_xor(plane, jnp.arange(PLANE, dtype=jnp.int32))
    T = tokens.shape[1]
    D = tokens.shape[2]
    N = PLANE * T
    L = attn_in.shape[0]
    head_dim = D // HEADS
    half = head_dim // 2
    scale = head_dim ** (-0.5)
    wide = 2 * head_dim
    in_cols = 3 * wide
    in_rows = attn_in.shape[1]
    rows_in = PLANE * in_rows
    FF = ffn_up.shape[2]
    up_cols = FF // (S * R)
    hidden_cols = O * up_cols
    gain_part = norm_gains.shape[1]
    bias_part = biases.shape[1]
    part = gain_part + bias_part
    along_z = [[o * (S // O) + i for o in range(O)] for i in range(S // O)]
    is_mine = jnp.arange(PLANE, dtype=jnp.int32) == plane

    def padded_rows(vector, width=D):
        rows = -(-vector.shape[0] // (16 * width)) * 16
        return jnp.pad(vector, (0, rows * width - vector.shape[0])).reshape(rows, width)

    def pack_columns(w):
        lead = w.shape[:-1]
        n = len(lead)
        qk = w[..., : 2 * D].reshape(*lead, 2, PLANE, 2, 2, half)
        qk = qk.transpose((n + 1,) + tuple(range(n)) + (n, n + 3, n + 2, n + 4)).reshape(PLANE, *lead, 2 * wide)
        v = w[..., 2 * D :].reshape(*lead, PLANE, wide)
        v = v.transpose((n,) + tuple(range(n)) + (n + 1,))
        return jnp.concatenate([qk, v], axis=-1)

    def unpack_columns(w):
        rows = w.shape[1]
        qk = w[:, :, : 2 * wide].reshape(PLANE, rows, 2, 2, 2, half)
        qk = qk.transpose(1, 2, 0, 4, 3, 5).reshape(rows, 2 * D)
        v = w[:, :, 2 * wide :].transpose(1, 0, 2).reshape(rows, D)
        return jnp.concatenate([qk, v], axis=1)

    def pack_hidden(w):
        rows = w.shape[0]
        return w.reshape(rows, O, PLANE, up_cols).transpose(2, 0, 1, 3).reshape(PLANE, rows, hidden_cols)

    def unpack_hidden(w):
        rows = w.shape[1]
        return w.reshape(PLANE, rows, O, up_cols).transpose(1, 2, 0, 3).reshape(rows, FF)

    def fold(w):
        n = w.shape[-2] // 2
        return jnp.concatenate([w[..., :n, :], w[..., n:, :]], axis=-1)

    def unfold(w):
        n = w.shape[-1] // 2
        return jnp.concatenate([w[..., :n], w[..., n:]], axis=-2)

    to_group = [(b, (b % O) * PLANE + b // O) for b in range(O * PLANE)]
    from_group = [(d, b) for b, d in to_group]
    small = jnp.concatenate([norm_gains.reshape(-1), biases.reshape(-1), colbert.reshape(-1)])
    even, odd = pack_first(attn_in[0], padded_rows(small, in_cols))
    core = across(odd, 1)
    got = tie(*[across(jnp.stack([even[k], core[k]]), 2 * k) for k in (1, 2, 3)])
    shard_out = lax.ppermute(attn_out, BOTH, to_group)
    table = turned(jnp.concatenate([seg_lengths[0], seg_kinds[0], pairing[0]]))
    seg_count = seg_lengths.shape[1]
    lengths, kinds = table[:seg_count], table[seg_count : 2 * seg_count]
    pairs_of = table[2 * seg_count :]
    hidden_low = turned(tokens[0])

    def attn_block(layer, shard):
        out = shard_out[layer].reshape(in_rows, PLANE, wide).transpose(1, 0, 2).reshape(rows_in, wide)
        return jnp.concatenate([shard, out], axis=1)

    def gather_far(x):
        return lax.all_gather(x, "seq", axis=0, axis_index_groups=along_z)

    own, small = unpack_first(even, core, got, shard_out[0])
    small = small.reshape(PLANE, -1)
    full_attn = [gather_far(own)]
    count_small = L * part
    col_plane = small[:, count_small : count_small + colbert.size].reshape(-1)
    params = small[None, :, :count_small]
    step = 1
    while step < O:
        other = across(params, PLANE * step)
        low_side = (far & step) == 0
        params = jnp.concatenate([jnp.where(low_side, params, other), jnp.where(low_side, other, params)], axis=0)
        step *= 2
    params = params.reshape(O * PLANE, count_small).astype(F32)
    gains_all = params[:, : L * gain_part].reshape(O * PLANE, L, gain_part).transpose(1, 0, 2).reshape(L, 2 * D)
    bias_all = params[:, L * gain_part :].reshape(O * PLANE, L, bias_part).transpose(1, 0, 2).reshape(L, -1)
    in_biases = pick(pack_columns(bias_all[:, : 3 * D]), plane, axis=0).reshape(1, L * in_cols)
    up_biases = pick(pack_hidden(bias_all[:, 4 * D : 4 * D + FF]), plane, axis=0).reshape(1, L * hidden_cols)
    rest_at = 4 * D + FF
    params = jnp.concatenate([gains_all, bias_all[:, 3 * D : 4 * D], bias_all[:, rest_at:]], axis=1).reshape(1, -1)
    GAIN_ONE, GAIN_TWO, BIAS_OUT, BIAS_DOWN, SHIFT_ONE, SHIFT_TWO = range(6)

    def at(layer, which):
        return (layer * 6 + which) * D

    rest = jnp.concatenate(
        [pack_hidden(ffn_up[0])]
        + [piece for layer in range(1, L) for piece in (pack_columns(attn_in[layer]), pack_hidden(ffn_up[layer]))],
        axis=-1,
    )
    rest = plane_exchange(rest, relative).reshape(rows_in, -1)
    full_ffn = []
    start = 0
    for layer in range(L):
        if layer > 0:
            full_attn.append(gather_far(attn_block(layer, rest[:, start : start + in_cols])))
            start += in_cols
        own = [fold(rest[:, start : start + hidden_cols]), ffn_down[layer]]
        start += hidden_cols
        if layer == L - 1:
            own.append(padded_rows(col_plane))
        full_ffn.append(gather_far(jnp.concatenate(own, axis=0)))
    w_col = full_ffn[L - 1][:, rows_in // 2 + up_cols :].reshape(O, -1)[:, : col_plane.size]
    w_col = w_col.reshape(D, colbert.shape[1])

    block_at = 4 * ((relative // 2 % 2) ^ (far % 2)) + 2 * (relative % 2) + relative // 4
    positions = (block_at[:, None] * T + jnp.arange(T, dtype=jnp.int32)[None, :]).reshape(N)
    held_segment, held_offset = token_info(positions, lengths, kinds)[:2]
    cos, sin = rope_angles(held_offset, head_dim)
    seg_row = held_segment.astype(F32)[None, :]
    table = jnp.concatenate([cos, sin, jnp.broadcast_to(seg_row.T, (N, wide - 2 * half))], axis=1)

    hidden = hidden_low
    records = []
    for layer in range(L):
        x_all = plane_gather(hidden_low)
        qkv, context, logs, even, odd = attn_forward(
            x_all, full_attn[layer], in_biases, layer * in_cols, table, seg_row, half, scale
        )
        terms, _ = plane_scatter(even, odd)
        first, normed, normed_low = add_norm(
            [hidden] + terms, params, at(layer, BIAS_OUT), at(layer, GAIN_ONE), at(layer, SHIFT_ONE)
        )
        normed_all = plane_gather(normed_low)
        act, slope, even, odd = ffn_forward(
            normed_all, full_ffn[layer], up_biases, layer * hidden_cols, hidden_cols
        )
        terms, _ = plane_scatter(even, odd)
        second, hidden, hidden_low = add_norm(
            [normed] + terms, params, at(layer, BIAS_DOWN), at(layer, GAIN_TWO), at(layer, SHIFT_TWO)
        )
        records.append((x_all, qkv, context, logs, first, normed_all, act, slope, second))
    hidden_out = turned(hidden_low, True)

    full_width = w_col.shape[1]
    row_positions = jnp.arange(N, dtype=jnp.int32)
    segment, offset, is_query, query_slot, doc_num = token_info(row_positions, lengths, kinds)
    codes = jnp.stack([jnp.where(is_query == 0, doc_num, -1), jnp.where(is_query == 1, query_slot, -1)])
    own_codes = lax.dynamic_slice(codes, (0, block_at[0] * T), (2, T))
    positive = jnp.repeat(pairs_of, QLEN)[:, None]
    temp = jnp.exp(log_scale)[None]
    hidden_low, cot = tie(hidden_low, cotangent[0])
    cot = turned(cot)
    col = dot(hidden_low, w_col)
    col_blocks = plane_gather(col.astype(BF))
    grad_out, grad_col_low, terms = head_kernel(
        col_blocks, col, codes, own_codes, positive, temp, w_col, 1.0 / (3 * NQ * R)
    )
    loss_terms = terms[0, :2]
    col_parts = dot_lt(hidden_low, grad_col_low).reshape(O, PLANE, in_rows, full_width).transpose(1, 0, 2, 3)
    col_parts = plane_sum(pick(col_parts.reshape(PLANE, O * in_rows, full_width), relative, axis=0))
    col_rows = jax.vmap(padded_rows)(col_parts.reshape(O, in_rows * full_width)).astype(BF)
    grad_parts = [cot, grad_out]

    def scatter_far(whole):
        whole = whole.reshape(-1, whole.shape[-1])
        return lax.psum_scatter(whole, "seq", scatter_dimension=0, tiled=True, axis_index_groups=along_z)

    outs = [[None] * L for _ in range(6)]

    def finish_out(layer, share_out):
        share_out = share_out.reshape(PLANE, in_rows, wide).transpose(1, 0, 2).reshape(in_rows, D)
        outs[1][layer] = lax.ppermute(share_out, BOTH, from_group).astype(F32)

    shares_ffn, shares_attn = [None] * L, [None] * L
    vectors = [None] * L
    for layer in reversed(range(L)):
        x_all, qkv, context, logs, first, normed_all, act, slope, second = records[layer]
        grad_second, grad_ffo, sums_two = norm_back(grad_parts, second, params, at(layer, GAIN_TWO))
        ffo_all = plane_gather(grad_ffo)
        if layer == L - 1:
            ffo_all, hidden_out = tie(ffo_all, hidden_out)
        grad_pre, grad_bias_up, even, odd = ffn_back(ffo_all, full_ffn[layer], slope)
        blocks = ffn_weights(normed_all, ffo_all, act, grad_pre, O, col_rows if layer == L - 1 else None)
        terms, blocks = plane_scatter(even, odd, blocks)
        shares_ffn[layer] = scatter_far(blocks)
        grad_first, grad_branch, sums_one = norm_back([grad_second] + terms, first, params, at(layer, GAIN_ONE))
        branch_all = plane_gather(grad_branch)
        if layer < L - 1:
            branch_all, shares_attn[layer + 1] = tie(branch_all, shares_attn[layer + 1])
        grad_mixed, grad_bias_in, even, odd = attn_back(
            branch_all, full_attn[layer], qkv, context, logs, table, seg_row, half, scale
        )

        gain_two, shift_two, down, gain_one, shift_one, out = [
            sums[0, k * D : (k + 1) * D] for sums in (sums_two, sums_one) for k in range(3)
        ]
        own_up = unpack_hidden(is_mine[:, None, None].astype(F32) * grad_bias_up[None])[0]
        gains = jnp.concatenate([gain_one, gain_two]).reshape(O, PLANE, gain_part)
        bias = jnp.concatenate([jnp.zeros((3 * D,), F32), out, own_up, down, shift_one, shift_two])
        vectors[layer] = jnp.concatenate([gains, bias.reshape(O, PLANE, bias_part)], axis=2)

        blocks = attn_weights(x_all, branch_all, context, grad_mixed, grad_bias_in, O, layer == 0)
        terms, blocks = plane_scatter(even, odd, blocks, layer == 0)
        terms, shares_ffn[layer] = tie(terms, shares_ffn[layer])
        if layer > 0:
            shares_attn[layer] = scatter_far(blocks[0])
            grad_parts = [grad_first] + terms

    got = [across(blocks[step], PLANE * step) for step in range(1, O)]
    entries = jnp.concatenate(vectors + [jnp.broadcast_to(loss_terms, (O, PLANE, 2))], axis=2)
    lines = pick(entries, far)
    for step in range(1, O):
        lines = lines + across(pick(entries, far ^ step), PLANE * step)
    loss_terms = lines[0, L * part :]
    lines = jnp.pad(lines[:, : L * part], ((0, 0), (0, in_rows * 128 - L * part))).reshape(PLANE, in_rows, 128)
    grad_tokens = turned((grad_first + sum(item.astype(F32) for item in terms)).astype(BF), True)
    got, lines, grad_tokens = tie(got, lines, grad_tokens)
    even, odd, last_out = pack_shares([blocks[0]] + got, shares_attn[1:], shares_ffn, lines, in_cols, hidden_cols)
    core = across(odd, 1)
    got = tie(*[across(jnp.stack([even[k], core[k]]), 2 * k) for k in (1, 2, 3)])
    w_in_grad, w_up_grad, lines, bias_in_grad = unpack_shares(even, core, got, L, in_cols, hidden_cols)
    mine = lines.reshape(-1)
    bias_in_grad = jnp.pad(bias_in_grad[:, 0], ((0, 0), (0, O * PLANE * bias_part - 3 * D)))
    bias_in_grad = pick(bias_in_grad.reshape(L, O * PLANE, bias_part), place, axis=1)
    for layer in range(L):
        outs[3][layer] = shares_ffn[layer][rows_in // 2 : rows_in // 2 + up_cols]
        finish_out(layer, shares_attn[layer][:rows_in, in_cols:] if layer > 0 else last_out)
        outs[4][layer] = mine[layer * part : layer * part + gain_part]
        outs[5][layer] = mine[layer * part + gain_part : (layer + 1) * part] + bias_in_grad[layer]
    col_share = shares_ffn[L - 1][rows_in // 2 + up_cols :].reshape(-1)[: in_rows * full_width]
    col_share = col_share.reshape(in_rows, full_width).astype(F32)
    outs[0], outs[2] = w_in_grad, w_up_grad
    stacked = [jnp.stack(items).astype(F32) if isinstance(items, list) else items for items in outs]
    return (
        hidden_out[None],
        loss_terms[:1],
        grad_tokens.astype(F32)[None],
        stacked[0],
        stacked[1],
        stacked[2],
        stacked[3],
        stacked[4],
        stacked[5],
        col_share,
        loss_terms[1:],
    )


def joined_2(value, axis, join):
    pieces = jax.tree.map(lambda part: lax.all_gather(part, axis), value)
    head = jax.tree.map(lambda part: part[0], pieces)
    tail = jax.tree.map(lambda part: part[1:], pieces)
    so_far, _ = lax.scan(lambda so_far, section: (join(so_far, section), None), head, tail)
    return so_far


def rope_tables(offset, head_dim):
    half = head_dim // 2
    inverse = jnp.exp(jnp.arange(half, dtype=jnp.float32) * (-2.0 * math.log(10000.0) / head_dim))
    angle = offset.astype(jnp.float32)[:, None] * inverse[None, :]
    return (jnp.cos(angle), jnp.sin(angle))


def rotate(flat, cos_table, sin_table):
    length = flat.shape[0]
    head_dim = flat.shape[1] // HEADS
    half = head_dim // 2
    shaped = flat.reshape(length, HEADS, head_dim)
    first_half = shaped[..., :half]
    second_half = shaped[..., half:]
    cos_three = cos_table[:, None, :]
    sin_three = sin_table[:, None, :]
    turned = jnp.concatenate(
        [
            first_half * cos_three - second_half * sin_three,
            second_half * cos_three + first_half * sin_three,
        ],
        axis=-1,
    )
    return turned.reshape(length, flat.shape[1])


def block_for(count):
    blocks = count
    while blocks > 1024 and blocks % 2 == 0:
        blocks = blocks // 2
    return blocks


def merge_pair(first, second):
    max_first, sum_first = first
    max_second, sum_second = second
    top = jnp.maximum(max_first, max_second)
    return (top, sum_first * jnp.exp(max_first - top) + sum_second * jnp.exp(max_second - top))


def matmul_left_t(left, right):
    return jnp.einsum("ti,to->io", left, right, preferred_element_type=jnp.float32)


def matmul_right_t(left, right):
    return jnp.einsum("to,io->ti", left, right, preferred_element_type=jnp.float32)


def body_wide(
    tokens,
    attn_in,
    attn_out,
    ffn_up,
    ffn_down,
    norm_gains,
    biases,
    colbert,
    log_scale,
    cotangent,
    seg_lengths,
    seg_kinds,
    pairing,
):
    rank = lax.axis_index("seq")
    local_len = tokens.shape[1]
    model_width = tokens.shape[2]
    head_dim = model_width // HEADS
    scale = head_dim ** (-0.5)
    lengths = seg_lengths[0]
    kinds = seg_kinds[0]
    positions = rank * local_len + jnp.arange(local_len, dtype=jnp.int32)
    segment, offset, is_query, query_slot, doc_num = token_info(positions, lengths, kinds)
    cos_table, sin_table = rope_tables(offset, head_dim)
    layer_count = attn_in.shape[0]

    def split_pieces(key_piece, value_piece):
        count = key_piece.shape[0]
        blocks = block_for(count)
        key_seg = token_info(jnp.arange(count, dtype=jnp.int32), lengths, kinds)[0]
        key_blocks = key_piece.reshape(count // blocks, blocks, HEADS, head_dim)
        value_blocks = value_piece.reshape(count // blocks, blocks, HEADS, head_dim)
        seg_blocks = key_seg.reshape(count // blocks, blocks)
        return (count, blocks, key_blocks, value_blocks, seg_blocks)

    def attend_back(queries, keys, values, context, log_total, grad_context):
        query_three = queries.reshape(local_len, HEADS, head_dim)
        grad_three = grad_context.reshape(local_len, HEADS, head_dim)
        delta = jnp.sum(
            grad_three.astype(jnp.float32) * context.reshape(local_len, HEADS, head_dim), axis=-1
        ).T

        def score_grads(
            query_blk, grad_blk, key_blk, value_blk, query_seg, key_seg, total_blk, delta_blk
        ):
            scores = (
                jnp.einsum("qhd,khd->hqk", query_blk, key_blk, preferred_element_type=jnp.float32)
                * scale
            )
            allowed = (query_seg[:, None] == key_seg[None, :])[None]
            probs = jnp.where(allowed, jnp.exp(scores - total_blk[..., None]), 0.0)
            grad_probs = jnp.einsum(
                "qhd,khd->hqk", grad_blk, value_blk, preferred_element_type=jnp.float32
            )
            grad_scores = (probs * (grad_probs - delta_blk[..., None])).astype(jnp.bfloat16)
            return (probs, grad_scores)

        grad_query = jnp.zeros((local_len, HEADS, head_dim), jnp.float32)
        count, blocks, key_blocks, value_blocks, seg_blocks = split_pieces(
            lax.all_gather(keys, "seq", axis=0, tiled=True),
            lax.all_gather(values, "seq", axis=0, tiled=True),
        )

        def advance(grad_acc, item):
            key_blk, value_blk, seg_blk = item
            probs, grad_scores = score_grads(
                query_three, grad_three, key_blk, value_blk, segment, seg_blk, log_total, delta
            )
            grad_acc = grad_acc + scale * jnp.einsum(
                "hqk,khd->qhd", grad_scores, key_blk, preferred_element_type=jnp.float32
            )
            grad_key = scale * jnp.einsum(
                "hqk,qhd->khd", grad_scores, query_three, preferred_element_type=jnp.float32
            )
            grad_value = jnp.einsum(
                "hqk,qhd->khd",
                probs.astype(jnp.bfloat16),
                grad_three,
                preferred_element_type=jnp.float32,
            )
            joined = jnp.concatenate(
                [grad_key.reshape(blocks, model_width), grad_value.reshape(blocks, model_width)],
                axis=1,
            )
            return (grad_acc, joined)

        grad_query, pieces_out = lax.scan(
            advance, grad_query, (key_blocks, value_blocks, seg_blocks)
        )
        grad_rows = pieces_out.reshape(count, 2 * model_width)
        grad_query, grad_rows = (grad_query, grad_rows)
        summed = lax.psum_scatter(
            grad_rows.astype(jnp.bfloat16), "seq", scatter_dimension=0, tiled=True
        ).astype(jnp.float32)
        grad_key_out = summed[:, :model_width]
        grad_value_out = summed[:, model_width:]
        return (grad_query.reshape(local_len, model_width), grad_key_out, grad_value_out)

    def unpack(full):
        w_in, w_out, w_up, w_down, gains, bias = full[:6]
        hidden_units = w_up.shape[1]
        gains_f = gains.astype(jnp.float32)
        bias_f = bias.astype(jnp.float32)
        width_three = 3 * model_width
        return (
            w_in,
            w_out,
            w_up,
            w_down,
            hidden_units,
            gains_f[:model_width],
            gains_f[model_width:],
            bias_f[:width_three],
            bias_f[width_three : 4 * model_width],
            bias_f[4 * model_width : 4 * model_width + hidden_units],
            bias_f[4 * model_width + hidden_units : 5 * model_width + hidden_units],
            bias_f[5 * model_width + hidden_units : 6 * model_width + hidden_units],
            bias_f[6 * model_width + hidden_units :],
        )

    def layer_backward(grad_out, full, record):
        (
            w_in,
            w_out,
            w_up,
            w_down,
            hidden_units,
            gain_one,
            gain_two,
            bias_in,
            bias_out,
            bias_up,
            bias_down,
            shift_one,
            shift_two,
        ) = unpack(full)
        (
            inputs_low,
            queries,
            keys,
            values,
            context,
            context_low,
            log_total,
            first,
            normed,
            normed_low,
            pre_act,
            act_low,
            second,
        ) = record
        unused, pull_two = jax.vjp(layer_norm, second, gain_two, shift_two)
        grad_second, grad_gain_two, grad_shift_two = pull_two(grad_out)
        grad_branch_two = grad_second.astype(jnp.bfloat16)
        grad_bias_down = jnp.sum(grad_branch_two.astype(jnp.float32), axis=0)
        grad_w_down = matmul_left_t(act_low, grad_branch_two)
        grad_act = matmul_right_t(grad_branch_two, w_down)
        unused, pull_gelu = jax.vjp(exact_gelu, pre_act)
        grad_pre = pull_gelu(grad_act)[0].astype(jnp.bfloat16)
        grad_bias_up = jnp.sum(grad_pre.astype(jnp.float32), axis=0)
        grad_w_up = matmul_left_t(normed_low, grad_pre)
        grad_normed = grad_second + matmul_right_t(grad_pre, w_up)
        unused, pull_one = jax.vjp(layer_norm, first, gain_one, shift_one)
        grad_first, grad_gain_one, grad_shift_one = pull_one(grad_normed)
        grad_branch = grad_first.astype(jnp.bfloat16)
        grad_bias_out = jnp.sum(grad_branch.astype(jnp.float32), axis=0)
        grad_w_out = matmul_left_t(context_low, grad_branch)
        grad_context = matmul_right_t(grad_branch, w_out).astype(jnp.bfloat16)
        grad_query, grad_key, grad_value = attend_back(
            queries, keys, values, context, log_total, grad_context
        )
        grad_mixed = jnp.concatenate(
            [
                rotate(grad_query, cos_table, -sin_table),
                rotate(grad_key, cos_table, -sin_table),
                grad_value,
            ],
            axis=1,
        ).astype(jnp.bfloat16)
        grad_bias_in = jnp.sum(grad_mixed.astype(jnp.float32), axis=0)
        grad_w_in = matmul_left_t(inputs_low, grad_mixed)
        grad_hidden = grad_first + matmul_right_t(grad_mixed, w_in)
        grad_gains = jnp.concatenate([grad_gain_one, grad_gain_two])
        grad_bias = jnp.concatenate(
            [
                grad_bias_in,
                grad_bias_out,
                grad_bias_up,
                grad_bias_down,
                grad_shift_one,
                grad_shift_two,
            ]
        )
        return (grad_hidden, (grad_w_in, grad_w_out, grad_w_up, grad_w_down, grad_gains, grad_bias))

    hidden = tokens[0].astype(jnp.float32)
    records = []
    gathered = []
    for layer_index in range(layer_count):
        full = (
            lax.all_gather(attn_in[layer_index], ("seq", "row"), axis=0, tiled=True),
            lax.all_gather(attn_out[layer_index], ("seq", "row"), axis=0, tiled=True),
            lax.all_gather(ffn_up[layer_index], ("seq", "row"), axis=0, tiled=True),
            lax.all_gather(ffn_down[layer_index], ("seq", "row"), axis=0, tiled=True),
            lax.all_gather(norm_gains[layer_index], ("seq", "row"), axis=0, tiled=True),
            lax.all_gather(biases[layer_index], ("seq", "row"), axis=0, tiled=True),
            lax.all_gather(colbert, ("seq", "row"), axis=0, tiled=True),
        )
        gathered.append(full)
        (
            layer_w_in,
            layer_w_out,
            layer_w_up,
            layer_w_down,
            layer_hidden_units,
            layer_gain_one,
            layer_gain_two,
            layer_bias_in,
            layer_bias_out,
            layer_bias_up,
            layer_bias_down,
            layer_shift_one,
            layer_shift_two,
        ) = unpack(full)
        layer_inputs_low = hidden.astype(jnp.bfloat16)
        mixed = (
            jnp.dot(layer_inputs_low, layer_w_in, preferred_element_type=jnp.float32)
            + layer_bias_in
        )
        layer_queries = rotate(mixed[:, :model_width], cos_table, sin_table).astype(jnp.bfloat16)
        layer_keys = rotate(mixed[:, model_width : 2 * model_width], cos_table, sin_table).astype(
            jnp.bfloat16
        )
        layer_values = mixed[:, 2 * model_width :].astype(jnp.bfloat16)
        attend_query_three = layer_queries.reshape(local_len, HEADS, head_dim)
        attend_initial = (
            jnp.full((HEADS, local_len), NEG_FILL, jnp.float32),
            jnp.zeros((HEADS, local_len), jnp.float32),
            jnp.zeros((local_len, HEADS, head_dim), jnp.float32),
        )
        absorb_carry = attend_initial
        absorb_count, absorb_blocks, absorb_key_blocks, absorb_value_blocks, absorb_seg_blocks = (
            split_pieces(
                lax.all_gather(layer_keys, "seq", axis=0, tiled=True),
                lax.all_gather(layer_values, "seq", axis=0, tiled=True),
            )
        )

        def absorb_advance(state, item):
            run_max, run_sum, accum = state
            key_blk, value_blk, seg_blk = item
            scores = (
                jnp.einsum(
                    "qhd,khd->hqk", attend_query_three, key_blk, preferred_element_type=jnp.float32
                )
                * scale
            )
            allowed = (segment[:, None] == seg_blk[None, :])[None]
            scores = jnp.where(allowed, scores, NEG_FILL)
            new_max = jnp.maximum(run_max, jnp.max(scores, axis=-1))
            weights = jnp.where(allowed, jnp.exp(scores - new_max[..., None]), 0.0)
            factor = jnp.exp(run_max - new_max)
            run_sum = run_sum * factor + jnp.sum(weights, axis=-1)
            accum = accum * factor.T[:, :, None] + jnp.einsum(
                "hqk,khd->qhd",
                weights.astype(jnp.bfloat16),
                value_blk,
                preferred_element_type=jnp.float32,
            )
            return ((new_max, run_sum, accum), None)

        absorb_carry, absorb_unused = lax.scan(
            absorb_advance,
            absorb_carry,
            (absorb_key_blocks, absorb_value_blocks, absorb_seg_blocks),
        )
        run_max, run_sum, accum = absorb_carry
        attend_context = (accum / run_sum.T[:, :, None]).reshape(local_len, model_width)
        attend_log_total = run_max + jnp.log(run_sum)
        layer_context_low = attend_context.astype(jnp.bfloat16)
        layer_first = (
            hidden
            + jnp.dot(layer_context_low, layer_w_out, preferred_element_type=jnp.float32)
            + layer_bias_out
        )
        layer_normed = layer_norm(layer_first, layer_gain_one, layer_shift_one)
        layer_normed_low = layer_normed.astype(jnp.bfloat16)
        layer_pre_act = (
            jnp.dot(layer_normed_low, layer_w_up, preferred_element_type=jnp.float32)
            + layer_bias_up
        )
        layer_act_low = exact_gelu(layer_pre_act).astype(jnp.bfloat16)
        layer_second = (
            layer_normed
            + jnp.dot(layer_act_low, layer_w_down, preferred_element_type=jnp.float32)
            + layer_bias_down
        )
        output = layer_norm(layer_second, layer_gain_two, layer_shift_two)
        layer_record = (
            layer_inputs_low,
            layer_queries,
            layer_keys,
            layer_values,
            attend_context,
            layer_context_low,
            attend_log_total,
            layer_first,
            layer_normed,
            layer_normed_low,
            layer_pre_act,
            layer_act_low,
            layer_second,
        )
        hidden = output
        record = layer_record
        records.append(record)
    w_col = gathered[layer_count - 1][6]
    final_low = hidden.astype(jnp.bfloat16)
    col = jnp.dot(final_low, w_col, preferred_element_type=jnp.float32)
    full_width = w_col.shape[1]
    part_widths = (full_width, full_width * 3 // 4, full_width // 2)
    query_total = NQ * QLEN
    doc_total = NSD + 1
    selector = (is_query == 1)[None, :] & (
        query_slot[None, :] == jnp.arange(query_total, dtype=jnp.int32)[:, None]
    )
    selector_low = selector.astype(jnp.bfloat16)
    embeds = [unit_rows(col[:, :part_width]).astype(jnp.bfloat16) for part_width in part_widths]
    picked = (
        lax.psum(
            jnp.dot(selector_low, embeds[0], preferred_element_type=jnp.float32).astype(
                jnp.bfloat16
            ),
            "seq",
        ).astype(jnp.float32),
        lax.psum(
            jnp.dot(selector_low, embeds[1], preferred_element_type=jnp.float32).astype(
                jnp.bfloat16
            ),
            "seq",
        ).astype(jnp.float32),
        lax.psum(
            jnp.dot(selector_low, embeds[2], preferred_element_type=jnp.float32).astype(
                jnp.bfloat16
            ),
            "seq",
        ).astype(jnp.float32),
    )
    query_emb = [item.astype(jnp.bfloat16) for item in picked]
    sims = jnp.stack(
        [
            jnp.einsum(
                "qc,tc->qt", query_emb[part], embeds[part], preferred_element_type=jnp.float32
            )
            for part in range(3)
        ]
    )
    doc_mask = (
        (is_query == 0)[:, None]
        & (doc_num[:, None] == jnp.arange(doc_total, dtype=jnp.int32)[None, :])
    )[None, None]
    scaled = jnp.where(doc_mask, SHARPNESS * sims[..., None], NEG_FILL)
    part_max = jnp.max(scaled, axis=2)
    part_sum = jnp.sum(jnp.where(doc_mask, jnp.exp(scaled - part_max[:, :, None, :]), 0.0), axis=2)
    top, total = joined_2((part_max, part_sum), "seq", merge_pair)
    soft = (top + jnp.log(total)) / SHARPNESS
    pair_sum = jnp.sum(soft.reshape(3, NQ, QLEN, doc_total), axis=2)
    inverse_temp = jnp.exp(log_scale[0])
    logits = pair_sum * inverse_temp / QLEN
    positive = pairing[0][None, :, None] == jnp.arange(doc_total, dtype=jnp.int32)[None, None, :]
    losses = jax.nn.logsumexp(logits, axis=-1) - jnp.sum(jnp.where(positive, logits, 0.0), axis=-1)
    loss_weight = 1.0 / (3 * NQ * lax.axis_size("row"))
    grad_logits = loss_weight * (jax.nn.softmax(logits, axis=-1) - positive.astype(jnp.float32))
    loss_total, temp_grad = lax.psum(
        (jnp.sum(losses).reshape(1) * loss_weight, jnp.sum(grad_logits * logits).reshape(1)), "row"
    )
    grad_pairs = grad_logits * inverse_temp / QLEN
    grad_soft = jnp.broadcast_to(grad_pairs[:, :, None, :], (3, NQ, QLEN, doc_total)).reshape(
        3, query_total, doc_total
    )
    shares = jnp.where(doc_mask, jnp.exp(scaled - top[:, :, None, :]), 0.0) / total[:, :, None, :]
    grad_sims = jnp.sum(shares * grad_soft[:, :, None, :], axis=-1).astype(jnp.bfloat16)
    grad_query_emb = (
        lax.psum(
            jnp.dot(grad_sims[0], embeds[0], preferred_element_type=jnp.float32).astype(
                jnp.bfloat16
            ),
            "seq",
        ).astype(jnp.float32),
        lax.psum(
            jnp.dot(grad_sims[1], embeds[1], preferred_element_type=jnp.float32).astype(
                jnp.bfloat16
            ),
            "seq",
        ).astype(jnp.float32),
        lax.psum(
            jnp.dot(grad_sims[2], embeds[2], preferred_element_type=jnp.float32).astype(
                jnp.bfloat16
            ),
            "seq",
        ).astype(jnp.float32),
    )
    selector_f = selector.astype(jnp.float32)
    grad_col = jnp.zeros((local_len, full_width), jnp.float32)
    for part in range(3):
        part_width = part_widths[part]
        grad_embed = jnp.einsum(
            "qt,qc->tc", grad_sims[part], query_emb[part], preferred_element_type=jnp.float32
        )
        grad_embed = grad_embed + jnp.einsum(
            "qt,qc->tc",
            selector_f,
            grad_query_emb[part],
            precision=HIGHEST,
            preferred_element_type=jnp.float32,
        )
        unused, pull_unit = jax.vjp(unit_rows, col[:, :part_width])
        grad_col = grad_col.at[:, :part_width].add(pull_unit(grad_embed)[0])
    grad_col_low = grad_col.astype(jnp.bfloat16)
    grad_w_col = matmul_left_t(final_low, grad_col_low)
    grad_hidden = cotangent[0].astype(jnp.float32) + matmul_right_t(grad_col_low, w_col)
    shard_lists = [[] for unused_slot in range(6)]
    col_share = None
    for layer_index in reversed(range(layer_count)):
        full = (
            lax.all_gather(attn_in[layer_index], ("seq", "row"), axis=0, tiled=True),
            lax.all_gather(attn_out[layer_index], ("seq", "row"), axis=0, tiled=True),
            lax.all_gather(ffn_up[layer_index], ("seq", "row"), axis=0, tiled=True),
            lax.all_gather(ffn_down[layer_index], ("seq", "row"), axis=0, tiled=True),
            lax.all_gather(norm_gains[layer_index], ("seq", "row"), axis=0, tiled=True),
            lax.all_gather(biases[layer_index], ("seq", "row"), axis=0, tiled=True),
            lax.all_gather(colbert, ("seq", "row"), axis=0, tiled=True),
        )
        grad_hidden, layer_grads = layer_backward(grad_hidden, full, records[layer_index])
        col_term = grad_w_col if layer_index == layer_count - 1 else jnp.zeros_like(grad_w_col)
        shares_out = (
            lax.psum_scatter(layer_grads[0], ("seq", "row"), scatter_dimension=0, tiled=True),
            lax.psum_scatter(layer_grads[1], ("seq", "row"), scatter_dimension=0, tiled=True),
            lax.psum_scatter(layer_grads[2], ("seq", "row"), scatter_dimension=0, tiled=True),
            lax.psum_scatter(layer_grads[3], ("seq", "row"), scatter_dimension=0, tiled=True),
            lax.psum_scatter(layer_grads[4], ("seq", "row"), scatter_dimension=0, tiled=True),
            lax.psum_scatter(layer_grads[5], ("seq", "row"), scatter_dimension=0, tiled=True),
            lax.psum_scatter(col_term, ("seq", "row"), scatter_dimension=0, tiled=True),
        )
        for slot in range(6):
            shard_lists[slot].insert(0, shares_out[slot])
        if layer_index == layer_count - 1:
            col_share = shares_out[6]
    stacked = [jnp.stack(items) for items in shard_lists]
    return (
        hidden.astype(jnp.bfloat16)[None],
        loss_total,
        grad_hidden[None],
        stacked[0],
        stacked[1],
        stacked[2],
        stacked[3],
        stacked[4],
        stacked[5],
        col_share,
        temp_grad,
    )


def solution(mesh):
    placed = (
        P("row", "seq", None),
        P(None, ("seq", "row"), None),
        P(None, ("seq", "row"), None),
        P(None, ("seq", "row"), None),
        P(None, ("seq", "row"), None),
        P(None, ("seq", "row")),
        P(None, ("seq", "row")),
        P(("seq", "row"), None),
        P(),
        P("row", "seq", None),
        P("row", None),
        P("row", None),
        P("row", None),
    )
    planes = mesh.shape["row"] == 4 and mesh.shape["seq"] * 4 == 4 * PLANE and HEADS == 2 * PLANE
    return jax.shard_map(
        body if planes else body_wide,
        mesh=mesh,
        in_specs=placed,
        out_specs=(
            P("row", "seq", None),
            P(),
            P("row", "seq", None),
            P(None, ("seq", "row"), None),
            P(None, ("seq", "row"), None),
            P(None, ("seq", "row"), None),
            P(None, ("seq", "row"), None),
            P(None, ("seq", "row")),
            P(None, ("seq", "row")),
            P(("seq", "row"), None),
            P(),
        ),
        check_vma=False,
    )
```

```python
import math

import jax
import jax.numpy as jnp
from jax import lax
from jax.experimental import pallas as pl
from jax.experimental.pallas import tpu as pltpu
from jax.sharding import PartitionSpec as P

HEADS = 16
QLEN = 32
NQ = 4
NSD = 3

NEG_FILL = -1e30
SHARPNESS = 16.0
HIGHEST = lax.Precision.HIGHEST
BF = jnp.bfloat16
F32 = jnp.float32

def dot(left, right):
    return jnp.dot(left, right, preferred_element_type=F32)


def dot_lt(left, right):
    return lax.dot_general(left, right, (((0,), (0,)), ((), ())), preferred_element_type=F32)


def dot_rt(left, right):
    return lax.dot_general(left, right, (((1,), (1,)), ((), ())), preferred_element_type=F32)


PLANE = 8
BOTH = ("seq", "row")


def across(x, mask):
    size = lax.axis_size("seq") * lax.axis_size("row")
    return lax.ppermute(x, BOTH, [(d, d ^ mask) for d in range(size)])


def turned(x, back=False):
    size = lax.axis_size("seq") * lax.axis_size("row")
    pairs = []
    for d in range(size):
        z, y, column, core = d // PLANE, d // 4 % 2, d // 2 % 2, d % 2
        to = (2 * core + column) * PLANE + 4 * y + 2 * (column ^ (z // 2)) + z % 2
        pairs.append((to, d) if back else (d, to))
    return lax.ppermute(x, BOTH, pairs)


def plane_gather(x):
    blocks = [x, None, across(x, 2), None, across(x, 4), None, across(x, 6), None]
    for k in range(0, PLANE, 2):
        blocks[k + 1] = across(blocks[k], 1)
    return blocks


def plane_scatter(even, odd, beside=None, first=False):
    core = across(odd, 1)
    if first:
        core, beside = tie(core, beside)
    parts = core_add(even, core)
    got = [across(parts[j], 2 * j) for j in (1, 2, 3)]
    if beside is not None and not first:
        got, beside = tie(got, beside)
    return [parts[0]] + got, beside


def plane_sum(parts):
    parts = parts.astype(BF)
    core = across(parts[1::2], 1).astype(F32) + parts[0::2].astype(F32)
    sent = core[1:].astype(BF)
    return core[0] + sum(across(sent[k - 1], 2 * k).astype(F32) for k in (1, 2, 3))


def plane_exchange(x, relative, before=None):
    x = pick(x, relative)
    core = across(x[1::2], 1)
    if before is not None:
        core, before = tie(core, before)
    got = tie(*[across(jnp.stack([x[2 * k], core[k]]), 2 * k) for k in (1, 2, 3)])
    x = pick(jnp.concatenate([x[:1], core[:1], *got]), relative)
    return x if before is None else (x, before)


def pick(x, index, axis=0):
    return x.at[(slice(None),) * axis + (index,)].get(mode="promise_in_bounds")


def tie(*values):
    return lax.optimization_barrier(values)


def token_info(positions, lengths, kinds):
    ends = jnp.cumsum(lengths)
    starts = ends - lengths
    query_count = jnp.cumsum(kinds) - kinds
    doc_count = jnp.cumsum(1 - kinds) - (1 - kinds)
    segment = jnp.sum((positions[:, None] >= ends[None, :]).astype(jnp.int32), axis=1)
    onehot = segment[:, None] == jnp.arange(lengths.shape[0], dtype=jnp.int32)[None, :]
    nothing = jnp.zeros((), jnp.int32)
    seg_start = jnp.sum(jnp.where(onehot, starts[None, :], nothing), axis=1)
    is_query = jnp.sum(jnp.where(onehot, kinds[None, :], nothing), axis=1)
    query_num = jnp.sum(jnp.where(onehot, query_count[None, :], nothing), axis=1)
    doc_num = jnp.sum(jnp.where(onehot, doc_count[None, :], nothing), axis=1)
    offset = positions - seg_start
    return (segment, offset, is_query, query_num * QLEN + offset, doc_num)


def rope_angles(offset, head_dim):
    half = head_dim // 2
    inverse = jnp.exp(jnp.arange(half, dtype=F32) * (-2.0 * math.log(10000.0) / head_dim))
    angle = offset.astype(F32)[:, None] * inverse[None, :]
    return jnp.cos(angle), jnp.sin(angle)


def layer_norm(rows, gain, shift):
    center = rows - jnp.mean(rows, axis=-1, keepdims=True)
    variance = jnp.mean(center * center, axis=-1, keepdims=True)
    return center * lax.rsqrt(variance + 1e-05) * gain + shift


def unit_rows(rows):
    return rows * lax.rsqrt(jnp.sum(rows * rows, axis=-1, keepdims=True) + 1e-06)


def exact_gelu(values):
    return jax.nn.gelu(values, approximate=False)


def head_masks(width):
    lane = lax.broadcasted_iota(jnp.int32, (1, width), 1)
    first_qk = (lane % (width // 2)) < (width // 4)
    first_v = lane < (width // 2)
    return first_qk, first_v


BIG, SMALL = 62, 16

IN_VMEM = pl.BlockSpec(memory_space=pltpu.VMEM)
IN_HBM = pl.BlockSpec(memory_space=pltpu.HBM)


def near(x):
    return (x, "near")


def held(x):
    return (x, "held")


def raw(x):
    return (x, "raw")


def call(kernel, ins, outs, scratch, flops, limit=BIG, light=True):
    arrays = [a for a, _ in ins]
    kept = [i for i, (_, kind) in enumerate(ins) if kind == "held"]
    left = [i for i, out in enumerate(outs) if len(out) == 3]
    pieces = [1 if outs[i][2] is True else outs[i][2] for i in left]
    moved = sum(a.size * a.dtype.itemsize for a in arrays)
    moved += sum(math.prod(out[0]) * jnp.dtype(out[1]).itemsize for out in outs)

    def wrapped(*refs):
        in_refs = list(refs[: len(ins)])
        out_refs = list(refs[len(ins) : len(ins) + len(outs)])
        rest = refs[len(ins) + len(outs) :]
        own, rest = rest[: len(scratch)], rest[len(scratch) :]
        in_bufs, out_bufs = rest[: len(kept)], rest[len(kept) : len(kept) + len(left)]
        sems = rest[len(kept) + len(left)] if kept or left else None
        pending = {}
        for k, i in enumerate(kept):
            pending[i] = pltpu.make_async_copy(in_refs[i], in_bufs[k], sems.at[k])
            pending[i].start()

        def getter(i, buf):
            def get():
                if i in pending:
                    pending.pop(i).wait()
                return buf

            return get

        for k, i in enumerate(kept):
            in_refs[i] = getter(i, in_bufs[k])
        leaving = {}

        def flusher(i, k, target):
            def flush(j=0):
                buf = out_bufs[k]
                if pieces[k] > 1:
                    buf, target_j = buf.at[j], target.at[j]
                else:
                    target_j = target
                leaving[i, j] = pltpu.make_async_copy(buf, target_j, sems.at[len(kept) + sum(pieces[:k]) + j])
                leaving[i, j].start()

            return flush

        for k, i in enumerate(left):
            out_refs[i] = (out_bufs[k], flusher(i, k, out_refs[i]))
        kernel(in_refs, out_refs, own)
        assert not pending and len(leaving) == sum(pieces)
        for copy in leaving.values():
            copy.wait()

    buffers = [pltpu.VMEM(*item) if isinstance(item, tuple) else item for item in scratch]
    buffers += [pltpu.VMEM(arrays[i].shape, arrays[i].dtype) for i in kept]
    buffers += [pltpu.VMEM(*outs[i][:2]) for i in left]
    if kept or left:
        buffers.append(pltpu.SemaphoreType.DMA((len(kept) + sum(pieces),)))
    return pl.pallas_call(
        wrapped,
        in_specs=[IN_VMEM if kind == "near" else IN_HBM for _, kind in ins],
        out_specs=tuple(IN_HBM if len(out) == 3 else IN_VMEM for out in outs),
        out_shape=tuple(jax.ShapeDtypeStruct(out[0], out[1]) for out in outs),
        scratch_shapes=buffers,
        compiler_params=pltpu.CompilerParams(vmem_limit_bytes=limit * 1024 * 1024),
        cost_estimate=pl.CostEstimate(flops=1 if light else flops, bytes_accessed=1 if light else moved, transcendentals=0),
    )(*arrays)


def core_add(even, got):
    count, T, D = even.shape

    def kernel(ins, outs, _):
        for j in range(count):
            outs[j][...] = (ins[0][j].astype(F32) + ins[1][j].astype(F32)).astype(outs[j].dtype)

    outs = [((T, D), F32)] + [((T, D), BF)] * (count - 1)
    return call(kernel, [near(even), near(got)], outs, [], even.size, SMALL)


def add_norm(parts, params, bias_at, gain_at, shift_at):
    T, D = parts[0].shape

    def kernel(ins, outs, _):
        params = ins[-1]
        (total, leave), normed, low = outs
        rows = params[:, bias_at : bias_at + D]
        for ref in ins[:-1]:
            rows = rows + ref[...].astype(F32)
        total[...] = rows
        leave()
        result = layer_norm(rows, params[:, gain_at : gain_at + D], params[:, shift_at : shift_at + D])
        normed[...] = result
        low[...] = result.astype(BF)

    outs = [((T, D), F32, True), ((T, D), F32), ((T, D), BF)]
    return call(kernel, [near(item) for item in (*parts, params)], outs, [], 10 * T * D, SMALL)


def norm_back(parts, rows, params, gain_at):
    T, D = rows.shape

    def kernel(ins, outs, _):
        rows, params = ins[-2:]
        wide_out, low_out, sums = outs
        grad = ins[0][...].astype(F32)
        for ref in ins[1:-2]:
            grad = grad + ref[...].astype(F32)
        rows = rows()[...]
        center = rows - jnp.mean(rows, axis=-1, keepdims=True)
        inverse = lax.rsqrt(jnp.mean(center * center, axis=-1, keepdims=True) + 1e-05)
        unit = center * inverse
        sums[:, :D] = jnp.sum(grad * unit, axis=0, keepdims=True)
        sums[:, D : 2 * D] = jnp.sum(grad, axis=0, keepdims=True)
        grad = grad * params[:, gain_at : gain_at + D]
        along = jnp.mean(grad * unit, axis=-1, keepdims=True)
        grad = inverse * (grad - jnp.mean(grad, axis=-1, keepdims=True) - unit * along)
        wide_out[...] = grad
        low = grad.astype(BF)
        low_out[...] = low
        sums[:, 2 * D :] = jnp.sum(low.astype(F32), axis=0, keepdims=True)

    outs = [((T, D), F32), ((T, D), BF), ((1, 3 * D), F32)]
    return call(kernel, [near(item) for item in parts] + [held(rows), near(params)], outs, [], 20 * T * D, SMALL)


def roll_halves(x):
    return pltpu.roll(x, x.shape[1] // 2, 1)


def load_attn(full, w_in, w_out):
    far = full.shape[0]
    D, cols = w_in.shape
    rows, wide = D // far, w_out.shape[0]
    part = wide // far
    for o in range(far):
        w_in[o * rows : (o + 1) * rows] = full[o, :rows, :cols]
        for j in range(rows // part):
            w_out[o * part : (o + 1) * part, j * wide : (j + 1) * wide] = full[o, j * part : (j + 1) * part, cols:]


def load_ffn(full, w_up, w_down):
    far = full.shape[0]
    D, H = w_up.shape
    up, down = D // far, H // far
    for o in range(far):
        w_up[o * up : o * up + up // 2] = full[o, : up // 2, :H]
        w_up[o * up + up // 2 : (o + 1) * up] = full[o, : up // 2, H:]
        w_down[o * down : (o + 1) * down] = full[o, up // 2 : up // 2 + down]


def rotary(table, rows, half):
    cos, sin = table[rows, :half], table[rows, half : 2 * half]
    return jnp.concatenate([cos, cos, cos, cos], axis=1), jnp.concatenate([-sin, -sin, sin, sin], axis=1)


def attn_forward(blocks, full, bias, bias_at, table, seg_row, half, scale):
    n = len(blocks)
    T, D = blocks[0].shape
    wide = 4 * half
    N = n * T
    step = 4
    across_block = N

    def kernel(ins, outs, scratch):
        full, table, bias, seg_row = ins[n:]
        (qkv, leave_qkv), (context, leave_context), (logs, leave_logs), even, odd = outs
        w_in, w_out, x, values_t, context_t, x_sems = scratch
        copies = block_copies(ins[:n], x, x_sems)
        start_all(copies)
        load_attn(full(), w_in, w_out)
        table = table()
        for k in range(0, n, step):
            wait_all(copies[k : k + step])
            rows = slice(k * T, (k + step) * T)
            mixed = dot(x[rows], w_in[...]) + bias[:, bias_at : bias_at + 3 * wide]
            cos, sin = rotary(table, rows, half)
            for t, factor in ((0, scale), (1, 1.0)):
                part = mixed[:, t * wide : (t + 1) * wide]
                part = (part * cos + roll_halves(part) * sin).astype(BF)
                qkv[rows, t * wide : (t + 1) * wide] = part * jnp.asarray(factor, BF)
            qkv[rows, 2 * wide :] = mixed[:, 2 * wide :].astype(BF)
        leave_qkv()
        values_t[...] = qkv[:, 2 * wide :].T
        first_qk, _ = head_masks(wide)
        zero = jnp.zeros((), BF)

        def part(c, carry):
            at = pl.ds(pl.multiple_of(c * across_block, 128), across_block)
            allowed = table[:, 2 * half : 2 * half + 1] == seg_row[:, at]
            for head in range(2):
                mine = first_qk if head == 0 else jnp.logical_not(first_qk)
                query = jnp.where(mine, qkv[at, :wide], zero)
                scores = jnp.where(allowed, dot_rt(qkv[:, wide : 2 * wide], query), NEG_FILL)
                top = jnp.max(scores, axis=0, keepdims=True)
                weights = jnp.exp(scores - top)
                total = jnp.sum(weights, axis=0, keepdims=True)
                heads = slice(head * 2 * half, (head + 1) * 2 * half)
                context_t[heads, at] = dot(values_t[heads, :], weights.astype(BF)) * (1.0 / total)
                logs[head : head + 1, at] = top + jnp.log(total)
            return carry

        lax.fori_loop(0, N // across_block, part, 0)
        leave_logs()
        context[...] = context_t[...].T.astype(BF)
        leave_context()
        for k in range(0, n, step):
            put_blocks(dot(context[k * T : (k + step) * T], w_out[...]).astype(BF), k, (even, odd), T)

    outs = [((N, 3 * wide), BF, True), ((N, wide), BF, True), ((2, N), F32, True)]
    outs += [((n // 2, T, D), BF, n // 2), ((n // 2, T, D), BF, n // 2)]
    flops = 2 * N * D * 4 * wide + 8 * N * N * wide
    sems = pltpu.SemaphoreType.DMA
    scratch = [((D, 3 * wide), BF), ((wide, D), BF), ((N, D), BF), ((wide, N), BF), ((wide, N), F32), sems((n,))]
    ins = [raw(item) for item in blocks] + [held(full), held(table), near(bias), near(seg_row)]
    return call(kernel, ins, outs, scratch, flops)


def lanes_of(count):
    return max(w for w in (384, 256, 128) if count % w == 0)


def fetch_ffn(full, w_up, w_down, sems):
    far = full.shape[0]
    D, H = w_up.shape
    up, down = D // far, H // far
    first, second = [], []
    for o in range(far):
        for part in range(2):
            first.append(
                pltpu.make_async_copy(
                    full.at[o, pl.ds(0, up // 2), pl.ds(part * H, H)],
                    w_up.at[pl.ds(o * up + part * (up // 2), up // 2)],
                    sems.at[3 * o + part],
                )
            )
        second.append(
            pltpu.make_async_copy(
                full.at[o, pl.ds(up // 2, down)], w_down.at[pl.ds(o * down, down)], sems.at[3 * o + 2]
            )
        )
    return first, second


def start_all(copies):
    for copy in copies:
        copy.start()


def wait_all(copies):
    for copy in copies:
        copy.wait()


def block_copies(blocks, whole, sems):
    T = blocks[0].shape[0]
    return [pltpu.make_async_copy(block, whole.at[pl.ds(k * T, T)], sems.at[k]) for k, block in enumerate(blocks)]


def ffn_forward(blocks, full, bias, bias_at, H):
    n = len(blocks)
    T, D = blocks[0].shape
    step = 4

    def kernel(ins, outs, scratch):
        full, bias = ins[n:]
        (act, leave_act), (slope, leave_slope), even, odd = outs
        w_up, w_down, x, w_sems, x_sems = scratch
        first, second = fetch_ffn(full, w_up, w_down, w_sems)
        copies = block_copies(ins[:n], x, x_sems)
        start_all(first)
        start_all(copies)
        start_all(second)
        wait_all(first)
        for k in range(0, n, step):
            wait_all(copies[k : k + step])
            rows = slice(k * T, (k + step) * T)
            pre = dot(x[rows], w_up[...]) + bias[:, bias_at : bias_at + H]
            below = 0.5 * (1.0 + lax.erf(pre * math.sqrt(0.5)))
            result = (pre * below).astype(BF)
            act[rows] = result
            slope[rows] = (below + pre * (math.sqrt(0.5 / math.pi) * jnp.exp(-0.5 * pre * pre))).astype(BF)
            if k == 0:
                wait_all(second)
            back = dot(act[rows], w_down[...]).astype(BF)
            put_blocks(back, k, (even, odd), T)
        leave_act()
        leave_slope()

    outs = [((n * T, H), BF, True), ((n * T, H), BF, True), ((n // 2, T, D), BF, n // 2), ((n // 2, T, D), BF, n // 2)]
    ins = [raw(item) for item in blocks] + [raw(full), near(bias)]
    sems = pltpu.SemaphoreType.DMA
    scratch = [((D, H), BF), ((H, D), BF), ((n * T, D), BF), sems((3 * full.shape[0],)), sems((n,))]
    return call(kernel, ins, outs, scratch, 4 * n * T * D * H)


def put_blocks(rows, first, halves, T):
    for i in range(rows.shape[0] // T):
        out, leave = halves[(first + i) % 2]
        out[(first + i) // 2] = rows[i * T : (i + 1) * T]
        leave((first + i) // 2)


def ffn_back(blocks, full, slope):
    n = len(blocks)
    T, D = blocks[0].shape
    H = slope.shape[1]
    step = 4

    def kernel(ins, outs, scratch):
        full, slope = ins[n:]
        grad_pre, bias_grad, even, odd = outs
        w_up, w_down, x, w_sems, x_sems = scratch
        first, second = fetch_ffn(full, w_up, w_down, w_sems)
        copies = block_copies(ins[:n], x, x_sems)
        start_all(second)
        start_all(copies)
        start_all(first)
        wait_all(second)
        total = jnp.zeros((1, H), F32)
        for k in range(0, n, step):
            wait_all(copies[k : k + step])
            rows = slice(k * T, (k + step) * T)
            grad = (dot_rt(x[rows], w_down[...]) * slope()[rows].astype(F32)).astype(BF)
            grad_pre[rows] = grad
            total = total + jnp.sum(grad.astype(F32), axis=0, keepdims=True)
            if k == 0:
                wait_all(first)
            put_blocks(dot_rt(grad_pre[rows], w_up[...]).astype(BF), k, (even, odd), T)
        bias_grad[...] = total

    outs = [((n * T, H), BF), ((1, H), F32), ((n // 2, T, D), BF, n // 2), ((n // 2, T, D), BF, n // 2)]
    ins = [raw(item) for item in blocks] + [raw(full), held(slope)]
    sems = pltpu.SemaphoreType.DMA
    scratch = [((D, H), BF), ((H, D), BF), ((n * T, D), BF), sems((3 * full.shape[0],)), sems((n,))]
    return call(kernel, ins, outs, scratch, 4 * n * T * D * H)


def ffn_weights(normed, grads, act, grad_pre, far, extra):
    n = len(normed)
    T, D = normed[0].shape
    N = n * T
    H = act.shape[1]
    up, down = D // far, H // far
    more = [] if extra is None else [near(extra)]
    count = up // 2 + down + (0 if extra is None else extra.shape[1])

    def kernel(ins, outs, scratch):
        act, grad_pre = ins[2 * n : 2 * n + 2]
        left, right, left_sems, right_sems = scratch
        out = outs[0]
        copies = block_copies(ins[:n], left, left_sems)
        later = block_copies(ins[n : 2 * n], right, right_sems)
        start_all(copies)
        start_all(later)
        wait_all(copies)
        for o in range(far):
            block = dot_lt(left[:, o * up : (o + 1) * up], grad_pre[...]).astype(BF)
            out[o, : up // 2, :H] = block[: up // 2]
            out[o, : up // 2, H:] = block[up // 2 :]
        wait_all(later)
        act = act()
        for o in range(far):
            block = dot_lt(act[:, o * down : (o + 1) * down], right[...]).astype(BF)
            out[o, up // 2 : up // 2 + down] = block
            if more:
                out[o, up // 2 + down :] = ins[2 * n + 2][o]

    sems = pltpu.SemaphoreType.DMA
    scratch = [((N, D), BF), ((N, D), BF), sems((n,)), sems((n,))]
    ins = [raw(item) for item in (*normed, *grads)] + [held(act), near(grad_pre)] + more
    return call(kernel, ins, [((far, count, D), BF)], scratch, 4 * N * D * H, light=False)[0]


def attn_back(blocks, full, qkv, context, logs, table, seg_row, half, scale):
    n = len(blocks)
    T, D = blocks[0].shape
    wide = 4 * half
    N = n * T
    step = 4
    across_block = lanes_of(N)

    def kernel(ins, outs, scratch):
        full, table, qkv, context, logs, seg_row = ins[n:]
        mixed, bias_grad, even, odd = outs
        w_in, w_out, x, grad, delta, cos, sin, acc_k, acc_v, x_sems = scratch
        copies = block_copies(ins[:n], x, x_sems)
        start_all(copies)
        load_attn(full(), w_in, w_out)
        for k in range(0, n, step):
            wait_all(copies[k : k + step])
            rows = slice(k * T, (k + step) * T)
            grad[rows] = dot_rt(x[rows], w_out[...]).astype(BF)
        table = table()
        cos[...], sin[...] = rotary(table, slice(None), half)
        acc_k[...] = jnp.zeros_like(acc_k)
        acc_v[...] = jnp.zeros_like(acc_v)
        qkv, logs = qkv(), logs()
        product = (grad[...].astype(F32) * context()[...].astype(F32)).T
        delta[0:1] = jnp.sum(product[: 2 * half], axis=0, keepdims=True)
        delta[1:2] = jnp.sum(product[2 * half :], axis=0, keepdims=True)
        first_qk, first_v = head_masks(wide)
        zero = jnp.zeros((), BF)

        def part(c, carry):
            at = pl.ds(pl.multiple_of(c * across_block, 128), across_block)
            allowed = table[:, 2 * half : 2 * half + 1] == seg_row[:, at]
            grad_query = []
            for head in range(2):
                mine = first_qk if head == 0 else jnp.logical_not(first_qk)
                mine_v = first_v if head == 0 else jnp.logical_not(first_v)
                query = jnp.where(mine, qkv[at, :wide], zero)
                grad_h = jnp.where(mine_v, grad[at, :], zero)
                scores = dot_rt(qkv[:, wide : 2 * wide], query) - logs[head : head + 1, at]
                probs = jnp.exp(jnp.where(allowed, scores, NEG_FILL))
                grad_probs = dot_rt(qkv[:, 2 * wide :], grad_h)
                grad_scores = (probs * (grad_probs - delta[head : head + 1, at])).astype(BF)
                acc_k[...] += dot(grad_scores, query)
                acc_v[...] += dot(probs.astype(BF), grad_h)
                grad_query.append(dot_lt(grad_scores, qkv[:, wide : 2 * wide]))
            result = jnp.where(first_qk, grad_query[0], grad_query[1]) * scale
            mixed[at, :wide] = (result * cos[at, :] - roll_halves(result) * sin[at, :]).astype(BF)
            return carry

        lax.fori_loop(0, N // across_block, part, 0)
        total = acc_k[...]
        mixed[:, wide : 2 * wide] = (total * cos[...] - roll_halves(total) * sin[...]).astype(BF)
        mixed[:, 2 * wide :] = acc_v[...].astype(BF)
        sums = jnp.zeros((1, 3 * wide), F32)
        for k in range(0, n, step):
            rows = slice(k * T, (k + step) * T)
            sums = sums + jnp.sum(mixed[rows].astype(F32), axis=0, keepdims=True)
            put_blocks(dot_rt(mixed[rows], w_in[...]).astype(BF), k, (even, odd), T)
        bias_grad[...] = sums

    outs = [((N, 3 * wide), BF), ((1, 3 * wide), F32), ((n // 2, T, D), BF, n // 2), ((n // 2, T, D), BF, n // 2)]
    scratch = [((D, 3 * wide), BF), ((wide, D), BF), ((N, D), BF), ((N, wide), BF), ((2, N), F32)]
    scratch += [((N, wide), F32)] * 4 + [pltpu.SemaphoreType.DMA((n,))]
    flops = 2 * N * D * 4 * wide + 20 * N * N * wide
    ins = [raw(item) for item in blocks] + [held(item) for item in (full, table, qkv, context, logs)] + [near(seg_row)]
    return call(kernel, ins, outs, scratch, flops)


def attn_weights(inputs, grads, context, mixed, bias_grad, far, relative):
    n = len(inputs)
    T, D = inputs[0].shape
    N = n * T
    wide = context.shape[1]
    rows = D // far
    part = wide // far
    size = lax.axis_size("row")

    def kernel(ins, outs, scratch):
        context, mixed, bias_grad = ins[2 * n :]
        left, right, left_sems, right_sems = scratch
        here = (lax.axis_index("seq") * size + lax.axis_index("row")) // PLANE
        copies = block_copies(ins[:n], left, left_sems)
        later = block_copies(ins[n : 2 * n], right, right_sems)
        start_all(copies)
        start_all(later)
        wait_all(copies)
        for k in range(far):
            if relative:
                lanes = pl.ds(pl.multiple_of((here ^ k) * rows, 128), rows)
                outs[k][:rows, : 3 * wide] = dot_lt(left[:, lanes], mixed[...]).astype(BF)
            else:
                outs[0][k, :rows, : 3 * wide] = dot_lt(left[:, k * rows : (k + 1) * rows], mixed[...]).astype(BF)
        wait_all(later)
        whole = dot_lt(context()[...], right[...]).astype(BF)
        extra = jnp.broadcast_to(bias_grad[...], (16, 3 * wide)).astype(BF)
        if relative:
            right[:wide, :D] = whole
        for k in range(far):
            out = outs[k] if relative else outs[0].at[k]
            if relative:
                block = right[pl.ds(pl.multiple_of((here ^ k) * part, 16), part), :]
            else:
                block = whole[k * part : (k + 1) * part]
            for j in range(rows // part):
                out[j * part : (j + 1) * part, 3 * wide :] = block[:, j * wide : (j + 1) * wide]
            out[rows:, : 3 * wide] = extra
            out[rows:, 3 * wide :] = jnp.zeros((16, wide), BF)

    sems = pltpu.SemaphoreType.DMA
    scratch = [((N, D), BF), ((N, D), BF), sems((n,)), sems((n,))]
    ins = [raw(item) for item in (*inputs, *grads)] + [held(context), near(mixed), near(bias_grad)]
    if relative:
        outs = [((rows + 16, 4 * wide), BF)] * far
    else:
        outs = [((far, rows + 16, 4 * wide), BF)]
    return call(kernel, ins, outs, scratch, 8 * N * D * wide, light=False)


def plane_index():
    return lax.axis_index("seq") % (PLANE // lax.axis_size("row")) * lax.axis_size("row") + lax.axis_index("row")


def head_kernel(blocks, own, codes, own_codes, positive, temp, w_col, loss_weight):
    n = len(blocks)
    T, C = own.shape
    N = n * T
    D = w_col.shape[0]
    slots = NQ * QLEN

    def kernel(ins, outs, scratch):
        own, codes, own_codes, positive, temp, w_col = ins[n:]
        grad, low, terms = outs
        held, embeds = scratch
        here = plane_index()
        upper = lax.rem(lax.axis_index("seq") // (PLANE // lax.axis_size("row")), 2)

        def place(c):
            column = lax.rem(c // 2, 2) ^ upper
            return pl.ds(pl.multiple_of((4 * column + 2 * lax.rem(c, 2) + c // 4) * T, 16), T)

        for k in range(n):
            held[place(here ^ k), :] = ins[k][...]
        lane = lax.broadcasted_iota(jnp.int32, (1, C), 1)
        slot = lax.broadcasted_iota(jnp.int32, (slots, 1), 0)
        doc, own_doc = codes[0:1, :], own_codes[0:1, :]
        select = jnp.where(codes[1:2, :] == slot, 1.0, 0.0).astype(BF)
        own_select = jnp.where(own_codes[1:2, :] == slot, 1.0, 0.0).astype(BF)
        rows = held[...].astype(F32)
        mine = own[...]
        heat = temp[...]
        wanted = lane == positive[...]
        valid = lane <= NSD
        loss = jnp.zeros((1, 1), F32)
        heat_grad = jnp.zeros((1, 1), F32)
        total = jnp.zeros((T, C), F32)
        for width in (C, C * 3 // 4, C // 2):
            inside = lane < width
            size = jnp.sum(jnp.where(inside, rows * rows, 0.0), axis=1, keepdims=True)
            embed = jnp.where(inside, rows * lax.rsqrt(size + 1e-06), 0.0).astype(BF)
            embeds[...] = embed
            query = dot(select, embed).astype(BF)
            powers = jnp.exp(SHARPNESS * dot_rt(query, embed))
            soft = jnp.zeros((slots, C), F32)
            sums = []
            for d in range(NSD + 1):
                sums.append(jnp.sum(jnp.where(doc == d, powers, 0.0), axis=1, keepdims=True))
                soft = jnp.where(lane == d, jnp.log(sums[d]) / SHARPNESS, soft)
            pair = jnp.sum(soft.reshape(NQ, QLEN, C), axis=1, keepdims=True)
            pair = jnp.broadcast_to(pair, (NQ, QLEN, C)).reshape(slots, C)
            logits = pair * heat / QLEN
            masked = jnp.where(valid, logits, NEG_FILL)
            top = jnp.max(masked, axis=1, keepdims=True)
            shares = jnp.exp(masked - top)
            share_sum = jnp.sum(shares, axis=1, keepdims=True)
            chosen = jnp.sum(jnp.where(wanted, logits, 0.0), axis=1, keepdims=True)
            losses = top + jnp.log(share_sum) - chosen
            loss = loss + jnp.sum(losses, axis=0, keepdims=True) * (loss_weight / QLEN)
            grad_logits = loss_weight * (shares / share_sum - jnp.where(wanted, 1.0, 0.0))
            along = jnp.sum(jnp.where(valid, grad_logits * logits, 0.0), axis=1, keepdims=True)
            heat_grad = heat_grad + jnp.sum(along, axis=0, keepdims=True) / QLEN
            grad_soft = grad_logits * heat / QLEN
            weight = jnp.zeros((slots, N), F32)
            own_weight = jnp.zeros((slots, T), F32)
            for d in range(NSD + 1):
                ratio = grad_soft[:, d : d + 1] / sums[d]
                weight = jnp.where(doc == d, ratio, weight)
                own_weight = jnp.where(own_doc == d, ratio, own_weight)
            grad_query = dot((powers * weight).astype(BF), embed)
            own_embed = embeds[place(here), :]
            own_powers = jnp.exp(SHARPNESS * dot_rt(query, own_embed))
            grad_embed = dot_lt((own_powers * own_weight).astype(BF), query)
            high = grad_query.astype(BF)
            rest = (grad_query - high.astype(F32)).astype(BF)
            grad_embed = grad_embed + dot_lt(own_select, high) + dot_lt(own_select, rest)
            size = jnp.sum(jnp.where(inside, mine * mine, 0.0), axis=1, keepdims=True)
            inverse = lax.rsqrt(size + 1e-06)
            along = jnp.sum(jnp.where(inside, grad_embed * mine, 0.0), axis=1, keepdims=True)
            part = inverse * grad_embed - mine * (inverse * inverse * inverse * along)
            total = total + jnp.where(inside, part, 0.0)
        low[...] = total.astype(BF)
        grad[...] = dot_rt(total.astype(BF), w_col[...])
        terms[...] = jnp.where(lane == 0, loss, jnp.where(lane == 1, heat_grad, 0.0))

    outs = [((T, D), F32), ((T, C), BF), ((1, C), F32)]
    ins = [near(item) for item in (*blocks, own, codes, own_codes, positive, temp, w_col)]
    return call(kernel, ins, outs, [((N, C), BF), ((N, C), BF)], 24 * slots * N * C, 40)


def swap_quarters(x):
    q = x.shape[1] // 4
    return jnp.concatenate([x[:, :q], x[:, 2 * q : 3 * q], x[:, q : 2 * q], x[:, 3 * q :]], axis=1)


def pack_first(w, small):
    rows, width = w.shape
    D, wide = width // 3, width // 3 // PLANE
    count = rows + small.shape[0]

    def kernel(ins, outs, _):
        w, small = ins
        here = plane_index()
        for k in range(PLANE):
            out = outs[k % 2].at[k // 2]
            for t in range(3):
                columns = w[:, pl.ds(pl.multiple_of(t * D + (here ^ k) * wide, 128), wide)]
                out[:rows, t * wide : (t + 1) * wide] = swap_quarters(columns) if t < 2 else columns
            out[rows:] = small[...]

    outs = [((PLANE // 2, count, 3 * wide), BF)] * 2
    return call(kernel, [near(w), near(small)], outs, [], w.size, SMALL)


def unpack_first(even, core, got, out_rows):
    rows, D = out_rows.shape
    count, cols = even.shape[1:]
    wide = cols // 3

    def kernel(ins, outs, _):
        even, core, *got, out_rows = ins
        block, below = outs
        here = plane_index()
        blocks = [even.at[0], core.at[0]] + [ref.at[j] for ref in got for j in range(2)]
        for k in range(PLANE):
            of = here ^ k
            block[pl.ds(pl.multiple_of(of * rows, 16), rows), :cols] = blocks[k][:rows]
            below[of] = blocks[k][rows:]
            block[k * rows : (k + 1) * rows, cols:] = out_rows[:, k * wide : (k + 1) * wide]

    outs = [((PLANE * rows, cols + wide), BF), ((PLANE, count - rows, cols), BF)]
    return call(kernel, [near(item) for item in (even, core, *got, out_rows)], outs, [], even.size, SMALL)


def pack_shares(sums, others, ffn, lines, in_cols, hidden_cols):
    rows, width = sums[0].shape[0] - 16, sums[0].shape[1]
    part = rows // PLANE
    L = len(ffn)
    count = L * (in_cols + hidden_cols) + 128
    bias_lines = in_cols // 128
    first_line = part - L * bias_lines

    def kernel(ins, outs, scratch):
        even, odd, last = outs
        attn = scratch[0]
        n = len(sums)
        total = ins[0][...].astype(F32)
        for ref in ins[1:n]:
            total = total + ref[...].astype(F32)
        attn[0] = total.astype(BF)
        for layer in range(1, L):
            attn[layer] = ins[n + layer - 1][...]
        last[...] = attn[0, :rows, in_cols:]
        ups = ins[n + L - 1 : n + 2 * L - 1]
        lines = ins[n + 2 * L - 1]
        here = plane_index()
        line = lax.broadcasted_iota(jnp.int32, (part, 128), 0)
        for k in range(PLANE):
            to = here ^ k
            out = (odd if k % 2 else even).at[k // 2]
            at = pl.ds(pl.multiple_of(to * part, 16), part)
            half = pl.ds(pl.multiple_of(lax.rem(to, PLANE // 2) * part, 16), part)
            for layer in range(L):
                out[:, layer * in_cols : (layer + 1) * in_cols] = attn[layer, at, :in_cols]
                folded = ups[layer][half, :]
                own = jnp.where(to < PLANE // 2, folded[:, :hidden_cols], folded[:, hidden_cols:])
                start = L * in_cols + layer * hidden_cols
                out[:, start : start + hidden_cols] = own
            block = lines[to]
            for layer in range(L):
                bias = attn[layer, rows : rows + 16, :in_cols].astype(F32)[:1]
                for j in range(bias_lines):
                    spot = line == first_line + layer * bias_lines + j
                    block = jnp.where(spot, bias[:, j * 128 : (j + 1) * 128], block)
            out[:, count - 128 :] = block.astype(BF)

    half = PLANE // 2
    outs = [((half, part, count), BF), ((half, part, count), BF), ((rows, width - in_cols), BF)]
    ins = [near(item) for item in (*sums, *others, *ffn, lines)]
    return call(kernel, ins, outs, [((L, rows + 16, width), BF)], rows * count, SMALL)


def unpack_shares(even, core, got, L, in_cols, hidden_cols):
    part, count = even.shape[1:]
    wide = in_cols // 3
    D, far = PLANE * wide, hidden_cols // 128
    bias_lines = in_cols // 128
    first_line = part - L * bias_lines

    def natural(x):
        q = wide // 4
        return jnp.concatenate([x[:, :q], x[:, 2 * q : 3 * q], x[:, q : 2 * q], x[:, 3 * q :]], axis=1)

    def kernel(ins, outs, scratch):
        even, core, *got = ins
        w_in, w_up, lines, bias = outs
        here = plane_index()
        blocks = [even.at[0], core.at[0]] + [ref.at[j] for ref in got for j in range(2)]
        total = jnp.zeros((part, 128), F32)
        for k in range(PLANE):
            block = blocks[k][...].astype(F32)
            of = here ^ k
            own_lines = block[:, count - 128 :]
            total = total + own_lines
            for layer in range(L):
                for t in range(3):
                    at = pl.ds(pl.multiple_of(t * D + of * wide, 128), wide)
                    start = layer * in_cols + t * wide
                    columns = block[:, start : start + wide]
                    row = first_line + layer * bias_lines + t
                    line = own_lines[row : row + 1]
                    if t < 2:
                        columns, line = natural(columns), natural(line)
                    w_in[layer, :, at] = columns
                    bias[layer, :, at] = line
                for o in range(far):
                    at = pl.ds(pl.multiple_of(o * PLANE * 128 + of * 128, 128), 128)
                    start = L * in_cols + layer * hidden_cols + o * 128
                    w_up[layer, :, at] = block[:, start : start + 128]
        lines[...] = total

    outs = [((L, part, 3 * D), F32), ((L, part, far * PLANE * 128), F32), ((part, 128), F32), ((L, 1, 3 * D), F32)]
    ins = [near(item) for item in (even, core, *got)]
    return call(kernel, ins, outs, [], part * count * PLANE, SMALL)


def body(
    tokens,
    attn_in,
    attn_out,
    ffn_up,
    ffn_down,
    norm_gains,
    biases,
    colbert,
    log_scale,
    cotangent,
    seg_lengths,
    seg_kinds,
    pairing,
):
    S = lax.axis_size("seq")
    R = lax.axis_size("row")
    O = S * R // PLANE
    place = lax.axis_index("seq") * R + lax.axis_index("row")
    plane, far = place % PLANE, place // PLANE
    relative = jnp.bitwise_xor(plane, jnp.arange(PLANE, dtype=jnp.int32))
    T = tokens.shape[1]
    D = tokens.shape[2]
    N = PLANE * T
    L = attn_in.shape[0]
    head_dim = D // HEADS
    half = head_dim // 2
    scale = head_dim ** (-0.5)
    wide = 2 * head_dim
    in_cols = 3 * wide
    in_rows = attn_in.shape[1]
    rows_in = PLANE * in_rows
    FF = ffn_up.shape[2]
    up_cols = FF // (S * R)
    hidden_cols = O * up_cols
    gain_part = norm_gains.shape[1]
    bias_part = biases.shape[1]
    part = gain_part + bias_part
    along_z = [[o * (S // O) + i for o in range(O)] for i in range(S // O)]
    is_mine = jnp.arange(PLANE, dtype=jnp.int32) == plane

    def padded_rows(vector, width=D):
        rows = -(-vector.shape[0] // (16 * width)) * 16
        return jnp.pad(vector, (0, rows * width - vector.shape[0])).reshape(rows, width)

    def pack_columns(w):
        lead = w.shape[:-1]
        n = len(lead)
        qk = w[..., : 2 * D].reshape(*lead, 2, PLANE, 2, 2, half)
        qk = qk.transpose((n + 1,) + tuple(range(n)) + (n, n + 3, n + 2, n + 4)).reshape(PLANE, *lead, 2 * wide)
        v = w[..., 2 * D :].reshape(*lead, PLANE, wide)
        v = v.transpose((n,) + tuple(range(n)) + (n + 1,))
        return jnp.concatenate([qk, v], axis=-1)

    def unpack_columns(w):
        rows = w.shape[1]
        qk = w[:, :, : 2 * wide].reshape(PLANE, rows, 2, 2, 2, half)
        qk = qk.transpose(1, 2, 0, 4, 3, 5).reshape(rows, 2 * D)
        v = w[:, :, 2 * wide :].transpose(1, 0, 2).reshape(rows, D)
        return jnp.concatenate([qk, v], axis=1)

    def pack_hidden(w):
        rows = w.shape[0]
        return w.reshape(rows, O, PLANE, up_cols).transpose(2, 0, 1, 3).reshape(PLANE, rows, hidden_cols)

    def unpack_hidden(w):
        rows = w.shape[1]
        return w.reshape(PLANE, rows, O, up_cols).transpose(1, 2, 0, 3).reshape(rows, FF)

    def fold(w):
        n = w.shape[-2] // 2
        return jnp.concatenate([w[..., :n, :], w[..., n:, :]], axis=-1)

    def unfold(w):
        n = w.shape[-1] // 2
        return jnp.concatenate([w[..., :n], w[..., n:]], axis=-2)

    to_group = [(b, (b % O) * PLANE + b // O) for b in range(O * PLANE)]
    from_group = [(d, b) for b, d in to_group]
    small = jnp.concatenate([norm_gains.reshape(-1), biases.reshape(-1), colbert.reshape(-1)])
    even, odd = pack_first(attn_in[0], padded_rows(small, in_cols))
    core = across(odd, 1)
    got = tie(*[across(jnp.stack([even[k], core[k]]), 2 * k) for k in (1, 2, 3)])
    shard_out = lax.ppermute(attn_out, BOTH, to_group)
    table = turned(jnp.concatenate([seg_lengths[0], seg_kinds[0], pairing[0]]))
    seg_count = seg_lengths.shape[1]
    lengths, kinds = table[:seg_count], table[seg_count : 2 * seg_count]
    pairs_of = table[2 * seg_count :]
    hidden_low = turned(tokens[0])

    def attn_block(layer, shard):
        out = shard_out[layer].reshape(in_rows, PLANE, wide).transpose(1, 0, 2).reshape(rows_in, wide)
        return jnp.concatenate([shard, out], axis=1)

    def gather_far(x):
        return lax.all_gather(x, "seq", axis=0, axis_index_groups=along_z)

    own, small = unpack_first(even, core, got, shard_out[0])
    small = small.reshape(PLANE, -1)
    full_attn = [gather_far(own)]
    count_small = L * part
    col_plane = small[:, count_small : count_small + colbert.size].reshape(-1)
    params = small[None, :, :count_small]
    step = 1
    while step < O:
        other = across(params, PLANE * step)
        low_side = (far & step) == 0
        params = jnp.concatenate([jnp.where(low_side, params, other), jnp.where(low_side, other, params)], axis=0)
        step *= 2
    params = params.reshape(O * PLANE, count_small).astype(F32)
    gains_all = params[:, : L * gain_part].reshape(O * PLANE, L, gain_part).transpose(1, 0, 2).reshape(L, 2 * D)
    bias_all = params[:, L * gain_part :].reshape(O * PLANE, L, bias_part).transpose(1, 0, 2).reshape(L, -1)
    in_biases = pick(pack_columns(bias_all[:, : 3 * D]), plane, axis=0).reshape(1, L * in_cols)
    up_biases = pick(pack_hidden(bias_all[:, 4 * D : 4 * D + FF]), plane, axis=0).reshape(1, L * hidden_cols)
    rest_at = 4 * D + FF
    params = jnp.concatenate([gains_all, bias_all[:, 3 * D : 4 * D], bias_all[:, rest_at:]], axis=1).reshape(1, -1)
    GAIN_ONE, GAIN_TWO, BIAS_OUT, BIAS_DOWN, SHIFT_ONE, SHIFT_TWO = range(6)

    def at(layer, which):
        return (layer * 6 + which) * D

    rest = jnp.concatenate(
        [pack_hidden(ffn_up[0])]
        + [piece for layer in range(1, L) for piece in (pack_columns(attn_in[layer]), pack_hidden(ffn_up[layer]))],
        axis=-1,
    )
    rest = plane_exchange(rest, relative).reshape(rows_in, -1)
    full_ffn = []
    start = 0
    for layer in range(L):
        if layer > 0:
            full_attn.append(gather_far(attn_block(layer, rest[:, start : start + in_cols])))
            start += in_cols
        own = [fold(rest[:, start : start + hidden_cols]), ffn_down[layer]]
        start += hidden_cols
        if layer == L - 1:
            own.append(padded_rows(col_plane))
        full_ffn.append(gather_far(jnp.concatenate(own, axis=0)))
    w_col = full_ffn[L - 1][:, rows_in // 2 + up_cols :].reshape(O, -1)[:, : col_plane.size]
    w_col = w_col.reshape(D, colbert.shape[1])

    block_at = 4 * ((relative // 2 % 2) ^ (far % 2)) + 2 * (relative % 2) + relative // 4
    positions = (block_at[:, None] * T + jnp.arange(T, dtype=jnp.int32)[None, :]).reshape(N)
    held_segment, held_offset = token_info(positions, lengths, kinds)[:2]
    cos, sin = rope_angles(held_offset, head_dim)
    seg_row = held_segment.astype(F32)[None, :]
    table = jnp.concatenate([cos, sin, jnp.broadcast_to(seg_row.T, (N, wide - 2 * half))], axis=1)

    hidden = hidden_low
    records = []
    for layer in range(L):
        x_all = plane_gather(hidden_low)
        qkv, context, logs, even, odd = attn_forward(
            x_all, full_attn[layer], in_biases, layer * in_cols, table, seg_row, half, scale
        )
        terms, _ = plane_scatter(even, odd)
        first, normed, normed_low = add_norm(
            [hidden] + terms, params, at(layer, BIAS_OUT), at(layer, GAIN_ONE), at(layer, SHIFT_ONE)
        )
        normed_all = plane_gather(normed_low)
        act, slope, even, odd = ffn_forward(
            normed_all, full_ffn[layer], up_biases, layer * hidden_cols, hidden_cols
        )
        terms, _ = plane_scatter(even, odd)
        second, hidden, hidden_low = add_norm(
            [normed] + terms, params, at(layer, BIAS_DOWN), at(layer, GAIN_TWO), at(layer, SHIFT_TWO)
        )
        records.append((x_all, qkv, context, logs, first, normed_all, act, slope, second))
    hidden_out = turned(hidden_low, True)

    full_width = w_col.shape[1]
    row_positions = jnp.arange(N, dtype=jnp.int32)
    segment, offset, is_query, query_slot, doc_num = token_info(row_positions, lengths, kinds)
    codes = jnp.stack([jnp.where(is_query == 0, doc_num, -1), jnp.where(is_query == 1, query_slot, -1)])
    own_codes = lax.dynamic_slice(codes, (0, block_at[0] * T), (2, T))
    positive = jnp.repeat(pairs_of, QLEN)[:, None]
    temp = jnp.exp(log_scale)[None]
    hidden_low, cot = tie(hidden_low, cotangent[0])
    cot = turned(cot)
    col = dot(hidden_low, w_col)
    col_blocks = plane_gather(col.astype(BF))
    grad_out, grad_col_low, terms = head_kernel(
        col_blocks, col, codes, own_codes, positive, temp, w_col, 1.0 / (3 * NQ * R)
    )
    loss_terms = terms[0, :2]
    col_parts = dot_lt(hidden_low, grad_col_low).reshape(O, PLANE, in_rows, full_width).transpose(1, 0, 2, 3)
    col_parts = plane_sum(pick(col_parts.reshape(PLANE, O * in_rows, full_width), relative, axis=0))
    col_rows = jax.vmap(padded_rows)(col_parts.reshape(O, in_rows * full_width)).astype(BF)
    grad_parts = [cot, grad_out]

    def scatter_far(whole):
        whole = whole.reshape(-1, whole.shape[-1])
        return lax.psum_scatter(whole, "seq", scatter_dimension=0, tiled=True, axis_index_groups=along_z)

    outs = [[None] * L for _ in range(6)]

    def finish_out(layer, share_out):
        share_out = share_out.reshape(PLANE, in_rows, wide).transpose(1, 0, 2).reshape(in_rows, D)
        outs[1][layer] = lax.ppermute(share_out, BOTH, from_group).astype(F32)

    shares_ffn, shares_attn = [None] * L, [None] * L
    vectors = [None] * L
    for layer in reversed(range(L)):
        x_all, qkv, context, logs, first, normed_all, act, slope, second = records[layer]
        grad_second, grad_ffo, sums_two = norm_back(grad_parts, second, params, at(layer, GAIN_TWO))
        ffo_all = plane_gather(grad_ffo)
        if layer == L - 1:
            ffo_all, hidden_out = tie(ffo_all, hidden_out)
        grad_pre, grad_bias_up, even, odd = ffn_back(ffo_all, full_ffn[layer], slope)
        blocks = ffn_weights(normed_all, ffo_all, act, grad_pre, O, col_rows if layer == L - 1 else None)
        terms, blocks = plane_scatter(even, odd, blocks)
        shares_ffn[layer] = scatter_far(blocks)
        grad_first, grad_branch, sums_one = norm_back([grad_second] + terms, first, params, at(layer, GAIN_ONE))
        branch_all = plane_gather(grad_branch)
        if layer < L - 1:
            branch_all, shares_attn[layer + 1] = tie(branch_all, shares_attn[layer + 1])
        grad_mixed, grad_bias_in, even, odd = attn_back(
            branch_all, full_attn[layer], qkv, context, logs, table, seg_row, half, scale
        )

        gain_two, shift_two, down, gain_one, shift_one, out = [
            sums[0, k * D : (k + 1) * D] for sums in (sums_two, sums_one) for k in range(3)
        ]
        own_up = unpack_hidden(is_mine[:, None, None].astype(F32) * grad_bias_up[None])[0]
        gains = jnp.concatenate([gain_one, gain_two]).reshape(O, PLANE, gain_part)
        bias = jnp.concatenate([jnp.zeros((3 * D,), F32), out, own_up, down, shift_one, shift_two])
        vectors[layer] = jnp.concatenate([gains, bias.reshape(O, PLANE, bias_part)], axis=2)

        blocks = attn_weights(x_all, branch_all, context, grad_mixed, grad_bias_in, O, layer == 0)
        terms, blocks = plane_scatter(even, odd, blocks, layer == 0)
        terms, shares_ffn[layer] = tie(terms, shares_ffn[layer])
        if layer > 0:
            shares_attn[layer] = scatter_far(blocks[0])
            grad_parts = [grad_first] + terms

    got = [across(blocks[step], PLANE * step) for step in range(1, O)]
    entries = jnp.concatenate(vectors + [jnp.broadcast_to(loss_terms, (O, PLANE, 2))], axis=2)
    entries, terms = tie(entries, terms)
    lines = pick(entries, far)
    for step in range(1, O):
        lines = lines + across(pick(entries, far ^ step), PLANE * step)
    loss_terms = lines[0, L * part :]
    lines = jnp.pad(lines[:, : L * part], ((0, 0), (0, in_rows * 128 - L * part))).reshape(PLANE, in_rows, 128)
    grad_tokens = turned((grad_first + sum(item.astype(F32) for item in terms)).astype(BF), True)
    got, lines, grad_tokens = tie(got, lines, grad_tokens)
    even, odd, last_out = pack_shares([blocks[0]] + got, shares_attn[1:], shares_ffn, lines, in_cols, hidden_cols)
    core = across(odd, 1)
    got = tie(*[across(jnp.stack([even[k], core[k]]), 2 * k) for k in (1, 2, 3)])
    w_in_grad, w_up_grad, lines, bias_in_grad = unpack_shares(even, core, got, L, in_cols, hidden_cols)
    mine = lines.reshape(-1)
    bias_in_grad = jnp.pad(bias_in_grad[:, 0], ((0, 0), (0, O * PLANE * bias_part - 3 * D)))
    bias_in_grad = pick(bias_in_grad.reshape(L, O * PLANE, bias_part), place, axis=1)
    for layer in range(L):
        outs[3][layer] = shares_ffn[layer][rows_in // 2 : rows_in // 2 + up_cols]
        finish_out(layer, shares_attn[layer][:rows_in, in_cols:] if layer > 0 else last_out)
        outs[4][layer] = mine[layer * part : layer * part + gain_part]
        outs[5][layer] = mine[layer * part + gain_part : (layer + 1) * part] + bias_in_grad[layer]
    col_share = shares_ffn[L - 1][rows_in // 2 + up_cols :].reshape(-1)[: in_rows * full_width]
    col_share = col_share.reshape(in_rows, full_width).astype(F32)
    outs[0], outs[2] = w_in_grad, w_up_grad
    stacked = [jnp.stack(items).astype(F32) if isinstance(items, list) else items for items in outs]
    return (
        hidden_out[None],
        loss_terms[:1],
        grad_tokens.astype(F32)[None],
        stacked[0],
        stacked[1],
        stacked[2],
        stacked[3],
        stacked[4],
        stacked[5],
        col_share,
        loss_terms[1:],
    )


def joined_2(value, axis, join):
    pieces = jax.tree.map(lambda part: lax.all_gather(part, axis), value)
    head = jax.tree.map(lambda part: part[0], pieces)
    tail = jax.tree.map(lambda part: part[1:], pieces)
    so_far, _ = lax.scan(lambda so_far, section: (join(so_far, section), None), head, tail)
    return so_far


def rope_tables(offset, head_dim):
    half = head_dim // 2
    inverse = jnp.exp(jnp.arange(half, dtype=jnp.float32) * (-2.0 * math.log(10000.0) / head_dim))
    angle = offset.astype(jnp.float32)[:, None] * inverse[None, :]
    return (jnp.cos(angle), jnp.sin(angle))


def rotate(flat, cos_table, sin_table):
    length = flat.shape[0]
    head_dim = flat.shape[1] // HEADS
    half = head_dim // 2
    shaped = flat.reshape(length, HEADS, head_dim)
    first_half = shaped[..., :half]
    second_half = shaped[..., half:]
    cos_three = cos_table[:, None, :]
    sin_three = sin_table[:, None, :]
    turned = jnp.concatenate(
        [
            first_half * cos_three - second_half * sin_three,
            second_half * cos_three + first_half * sin_three,
        ],
        axis=-1,
    )
    return turned.reshape(length, flat.shape[1])


def block_for(count):
    blocks = count
    while blocks > 1024 and blocks % 2 == 0:
        blocks = blocks // 2
    return blocks


def merge_pair(first, second):
    max_first, sum_first = first
    max_second, sum_second = second
    top = jnp.maximum(max_first, max_second)
    return (top, sum_first * jnp.exp(max_first - top) + sum_second * jnp.exp(max_second - top))


def matmul_left_t(left, right):
    return jnp.einsum("ti,to->io", left, right, preferred_element_type=jnp.float32)


def matmul_right_t(left, right):
    return jnp.einsum("to,io->ti", left, right, preferred_element_type=jnp.float32)


def body_wide(
    tokens,
    attn_in,
    attn_out,
    ffn_up,
    ffn_down,
    norm_gains,
    biases,
    colbert,
    log_scale,
    cotangent,
    seg_lengths,
    seg_kinds,
    pairing,
):
    rank = lax.axis_index("seq")
    local_len = tokens.shape[1]
    model_width = tokens.shape[2]
    head_dim = model_width // HEADS
    scale = head_dim ** (-0.5)
    lengths = seg_lengths[0]
    kinds = seg_kinds[0]
    positions = rank * local_len + jnp.arange(local_len, dtype=jnp.int32)
    segment, offset, is_query, query_slot, doc_num = token_info(positions, lengths, kinds)
    cos_table, sin_table = rope_tables(offset, head_dim)
    layer_count = attn_in.shape[0]

    def split_pieces(key_piece, value_piece):
        count = key_piece.shape[0]
        blocks = block_for(count)
        key_seg = token_info(jnp.arange(count, dtype=jnp.int32), lengths, kinds)[0]
        key_blocks = key_piece.reshape(count // blocks, blocks, HEADS, head_dim)
        value_blocks = value_piece.reshape(count // blocks, blocks, HEADS, head_dim)
        seg_blocks = key_seg.reshape(count // blocks, blocks)
        return (count, blocks, key_blocks, value_blocks, seg_blocks)

    def attend_back(queries, keys, values, context, log_total, grad_context):
        query_three = queries.reshape(local_len, HEADS, head_dim)
        grad_three = grad_context.reshape(local_len, HEADS, head_dim)
        delta = jnp.sum(
            grad_three.astype(jnp.float32) * context.reshape(local_len, HEADS, head_dim), axis=-1
        ).T

        def score_grads(
            query_blk, grad_blk, key_blk, value_blk, query_seg, key_seg, total_blk, delta_blk
        ):
            scores = (
                jnp.einsum("qhd,khd->hqk", query_blk, key_blk, preferred_element_type=jnp.float32)
                * scale
            )
            allowed = (query_seg[:, None] == key_seg[None, :])[None]
            probs = jnp.where(allowed, jnp.exp(scores - total_blk[..., None]), 0.0)
            grad_probs = jnp.einsum(
                "qhd,khd->hqk", grad_blk, value_blk, preferred_element_type=jnp.float32
            )
            grad_scores = (probs * (grad_probs - delta_blk[..., None])).astype(jnp.bfloat16)
            return (probs, grad_scores)

        grad_query = jnp.zeros((local_len, HEADS, head_dim), jnp.float32)
        count, blocks, key_blocks, value_blocks, seg_blocks = split_pieces(
            lax.all_gather(keys, "seq", axis=0, tiled=True),
            lax.all_gather(values, "seq", axis=0, tiled=True),
        )

        def advance(grad_acc, item):
            key_blk, value_blk, seg_blk = item
            probs, grad_scores = score_grads(
                query_three, grad_three, key_blk, value_blk, segment, seg_blk, log_total, delta
            )
            grad_acc = grad_acc + scale * jnp.einsum(
                "hqk,khd->qhd", grad_scores, key_blk, preferred_element_type=jnp.float32
            )
            grad_key = scale * jnp.einsum(
                "hqk,qhd->khd", grad_scores, query_three, preferred_element_type=jnp.float32
            )
            grad_value = jnp.einsum(
                "hqk,qhd->khd",
                probs.astype(jnp.bfloat16),
                grad_three,
                preferred_element_type=jnp.float32,
            )
            joined = jnp.concatenate(
                [grad_key.reshape(blocks, model_width), grad_value.reshape(blocks, model_width)],
                axis=1,
            )
            return (grad_acc, joined)

        grad_query, pieces_out = lax.scan(
            advance, grad_query, (key_blocks, value_blocks, seg_blocks)
        )
        grad_rows = pieces_out.reshape(count, 2 * model_width)
        grad_query, grad_rows = (grad_query, grad_rows)
        summed = lax.psum_scatter(
            grad_rows.astype(jnp.bfloat16), "seq", scatter_dimension=0, tiled=True
        ).astype(jnp.float32)
        grad_key_out = summed[:, :model_width]
        grad_value_out = summed[:, model_width:]
        return (grad_query.reshape(local_len, model_width), grad_key_out, grad_value_out)

    def unpack(full):
        w_in, w_out, w_up, w_down, gains, bias = full[:6]
        hidden_units = w_up.shape[1]
        gains_f = gains.astype(jnp.float32)
        bias_f = bias.astype(jnp.float32)
        width_three = 3 * model_width
        return (
            w_in,
            w_out,
            w_up,
            w_down,
            hidden_units,
            gains_f[:model_width],
            gains_f[model_width:],
            bias_f[:width_three],
            bias_f[width_three : 4 * model_width],
            bias_f[4 * model_width : 4 * model_width + hidden_units],
            bias_f[4 * model_width + hidden_units : 5 * model_width + hidden_units],
            bias_f[5 * model_width + hidden_units : 6 * model_width + hidden_units],
            bias_f[6 * model_width + hidden_units :],
        )

    def layer_backward(grad_out, full, record):
        (
            w_in,
            w_out,
            w_up,
            w_down,
            hidden_units,
            gain_one,
            gain_two,
            bias_in,
            bias_out,
            bias_up,
            bias_down,
            shift_one,
            shift_two,
        ) = unpack(full)
        (
            inputs_low,
            queries,
            keys,
            values,
            context,
            context_low,
            log_total,
            first,
            normed,
            normed_low,
            pre_act,
            act_low,
            second,
        ) = record
        unused, pull_two = jax.vjp(layer_norm, second, gain_two, shift_two)
        grad_second, grad_gain_two, grad_shift_two = pull_two(grad_out)
        grad_branch_two = grad_second.astype(jnp.bfloat16)
        grad_bias_down = jnp.sum(grad_branch_two.astype(jnp.float32), axis=0)
        grad_w_down = matmul_left_t(act_low, grad_branch_two)
        grad_act = matmul_right_t(grad_branch_two, w_down)
        unused, pull_gelu = jax.vjp(exact_gelu, pre_act)
        grad_pre = pull_gelu(grad_act)[0].astype(jnp.bfloat16)
        grad_bias_up = jnp.sum(grad_pre.astype(jnp.float32), axis=0)
        grad_w_up = matmul_left_t(normed_low, grad_pre)
        grad_normed = grad_second + matmul_right_t(grad_pre, w_up)
        unused, pull_one = jax.vjp(layer_norm, first, gain_one, shift_one)
        grad_first, grad_gain_one, grad_shift_one = pull_one(grad_normed)
        grad_branch = grad_first.astype(jnp.bfloat16)
        grad_bias_out = jnp.sum(grad_branch.astype(jnp.float32), axis=0)
        grad_w_out = matmul_left_t(context_low, grad_branch)
        grad_context = matmul_right_t(grad_branch, w_out).astype(jnp.bfloat16)
        grad_query, grad_key, grad_value = attend_back(
            queries, keys, values, context, log_total, grad_context
        )
        grad_mixed = jnp.concatenate(
            [
                rotate(grad_query, cos_table, -sin_table),
                rotate(grad_key, cos_table, -sin_table),
                grad_value,
            ],
            axis=1,
        ).astype(jnp.bfloat16)
        grad_bias_in = jnp.sum(grad_mixed.astype(jnp.float32), axis=0)
        grad_w_in = matmul_left_t(inputs_low, grad_mixed)
        grad_hidden = grad_first + matmul_right_t(grad_mixed, w_in)
        grad_gains = jnp.concatenate([grad_gain_one, grad_gain_two])
        grad_bias = jnp.concatenate(
            [
                grad_bias_in,
                grad_bias_out,
                grad_bias_up,
                grad_bias_down,
                grad_shift_one,
                grad_shift_two,
            ]
        )
        return (grad_hidden, (grad_w_in, grad_w_out, grad_w_up, grad_w_down, grad_gains, grad_bias))

    hidden = tokens[0].astype(jnp.float32)
    records = []
    gathered = []
    for layer_index in range(layer_count):
        full = (
            lax.all_gather(attn_in[layer_index], ("seq", "row"), axis=0, tiled=True),
            lax.all_gather(attn_out[layer_index], ("seq", "row"), axis=0, tiled=True),
            lax.all_gather(ffn_up[layer_index], ("seq", "row"), axis=0, tiled=True),
            lax.all_gather(ffn_down[layer_index], ("seq", "row"), axis=0, tiled=True),
            lax.all_gather(norm_gains[layer_index], ("seq", "row"), axis=0, tiled=True),
            lax.all_gather(biases[layer_index], ("seq", "row"), axis=0, tiled=True),
            lax.all_gather(colbert, ("seq", "row"), axis=0, tiled=True),
        )
        gathered.append(full)
        (
            layer_w_in,
            layer_w_out,
            layer_w_up,
            layer_w_down,
            layer_hidden_units,
            layer_gain_one,
            layer_gain_two,
            layer_bias_in,
            layer_bias_out,
            layer_bias_up,
            layer_bias_down,
            layer_shift_one,
            layer_shift_two,
        ) = unpack(full)
        layer_inputs_low = hidden.astype(jnp.bfloat16)
        mixed = (
            jnp.dot(layer_inputs_low, layer_w_in, preferred_element_type=jnp.float32)
            + layer_bias_in
        )
        layer_queries = rotate(mixed[:, :model_width], cos_table, sin_table).astype(jnp.bfloat16)
        layer_keys = rotate(mixed[:, model_width : 2 * model_width], cos_table, sin_table).astype(
            jnp.bfloat16
        )
        layer_values = mixed[:, 2 * model_width :].astype(jnp.bfloat16)
        attend_query_three = layer_queries.reshape(local_len, HEADS, head_dim)
        attend_initial = (
            jnp.full((HEADS, local_len), NEG_FILL, jnp.float32),
            jnp.zeros((HEADS, local_len), jnp.float32),
            jnp.zeros((local_len, HEADS, head_dim), jnp.float32),
        )
        absorb_carry = attend_initial
        absorb_count, absorb_blocks, absorb_key_blocks, absorb_value_blocks, absorb_seg_blocks = (
            split_pieces(
                lax.all_gather(layer_keys, "seq", axis=0, tiled=True),
                lax.all_gather(layer_values, "seq", axis=0, tiled=True),
            )
        )

        def absorb_advance(state, item):
            run_max, run_sum, accum = state
            key_blk, value_blk, seg_blk = item
            scores = (
                jnp.einsum(
                    "qhd,khd->hqk", attend_query_three, key_blk, preferred_element_type=jnp.float32
                )
                * scale
            )
            allowed = (segment[:, None] == seg_blk[None, :])[None]
            scores = jnp.where(allowed, scores, NEG_FILL)
            new_max = jnp.maximum(run_max, jnp.max(scores, axis=-1))
            weights = jnp.where(allowed, jnp.exp(scores - new_max[..., None]), 0.0)
            factor = jnp.exp(run_max - new_max)
            run_sum = run_sum * factor + jnp.sum(weights, axis=-1)
            accum = accum * factor.T[:, :, None] + jnp.einsum(
                "hqk,khd->qhd",
                weights.astype(jnp.bfloat16),
                value_blk,
                preferred_element_type=jnp.float32,
            )
            return ((new_max, run_sum, accum), None)

        absorb_carry, absorb_unused = lax.scan(
            absorb_advance,
            absorb_carry,
            (absorb_key_blocks, absorb_value_blocks, absorb_seg_blocks),
        )
        run_max, run_sum, accum = absorb_carry
        attend_context = (accum / run_sum.T[:, :, None]).reshape(local_len, model_width)
        attend_log_total = run_max + jnp.log(run_sum)
        layer_context_low = attend_context.astype(jnp.bfloat16)
        layer_first = (
            hidden
            + jnp.dot(layer_context_low, layer_w_out, preferred_element_type=jnp.float32)
            + layer_bias_out
        )
        layer_normed = layer_norm(layer_first, layer_gain_one, layer_shift_one)
        layer_normed_low = layer_normed.astype(jnp.bfloat16)
        layer_pre_act = (
            jnp.dot(layer_normed_low, layer_w_up, preferred_element_type=jnp.float32)
            + layer_bias_up
        )
        layer_act_low = exact_gelu(layer_pre_act).astype(jnp.bfloat16)
        layer_second = (
            layer_normed
            + jnp.dot(layer_act_low, layer_w_down, preferred_element_type=jnp.float32)
            + layer_bias_down
        )
        output = layer_norm(layer_second, layer_gain_two, layer_shift_two)
        layer_record = (
            layer_inputs_low,
            layer_queries,
            layer_keys,
            layer_values,
            attend_context,
            layer_context_low,
            attend_log_total,
            layer_first,
            layer_normed,
            layer_normed_low,
            layer_pre_act,
            layer_act_low,
            layer_second,
        )
        hidden = output
        record = layer_record
        records.append(record)
    w_col = gathered[layer_count - 1][6]
    final_low = hidden.astype(jnp.bfloat16)
    col = jnp.dot(final_low, w_col, preferred_element_type=jnp.float32)
    full_width = w_col.shape[1]
    part_widths = (full_width, full_width * 3 // 4, full_width // 2)
    query_total = NQ * QLEN
    doc_total = NSD + 1
    selector = (is_query == 1)[None, :] & (
        query_slot[None, :] == jnp.arange(query_total, dtype=jnp.int32)[:, None]
    )
    selector_low = selector.astype(jnp.bfloat16)
    embeds = [unit_rows(col[:, :part_width]).astype(jnp.bfloat16) for part_width in part_widths]
    picked = (
        lax.psum(
            jnp.dot(selector_low, embeds[0], preferred_element_type=jnp.float32).astype(
                jnp.bfloat16
            ),
            "seq",
        ).astype(jnp.float32),
        lax.psum(
            jnp.dot(selector_low, embeds[1], preferred_element_type=jnp.float32).astype(
                jnp.bfloat16
            ),
            "seq",
        ).astype(jnp.float32),
        lax.psum(
            jnp.dot(selector_low, embeds[2], preferred_element_type=jnp.float32).astype(
                jnp.bfloat16
            ),
            "seq",
        ).astype(jnp.float32),
    )
    query_emb = [item.astype(jnp.bfloat16) for item in picked]
    sims = jnp.stack(
        [
            jnp.einsum(
                "qc,tc->qt", query_emb[part], embeds[part], preferred_element_type=jnp.float32
            )
            for part in range(3)
        ]
    )
    doc_mask = (
        (is_query == 0)[:, None]
        & (doc_num[:, None] == jnp.arange(doc_total, dtype=jnp.int32)[None, :])
    )[None, None]
    scaled = jnp.where(doc_mask, SHARPNESS * sims[..., None], NEG_FILL)
    part_max = jnp.max(scaled, axis=2)
    part_sum = jnp.sum(jnp.where(doc_mask, jnp.exp(scaled - part_max[:, :, None, :]), 0.0), axis=2)
    top, total = joined_2((part_max, part_sum), "seq", merge_pair)
    soft = (top + jnp.log(total)) / SHARPNESS
    pair_sum = jnp.sum(soft.reshape(3, NQ, QLEN, doc_total), axis=2)
    inverse_temp = jnp.exp(log_scale[0])
    logits = pair_sum * inverse_temp / QLEN
    positive = pairing[0][None, :, None] == jnp.arange(doc_total, dtype=jnp.int32)[None, None, :]
    losses = jax.nn.logsumexp(logits, axis=-1) - jnp.sum(jnp.where(positive, logits, 0.0), axis=-1)
    loss_weight = 1.0 / (3 * NQ * lax.axis_size("row"))
    grad_logits = loss_weight * (jax.nn.softmax(logits, axis=-1) - positive.astype(jnp.float32))
    loss_total, temp_grad = lax.psum(
        (jnp.sum(losses).reshape(1) * loss_weight, jnp.sum(grad_logits * logits).reshape(1)), "row"
    )
    grad_pairs = grad_logits * inverse_temp / QLEN
    grad_soft = jnp.broadcast_to(grad_pairs[:, :, None, :], (3, NQ, QLEN, doc_total)).reshape(
        3, query_total, doc_total
    )
    shares = jnp.where(doc_mask, jnp.exp(scaled - top[:, :, None, :]), 0.0) / total[:, :, None, :]
    grad_sims = jnp.sum(shares * grad_soft[:, :, None, :], axis=-1).astype(jnp.bfloat16)
    grad_query_emb = (
        lax.psum(
            jnp.dot(grad_sims[0], embeds[0], preferred_element_type=jnp.float32).astype(
                jnp.bfloat16
            ),
            "seq",
        ).astype(jnp.float32),
        lax.psum(
            jnp.dot(grad_sims[1], embeds[1], preferred_element_type=jnp.float32).astype(
                jnp.bfloat16
            ),
            "seq",
        ).astype(jnp.float32),
        lax.psum(
            jnp.dot(grad_sims[2], embeds[2], preferred_element_type=jnp.float32).astype(
                jnp.bfloat16
            ),
            "seq",
        ).astype(jnp.float32),
    )
    selector_f = selector.astype(jnp.float32)
    grad_col = jnp.zeros((local_len, full_width), jnp.float32)
    for part in range(3):
        part_width = part_widths[part]
        grad_embed = jnp.einsum(
            "qt,qc->tc", grad_sims[part], query_emb[part], preferred_element_type=jnp.float32
        )
        grad_embed = grad_embed + jnp.einsum(
            "qt,qc->tc",
            selector_f,
            grad_query_emb[part],
            precision=HIGHEST,
            preferred_element_type=jnp.float32,
        )
        unused, pull_unit = jax.vjp(unit_rows, col[:, :part_width])
        grad_col = grad_col.at[:, :part_width].add(pull_unit(grad_embed)[0])
    grad_col_low = grad_col.astype(jnp.bfloat16)
    grad_w_col = matmul_left_t(final_low, grad_col_low)
    grad_hidden = cotangent[0].astype(jnp.float32) + matmul_right_t(grad_col_low, w_col)
    shard_lists = [[] for unused_slot in range(6)]
    col_share = None
    for layer_index in reversed(range(layer_count)):
        full = (
            lax.all_gather(attn_in[layer_index], ("seq", "row"), axis=0, tiled=True),
            lax.all_gather(attn_out[layer_index], ("seq", "row"), axis=0, tiled=True),
            lax.all_gather(ffn_up[layer_index], ("seq", "row"), axis=0, tiled=True),
            lax.all_gather(ffn_down[layer_index], ("seq", "row"), axis=0, tiled=True),
            lax.all_gather(norm_gains[layer_index], ("seq", "row"), axis=0, tiled=True),
            lax.all_gather(biases[layer_index], ("seq", "row"), axis=0, tiled=True),
            lax.all_gather(colbert, ("seq", "row"), axis=0, tiled=True),
        )
        grad_hidden, layer_grads = layer_backward(grad_hidden, full, records[layer_index])
        col_term = grad_w_col if layer_index == layer_count - 1 else jnp.zeros_like(grad_w_col)
        shares_out = (
            lax.psum_scatter(layer_grads[0], ("seq", "row"), scatter_dimension=0, tiled=True),
            lax.psum_scatter(layer_grads[1], ("seq", "row"), scatter_dimension=0, tiled=True),
            lax.psum_scatter(layer_grads[2], ("seq", "row"), scatter_dimension=0, tiled=True),
            lax.psum_scatter(layer_grads[3], ("seq", "row"), scatter_dimension=0, tiled=True),
            lax.psum_scatter(layer_grads[4], ("seq", "row"), scatter_dimension=0, tiled=True),
            lax.psum_scatter(layer_grads[5], ("seq", "row"), scatter_dimension=0, tiled=True),
            lax.psum_scatter(col_term, ("seq", "row"), scatter_dimension=0, tiled=True),
        )
        for slot in range(6):
            shard_lists[slot].insert(0, shares_out[slot])
        if layer_index == layer_count - 1:
            col_share = shares_out[6]
    stacked = [jnp.stack(items) for items in shard_lists]
    return (
        hidden.astype(jnp.bfloat16)[None],
        loss_total,
        grad_hidden[None],
        stacked[0],
        stacked[1],
        stacked[2],
        stacked[3],
        stacked[4],
        stacked[5],
        col_share,
        temp_grad,
    )


def solution(mesh):
    placed = (
        P("row", "seq", None),
        P(None, ("seq", "row"), None),
        P(None, ("seq", "row"), None),
        P(None, ("seq", "row"), None),
        P(None, ("seq", "row"), None),
        P(None, ("seq", "row")),
        P(None, ("seq", "row")),
        P(("seq", "row"), None),
        P(),
        P("row", "seq", None),
        P("row", None),
        P("row", None),
        P("row", None),
    )
    planes = mesh.shape["row"] == 4 and mesh.shape["seq"] * 4 == 4 * PLANE and HEADS == 2 * PLANE
    return jax.shard_map(
        body if planes else body_wide,
        mesh=mesh,
        in_specs=placed,
        out_specs=(
            P("row", "seq", None),
            P(),
            P("row", "seq", None),
            P(None, ("seq", "row"), None),
            P(None, ("seq", "row"), None),
            P(None, ("seq", "row"), None),
            P(None, ("seq", "row"), None),
            P(None, ("seq", "row")),
            P(None, ("seq", "row")),
            P(("seq", "row"), None),
            P(),
        ),
        check_vma=False,
    )
```
